32 devices in a mesh: section: 4 (over y, x), dp: 8 (over z, core).
Axes of the slice: x: 2, y: 2, z: 4, core: 2. Of those that a mesh axis runs over, the one named last changes fastest.
Arguments:
- images: bfloat16 [4, 6144, 512], P(None, 'dp'), may hold values from -6 to 6
- counts: int32 [4, 8], P(None, 'dp'), may hold values from 384 to 768, as said below
- pool_index: int32 [4, 8, 192], P(None, 'dp'), may hold values from 0 to 3
- conv_w: float32 [2, 4608, 512], P(None, 'dp'), may hold values from -0.09375 to 0.09375
- squeeze_w: float32 [2, 3, 512, 128], P(None, None, 'dp'), may hold values from -0.25 to 0.25
- expand_w: float32 [2, 3, 128, 512], P(None, None, 'dp'), may hold values from -1 to 1
- gain: float32 [2, 512], replicated, may hold values from 0.25 to 1.75
- bias: float32 [2, 512], replicated, may hold values from -3 to 3
- cotangent: bfloat16 [4, 3, 1536, 512], P(None, None, 'dp'), may hold values from -6 to 6
Outputs:
- task_out: bfloat16 [4, 3, 1536, 512], P('section', None, 'dp')
- image_grad: bfloat16 [4, 6144, 512], P('section', 'dp')
- conv_grad: float32 [2, 4608, 512], P(None, 'dp')
- squeeze_grad: float32 [2, 3, 512, 128], P(None, None, 'dp')
- expand_grad: float32 [2, 3, 128, 512], P(None, None, 'dp')
- gain_grad: float32 [2, 512], replicated
- bias_grad: float32 [2, 512], replicated
The draws below stay inside these ranges and needn't reach their ends.
Inputs may be any that keep to these rules, and one draw needn't show every extreme that they name: `counts`: in every micro-batch some device has all 768 slots valid.
All inputs are finite; a program needn't handle non-finite values.
Results may differ from the reference program's by a relative error of at most 0.013.
The reference program's roundings to bfloat16 on the way count: a program that leaves them out, or rounds other values in their place, can miss the bound.
Values may be sent and summed in bfloat16 or wider, within the bound.
A program may use at most 512 MiB of HBM per device.

```python
import jax
import jax.numpy as jnp
from jax import lax

CH = 512
BOTTLE = 128
TASKS = 3
WID = 384
LAYERS = 2
MICRO = 4
PIX = 768
HEIGHT = 16
ROWS = 6144
POOLED = 1536
N_DP = 8


def draw_counts(key, part):
    key = jax.random.fold_in(key, 11)
    values = jax.random.randint(key, (MICRO, N_DP), PIX // 2, PIX + 1)
    fullest = jax.random.randint(jax.random.fold_in(key, 2), (MICRO,), 0, N_DP)
    places = jnp.arange(N_DP, dtype=jnp.int32)
    return jnp.where(places[None, :] == fullest[:, None], PIX, values).astype(jnp.int32)


def place_ends(array, rng, least, high):
    index_at = [jax.random.randint(jax.random.fold_in(rng, axis), (), 0, length) for axis, length in enumerate(array.shape)]
    main_axis = array.shape.index(max(array.shape))
    beside = index_at[:main_axis] + [(index_at[main_axis] + 1) % array.shape[main_axis]] + index_at[main_axis + 1:]
    return array.at[tuple(index_at)].set(least).at[tuple(beside)].set(high)


def steps_of(key, shape, split, smallest, largest):
    loudness = 1.0
    for position, shards_of in split:
        steps = jax.random.uniform(jax.random.fold_in(jax.random.fold_in(key, 6), position), (shards_of,), jnp.float32, smallest / len(split), largest / len(split))
        loudness = loudness * jnp.repeat(jnp.exp(steps), shape[position] // shards_of).reshape((-1,) + (1,) * (len(shape) - 1 - position))
    return loudness


def noise(key, dims, deviation, most, shards=(), kind=jnp.bfloat16):
    values = jax.random.normal(key, dims, jnp.float32) * deviation
    if len(shards) > 0:
        values = steps_of(key, dims, shards, -0.22, 0.18) * values
    return jnp.clip(values, min=-most, max=most).astype(kind)


def setup_inputs(seed: int = 0) -> dict:
    key_of = jax.random.split(jax.random.key(seed), 10)
    images = noise(key_of[0], (MICRO, ROWS, CH), 1.0, 6.0, ((1, 8),))
    counts = draw_counts(jax.random.fold_in(key_of[9], 71), 0)
    pool_index = place_ends(jax.random.randint(key_of[2], (MICRO, HEIGHT // 2, WID // 2), 0, 4), jax.random.fold_in(key_of[2], 1), 0, 3).astype(jnp.int32)
    conv_w = noise(key_of[3], (LAYERS, 9 * CH, CH), (9 * CH) ** -0.5, 0.09375, ((1, 8),), jnp.float32)
    squeeze_w = noise(key_of[4], (LAYERS, TASKS, CH, BOTTLE), CH ** -0.5, 0.25, ((2, 8),), jnp.float32)
    expand_w = noise(key_of[5], (LAYERS, TASKS, BOTTLE, CH), (BOTTLE // 4) ** -0.5, 1.0, ((2, 8),), jnp.float32)
    gain = jnp.clip(1.0 + 0.15 * jax.random.normal(key_of[6], (LAYERS, CH), jnp.float32), 0.25, 1.75)
    bias = noise(key_of[7], (LAYERS, CH), 0.5, 3.0, (), jnp.float32)
    cotangent = noise(key_of[8], (MICRO, TASKS, POOLED, CH), 1.0, 6.0, ((2, 8),))
    return {"images": images, "counts": counts, "pool_index": pool_index, "conv_w": conv_w, "squeeze_w": squeeze_w, "expand_w": expand_w, "gain": gain, "bias": bias, "cotangent": cotangent}


EPS = 1e-05

@jax.custom_vjp
def low(v):
    return lax.optimization_barrier(v.astype(jnp.bfloat16)).astype(jnp.float32)

@jax.custom_vjp
def low_back(v):
    return v

def low_keep(v):
    return (low(v), None)

def low_pass(kept, grad):
    return (grad,)

def back_keep(v):
    return (v, None)

def back_low(kept, grad):
    return (low(grad),)
low.defvjp(low_keep, low_pass)
low_back.defvjp(back_keep, back_low)

def conv_grid(field, weights):
    grid = jnp.pad(field.reshape(HEIGHT, WID, CH), ((1, 1), (1, 1), (0, 0)))
    taps = [grid[tap // 3:tap // 3 + HEIGHT, tap % 3:tap % 3 + WID].reshape(HEIGHT * WID, CH) for tap in range(9)]
    return jnp.dot(jnp.concatenate(taps, 1), weights, precision=lax.Precision.HIGHEST)

def conv_block(field, keep, weights, norm_scale, beta):
    hidden = low_back(conv_grid(field, weights))
    mask_count = jnp.sum(keep)
    centre = lax.optimization_barrier(jnp.sum(keep * hidden, 0)) / mask_count
    spread = lax.optimization_barrier(jnp.sum(keep * hidden * hidden, 0)) / mask_count - centre * centre
    normed = norm_scale * (hidden - centre) * lax.rsqrt(spread + EPS) + beta
    return low(keep * jax.nn.gelu(normed))

def gate_apply(source, feature, keep, squeeze_mat, expand_mat):
    squeezed = low_back(jnp.dot(low(source), squeeze_mat, precision=lax.Precision.HIGHEST))
    expanded = low_back(jnp.dot(low(jax.nn.gelu(squeezed)), expand_mat, precision=lax.Precision.HIGHEST))
    return keep * jax.nn.sigmoid(expanded) * feature

def pool_pick(field, picks):
    windows = field.reshape(HEIGHT // 2, 2, WID // 2, 2, CH)
    picked = jnp.zeros((HEIGHT // 2, WID // 2, CH), field.dtype)
    for corner in range(4):
        picked = picked + jnp.where((picks == corner)[:, :, None], windows[:, corner // 2, :, corner % 2, :], 0.0)
    return picked.reshape(POOLED, CH)

def reference(images, counts, pool_index, conv_w, squeeze_w, expand_w, gain, bias, cotangent):
    slots = jnp.arange(PIX, dtype=jnp.int32)
    valid_mask = (slots[None, None, :] < counts[:, :, None]).astype(jnp.float32).reshape(MICRO, ROWS, 1)

    def forward(inputs, conv_all, squeeze_all, expand_all, gains, biases):
        conv_low, squeeze_low, expand_low = (low(conv_all), low(squeeze_all), low(expand_all))
        results = []
        for micro_idx in range(MICRO):
            keep = valid_mask[micro_idx]
            first = conv_block(keep * inputs[micro_idx], keep, conv_low[0], gains[0], biases[0])
            first_b = low_back(first)
            task_first = [low_back(low(gate_apply(first_b, first_b, keep, squeeze_low[0, task], expand_low[0, task]))) for task in range(TASKS)]
            second = conv_block(low_back(first_b), keep, conv_low[1], gains[1], biases[1])
            second_b = low_back(second)
            pooled = [pool_pick(gate_apply(second_b + task_first[task], second_b, keep, squeeze_low[1, task], expand_low[1, task]), pool_index[micro_idx]) for task in range(TASKS)]
            results.append(jnp.stack(pooled))
        return jnp.stack(results)
    output, pullback = jax.vjp(forward, images.astype(jnp.float32), conv_w, squeeze_w, expand_w, gain, bias)
    grads = pullback(cotangent.astype(jnp.float32))
    return (output.astype(jnp.bfloat16), grads[0].astype(jnp.bfloat16), grads[1], grads[2], grads[3], grads[4], grads[5])
```

```python
import jax
import jax.numpy as jnp
from jax import lax
from jax.sharding import PartitionSpec as P

EPS = 1e-05
BF16 = jnp.bfloat16
F32 = jnp.float32


def gelu_back(point, upstream):
    return jax.vjp(jax.nn.gelu, point)[1](upstream)[0]


def with_halo(value, axis):
    size = lax.axis_size(axis)
    up = [(i, i + 1) for i in range(size - 1)]
    down = [(j, i) for i, j in up]
    before = lax.ppermute(value[-1:], axis, up)
    after = lax.ppermute(value[:1], axis, down)
    return jnp.concatenate([before, value, after], axis=0)


def conv(padded, taps):
    out = lax.conv_general_dilated(
        padded[None],
        taps,
        (1, 1),
        ((0, 0), (1, 1)),
        dimension_numbers=("NHWC", "HWIO", "NHWC"),
        preferred_element_type=F32,
    )
    return out.reshape(-1, out.shape[-1])


def conv_input_grad(d_padded, taps):
    out = lax.conv_general_dilated(
        d_padded[None],
        taps[::-1, ::-1],
        (1, 1),
        ((0, 0), (1, 1)),
        dimension_numbers=("NHWC", "HWOI", "NHWC"),
        preferred_element_type=F32,
    )
    return out.reshape(-1, out.shape[-1])


def conv_weight_grad(padded, d_hidden):
    out = lax.conv_general_dilated(
        padded[None],
        d_hidden[None],
        (1, 1),
        ((0, 0), (1, 1)),
        dimension_numbers=("CHWN", "IHWO", "HWNC"),
        preferred_element_type=F32,
    )
    return out.reshape(-1, out.shape[-1])


def gate_forward(source, w_squeeze, w_expand):
    squeezed = jnp.einsum("tpc,tcb->tpb", source, w_squeeze, preferred_element_type=F32)
    excited = jax.nn.gelu(squeezed).astype(BF16)
    expanded = jnp.einsum("tpb,tbc->tpc", excited, w_expand, preferred_element_type=F32)
    return squeezed, excited, jax.nn.sigmoid(expanded)


def gate_backward(d_task, field, source, squeezed, excited, gate_val, w_squeeze, w_expand):
    d_expanded = (d_task * field[None] * gate_val * (1.0 - gate_val)).astype(BF16)
    d_excited = jnp.einsum("tpc,tbc->tpb", d_expanded, w_expand, preferred_element_type=F32)
    d_squeezed = gelu_back(squeezed, d_excited).astype(BF16)
    d_source = jnp.einsum("tpb,tcb->tpc", d_squeezed, w_squeeze, preferred_element_type=F32)
    grad_squeeze = jnp.einsum("tpc,tpb->tcb", source, d_squeezed, preferred_element_type=F32)
    grad_expand = jnp.einsum("tpb,tpc->tbc", excited, d_expanded, preferred_element_type=F32)
    return d_source, grad_squeeze, grad_expand


def pool_pick(field, pick):
    tasks, _, width = field.shape
    half_rows, half_columns = pick.shape
    windows = field.reshape(tasks, half_rows, 2, half_columns, 2, width)
    picked = jnp.zeros((tasks, half_rows, half_columns, width), F32)
    for corner in range(4):
        hit = (pick == corner)[None, :, :, None]
        picked = picked + jnp.where(hit, windows[:, :, corner // 2, :, corner % 2, :], 0.0)
    return picked.reshape(tasks, half_rows * half_columns, width)


def pool_spread(d_pooled, pick):
    tasks, _, width = d_pooled.shape
    half_rows, half_columns = pick.shape
    grid = d_pooled.reshape(tasks, half_rows, half_columns, width)
    rows = [
        jnp.stack(
            [jnp.where((pick == 2 * dy + dx)[None, :, :, None], grid, 0.0) for dx in range(2)], 3
        )
        for dy in range(2)
    ]
    return jnp.stack(rows, 2).reshape(tasks, half_rows * 2 * half_columns * 2, width)


def on_device(images, counts, pool_index, conv_w, squeeze_w, expand_w, gain, bias, cotangent):
    sections = lax.axis_size("section")
    here = lax.axis_index("section")
    micro, pixels, width = images.shape
    layers = conv_w.shape[0]
    tasks = squeeze_w.shape[1]
    rows = 2 * pool_index.shape[1]
    columns = 2 * pool_index.shape[2]
    share = micro // sections

    def own(value):
        return lax.dynamic_slice_in_dim(value, here * share, share, 0)

    images, counts, pool_index, cotangent = (
        own(images),
        own(counts),
        own(pool_index),
        own(cotangent),
    )

    def gather(value, axis):
        return lax.all_gather(value.astype(BF16), "dp", axis=axis, tiled=True)

    taps = [gather(conv_w[l], 0).reshape(3, 3, width, width) for l in range(layers)]
    w_squeeze = [gather(squeeze_w[l], 1) for l in range(layers)]
    w_expand = [gather(expand_w[l], 1) for l in range(layers)]
    slots = jnp.arange(pixels, dtype=jnp.int32)[:, None]

    def block_forward(field, mask, total, layer):
        padded = with_halo(field.reshape(rows, columns, width), "dp")
        hidden = conv(padded, taps[layer])
        sums = lax.psum(
            jnp.stack([jnp.sum(mask * hidden, 0), jnp.sum(mask * hidden * hidden, 0)]), "dp"
        )
        centre = sums[0] / total
        inverse = lax.rsqrt(sums[1] / total - centre * centre + EPS)
        normed = gain[layer] * (hidden - centre) * inverse + bias[layer]
        out = (mask * jax.nn.gelu(normed)).astype(BF16)
        return out, (padded, hidden, centre, inverse)

    def block_backward(d_out, kept, mask, total, layer):
        padded, hidden, centre, inverse = kept
        centred = (hidden - centre) * inverse
        normed = gain[layer] * (hidden - centre) * inverse + bias[layer]
        d_norm = gelu_back(normed, mask * d_out)
        gain_sum = jnp.sum(d_norm * centred, 0)
        bias_sum = jnp.sum(d_norm, 0)
        sums = gain[layer] * lax.psum(jnp.stack([bias_sum, gain_sum]), "dp")
        d_hidden = (
            mask * inverse * (gain[layer] * d_norm - sums[0] / total - centred * sums[1] / total)
        ).astype(BF16)
        d_hidden = d_hidden.reshape(rows, columns, width)
        d_x = conv_input_grad(with_halo(d_hidden, "dp"), taps[layer])
        return d_x, conv_weight_grad(padded, d_hidden), gain_sum, bias_sum

    outs, image_grads = [], []
    grads = None
    totals = lax.psum(counts[:, 0], "dp").astype(F32)
    for m in range(share):
        total = totals[m]
        mask = (slots < counts[m, 0]).astype(F32)
        first_in = jnp.where(slots < counts[m, 0], images[m], jnp.zeros((), BF16))
        f1, kept_0 = block_forward(first_in, mask, total, 0)
        f1_f = f1.astype(F32)
        source_0 = jnp.broadcast_to(f1[None], (tasks, pixels, width))
        squeezed_0, excited_0, gate_0 = gate_forward(source_0, w_squeeze[0], w_expand[0])
        t1 = (mask[None] * gate_0 * f1_f[None]).astype(BF16)
        f2, kept_1 = block_forward(f1, mask, total, 1)
        f2_f = f2.astype(F32)
        source_1 = (f2_f[None] + t1.astype(F32)).astype(BF16)
        squeezed_1, excited_1, gate_1 = gate_forward(source_1, w_squeeze[1], w_expand[1])
        outs.append(pool_pick(mask[None] * gate_1 * f2_f[None], pool_index[m]).astype(BF16))

        d_task = pool_spread(cotangent[m].astype(F32), pool_index[m])
        d_source, gs_1, ge_1 = gate_backward(
            d_task, mask * f2_f, source_1, squeezed_1, excited_1, gate_1, w_squeeze[1], w_expand[1]
        )
        d_f2 = (jnp.sum(d_source, 0) + mask * jnp.sum(d_task * gate_1, 0)).astype(BF16)
        d_t1 = d_source.astype(BF16).astype(F32)
        d_x1, gc_1, gain_1, bias_1 = block_backward(d_f2.astype(F32), kept_1, mask, total, 1)
        d_source, gs_0, ge_0 = gate_backward(
            d_t1, mask * f1_f, source_0, squeezed_0, excited_0, gate_0, w_squeeze[0], w_expand[0]
        )
        d_f1 = (
            d_x1.astype(BF16).astype(F32)
            + jnp.sum(d_source, 0)
            + mask * jnp.sum(d_t1 * gate_0, 0)
        ).astype(BF16)
        d_x0, gc_0, gain_0, bias_0 = block_backward(d_f1.astype(F32), kept_0, mask, total, 0)
        image_grads.append((mask * d_x0).astype(BF16))
        here_grads = [
            [gc_0, gc_1],
            [gs_0, gs_1],
            [ge_0, ge_1],
            jnp.stack([gain_0, gain_1]),
            jnp.stack([bias_0, bias_1]),
        ]
        grads = here_grads if grads is None else jax.tree.map(jnp.add, grads, here_grads)

    def reduced(value, axis):
        part = lax.psum_scatter(value, "dp", scatter_dimension=axis, tiled=True)
        return lax.psum(part.astype(BF16), "section").astype(F32)

    conv_grad = jnp.stack([reduced(g, 0) for g in grads[0]])
    squeeze_grad = jnp.stack([reduced(g, 1) for g in grads[1]])
    expand_grad = jnp.stack([reduced(g, 1) for g in grads[2]])
    gain_grad, bias_grad = lax.psum((grads[3], grads[4]), ("section", "dp"))
    return (
        jnp.stack(outs),
        jnp.stack(image_grads),
        conv_grad,
        squeeze_grad,
        expand_grad,
        gain_grad,
        bias_grad,
    )


def solution(mesh):
    placed = (
        P(None, "dp", None),
        P(None, "dp"),
        P(None, "dp", None),
        P(None, "dp", None),
        P(None, None, "dp", None),
        P(None, None, "dp", None),
        P(),
        P(),
        P(None, None, "dp", None),
    )
    return jax.shard_map(
        on_device,
        mesh=mesh,
        in_specs=placed,
        out_specs=(
            P("section", None, "dp", None),
            P("section", "dp", None),
            P(None, "dp", None),
            P(None, None, "dp", None),
            P(None, None, "dp", None),
            P(),
            P(),
        ),
        check_vma=False,
    )
```

```python
import functools
import types

import jax
import jax.numpy as jnp
from jax import lax
from jax.experimental import pallas as pl
from jax.experimental.pallas import tpu as pltpu
from jax.sharding import PartitionSpec as P

EPS = 1e-05
BF16 = jnp.bfloat16
F32 = jnp.float32
VMEM_BYTES = 62 * 1024 * 1024


def gelu_back(point, upstream):
    return jax.vjp(jax.nn.gelu, point)[1](upstream)[0]


def with_halo(value, axis):
    size = lax.axis_size(axis)
    up = [(i, i + 1) for i in range(size - 1)]
    down = [(j, i) for i, j in up]
    before = lax.ppermute(value[-1:], axis, up)
    after = lax.ppermute(value[:1], axis, down)
    return jnp.concatenate([before, value, after], axis=0)


def conv(padded, taps):
    out = lax.conv_general_dilated(
        padded[None],
        taps,
        (1, 1),
        ((0, 0), (1, 1)),
        dimension_numbers=("NHWC", "HWIO", "NHWC"),
        preferred_element_type=F32,
    )
    return out.reshape(-1, out.shape[-1])


def conv_input_grad(d_padded, taps):
    out = lax.conv_general_dilated(
        d_padded[None],
        taps[::-1, ::-1],
        (1, 1),
        ((0, 0), (1, 1)),
        dimension_numbers=("NHWC", "HWOI", "NHWC"),
        preferred_element_type=F32,
    )
    return out.reshape(-1, out.shape[-1])


def conv_weight_grad(padded, d_hidden):
    out = lax.conv_general_dilated(
        padded[None],
        d_hidden[None],
        (1, 1),
        ((0, 0), (1, 1)),
        dimension_numbers=("CHWN", "IHWO", "HWNC"),
        preferred_element_type=F32,
    )
    return out.reshape(-1, out.shape[-1])


def gate_forward(source, w_squeeze, w_expand):
    squeezed = jnp.einsum("tpc,tcb->tpb", source, w_squeeze, preferred_element_type=F32)
    excited = jax.nn.gelu(squeezed).astype(BF16)
    expanded = jnp.einsum("tpb,tbc->tpc", excited, w_expand, preferred_element_type=F32)
    return squeezed, excited, jax.nn.sigmoid(expanded)


def gate_backward(d_task, field, source, squeezed, excited, gate_val, w_squeeze, w_expand):
    d_expanded = (d_task * field[None] * gate_val * (1.0 - gate_val)).astype(BF16)
    d_excited = jnp.einsum("tpc,tbc->tpb", d_expanded, w_expand, preferred_element_type=F32)
    d_squeezed = gelu_back(squeezed, d_excited).astype(BF16)
    d_source = jnp.einsum("tpb,tcb->tpc", d_squeezed, w_squeeze, preferred_element_type=F32)
    grad_squeeze = jnp.einsum("tpc,tpb->tcb", source, d_squeezed, preferred_element_type=F32)
    grad_expand = jnp.einsum("tpb,tpc->tbc", excited, d_expanded, preferred_element_type=F32)
    return d_source, grad_squeeze, grad_expand


def pool_pick(field, pick):
    tasks, _, width = field.shape
    half_rows, half_columns = pick.shape
    windows = field.reshape(tasks, half_rows, 2, half_columns, 2, width)
    picked = jnp.zeros((tasks, half_rows, half_columns, width), F32)
    for corner in range(4):
        hit = (pick == corner)[None, :, :, None]
        picked = picked + jnp.where(hit, windows[:, :, corner // 2, :, corner % 2, :], 0.0)
    return picked.reshape(tasks, half_rows * half_columns, width)


def pool_spread(d_pooled, pick):
    tasks, _, width = d_pooled.shape
    half_rows, half_columns = pick.shape
    grid = d_pooled.reshape(tasks, half_rows, half_columns, width)
    rows = [
        jnp.stack(
            [jnp.where((pick == 2 * dy + dx)[None, :, :, None], grid, 0.0) for dx in range(2)], 3
        )
        for dy in range(2)
    ]
    return jnp.stack(rows, 2).reshape(tasks, half_rows * 2 * half_columns * 2, width)


def on_device(images, counts, pool_index, conv_w, squeeze_w, expand_w, gain, bias, cotangent):
    sections = lax.axis_size("section")
    here = lax.axis_index("section")
    micro, pixels, width = images.shape
    layers = conv_w.shape[0]
    tasks = squeeze_w.shape[1]
    rows = 2 * pool_index.shape[1]
    columns = 2 * pool_index.shape[2]
    share = micro // sections

    def own(value):
        return lax.dynamic_slice_in_dim(value, here * share, share, 0)

    images, counts, pool_index, cotangent = (
        own(images),
        own(counts),
        own(pool_index),
        own(cotangent),
    )

    def gather(value, axis):
        return lax.all_gather(value.astype(BF16), "dp", axis=axis, tiled=True)

    taps = [gather(conv_w[l], 0).reshape(3, 3, width, width) for l in range(layers)]
    w_squeeze = [gather(squeeze_w[l], 1) for l in range(layers)]
    w_expand = [gather(expand_w[l], 1) for l in range(layers)]
    slots = jnp.arange(pixels, dtype=jnp.int32)[:, None]

    def block_forward(field, mask, total, layer):
        padded = with_halo(field.reshape(rows, columns, width), "dp")
        hidden = conv(padded, taps[layer])
        sums = lax.psum(
            jnp.stack([jnp.sum(mask * hidden, 0), jnp.sum(mask * hidden * hidden, 0)]), "dp"
        )
        centre = sums[0] / total
        inverse = lax.rsqrt(sums[1] / total - centre * centre + EPS)
        normed = gain[layer] * (hidden - centre) * inverse + bias[layer]
        out = (mask * jax.nn.gelu(normed)).astype(BF16)
        return out, (padded, hidden, centre, inverse)

    def block_backward(d_out, kept, mask, total, layer):
        padded, hidden, centre, inverse = kept
        centred = (hidden - centre) * inverse
        normed = gain[layer] * (hidden - centre) * inverse + bias[layer]
        d_norm = gelu_back(normed, mask * d_out)
        gain_sum = jnp.sum(d_norm * centred, 0)
        bias_sum = jnp.sum(d_norm, 0)
        sums = gain[layer] * lax.psum(jnp.stack([bias_sum, gain_sum]), "dp")
        d_hidden = (
            mask * inverse * (gain[layer] * d_norm - sums[0] / total - centred * sums[1] / total)
        ).astype(BF16)
        d_hidden = d_hidden.reshape(rows, columns, width)
        d_x = conv_input_grad(with_halo(d_hidden, "dp"), taps[layer])
        return d_x, conv_weight_grad(padded, d_hidden), gain_sum, bias_sum

    outs, image_grads = [], []
    grads = None
    totals = lax.psum(counts[:, 0], "dp").astype(F32)
    for m in range(share):
        total = totals[m]
        mask = (slots < counts[m, 0]).astype(F32)
        first_in = jnp.where(slots < counts[m, 0], images[m], jnp.zeros((), BF16))
        f1, kept_0 = block_forward(first_in, mask, total, 0)
        f1_f = f1.astype(F32)
        source_0 = jnp.broadcast_to(f1[None], (tasks, pixels, width))
        squeezed_0, excited_0, gate_0 = gate_forward(source_0, w_squeeze[0], w_expand[0])
        t1 = (mask[None] * gate_0 * f1_f[None]).astype(BF16)
        f2, kept_1 = block_forward(f1, mask, total, 1)
        f2_f = f2.astype(F32)
        source_1 = (f2_f[None] + t1.astype(F32)).astype(BF16)
        squeezed_1, excited_1, gate_1 = gate_forward(source_1, w_squeeze[1], w_expand[1])
        outs.append(pool_pick(mask[None] * gate_1 * f2_f[None], pool_index[m]).astype(BF16))

        d_task = pool_spread(cotangent[m].astype(F32), pool_index[m])
        d_source, gs_1, ge_1 = gate_backward(
            d_task, mask * f2_f, source_1, squeezed_1, excited_1, gate_1, w_squeeze[1], w_expand[1]
        )
        d_f2 = (jnp.sum(d_source, 0) + mask * jnp.sum(d_task * gate_1, 0)).astype(BF16)
        d_t1 = d_source.astype(BF16).astype(F32)
        d_x1, gc_1, gain_1, bias_1 = block_backward(d_f2.astype(F32), kept_1, mask, total, 1)
        d_source, gs_0, ge_0 = gate_backward(
            d_t1, mask * f1_f, source_0, squeezed_0, excited_0, gate_0, w_squeeze[0], w_expand[0]
        )
        d_f1 = (
            d_x1.astype(BF16).astype(F32)
            + jnp.sum(d_source, 0)
            + mask * jnp.sum(d_t1 * gate_0, 0)
        ).astype(BF16)
        d_x0, gc_0, gain_0, bias_0 = block_backward(d_f1.astype(F32), kept_0, mask, total, 0)
        image_grads.append((mask * d_x0).astype(BF16))
        here_grads = [
            [gc_0, gc_1],
            [gs_0, gs_1],
            [ge_0, ge_1],
            jnp.stack([gain_0, gain_1]),
            jnp.stack([bias_0, bias_1]),
        ]
        grads = here_grads if grads is None else jax.tree.map(jnp.add, grads, here_grads)

    def reduced(value, axis):
        part = lax.psum_scatter(value, "dp", scatter_dimension=axis, tiled=True)
        return lax.psum(part.astype(BF16), "section").astype(F32)

    conv_grad = jnp.stack([reduced(g, 0) for g in grads[0]])
    squeeze_grad = jnp.stack([reduced(g, 1) for g in grads[1]])
    expand_grad = jnp.stack([reduced(g, 1) for g in grads[2]])
    gain_grad, bias_grad = lax.psum((grads[3], grads[4]), ("section", "dp"))
    return (
        jnp.stack(outs),
        jnp.stack(image_grads),
        conv_grad,
        squeeze_grad,
        expand_grad,
        gain_grad,
        bias_grad,
    )


GELU_C = 0.7978845608028654
GELU_K = 0.044715
MESH = pl.DeviceIdType.MESH


def gelu_pair(x):
    square = x * x
    t = jnp.tanh(GELU_C * x * (1.0 + GELU_K * square))
    half = 0.5 * (1.0 + t)
    slope = half + 0.5 * x * (1.0 - t * t) * (GELU_C * (1.0 + 3.0 * GELU_K * square))
    return x * half, slope


def dot(a, b):
    return jnp.dot(a, b, preferred_element_type=F32)


def dot_nt(a, b):
    return lax.dot_general(a, b, (((1,), (1,)), ((), ())), preferred_element_type=F32)


def dot_tn(a, b):
    return lax.dot_general(a, b, (((0,), (0,)), ((), ())), preferred_element_type=F32)


def step_kernel(
    dims,
    counts,
    pick_ref,
    gain,
    bias,
    images,
    conv_w,
    squeeze_w,
    expand_w,
    cotangent,
    out_task,
    out_image,
    out_conv,
    out_squeeze,
    out_expand,
    out_gain,
    out_bias,
    *scratch,
):
    r = types.SimpleNamespace(**jax.tree.unflatten(dims.tree, scratch))
    n_dp, cols, pixels, width, tasks, bottle = (
        dims.n_dp,
        dims.cols,
        dims.pixels,
        dims.width,
        dims.tasks,
        dims.bottle,
    )
    n_z = n_dp // 2
    windows = cols // 2
    lanes = 128
    n_lane = width // lanes
    shard_rows = dims.shard_rows
    s = lax.axis_index("section")
    d = lax.axis_index("dp")
    z, c = d // 2, d % 2
    sib = 2 * z + 1 - c
    plane = [s + 1 - 2 * (s % 2), (s + 2) % 4, 3 - s]

    def rem(a, b):
        return lax.rem(a, b)

    def z_at(step):
        return rem(z + step, n_z)

    def remote(src, dst, send, recv, device):
        return pltpu.make_async_remote_copy(
            src_ref=src,
            dst_ref=dst,
            send_sem=send,
            recv_sem=recv,
            device_id=device,
            device_id_type=MESH,
        )

    def al(v, m):
        return pl.multiple_of(v, m)

    barrier = pltpu.get_barrier_semaphore()
    for step in range(1, n_dp):
        pl.semaphore_signal(
            barrier, inc=1, device_id=(s, rem(d + step, n_dp)), device_id_type=MESH
        )
    for p in plane:
        pl.semaphore_signal(barrier, inc=1, device_id=(p, d), device_id_type=MESH)

    def load(i, src, dst):
        return pltpu.make_async_copy(src, dst, r.load.at[i])

    staging = [r.h1, r.slope0]
    conv_rows = shard_rows[0]

    def conv_load(layer, j):
        lane = slice(j * lanes, (j + 1) * lanes)
        return load(
            5 + layer * n_lane + j,
            conv_w.at[layer, :, lane],
            staging[layer].at[j, 0:conv_rows],
        )

    loads = [
        load(1, squeeze_w, r.sst),
        load(2, expand_w, r.est),
        load(3, images.at[s], r.xin),
        load(4, cotangent.at[s], r.cin),
    ]
    for j in range(n_lane):
        conv_load(0, j).start()
    for item in loads[:2]:
        item.start()
    for j in range(n_lane):
        conv_load(1, j).start()
    for item in loads[2:]:
        item.start()

    full = [r.w0, r.gp, r.w1]

    def shard(kind, buf, which):
        rows = shard_rows[kind]
        return buf.at[pl.ds(al(which * rows, 16), rows)]

    def quarter(kind, buf, which, q):
        rows = shard_rows[kind]
        return buf.at[pl.ds(al(which * rows + q * (rows // 4), 16), rows // 4)]

    def ag_z_copy(kind, step, owner):
        view = quarter(kind, full[kind], owner, s)
        return remote(
            view,
            view,
            r.ag_zs.at[kind, step - 1],
            r.ag_zr.at[kind, step - 1],
            (s, 2 * z_at(step) + c),
        )

    def ag_p_copy(kind, step, p, q):
        owner = 2 * z_at(n_z - step) + c
        view = quarter(kind, full[kind], owner, q)
        i = (step - 1) * 3 + p
        return remote(view, view, r.ag_ps.at[kind, i], r.ag_pr.at[kind, i], (plane[p], d))

    def ag_s_copy(kind, step, core):
        view = shard(kind, full[kind], 2 * z_at(n_z - step if step else 0) + core)
        return remote(view, view, r.ag_ss.at[kind, step], r.ag_sr.at[kind, step], (s, sib))

    def ag_start(kind):
        for step in range(1, n_z):
            ag_z_copy(kind, step, d).start()
        ag_s_copy(kind, 0, c).start()

    def ag_z(kind, step):
        owner = 2 * z_at(n_z - step) + c
        ag_z_copy(kind, step, owner).wait_recv()
        for p in range(3):
            ag_p_copy(kind, step, p, s).start()

    def ag_p(kind, step):
        for p in range(3):
            ag_p_copy(kind, step, p, plane[p]).wait_recv()
        ag_s_copy(kind, step, c).start()

    def ag_sib(kind):
        for step in range(n_z):
            ag_s_copy(kind, step, 1 - c).wait_recv()

    def ag_end(kind):
        for step in range(1, n_z):
            ag_z_copy(kind, step, d).wait_send()
            for p in range(3):
                ag_p_copy(kind, step, p, s).wait_send()
        for step in range(n_z):
            ag_s_copy(kind, step, c).wait_send()

    def cast_conv(layer, buf):
        for j in range(n_lane):
            conv_load(layer, j).wait()

        def body(j, _):
            buf[pl.ds(al(d * conv_rows, 16), conv_rows), pl.ds(al(j * lanes, lanes), lanes)] = (
                staging[layer][j, 0:conv_rows, :].astype(BF16)
            )
            return 0

        lax.fori_loop(0, n_lane, body, 0)

    g_rows = shard_rows[1]
    e_rows = n_ex = bottle // n_dp
    s_rows = width // n_dp
    n_sub = s_rows // e_rows

    def ex_row(which, l, t):
        return al(which * g_rows + (l * tasks + t) * e_rows, 16)

    def sq_row(which, l, t):
        return al(which * g_rows + (2 * tasks + l * tasks + t) * e_rows, 16)

    cast_conv(0, r.w0)
    pl.semaphore_wait(barrier, n_dp - 1 + 3)
    ag_start(0)
    loads[0].wait()
    loads[1].wait()
    for l in range(2):
        for t in range(tasks):
            r.gp[pl.ds(ex_row(d, l, t), e_rows), :] = r.est[l, t].astype(BF16)
            for k in range(n_sub):
                r.gp[pl.ds(sq_row(d, l, t), e_rows), k * lanes : (k + 1) * lanes] = r.sst[
                    l, t, k * e_rows : (k + 1) * e_rows, :
                ].astype(BF16)
    ag_start(1)
    cast_conv(1, r.w1)
    ag_start(2)

    count = counts[s, 0]
    pick_tile = pick_ref[...]
    slot_pick = (
        (pick_tile // 2) * cols
        + 2 * lax.broadcasted_iota(jnp.int32, (windows, lanes), 0)
        + pick_tile % 2
    )
    r.mp[...] = jnp.where(slot_pick < count, 1.0, 0.0).astype(F32)

    def lane_at(j, base=0):
        return pl.ds(al(base + j * lanes, lanes), lanes)

    def valid_rows(start, rows):
        return (lax.broadcasted_iota(jnp.int32, (rows, lanes), 0) + start) < count

    def shift_in(value_of, buf, block):
        def body(j, _):
            v = value_of(j)
            at = lax.broadcasted_iota(jnp.int32, (cols, lanes), 0)
            before = jnp.where(at == 0, 0.0, pltpu.roll(v, 1, 0))
            after = jnp.where(at == cols - 1, 0.0, pltpu.roll(v, cols - 1, 0))
            rows = pl.ds(block * cols, cols)
            buf[rows, lane_at(j)] = before.astype(BF16)
            buf[rows, lane_at(j, width)] = v.astype(BF16)
            buf[rows, lane_at(j, 2 * width)] = after.astype(BF16)
            return 0

        lax.fori_loop(0, n_lane, body, 0)

    @pl.when(d == 0)
    def _():
        r.halo[:, 0] = jnp.zeros_like(r.halo[:, 0])

    @pl.when(d == n_dp - 1)
    def _():
        r.halo[:, 1] = jnp.zeros_like(r.halo[:, 1])

    def halo_down(e, buf):
        return remote(
            buf.at[2 * cols : 3 * cols, width : 2 * width],
            r.halo.at[e, 0],
            r.halo_s.at[e, 0],
            r.halo_r.at[e, 0],
            (s, rem(d + 1, n_dp)),
        )

    def halo_up(e, buf):
        return remote(
            buf.at[cols : 2 * cols, width : 2 * width],
            r.halo.at[e, 1],
            r.halo_s.at[e, 1],
            r.halo_r.at[e, 1],
            (s, rem(d + n_dp - 1, n_dp)),
        )

    def halo_start(e, buf):
        @pl.when(d < n_dp - 1)
        def _():
            halo_down(e, buf).start()

        @pl.when(d > 0)
        def _():
            halo_up(e, buf).start()

    def halo_finish(e, buf):
        @pl.when(d > 0)
        def _():
            halo_down(e, buf).wait_recv()

        @pl.when(d < n_dp - 1)
        def _():
            halo_up(e, buf).wait_recv()

        shift_in(lambda j: r.halo[e, 0, :, lane_at(j)].astype(F32), buf, 0)
        shift_in(lambda j: r.halo[e, 1, :, lane_at(j)].astype(F32), buf, 3)

    def halo_sent(e, buf):
        @pl.when(d < n_dp - 1)
        def _():
            halo_down(e, buf).wait_send()

        @pl.when(d > 0)
        def _():
            halo_up(e, buf).wait_send()

    def ex_copy(k, step, owner):
        return remote(
            r.ex_out.at[k],
            r.ex_in.at[k, owner],
            r.ex_s.at[k, step - 1],
            r.ex_r.at[k, step - 1],
            (s, rem(d + step, n_dp)),
        )

    def ex_start(k):
        for step in range(1, n_dp):
            ex_copy(k, step, d).start()
        r.ex_in[k, d] = r.ex_out[k]

    def ex_finish(k):
        for step in range(1, n_dp):
            ex_copy(k, step, rem(d + n_dp - step, n_dp)).wait_recv()
        total = r.ex_in[k, 0]
        for i in range(1, n_dp):
            total = total + r.ex_in[k, i]
        return total

    def conv_forward(xc, w, h):
        span = 3 * width
        half = width // 2
        for n in range(2):
            acc = None
            for a in range(3):
                term = dot(
                    xc[a * cols : a * cols + pixels, :],
                    w[a * span : (a + 1) * span, n * half : (n + 1) * half],
                )
                acc = term if acc is None else acc + term
            for j in range(n_lane // 2):
                h[n * (n_lane // 2) + j] = acc[:, j * lanes : (j + 1) * lanes]

    def conv_back(dc, w):
        acc = None
        for a in range(3):
            for b in range(3):
                term = dot_nt(
                    dc[(2 - a) * cols : (2 - a) * cols + pixels, (2 - b) * width : (3 - b) * width],
                    w[(3 * a + b) * width : (3 * a + b + 1) * width, :],
                )
                acc = term if acc is None else acc + term
        for j in range(n_lane):
            r.fbuf[j] = acc[:, j * lanes : (j + 1) * lanes]

    quarter_rows = pixels // 4

    def stats(h, k):
        def body(j, _):
            first = jnp.zeros((1, lanes), F32)
            second = jnp.zeros((1, lanes), F32)
            for i in range(4):
                v = h[j, i * quarter_rows : (i + 1) * quarter_rows, :]
                kept = jnp.where(valid_rows(i * quarter_rows, quarter_rows), v, 0.0)
                first = first + jnp.sum(kept, 0, keepdims=True)
                second = second + jnp.sum(kept * v, 0, keepdims=True)
            r.ex_out[k, 0:1, lane_at(j)] = first
            r.ex_out[k, 1:2, lane_at(j)] = second
            return 0

        r.ex_out[k] = jnp.broadcast_to(count.astype(F32), (8, width))
        lax.fori_loop(0, n_lane, body, 0)

    def norm_of(sums, layer):
        total = sums[2:3, :]
        centre = sums[0:1, :] / total
        inverse = lax.rsqrt(sums[1:2, :] / total - centre * centre + EPS)
        r.norm[layer, 0:1, :] = centre
        r.norm[layer, 1:2, :] = inverse
        r.norm[layer, 2:3, :] = gain[layer : layer + 1, :] * inverse
        r.norm[layer, 3:4, :] = 1.0 / total

    def corner_rows(k):
        return pl.ds((k // 2) * cols + k % 2, windows, stride=2)

    def picked(ref, j):
        out = None
        which = pick_ref[...]
        for k in range(4):
            part = jnp.where(which == k, ref[j, corner_rows(k), :], 0.0)
            out = part if out is None else out + part
        return out

    loads[2].wait()

    def image_row(i):
        def value(j):
            v = r.xin[i * cols : (i + 1) * cols, lane_at(j)].astype(F32)
            return jnp.where(valid_rows(i * cols, cols), v, 0.0)

        return value

    shift_in(image_row(0), r.xc0, 1)
    shift_in(image_row(1), r.xc0, 2)
    halo_start(0, r.xc0)
    for step in range(1, n_z):
        ag_z(0, step)
    halo_finish(0, r.xc0)
    for step in range(1, n_z):
        ag_z(1, step)
    for step in range(1, n_z):
        ag_p(0, step)
        ag_z(2, step)
    ag_sib(0)

    conv_forward(r.xc0, r.w0, r.h0)
    stats(r.h0, 0)
    ex_start(0)
    for step in range(1, n_z):
        ag_p(1, step)
    norm_of(ex_finish(0), 0)

    def block_0(j, _):
        lane = lane_at(j)
        for i in range(4):
            rows = slice(i * quarter_rows, (i + 1) * quarter_rows)
            normed = (r.h0[j, rows, :] - r.norm[0, 0:1, lane]) * r.norm[
                0, 2:3, lane
            ] + bias[0:1, lane]
            g, slope = gelu_pair(normed)
            ok = valid_rows(i * quarter_rows, quarter_rows)
            r.fbuf[j, rows, :] = jnp.where(ok, g, 0.0).astype(BF16).astype(F32)
            r.slope0[j, rows, :] = jnp.where(ok, slope, 0.0)
        f1p = picked(r.fbuf, j)
        r.f1p[:, lane] = f1p
        r.f1b[:, lane] = f1p.astype(BF16)
        return 0

    lax.fori_loop(0, n_lane, block_0, 0)
    shift_in(lambda j: r.fbuf[j, 0:cols, :], r.xc1, 1)
    shift_in(lambda j: r.fbuf[j, cols : 2 * cols, :], r.xc1, 2)
    halo_start(1, r.xc1)
    ag_sib(1)

    def unpack(i, _):
        for l in range(2):
            for t in range(tasks):
                r.ex_w[l, t, pl.ds(al(i * e_rows, 16), e_rows), :] = r.gp[
                    pl.ds(ex_row(i, l, t), e_rows), :
                ]
                for k in range(n_sub):
                    r.sq_w[
                        l,
                        pl.ds(al(i * s_rows + k * e_rows, 16), e_rows),
                        t * bottle : (t + 1) * bottle,
                    ] = r.gp[pl.ds(sq_row(i, l, t), e_rows), k * lanes : (k + 1) * lanes]
        return 0

    lax.fori_loop(0, n_dp, unpack, 0)
    mask_pick = jnp.concatenate([r.mp[...]] * n_lane, axis=1)
    g, slope = gelu_pair(dot(r.f1b[...], r.sq_w[0]))
    r.excited0[...] = g.astype(BF16)
    r.eslope0[...] = slope

    def task_lane(t):
        return pl.ds(al(t * bottle, lanes), bottle)

    def gate_0(t, _):
        value = jax.nn.sigmoid(dot(r.excited0[:, task_lane(t)], r.ex_w[0, t]))
        r.gate0[t] = value
        r.t1[t] = (mask_pick * value * r.f1p[...]).astype(BF16)
        return 0

    lax.fori_loop(0, tasks, gate_0, 0)
    halo_finish(1, r.xc1)
    for step in range(1, n_z):
        ag_p(2, step)
    ag_sib(2)

    conv_forward(r.xc1, r.w1, r.h1)
    stats(r.h1, 1)
    ex_start(1)
    for kind in range(3):
        ag_end(kind)
    norm_of(ex_finish(1), 1)

    def block_1(j, _):
        lane = lane_at(j)
        off = picked(r.h1, j) - r.norm[1, 0:1, lane]
        g, slope = gelu_pair(off * r.norm[1, 2:3, lane] + bias[1:2, lane])
        r.f2p[:, lane] = (r.mp[...] * g).astype(BF16).astype(F32)
        r.slope1[:, lane] = r.mp[...] * slope
        r.centred1[:, lane] = off * r.norm[1, 1:2, lane]
        return 0

    lax.fori_loop(0, n_lane, block_1, 0)
    loads[3].wait()
    r.df2[...] = jnp.zeros_like(r.df2)

    def pack_grads(l, t, grad_squeeze, grad_expand):
        r.gs_st[...] = grad_squeeze
        r.ge_st[...] = grad_expand

        def body(i, _):
            r.gp[pl.ds(ex_row(i, l, t), e_rows), :] = r.ge_st[
                pl.ds(al(i * e_rows, 16), e_rows), :
            ].astype(BF16)
            for k in range(n_sub):
                r.gp[pl.ds(sq_row(i, l, t), e_rows), k * lanes : (k + 1) * lanes] = r.gs_st[
                    pl.ds(al(i * s_rows + k * e_rows, 16), e_rows), :
                ].astype(BF16)
            return 0

        lax.fori_loop(0, n_dp, body, 0)

    def gate_1(t, _):
        w_s = r.sq_w[1, :, task_lane(t)]
        w_e = r.ex_w[1, t]
        f2p = r.f2p[...]
        source = (f2p + r.t1[t].astype(F32)).astype(BF16)
        g, slope = gelu_pair(dot(source, w_s))
        excited = g.astype(BF16)
        value = jax.nn.sigmoid(dot(excited, w_e))
        field = mask_pick * f2p
        d_task = r.cin[t].astype(F32)
        r.cin[t] = (value * field).astype(BF16)
        d_expanded = (d_task * field * value * (1.0 - value)).astype(BF16)
        d_squeezed = (slope * dot_nt(d_expanded, w_e)).astype(BF16)
        d_source = dot_nt(d_squeezed, w_s)
        r.t1[t] = d_source.astype(BF16)
        r.df2[...] += d_source + mask_pick * d_task * value
        pack_grads(1, t, dot_tn(source, d_squeezed), dot_tn(excited, d_expanded))
        return 0

    lax.fori_loop(0, tasks, gate_1, 0)
    task_store = pltpu.make_async_copy(r.cin, out_task.at[0], r.store.at[0])
    task_store.start()

    def back_1(j, _):
        lane = lane_at(j)
        d_norm = r.slope1[:, lane] * r.df2[:, lane].astype(BF16).astype(F32)
        r.df2[:, lane] = d_norm
        r.ex_out[2, 0:1, lane] = jnp.sum(d_norm, 0, keepdims=True)
        r.ex_out[2, 1:2, lane] = jnp.sum(d_norm * r.centred1[:, lane], 0, keepdims=True)
        return 0

    r.ex_out[2] = jnp.zeros((8, width), F32)
    lax.fori_loop(0, n_lane, back_1, 0)
    ex_start(2)

    r.df1[...] = jnp.zeros_like(r.df1)

    def gate_0_back(t, _):
        w_s = r.sq_w[0, :, task_lane(t)]
        w_e = r.ex_w[0, t]
        value = r.gate0[t]
        d_task = r.t1[t].astype(F32)
        excited = r.excited0[:, task_lane(t)]
        d_expanded = (d_task * (mask_pick * r.f1p[...]) * value * (1.0 - value)).astype(BF16)
        d_squeezed = (r.eslope0[:, task_lane(t)] * dot_nt(d_expanded, w_e)).astype(BF16)
        r.df1[...] += dot_nt(d_squeezed, w_s) + mask_pick * d_task * value
        pack_grads(0, t, dot_tn(r.f1b[...], d_squeezed), dot_tn(excited, d_expanded))
        return 0

    lax.fori_loop(0, tasks, gate_0_back, 0)

    r.sums[...] = jnp.zeros_like(r.sums)

    def back_terms(k, layer):
        sums = ex_finish(k)
        r.sums[2 * layer : 2 * layer + 2, :] = sums[0:2, :]
        scale = gain[layer : layer + 1, :] * r.norm[layer, 3:4, :] * r.norm[layer, 1:2, :]
        r.norm[layer, 4:5, :] = scale * sums[0:1, :]
        r.norm[layer, 5:6, :] = scale * r.norm[layer, 1:2, :] * sums[1:2, :]

    back_terms(2, 1)

    def hidden_grad_1(j, _):
        lane = lane_at(j)
        norm = r.norm
        for k in range(4):
            at = corner_rows(k)
            spread = jnp.where(pick_ref[...] == k, r.df2[:, lane] * norm[1, 2:3, lane], 0.0)
            value = spread - (
                norm[1, 4:5, lane] + (r.h1[j, at, :] - norm[1, 0:1, lane]) * norm[1, 5:6, lane]
            )
            slot = (k // 2) * cols + k % 2 + 2 * lax.broadcasted_iota(
                jnp.int32, (windows, lanes), 0
            )
            r.fbuf[j, at, :] = jnp.where(slot < count, value, 0.0)
        return 0

    lax.fori_loop(0, n_lane, hidden_grad_1, 0)
    shift_in(lambda j: r.fbuf[j, 0:cols, :], r.dc, 1)
    shift_in(lambda j: r.fbuf[j, cols : 2 * cols, :], r.dc, 2)
    halo_start(2, r.dc)

    grads = [r.w1, r.gp, r.g1]

    def pair_of(k):
        return z_at(1 + k)

    def rs_a_copy(kind, k, core):
        return remote(
            shard(kind, grads[kind], 2 * pair_of(k) + core),
            r.ra[kind].at[k],
            r.rs_as.at[kind, k],
            r.rs_ar.at[kind, k],
            (s, sib),
        )

    def rs_b_copy(kind, k, p):
        return remote(
            quarter(kind, grads[kind], 2 * pair_of(k) + c, plane[p]),
            r.rb[kind].at[p, k],
            r.rs_bs.at[kind, k, p],
            r.rs_br.at[kind, k, p],
            (plane[p], d),
        )

    def rs_c_copy(kind, k):
        return remote(
            r.qs[kind].at[k],
            r.rc[kind].at[k],
            r.rs_cs.at[kind, k],
            r.rs_cr.at[kind, k],
            (s, 2 * pair_of(k) + c),
        )

    def rs_d_copy(kind, p, q):
        rows = shard_rows[kind] // 4
        view = r.td[kind].at[pl.ds(al(q * rows, 16), rows)]
        return remote(view, view, r.rs_ds.at[kind, p], r.rs_dr.at[kind, p], (plane[p], d))

    def conv_weight(kind, xc, k):
        tile = 2 * shard_rows[kind] // 3
        per = 3 * width // tile

        def body(i, _):
            g = pair_of(k) * 3 + i
            a = g // per
            term = dot_tn(
                xc[pl.ds(al(a * cols, 16), pixels), pl.ds(al((g % per) * tile, lanes), tile)],
                r.dc[cols : 3 * cols, width : 2 * width],
            )
            grads[kind][pl.ds(al(g * tile, 16), tile), :] = term.astype(BF16)
            return 0

        lax.fori_loop(0, 3, body, 0)

    def rs_a(kind, k):
        rs_a_copy(kind, k, 1 - c).start()

    def rs_b(kind, k):
        rs_a_copy(kind, k, c).wait_recv()
        rows = shard_rows[kind]
        tile = rows // 4
        start = (2 * pair_of(k) + c) * rows

        def body(i, _):
            at = pl.ds(al(start + i * tile, 16), tile)
            grads[kind][at, :] = (
                grads[kind][at, :].astype(F32)
                + r.ra[kind][k, pl.ds(al(i * tile, 16), tile), :].astype(F32)
            ).astype(BF16)
            return 0

        lax.fori_loop(0, 4, body, 0)
        for p in range(3):
            rs_b_copy(kind, k, p).start()

    def rs_c(kind, k):
        for p in range(3):
            rs_b_copy(kind, k, p).wait_recv()
        rows = shard_rows[kind] // 4
        at = pl.ds(al((2 * pair_of(k) + c) * shard_rows[kind] + s * rows, 16), rows)
        total = grads[kind][at, :].astype(F32)
        for p in range(3):
            total = total + r.rb[kind][p, k].astype(F32)
        if k < n_z - 1:
            r.qs[kind][k] = total.astype(BF16)
            rs_c_copy(kind, k).start()
        else:
            r.qf[kind][...] = total

    def rs_d(kind):
        total = r.qf[kind][...]
        for k in range(n_z - 1):
            rs_c_copy(kind, k).wait_recv()
            total = total + r.rc[kind][k].astype(F32)
        rows = shard_rows[kind] // 4
        r.td[kind][pl.ds(al(s * rows, 16), rows), :] = total.astype(BF16)
        for p in range(3):
            rs_d_copy(kind, p, s).start()

    def rs_e(kind):
        for p in range(3):
            rs_d_copy(kind, p, plane[p]).wait_recv()

    def rs_end(kind):
        for k in range(n_z):
            rs_a_copy(kind, k, 1 - c).wait_send()
            for p in range(3):
                rs_b_copy(kind, k, p).wait_send()
            if k < n_z - 1:
                rs_c_copy(kind, k).wait_send()
        for p in range(3):
            rs_d_copy(kind, p, s).wait_send()

    for k in range(n_z):
        conv_weight(2, r.xc1, k)
        rs_a(2, k)
        if k > 0:
            rs_b(2, k - 1)
    rs_b(2, n_z - 1)
    for k in range(n_z):
        rs_a(1, k)

    halo_finish(2, r.dc)
    conv_back(r.dc, r.w1)
    halo_sent(2, r.dc)
    for k in range(n_z):
        rs_b(1, k)

    def back_0(j, _):
        lane = lane_at(j)
        norm = r.norm
        first = jnp.zeros((1, lanes), F32)
        second = jnp.zeros((1, lanes), F32)
        for k in range(4):
            at = corner_rows(k)
            d_field = r.fbuf[j, at, :].astype(BF16).astype(F32) + jnp.where(
                pick_ref[...] == k, r.df1[:, lane], 0.0
            )
            d_norm = r.slope0[j, at, :] * d_field.astype(BF16).astype(F32)
            r.fbuf[j, at, :] = d_norm
            centred = (r.h0[j, at, :] - norm[0, 0:1, lane]) * norm[0, 1:2, lane]
            first = first + jnp.sum(d_norm, 0, keepdims=True)
            second = second + jnp.sum(d_norm * centred, 0, keepdims=True)
        r.ex_out[3, 0:1, lane] = first
        r.ex_out[3, 1:2, lane] = second
        return 0

    r.ex_out[3] = jnp.zeros((8, width), F32)
    lax.fori_loop(0, n_lane, back_0, 0)
    ex_start(3)
    for k in range(n_z):
        rs_c(2, k)
    back_terms(3, 0)

    def sums_copy(p, q):
        return remote(
            r.sums,
            r.sums_in.at[q],
            r.sums_s.at[p],
            r.sums_r.at[p],
            (plane[p], d),
        )

    for p in range(3):
        sums_copy(p, s).start()
    r.sums_in[s] = r.sums[...]

    def hidden_grad_0(row):
        def value(j):
            lane = lane_at(j)
            norm = r.norm
            rows = slice(row * cols, (row + 1) * cols)
            out = r.fbuf[j, rows, :] * norm[0, 2:3, lane] - (
                norm[0, 4:5, lane] + (r.h0[j, rows, :] - norm[0, 0:1, lane]) * norm[0, 5:6, lane]
            )
            return jnp.where(valid_rows(row * cols, cols), out, 0.0)

        return value

    shift_in(hidden_grad_0(0), r.dc, 1)
    shift_in(hidden_grad_0(1), r.dc, 2)
    halo_start(3, r.dc)
    for k in range(n_z):
        conv_weight(0, r.xc0, k)
        rs_a(0, k)
        if k > 0:
            rs_b(0, k - 1)
    rs_b(0, n_z - 1)
    for k in range(n_z):
        rs_c(1, k)
    rs_d(2)
    rs_d(1)

    halo_finish(3, r.dc)
    conv_back(r.dc, r.w0)

    def image_out(j, _):
        lane = lane_at(j)
        for i in range(4):
            rows = slice(i * quarter_rows, (i + 1) * quarter_rows)
            r.xin[rows, lane] = jnp.where(
                valid_rows(i * quarter_rows, quarter_rows), r.fbuf[j, rows, :], 0.0
            ).astype(BF16)
        return 0

    lax.fori_loop(0, n_lane, image_out, 0)
    image_store = pltpu.make_async_copy(r.xin, out_image.at[0], r.store.at[1])
    image_store.start()

    for k in range(n_z):
        rs_c(0, k)

    def conv_out(kind, layer, i):
        rs_e(kind)
        copies = []
        for j in range(n_lane):
            lane = slice(j * lanes, (j + 1) * lanes)
            staging[layer][j, 0:conv_rows, :] = r.td[kind][:, lane].astype(F32)
            copies.append(
                pltpu.make_async_copy(
                    staging[layer].at[j, 0:conv_rows],
                    out_conv.at[layer, :, lane],
                    r.store.at[i + j],
                )
            )
            copies[-1].start()
        return copies

    conv_store_1 = conv_out(2, 1, 4)
    rs_e(1)
    for l in range(2):
        for t in range(tasks):
            at = (l * tasks + t) * e_rows
            r.est[l, t] = r.td[1][at : at + e_rows, :].astype(F32)
            at = at + 2 * tasks * e_rows
            for k in range(n_sub):
                r.sst[l, t, k * e_rows : (k + 1) * e_rows, :] = r.td[1][
                    at : at + e_rows, k * lanes : (k + 1) * lanes
                ].astype(F32)
    squeeze_store = pltpu.make_async_copy(r.sst, out_squeeze, r.store.at[2])
    expand_store = pltpu.make_async_copy(r.est, out_expand, r.store.at[3])
    squeeze_store.start()
    expand_store.start()
    for p in range(3):
        sums_copy(p, plane[p]).wait_recv()
    total = r.sums_in[0]
    for i in range(1, 4):
        total = total + r.sums_in[i]
    for l in range(2):
        out_bias[l : l + 1, :] = total[2 * l : 2 * l + 1, :]
        out_gain[l : l + 1, :] = total[2 * l + 1 : 2 * l + 2, :]
    rs_d(0)
    conv_store_0 = conv_out(0, 0, 4 + n_lane)
    for kind in range(3):
        rs_end(kind)
    for p in range(3):
        sums_copy(p, s).wait_send()
    for k in range(4):
        for step in range(1, n_dp):
            ex_copy(k, step, d).wait_send()
    halo_sent(0, r.xc0)
    halo_sent(1, r.xc1)
    halo_sent(3, r.dc)
    for copy in (
        task_store,
        image_store,
        squeeze_store,
        expand_store,
        *conv_store_1,
        *conv_store_0,
    ):
        copy.wait()


def fused(images, counts, pool_index, conv_w, squeeze_w, expand_w, gain, bias, cotangent):
    n_dp = lax.axis_size("dp")
    here = lax.axis_index("section")
    micro, pixels, width = images.shape
    tasks, bottle = squeeze_w.shape[1], squeeze_w.shape[3]
    cols = 2 * pool_index.shape[2]
    windows = cols // 2
    own_pick = lax.dynamic_index_in_dim(pool_index, here, 0, keepdims=False)
    pick = jnp.broadcast_to(own_pick.reshape(windows, 1), (windows, 128))
    conv_rows = conv_w.shape[1]
    gate_rows = 4 * tasks * expand_w.shape[2]
    shard_rows = (conv_rows, gate_rows, conv_rows)
    n_z = n_dp // 2
    vm = pltpu.VMEM
    dma = pltpu.SemaphoreType.DMA
    scratch = dict(
        load=dma((5 + 2 * (width // 128),)),
        store=dma((4 + 2 * (width // 128),)),
        sst=vm(squeeze_w.shape, F32),
        est=vm(expand_w.shape, F32),
        xin=vm((pixels, width), BF16),
        cin=vm((tasks, windows, width), BF16),
        w0=vm((n_dp * conv_rows, width), BF16),
        gp=vm((n_dp * gate_rows, width), BF16),
        w1=vm((n_dp * conv_rows, width), BF16),
        g1=vm((n_dp * conv_rows, width), BF16),
        sq_w=vm((2, width, tasks * bottle), BF16),
        ex_w=vm((2, tasks, bottle, width), BF16),
        ag_zs=dma((3, n_z - 1)),
        ag_zr=dma((3, n_z - 1)),
        ag_ps=dma((3, 3 * (n_z - 1))),
        ag_pr=dma((3, 3 * (n_z - 1))),
        ag_ss=dma((3, n_z)),
        ag_sr=dma((3, n_z)),
        mp=vm((windows, 128), F32),
        halo=vm((4, 2, cols, width), BF16),
        halo_s=dma((4, 2)),
        halo_r=dma((4, 2)),
        ex_out=vm((4, 8, width), F32),
        ex_in=vm((4, n_dp, 8, width), F32),
        ex_s=dma((4, n_dp - 1)),
        ex_r=dma((4, n_dp - 1)),
        norm=vm((2, 8, width), F32),
        xc0=vm((4 * cols, 3 * width), BF16),
        xc1=vm((4 * cols, 3 * width), BF16),
        dc=vm((4 * cols, 3 * width), BF16),
        h0=vm((width // 128, pixels, 128), F32),
        h1=vm((width // 128, pixels, 128), F32),
        slope0=vm((width // 128, pixels, 128), F32),
        fbuf=vm((width // 128, pixels, 128), F32),
        f1p=vm((windows, width), F32),
        f1b=vm((windows, width), BF16),
        excited0=vm((windows, tasks * bottle), BF16),
        eslope0=vm((windows, tasks * bottle), F32),
        gate0=vm((tasks, windows, width), F32),
        t1=vm((tasks, windows, width), BF16),
        f2p=vm((windows, width), F32),
        slope1=vm((windows, width), F32),
        centred1=vm((windows, width), F32),
        df2=vm((windows, width), F32),
        df1=vm((windows, width), F32),
        gs_st=vm((width, bottle), F32),
        ge_st=vm((bottle, width), F32),
        sums=vm((8, width), F32),
        sums_in=vm((4, 8, width), F32),
        sums_s=dma((3,)),
        sums_r=dma((3,)),
        rs_as=dma((3, n_z)),
        rs_ar=dma((3, n_z)),
        rs_bs=dma((3, n_z, 3)),
        rs_br=dma((3, n_z, 3)),
        rs_cs=dma((3, n_z - 1)),
        rs_cr=dma((3, n_z - 1)),
        rs_ds=dma((3, 3)),
        rs_dr=dma((3, 3)),
    )
    quarters = [rows // 4 for rows in shard_rows]
    scratch.update(
        ra=[vm((n_z, rows, width), BF16) for rows in shard_rows],
        rb=[vm((3, n_z, rows, width), BF16) for rows in quarters],
        qs=[vm((n_z - 1, rows, width), BF16) for rows in quarters],
        qf=[vm((rows, width), F32) for rows in quarters],
        rc=[vm((n_z - 1, rows, width), BF16) for rows in quarters],
        td=[vm((rows, width), BF16) for rows in shard_rows],
    )
    buffers, tree = jax.tree.flatten(scratch, is_leaf=lambda v: not isinstance(v, (dict, list)))
    dims = types.SimpleNamespace(
        tree=tree,
        n_dp=n_dp,
        cols=cols,
        pixels=pixels,
        width=width,
        tasks=tasks,
        bottle=bottle,
        shard_rows=shard_rows,
    )
    any_spec = pl.BlockSpec(memory_space=pl.ANY)
    vmem_spec = pl.BlockSpec(memory_space=pltpu.VMEM)
    smem_spec = pl.BlockSpec(memory_space=pltpu.SMEM)
    return pl.pallas_call(
        functools.partial(step_kernel, dims),
        out_shape=(
            jax.ShapeDtypeStruct((1, tasks, windows, width), BF16),
            jax.ShapeDtypeStruct((1, pixels, width), BF16),
            jax.ShapeDtypeStruct(conv_w.shape, F32),
            jax.ShapeDtypeStruct(squeeze_w.shape, F32),
            jax.ShapeDtypeStruct(expand_w.shape, F32),
            jax.ShapeDtypeStruct(gain.shape, F32),
            jax.ShapeDtypeStruct(bias.shape, F32),
        ),
        in_specs=[smem_spec, vmem_spec, vmem_spec, vmem_spec] + [any_spec] * 5,
        out_specs=(any_spec,) * 5 + (vmem_spec,) * 2,
        scratch_shapes=tuple(buffers),
        compiler_params=pltpu.CompilerParams(
            collective_id=0, has_side_effects=True, vmem_limit_bytes=VMEM_BYTES
        ),
    )(counts, pick, gain, bias, images, conv_w, squeeze_w, expand_w, cotangent)


def fits_kernel(mesh, args):
    images, counts, pool_index, conv_w, squeeze_w, expand_w = args[:6]
    sections, n_dp = mesh.shape["section"], mesh.shape["dp"]
    conv_rows = conv_w.shape[1] // n_dp
    e_rows = expand_w.shape[2] // n_dp
    return (
        sections == 4
        and images.shape[0] == sections
        and n_dp % 2 == 0
        and pool_index.shape[1] == n_dp
        and conv_rows % 64 == 0
        and e_rows == 16
        and squeeze_w.shape[2] // n_dp == 4 * e_rows
        and squeeze_w.shape[3] == 128
        and images.shape[2] == 4 * 128
    )


def solution(mesh):
    placed = (
        P(None, "dp", None),
        P(None, "dp"),
        P(None, "dp", None),
        P(None, "dp", None),
        P(None, None, "dp", None),
        P(None, None, "dp", None),
        P(),
        P(),
        P(None, None, "dp", None),
    )
    def run(*args):
        return mapped(fused if fits_kernel(mesh, args) else on_device)(*args)

    def mapped(body):
        return jax.shard_map(
        body,
        mesh=mesh,
        in_specs=placed,
        out_specs=(
            P("section", None, "dp", None),
            P("section", "dp", None),
            P(None, "dp", None),
            P(None, None, "dp", None),
            P(None, None, "dp", None),
            P(),
            P(),
        ),
        check_vma=False,
    )

    return run
```

```python
import functools
import types

import jax
import jax.numpy as jnp
from jax import lax
from jax.experimental import pallas as pl
from jax.experimental.pallas import tpu as pltpu
from jax.sharding import PartitionSpec as P

EPS = 1e-05
BF16 = jnp.bfloat16
F32 = jnp.float32
VMEM_BYTES = 62 * 1024 * 1024


def gelu_back(point, upstream):
    return jax.vjp(jax.nn.gelu, point)[1](upstream)[0]


def with_halo(value, axis):
    size = lax.axis_size(axis)
    up = [(i, i + 1) for i in range(size - 1)]
    down = [(j, i) for i, j in up]
    before = lax.ppermute(value[-1:], axis, up)
    after = lax.ppermute(value[:1], axis, down)
    return jnp.concatenate([before, value, after], axis=0)


def conv(padded, taps):
    out = lax.conv_general_dilated(
        padded[None],
        taps,
        (1, 1),
        ((0, 0), (1, 1)),
        dimension_numbers=("NHWC", "HWIO", "NHWC"),
        preferred_element_type=F32,
    )
    return out.reshape(-1, out.shape[-1])


def conv_input_grad(d_padded, taps):
    out = lax.conv_general_dilated(
        d_padded[None],
        taps[::-1, ::-1],
        (1, 1),
        ((0, 0), (1, 1)),
        dimension_numbers=("NHWC", "HWOI", "NHWC"),
        preferred_element_type=F32,
    )
    return out.reshape(-1, out.shape[-1])


def conv_weight_grad(padded, d_hidden):
    out = lax.conv_general_dilated(
        padded[None],
        d_hidden[None],
        (1, 1),
        ((0, 0), (1, 1)),
        dimension_numbers=("CHWN", "IHWO", "HWNC"),
        preferred_element_type=F32,
    )
    return out.reshape(-1, out.shape[-1])


def gate_forward(source, w_squeeze, w_expand):
    squeezed = jnp.einsum("tpc,tcb->tpb", source, w_squeeze, preferred_element_type=F32)
    excited = jax.nn.gelu(squeezed).astype(BF16)
    expanded = jnp.einsum("tpb,tbc->tpc", excited, w_expand, preferred_element_type=F32)
    return squeezed, excited, jax.nn.sigmoid(expanded)


def gate_backward(d_task, field, source, squeezed, excited, gate_val, w_squeeze, w_expand):
    d_expanded = (d_task * field[None] * gate_val * (1.0 - gate_val)).astype(BF16)
    d_excited = jnp.einsum("tpc,tbc->tpb", d_expanded, w_expand, preferred_element_type=F32)
    d_squeezed = gelu_back(squeezed, d_excited).astype(BF16)
    d_source = jnp.einsum("tpb,tcb->tpc", d_squeezed, w_squeeze, preferred_element_type=F32)
    grad_squeeze = jnp.einsum("tpc,tpb->tcb", source, d_squeezed, preferred_element_type=F32)
    grad_expand = jnp.einsum("tpb,tpc->tbc", excited, d_expanded, preferred_element_type=F32)
    return d_source, grad_squeeze, grad_expand


def pool_pick(field, pick):
    tasks, _, width = field.shape
    half_rows, half_columns = pick.shape
    windows = field.reshape(tasks, half_rows, 2, half_columns, 2, width)
    picked = jnp.zeros((tasks, half_rows, half_columns, width), F32)
    for corner in range(4):
        hit = (pick == corner)[None, :, :, None]
        picked = picked + jnp.where(hit, windows[:, :, corner // 2, :, corner % 2, :], 0.0)
    return picked.reshape(tasks, half_rows * half_columns, width)


def pool_spread(d_pooled, pick):
    tasks, _, width = d_pooled.shape
    half_rows, half_columns = pick.shape
    grid = d_pooled.reshape(tasks, half_rows, half_columns, width)
    rows = [
        jnp.stack(
            [jnp.where((pick == 2 * dy + dx)[None, :, :, None], grid, 0.0) for dx in range(2)], 3
        )
        for dy in range(2)
    ]
    return jnp.stack(rows, 2).reshape(tasks, half_rows * 2 * half_columns * 2, width)


def on_device(images, counts, pool_index, conv_w, squeeze_w, expand_w, gain, bias, cotangent):
    sections = lax.axis_size("section")
    here = lax.axis_index("section")
    micro, pixels, width = images.shape
    layers = conv_w.shape[0]
    tasks = squeeze_w.shape[1]
    rows = 2 * pool_index.shape[1]
    columns = 2 * pool_index.shape[2]
    share = micro // sections

    def own(value):
        return lax.dynamic_slice_in_dim(value, here * share, share, 0)

    images, counts, pool_index, cotangent = (
        own(images),
        own(counts),
        own(pool_index),
        own(cotangent),
    )

    def gather(value, axis):
        return lax.all_gather(value.astype(BF16), "dp", axis=axis, tiled=True)

    taps = [gather(conv_w[l], 0).reshape(3, 3, width, width) for l in range(layers)]
    w_squeeze = [gather(squeeze_w[l], 1) for l in range(layers)]
    w_expand = [gather(expand_w[l], 1) for l in range(layers)]
    slots = jnp.arange(pixels, dtype=jnp.int32)[:, None]

    def block_forward(field, mask, total, layer):
        padded = with_halo(field.reshape(rows, columns, width), "dp")
        hidden = conv(padded, taps[layer])
        sums = lax.psum(
            jnp.stack([jnp.sum(mask * hidden, 0), jnp.sum(mask * hidden * hidden, 0)]), "dp"
        )
        centre = sums[0] / total
        inverse = lax.rsqrt(sums[1] / total - centre * centre + EPS)
        normed = gain[layer] * (hidden - centre) * inverse + bias[layer]
        out = (mask * jax.nn.gelu(normed)).astype(BF16)
        return out, (padded, hidden, centre, inverse)

    def block_backward(d_out, kept, mask, total, layer):
        padded, hidden, centre, inverse = kept
        centred = (hidden - centre) * inverse
        normed = gain[layer] * (hidden - centre) * inverse + bias[layer]
        d_norm = gelu_back(normed, mask * d_out)
        gain_sum = jnp.sum(d_norm * centred, 0)
        bias_sum = jnp.sum(d_norm, 0)
        sums = gain[layer] * lax.psum(jnp.stack([bias_sum, gain_sum]), "dp")
        d_hidden = (
            mask * inverse * (gain[layer] * d_norm - sums[0] / total - centred * sums[1] / total)
        ).astype(BF16)
        d_hidden = d_hidden.reshape(rows, columns, width)
        d_x = conv_input_grad(with_halo(d_hidden, "dp"), taps[layer])
        return d_x, conv_weight_grad(padded, d_hidden), gain_sum, bias_sum

    outs, image_grads = [], []
    grads = None
    totals = lax.psum(counts[:, 0], "dp").astype(F32)
    for m in range(share):
        total = totals[m]
        mask = (slots < counts[m, 0]).astype(F32)
        first_in = jnp.where(slots < counts[m, 0], images[m], jnp.zeros((), BF16))
        f1, kept_0 = block_forward(first_in, mask, total, 0)
        f1_f = f1.astype(F32)
        source_0 = jnp.broadcast_to(f1[None], (tasks, pixels, width))
        squeezed_0, excited_0, gate_0 = gate_forward(source_0, w_squeeze[0], w_expand[0])
        t1 = (mask[None] * gate_0 * f1_f[None]).astype(BF16)
        f2, kept_1 = block_forward(f1, mask, total, 1)
        f2_f = f2.astype(F32)
        source_1 = (f2_f[None] + t1.astype(F32)).astype(BF16)
        squeezed_1, excited_1, gate_1 = gate_forward(source_1, w_squeeze[1], w_expand[1])
        outs.append(pool_pick(mask[None] * gate_1 * f2_f[None], pool_index[m]).astype(BF16))

        d_task = pool_spread(cotangent[m].astype(F32), pool_index[m])
        d_source, gs_1, ge_1 = gate_backward(
            d_task, mask * f2_f, source_1, squeezed_1, excited_1, gate_1, w_squeeze[1], w_expand[1]
        )
        d_f2 = (jnp.sum(d_source, 0) + mask * jnp.sum(d_task * gate_1, 0)).astype(BF16)
        d_t1 = d_source.astype(BF16).astype(F32)
        d_x1, gc_1, gain_1, bias_1 = block_backward(d_f2.astype(F32), kept_1, mask, total, 1)
        d_source, gs_0, ge_0 = gate_backward(
            d_t1, mask * f1_f, source_0, squeezed_0, excited_0, gate_0, w_squeeze[0], w_expand[0]
        )
        d_f1 = (
            d_x1.astype(BF16).astype(F32)
            + jnp.sum(d_source, 0)
            + mask * jnp.sum(d_t1 * gate_0, 0)
        ).astype(BF16)
        d_x0, gc_0, gain_0, bias_0 = block_backward(d_f1.astype(F32), kept_0, mask, total, 0)
        image_grads.append((mask * d_x0).astype(BF16))
        here_grads = [
            [gc_0, gc_1],
            [gs_0, gs_1],
            [ge_0, ge_1],
            jnp.stack([gain_0, gain_1]),
            jnp.stack([bias_0, bias_1]),
        ]
        grads = here_grads if grads is None else jax.tree.map(jnp.add, grads, here_grads)

    def reduced(value, axis):
        part = lax.psum_scatter(value, "dp", scatter_dimension=axis, tiled=True)
        return lax.psum(part.astype(BF16), "section").astype(F32)

    conv_grad = jnp.stack([reduced(g, 0) for g in grads[0]])
    squeeze_grad = jnp.stack([reduced(g, 1) for g in grads[1]])
    expand_grad = jnp.stack([reduced(g, 1) for g in grads[2]])
    gain_grad, bias_grad = lax.psum((grads[3], grads[4]), ("section", "dp"))
    return (
        jnp.stack(outs),
        jnp.stack(image_grads),
        conv_grad,
        squeeze_grad,
        expand_grad,
        gain_grad,
        bias_grad,
    )


GELU_C = 0.7978845608028654
GELU_K = 0.044715
MESH = pl.DeviceIdType.MESH


def gelu_pair(x):
    square = x * x
    t = jnp.tanh(GELU_C * x * (1.0 + GELU_K * square))
    half = 0.5 * (1.0 + t)
    slope = half + 0.5 * x * (1.0 - t * t) * (GELU_C * (1.0 + 3.0 * GELU_K * square))
    return x * half, slope


def dot(a, b):
    return jnp.dot(a, b, preferred_element_type=F32)


def dot_nt(a, b):
    return lax.dot_general(a, b, (((1,), (1,)), ((), ())), preferred_element_type=F32)


def dot_tn(a, b):
    return lax.dot_general(a, b, (((0,), (0,)), ((), ())), preferred_element_type=F32)


def step_kernel(
    dims,
    counts,
    picks,
    gain,
    bias,
    images,
    conv_w,
    squeeze_w,
    expand_w,
    cotangent,
    out_task,
    out_image,
    out_reduced_0,
    out_reduced_1,
    out_reduced_2,
    out_gain,
    out_bias,
    *scratch,
):
    out_reduced = (out_reduced_0, out_reduced_1, out_reduced_2)
    r = types.SimpleNamespace(**jax.tree.unflatten(dims.tree, scratch))
    n_dp, cols, pixels, width, tasks, bottle = (
        dims.n_dp,
        dims.cols,
        dims.pixels,
        dims.width,
        dims.tasks,
        dims.bottle,
    )
    n_z = n_dp // 2
    windows = cols // 2
    lanes = 128
    n_lane = width // lanes
    shard_rows = dims.shard_rows
    s = lax.axis_index("section")
    d = lax.axis_index("dp")
    z, c = d // 2, d % 2
    sib = 2 * z + 1 - c
    plane = [s + 1 - 2 * (s % 2), (s + 2) % 4, 3 - s]

    def rem(a, b):
        return lax.rem(a, b)

    def z_at(step):
        return rem(z + step, n_z)

    def remote(src, dst, send, recv, device):
        return pltpu.make_async_remote_copy(
            src_ref=src,
            dst_ref=dst,
            send_sem=send,
            recv_sem=recv,
            device_id=device,
            device_id_type=MESH,
        )

    def al(v, m):
        return pl.multiple_of(v, m)

    barrier = pltpu.get_barrier_semaphore()
    for step in range(1, n_dp):
        pl.semaphore_signal(
            barrier, inc=1, device_id=(s, rem(d + step, n_dp)), device_id_type=MESH
        )
    for p in plane:
        pl.semaphore_signal(barrier, inc=1, device_id=(p, d), device_id_type=MESH)

    def load(i, src, dst):
        return pltpu.make_async_copy(src, dst, r.load.at[i])

    staging = [r.h1, r.slope0]
    conv_rows = shard_rows[0]

    def conv_load(layer, j):
        lane = slice(j * lanes, (j + 1) * lanes)
        return load(
            5 + layer * n_lane + j,
            conv_w.at[layer, :, lane],
            staging[layer].at[j, 0:conv_rows],
        )

    loads = [
        load(1, squeeze_w, r.sst),
        load(2, expand_w, r.est),
        load(3, images.at[s], r.xin),
        load(4, cotangent.at[s], r.cin),
    ]
    loads[2].start()
    for layer in range(2):
        for j in range(n_lane):
            conv_load(layer, j).start()
    for i in (0, 1, 3):
        loads[i].start()

    full = [r.w0, r.gp, r.w1]

    def shard(kind, buf, which):
        rows = shard_rows[kind]
        return buf.at[pl.ds(al(which * rows, 16), rows)]

    def quarter(kind, buf, which, q):
        rows = shard_rows[kind]
        return buf.at[pl.ds(al(which * rows + q * (rows // 4), 16), rows // 4)]


    def z_of(way, hop):
        return z_at(n_z - hop if way == 0 else hop)

    def has(way, hop):
        return z >= hop if way == 0 else z < n_z - hop

    def hop_id(way, hop):
        return (hop - 1) * 2 + way

    def ag_z_copy(kind, way, hop, owner):
        view = quarter(kind, full[kind], 2 * owner + c, s)
        i = hop_id(way, hop)
        return remote(
            view,
            view,
            r.ag_zs.at[kind, i],
            r.ag_zr.at[kind, i],
            (s, 2 * z_at(1 if way == 0 else n_z - 1) + c),
        )

    def ag_pass(kind, way, hop, do):
        here_has = has(way, hop - 1) if hop > 1 else True
        there = z < n_z - 1 if way == 0 else z > 0
        owner = z_of(way, hop - 1)

        @pl.when(jnp.logical_and(here_has, there))
        def _():
            do(ag_z_copy(kind, way, hop, owner))

    halves = [slice(0, width // 2), slice(width // 2, width)]

    def ag_p_copy(kind, way, hop, leg, q):
        view = quarter(kind, full[kind], 2 * z_of(way, hop) + c, q)
        if leg >= 2:
            view = view.at[:, halves[leg - 2]]
        to = plane[(0, 1, 1, 0)[leg]]
        i = hop_id(way, hop) * 4 + leg
        return remote(view, view, r.ag_ps.at[kind, i], r.ag_pr.at[kind, i], (to, d))

    def ag_own_copy(kind, core):
        view = shard(kind, full[kind], 2 * z + core)
        return remote(view, view, r.ag_os.at[kind], r.ag_or.at[kind], (s, sib))

    def ag_s_copy(kind, way, hop, q, i, core):
        view = quarter(kind, full[kind], 2 * z_of(way, hop) + core, q)
        i = hop_id(way, hop) * 4 + i
        return remote(view, view, r.ag_ss.at[kind, i], r.ag_sr.at[kind, i], (s, sib))

    others = [s] + plane

    def ag_start(kind):
        for way in range(2):
            ag_pass(kind, way, 1, lambda copy: copy.start())
        ag_own_copy(kind, c).start()

    def for_hop(hop, do):
        for way in range(2):

            @pl.when(has(way, hop))
            def _():
                do(way)

    def ag_z(kind, hop):
        def do(way):
            ag_z_copy(kind, way, hop, z_of(way, hop)).wait_recv()
            if hop < n_z - 1:
                ag_pass(kind, way, hop + 1, lambda copy: copy.start())
            if kind != 1:
                for leg in range(2):
                    ag_p_copy(kind, way, hop, leg, s).start()
            ag_s_copy(kind, way, hop, s, 0, c).start()

        for_hop(hop, do)

    def ag_l(kind, hop):
        def do(way):
            for leg in range(2):
                ag_p_copy(kind, way, hop, leg, s).start()

        for_hop(hop, do)

    def ag_r(kind, hop):
        def do(way):
            for leg in range(2):
                ag_p_copy(kind, way, hop, leg, plane[leg]).wait_recv()
                ag_p_copy(kind, way, hop, 2 + leg, plane[leg]).start()
                ag_s_copy(kind, way, hop, plane[leg], 1 + leg, c).start()

        for_hop(hop, do)

    def ag_p(kind, hop):
        def do(way):
            for leg in range(2):
                ag_p_copy(kind, way, hop, 2 + leg, plane[2]).wait_recv()
            ag_s_copy(kind, way, hop, plane[2], 3, c).start()

        for_hop(hop, do)

    def ag_sib(kind):
        ag_own_copy(kind, 1 - c).wait_recv()
        for hop in range(1, n_z):

            def do(way):
                for i in range(4):
                    ag_s_copy(kind, way, hop, others[i], i, 1 - c).wait_recv()

            for_hop(hop, do)

    def ag_end(kind):
        ag_own_copy(kind, c).wait_send()
        for hop in range(1, n_z):

            def do(way):
                for leg in range(2):
                    ag_p_copy(kind, way, hop, leg, s).wait_send()
                    ag_p_copy(kind, way, hop, 2 + leg, plane[leg]).wait_send()
                for i in range(4):
                    ag_s_copy(kind, way, hop, others[i], i, c).wait_send()

            for way in range(2):
                ag_pass(kind, way, hop, lambda copy: copy.wait_send())
            for_hop(hop, do)

    def cast_conv(layer, buf):
        for j in range(n_lane):
            conv_load(layer, j).wait()

        def body(j, _):
            buf[pl.ds(al(d * conv_rows, 16), conv_rows), pl.ds(al(j * lanes, lanes), lanes)] = (
                staging[layer][j, 0:conv_rows, :].astype(BF16)
            )
            return 0

        lax.fori_loop(0, n_lane, body, 0)

    g_rows = shard_rows[1]
    e_rows = n_ex = bottle // n_dp
    s_rows = width // n_dp
    n_sub = s_rows // e_rows

    def ex_row(which, l, t):
        return al(which * g_rows + (l * tasks + t) * e_rows, 16)

    def sq_row(which, l, t):
        return al(which * g_rows + (2 * tasks + l * tasks + t) * e_rows, 16)

    count = counts[s]
    wide = 2 * lanes
    pick_row = jnp.concatenate(
        [picks[s].astype(F32), jnp.zeros((1, wide - windows), F32)], axis=1
    )
    pick_tile = jnp.broadcast_to(pick_row, (lanes, wide)).T[:windows, :].astype(jnp.int32)
    pick_ref = r.pick
    pick_ref[...] = pick_tile
    slot_pick = (
        (pick_tile // 2) * cols
        + 2 * lax.broadcasted_iota(jnp.int32, (windows, lanes), 0)
        + pick_tile % 2
    )
    r.mp[...] = jnp.where(slot_pick < count, 1.0, 0.0).astype(F32)

    def lane_at(j, base=0):
        return pl.ds(al(base + j * lanes, lanes), lanes)

    def valid_rows(start, rows):
        return (lax.broadcasted_iota(jnp.int32, (rows, lanes), 0) + start) < count

    def shift_in(value_of, buf, block):
        def body(j, _):
            v = value_of(j)
            at = lax.broadcasted_iota(jnp.int32, (cols, lanes), 0)
            before = jnp.where(at == 0, 0.0, pltpu.roll(v, 1, 0))
            after = jnp.where(at == cols - 1, 0.0, pltpu.roll(v, cols - 1, 0))
            rows = pl.ds(block * cols, cols)
            buf[rows, lane_at(j)] = before.astype(BF16)
            buf[rows, lane_at(j, width)] = v.astype(BF16)
            buf[rows, lane_at(j, 2 * width)] = after.astype(BF16)
            return 0

        lax.fori_loop(0, n_lane, body, 0)

    @pl.when(d == 0)
    def _():
        r.halo[:, 0] = jnp.zeros_like(r.halo[:, 0])

    @pl.when(d == n_dp - 1)
    def _():
        r.halo[:, 1] = jnp.zeros_like(r.halo[:, 1])

    def halo_down(e, buf):
        return remote(
            buf.at[2 * cols : 3 * cols, width : 2 * width],
            r.halo.at[e % 2, 0],
            r.halo_s.at[e, 0],
            r.halo_r.at[e, 0],
            (s, rem(d + 1, n_dp)),
        )

    def halo_up(e, buf):
        return remote(
            buf.at[cols : 2 * cols, width : 2 * width],
            r.halo.at[e % 2, 1],
            r.halo_s.at[e, 1],
            r.halo_r.at[e, 1],
            (s, rem(d + n_dp - 1, n_dp)),
        )

    def halo_start(e, buf):
        @pl.when(d < n_dp - 1)
        def _():
            halo_down(e, buf).start()

        @pl.when(d > 0)
        def _():
            halo_up(e, buf).start()

    def halo_finish(e, buf):
        @pl.when(d > 0)
        def _():
            halo_down(e, buf).wait_recv()

        @pl.when(d < n_dp - 1)
        def _():
            halo_up(e, buf).wait_recv()

        shift_in(lambda j: r.halo[e % 2, 0, :, lane_at(j)].astype(F32), buf, 0)
        shift_in(lambda j: r.halo[e % 2, 1, :, lane_at(j)].astype(F32), buf, 3)

    def halo_sent(e, buf):
        @pl.when(d < n_dp - 1)
        def _():
            halo_down(e, buf).wait_send()

        @pl.when(d > 0)
        def _():
            halo_up(e, buf).wait_send()

    def ex_copy(k, step, owner):
        return remote(
            r.ex_out.at[k],
            r.ex_in.at[k, owner],
            r.ex_s.at[k, step - 1],
            r.ex_r.at[k, step - 1],
            (s, rem(d + step, n_dp)),
        )

    def ex_start(k):
        for step in range(1, n_dp):
            ex_copy(k, step, d).start()
        r.ex_in[k, d] = r.ex_out[k]

    def ex_finish(k):
        for step in range(1, n_dp):
            ex_copy(k, step, rem(d + n_dp - step, n_dp)).wait_recv()
        total = r.ex_in[k, 0]
        for i in range(1, n_dp):
            total = total + r.ex_in[k, i]
        return [
            jnp.concatenate([total[i * n_lane + j : i * n_lane + j + 1] for j in range(n_lane)], 1)
            for i in range(2)
        ]

    def ex_put(k, i, j, value):
        r.ex_out[k, pl.ds(i * n_lane + j, 1), :] = value

    def conv_forward(xc, w, h, row):
        span = 3 * width
        acc = None
        for a in range(3):
            term = dot(
                xc[(a + row) * cols : (a + row + 1) * cols, :], w[a * span : (a + 1) * span, :]
            )
            acc = term if acc is None else acc + term
        for j in range(n_lane):
            h[j, row * cols : (row + 1) * cols, :] = acc[:, j * lanes : (j + 1) * lanes]

    def conv_back(dc, w, row, part):
        acc = None
        for a in range(3):
            block = 2 - a + row
            if (block in (0, 3)) != (part == 1):
                continue
            for b in range(3):
                term = dot_nt(
                    dc[block * cols : (block + 1) * cols, (2 - b) * width : (3 - b) * width],
                    w[(3 * a + b) * width : (3 * a + b + 1) * width, :],
                )
                acc = term if acc is None else acc + term
        for j in range(n_lane):
            at = (j, slice(row * cols, (row + 1) * cols), slice(None))
            piece = acc[:, j * lanes : (j + 1) * lanes]
            r.fbuf[at] = piece if part == 0 else r.fbuf[at] + piece

    quarter_rows = pixels // 4

    def stats(h, k):
        def body(j, _):
            first = jnp.zeros((1, lanes), F32)
            second = jnp.zeros((1, lanes), F32)
            for i in range(4):
                v = h[j, i * quarter_rows : (i + 1) * quarter_rows, :]
                kept = jnp.where(valid_rows(i * quarter_rows, quarter_rows), v, 0.0)
                first = first + jnp.sum(kept, 0, keepdims=True)
                second = second + jnp.sum(kept * v, 0, keepdims=True)
            ex_put(k, 0, j, first)
            ex_put(k, 1, j, second)
            return 0

        lax.fori_loop(0, n_lane, body, 0)

    def norm_of(sums, layer):
        total = r.total[0:1, :]
        centre = sums[0] / total
        inverse = lax.rsqrt(sums[1] / total - centre * centre + EPS)
        r.norm[layer, 0:1, :] = centre
        r.norm[layer, 1:2, :] = inverse
        r.norm[layer, 2:3, :] = gain[layer : layer + 1, :] * inverse
        r.norm[layer, 3:4, :] = 1.0 / total

    def corner_rows(k):
        return pl.ds((k // 2) * cols + k % 2, windows, stride=2)

    def picked(ref, j):
        out = None
        which = pick_ref[...]
        for k in range(4):
            part = jnp.where(which == k, ref[j, corner_rows(k), :], 0.0)
            out = part if out is None else out + part
        return out

    loads[2].wait()

    def image_row(i):
        def value(j):
            v = r.xin[i * cols : (i + 1) * cols, lane_at(j)].astype(F32)
            return jnp.where(valid_rows(i * cols, cols), v, 0.0)

        return value

    shift_in(image_row(0), r.xc0, 1)
    shift_in(image_row(1), r.xc0, 2)
    cast_conv(0, r.w0)
    pl.semaphore_wait(barrier, n_dp - 1 + 3)
    ag_start(0)
    r.ex_out[4] = jnp.broadcast_to(count.astype(F32), (8, lanes))
    ex_start(4)
    loads[0].wait()
    loads[1].wait()
    for l in range(2):
        for t in range(tasks):
            r.gp[pl.ds(ex_row(d, l, t), e_rows), :] = r.est[l, t].astype(BF16)
            for k in range(n_sub):
                r.gp[pl.ds(sq_row(d, l, t), e_rows), k * lanes : (k + 1) * lanes] = r.sst[
                    l, t, k * e_rows : (k + 1) * e_rows, :
                ].astype(BF16)
    cast_conv(1, r.w1)
    ag_z(0, 1)
    ag_z(0, 2)
    halo_start(0, r.xc0)
    ag_r(0, 1)
    ag_z(0, 3)
    ag_start(2)
    ag_r(0, 2)
    ag_p(0, 1)
    ag_r(0, 3)
    ag_p(0, 2)
    halo_finish(0, r.xc0)
    ag_z(2, 1)
    ag_start(1)
    ag_p(0, 3)
    r.total[...] = jnp.concatenate([ex_finish(4)[0]] * 8, axis=0)
    ag_sib(0)
    conv_forward(r.xc0, r.w0, r.h0, 0)
    conv_forward(r.xc0, r.w0, r.h0, 1)
    stats(r.h0, 0)
    ex_start(0)
    halo_sent(0, r.xc0)
    ag_z(2, 2)
    ag_r(2, 1)
    norm_of(ex_finish(0), 0)

    def block_0(j, _):
        lane = lane_at(j)
        for i in range(4):
            rows = slice(i * quarter_rows, (i + 1) * quarter_rows)
            normed = (r.h0[j, rows, :] - r.norm[0, 0:1, lane]) * r.norm[
                0, 2:3, lane
            ] + bias[0:1, lane]
            g, slope = gelu_pair(normed)
            ok = valid_rows(i * quarter_rows, quarter_rows)
            r.fbuf[j, rows, :] = jnp.where(ok, g, 0.0).astype(BF16).astype(F32)
            r.slope0[j, rows, :] = jnp.where(ok, slope, 0.0)
        f1p = picked(r.fbuf, j)
        r.f1p[:, lane] = f1p
        r.f1b[:, lane] = f1p.astype(BF16)
        return 0

    lax.fori_loop(0, n_lane, block_0, 0)
    shift_in(lambda j: r.fbuf[j, 0:cols, :], r.xc1, 1)
    shift_in(lambda j: r.fbuf[j, cols : 2 * cols, :], r.xc1, 2)
    halo_start(1, r.xc1)
    ag_z(2, 3)
    ag_r(2, 2)
    ag_p(2, 1)
    ag_r(2, 3)
    ag_p(2, 2)
    for hop in range(1, n_z):
        ag_z(1, hop)
        ag_l(1, hop)
    halo_finish(1, r.xc1)
    ag_p(2, 3)
    ag_sib(2)
    conv_forward(r.xc1, r.w1, r.h1, 0)
    for hop in range(1, n_z):
        ag_r(1, hop)
    conv_forward(r.xc1, r.w1, r.h1, 1)
    stats(r.h1, 1)
    ex_start(1)
    for hop in range(1, n_z):
        ag_p(1, hop)
    ag_sib(1)

    def unpack(i, _):
        for l in range(2):
            for t in range(tasks):
                r.ex_w[l, t, pl.ds(al(i * e_rows, 16), e_rows), :] = r.gp[
                    pl.ds(ex_row(i, l, t), e_rows), :
                ]
                for k in range(n_sub):
                    r.sq_w[
                        l,
                        pl.ds(al(i * s_rows + k * e_rows, 16), e_rows),
                        t * bottle : (t + 1) * bottle,
                    ] = r.gp[pl.ds(sq_row(i, l, t), e_rows), k * lanes : (k + 1) * lanes]
        return 0

    lax.fori_loop(0, n_dp, unpack, 0)
    mask_pick = jnp.concatenate([r.mp[...]] * n_lane, axis=1)
    g, slope = gelu_pair(dot(r.f1b[...], r.sq_w[0]))
    r.excited0[...] = g.astype(BF16)
    r.eslope0[...] = slope

    def task_lane(t):
        return pl.ds(al(t * bottle, lanes), bottle)

    def gate_0(t, _):
        value = jax.nn.sigmoid(dot(r.excited0[:, task_lane(t)], r.ex_w[0, t]))
        r.gate0[t] = value
        r.t1[t] = (mask_pick * value * r.f1p[...]).astype(BF16)
        return 0

    lax.fori_loop(0, tasks, gate_0, 0)
    norm_of(ex_finish(1), 1)

    for kind in range(3):
        ag_end(kind)

    def block_1(j, _):
        lane = lane_at(j)
        off = picked(r.h1, j) - r.norm[1, 0:1, lane]
        g, slope = gelu_pair(off * r.norm[1, 2:3, lane] + bias[1:2, lane])
        r.f2p[:, lane] = (r.mp[...] * g).astype(BF16).astype(F32)
        r.slope1[:, lane] = r.mp[...] * slope
        r.centred1[:, lane] = off * r.norm[1, 1:2, lane]
        return 0

    lax.fori_loop(0, n_lane, block_1, 0)
    grads = [r.w1, r.gp, r.g1]

    def pair_of(k):
        return z_at(1 + k)

    def rs_a_copy(kind, k, core):
        return remote(
            shard(kind, grads[kind], 2 * pair_of(k) + core),
            r.ra[kind].at[k],
            r.rs_as.at[kind, k],
            r.rs_ar.at[kind, k],
            (s, sib),
        )

    def rs_b_copy(kind, k, way):
        o = 2 * pair_of(k) + c
        half = (0, 0, 1, 1, 0, 1)[way]
        to = plane[(0, 0, 1, 1, 1, 0)[way]]
        q = to if way in (0, 2, 4, 5) else plane[2]
        return remote(
            quarter(kind, grads[kind], o, q).at[:, halves[half]],
            r.rb[kind].at[k, way],
            r.rs_bs.at[kind, k, way],
            r.rs_br.at[kind, k, way],
            (to, d),
        )

    def rs_c_copy(kind, k):
        return remote(
            r.qs[kind].at[k],
            r.rc[kind].at[k],
            r.rs_cs.at[kind, k],
            r.rs_cr.at[kind, k],
            (s, 2 * pair_of(k) + c),
        )

    def rs_d_copy(kind, leg, q):
        rows = shard_rows[kind] // 4
        view = r.td[kind].at[pl.ds(al(q * rows, 16), rows)]
        if leg >= 2:
            view = view.at[:, halves[leg - 2]]
        to = plane[(0, 1, 1, 0)[leg]]
        return remote(view, view, r.rs_ds.at[kind, leg], r.rs_dr.at[kind, leg], (to, d))

    def conv_weight(kind, xc, k):
        tile = 2 * shard_rows[kind] // 3
        per = 3 * width // tile

        for i in range(3):
            g = pair_of(k) * 3 + i
            a = g // per
            term = dot_tn(
                xc[pl.ds(al(a * cols, 16), pixels), pl.ds(al((g % per) * tile, lanes), tile)],
                r.dc[cols : 3 * cols, width : 2 * width],
            )
            grads[kind][pl.ds(al(g * tile, 16), tile), :] = term.astype(BF16)

    def rs_a(kind, k):
        rs_a_copy(kind, k, 1 - c).start()

    def rs_b(kind, k):
        rs_a_copy(kind, k, c).wait_recv()
        rows = shard_rows[kind]
        tile = rows // 4
        start = (2 * pair_of(k) + c) * rows

        def body(i, _):
            at = pl.ds(al(start + i * tile, 16), tile)
            grads[kind][at, :] = (
                grads[kind][at, :].astype(F32)
                + r.ra[kind][k, pl.ds(al(i * tile, 16), tile), :].astype(F32)
            ).astype(BF16)
            return 0

        lax.fori_loop(0, 4, body, 0)
        for way in range(4):
            rs_b_copy(kind, k, way).start()

    def quarter_at(kind, k, q):
        rows = shard_rows[kind]
        return pl.ds(al((2 * pair_of(k) + c) * rows + q * (rows // 4), 16), rows // 4)

    def rs_r(kind, k):
        for half in range(2):
            rs_b_copy(kind, k, 2 * half).wait_recv()
            rs_b_copy(kind, k, 2 * half + 1).wait_recv()
            at = quarter_at(kind, k, plane[1 - half])
            grads[kind][at, halves[half]] = (
                grads[kind][at, halves[half]].astype(F32)
                + r.rb[kind][k, 2 * half + 1].astype(F32)
            ).astype(BF16)
            rs_b_copy(kind, k, 4 + half).start()

    def rs_c(kind, k):
        at = quarter_at(kind, k, s)
        parts = []
        for half in range(2):
            rs_b_copy(kind, k, 4 + half).wait_recv()
            parts.append(
                grads[kind][at, halves[half]].astype(F32)
                + r.rb[kind][k, 2 * half].astype(F32)
                + r.rb[kind][k, 4 + half].astype(F32)
            )
        total = jnp.concatenate(parts, axis=1)
        if k < n_z - 1:
            r.qs[kind][k] = total.astype(BF16)
            rs_c_copy(kind, k).start()
        else:
            r.qf[kind][...] = total

    def rs_d(kind):
        total = r.qf[kind][...]
        for k in range(n_z - 1):
            rs_c_copy(kind, k).wait_recv()
            total = total + r.rc[kind][k].astype(F32)
        rows = shard_rows[kind] // 4
        r.td[kind][pl.ds(al(s * rows, 16), rows), :] = total.astype(BF16)
        for leg in range(2):
            rs_d_copy(kind, leg, s).start()

    def rs_dr(kind):
        for leg in range(2):
            rs_d_copy(kind, leg, plane[leg]).wait_recv()
            rs_d_copy(kind, 2 + leg, plane[leg]).start()

    def rs_e(kind):
        for leg in range(2):
            rs_d_copy(kind, 2 + leg, plane[2]).wait_recv()

    def rs_end(kind):
        for k in range(n_z):
            rs_a_copy(kind, k, 1 - c).wait_send()
            for way in range(6):
                rs_b_copy(kind, k, way).wait_send()
            if k < n_z - 1:
                rs_c_copy(kind, k).wait_send()
        for leg in range(2):
            rs_d_copy(kind, leg, s).wait_send()
            rs_d_copy(kind, 2 + leg, plane[leg]).wait_send()

    loads[3].wait()
    r.df2[...] = jnp.zeros_like(r.df2)

    def pack_grads(l, t, grad_squeeze, grad_expand):
        r.fbuf[0, 0:width, :] = grad_squeeze
        for j in range(n_lane):
            r.fbuf[1, j * bottle : (j + 1) * bottle, :] = grad_expand[:, j * lanes : (j + 1) * lanes]

        def body(i, _):
            for j in range(n_lane):
                lane = slice(j * lanes, (j + 1) * lanes)
                r.gp[pl.ds(ex_row(i, l, t), e_rows), lane] = r.fbuf[
                    1, pl.ds(al(j * bottle + i * e_rows, 16), e_rows), :
                ].astype(BF16)
            for k in range(n_sub):
                r.gp[pl.ds(sq_row(i, l, t), e_rows), k * lanes : (k + 1) * lanes] = r.fbuf[
                    0, pl.ds(al(i * s_rows + k * e_rows, 16), e_rows), :
                ].astype(BF16)
            return 0

        lax.fori_loop(0, n_dp, body, 0)

    def kept(i):
        return pl.ds(al(i * windows, 16), windows)

    def gate_1(t, _):
        w_s = r.sq_w[1, :, task_lane(t)]
        w_e = r.ex_w[1, t]
        f2p = r.f2p[...]
        source = (f2p + r.t1[t].astype(F32)).astype(BF16)
        g, slope = gelu_pair(dot(source, w_s))
        excited = g.astype(BF16)
        value = jax.nn.sigmoid(dot(excited, w_e))
        field = mask_pick * f2p
        d_task = r.cin[t].astype(F32)
        r.cin[t] = (value * field).astype(BF16)
        d_expanded = (d_task * field * value * (1.0 - value)).astype(BF16)
        d_squeezed = (slope * dot_nt(d_expanded, w_e)).astype(BF16)
        d_source = dot_nt(d_squeezed, w_s)
        r.t1[t] = d_source.astype(BF16)
        r.df2[...] += d_source + mask_pick * d_task * value
        r.g1[kept(t), :] = source
        r.g1[kept(tasks + t), :] = d_expanded
        r.g1[kept(2 * tasks), task_lane(t)] = excited
        r.g1[kept(2 * tasks + 1), task_lane(t)] = d_squeezed
        return 0

    def gate_1_weight(t, _):
        pack_grads(
            1,
            t,
            dot_tn(r.g1[kept(t), :], r.g1[kept(2 * tasks + 1), task_lane(t)]),
            dot_tn(r.g1[kept(2 * tasks), task_lane(t)], r.g1[kept(tasks + t), :]),
        )
        return 0

    lax.fori_loop(0, tasks, gate_1, 0)
    task_store = pltpu.make_async_copy(r.cin, out_task.at[0], r.store.at[0])
    task_store.start()

    def back_1(j, _):
        lane = lane_at(j)
        d_norm = r.slope1[:, lane] * r.df2[:, lane].astype(BF16).astype(F32)
        r.df2[:, lane] = d_norm
        ex_put(2, 0, j, jnp.sum(d_norm, 0, keepdims=True))
        ex_put(2, 1, j, jnp.sum(d_norm * r.centred1[:, lane], 0, keepdims=True))
        return 0

    lax.fori_loop(0, n_lane, back_1, 0)
    ex_start(2)

    r.df1[...] = jnp.zeros_like(r.df1)

    def gate_0_back(t, _):
        w_s = r.sq_w[0, :, task_lane(t)]
        w_e = r.ex_w[0, t]
        value = r.gate0[t]
        d_task = r.t1[t].astype(F32)
        excited = r.excited0[:, task_lane(t)]
        d_expanded = (d_task * (mask_pick * r.f1p[...]) * value * (1.0 - value)).astype(BF16)
        d_squeezed = (r.eslope0[:, task_lane(t)] * dot_nt(d_expanded, w_e)).astype(BF16)
        r.df1[...] += dot_nt(d_squeezed, w_s) + mask_pick * d_task * value
        pack_grads(0, t, dot_tn(r.f1b[...], d_squeezed), dot_tn(excited, d_expanded))
        return 0

    lax.fori_loop(0, tasks, gate_0_back, 0)
    lax.fori_loop(0, tasks, gate_1_weight, 0)

    r.sums[...] = jnp.zeros_like(r.sums)

    def back_terms(k, layer):
        sums = ex_finish(k)
        r.sums[2 * layer : 2 * layer + 1, :] = sums[0]
        r.sums[2 * layer + 1 : 2 * layer + 2, :] = sums[1]
        scale = gain[layer : layer + 1, :] * r.norm[layer, 3:4, :] * r.norm[layer, 1:2, :]
        r.norm[layer, 4:5, :] = scale * sums[0]
        r.norm[layer, 5:6, :] = scale * r.norm[layer, 1:2, :] * sums[1]

    for k in range(n_z):
        rs_a(1, k)
    back_terms(2, 1)

    def hidden_grad_1(j, _):
        lane = lane_at(j)
        norm = r.norm
        for k in range(4):
            at = corner_rows(k)
            spread = jnp.where(pick_ref[...] == k, r.df2[:, lane] * norm[1, 2:3, lane], 0.0)
            value = spread - (
                norm[1, 4:5, lane] + (r.h1[j, at, :] - norm[1, 0:1, lane]) * norm[1, 5:6, lane]
            )
            slot = (k // 2) * cols + k % 2 + 2 * lax.broadcasted_iota(
                jnp.int32, (windows, lanes), 0
            )
            r.fbuf[j, at, :] = jnp.where(slot < count, value, 0.0)
        return 0

    lax.fori_loop(0, n_lane, hidden_grad_1, 0)
    shift_in(lambda j: r.fbuf[j, 0:cols, :], r.dc, 1)
    shift_in(lambda j: r.fbuf[j, cols : 2 * cols, :], r.dc, 2)
    halo_start(2, r.dc)

    for k in range(n_z):
        rs_b(1, k)
    conv_weight(2, r.xc1, 0)
    rs_a(2, 0)
    conv_back(r.dc, r.w1, 0, 0)
    conv_back(r.dc, r.w1, 1, 0)
    rs_b(2, 0)
    conv_weight(2, r.xc1, 1)
    rs_a(2, 1)
    halo_finish(2, r.dc)
    conv_back(r.dc, r.w1, 0, 1)
    conv_back(r.dc, r.w1, 1, 1)
    for k in range(n_z):
        rs_r(1, k)
    rs_b(2, 1)
    def back_0(j, _):
        lane = lane_at(j)
        norm = r.norm
        first = jnp.zeros((1, lanes), F32)
        second = jnp.zeros((1, lanes), F32)
        for k in range(4):
            at = corner_rows(k)
            d_field = r.fbuf[j, at, :].astype(BF16).astype(F32) + jnp.where(
                pick_ref[...] == k, r.df1[:, lane], 0.0
            )
            d_norm = r.slope0[j, at, :] * d_field.astype(BF16).astype(F32)
            r.fbuf[j, at, :] = d_norm
            centred = (r.h0[j, at, :] - norm[0, 0:1, lane]) * norm[0, 1:2, lane]
            first = first + jnp.sum(d_norm, 0, keepdims=True)
            second = second + jnp.sum(d_norm * centred, 0, keepdims=True)
        ex_put(3, 0, j, first)
        ex_put(3, 1, j, second)
        return 0

    lax.fori_loop(0, n_lane, back_0, 0)
    ex_start(3)
    conv_weight(2, r.xc1, 2)
    rs_a(2, 2)
    conv_weight(2, r.xc1, 3)
    rs_a(2, 3)
    halo_sent(2, r.dc)
    back_terms(3, 0)

    def sums_copy(p, q):
        return remote(
            r.sums,
            r.sums_in.at[q],
            r.sums_s.at[p],
            r.sums_r.at[p],
            (plane[p], d),
        )

    for p in range(3):
        sums_copy(p, s).start()
    r.sums_in[s] = r.sums[...]

    def hidden_grad_0(row):
        def value(j):
            lane = lane_at(j)
            norm = r.norm
            rows = slice(row * cols, (row + 1) * cols)
            out = r.fbuf[j, rows, :] * norm[0, 2:3, lane] - (
                norm[0, 4:5, lane] + (r.h0[j, rows, :] - norm[0, 0:1, lane]) * norm[0, 5:6, lane]
            )
            return jnp.where(valid_rows(row * cols, cols), out, 0.0)

        return value

    shift_in(hidden_grad_0(0), r.dc, 1)
    shift_in(hidden_grad_0(1), r.dc, 2)
    halo_start(3, r.dc)
    rs_b(2, 2)
    rs_r(2, 0)
    conv_weight(0, r.xc0, 0)
    rs_a(0, 0)
    rs_b(2, 3)
    for k in range(n_z):
        rs_c(1, k)
    rs_r(2, 1)
    conv_weight(0, r.xc0, 1)
    rs_a(0, 1)
    rs_c(2, 0)
    rs_b(0, 0)
    conv_weight(0, r.xc0, 2)
    rs_a(0, 2)
    conv_weight(0, r.xc0, 3)
    rs_a(0, 3)
    rs_r(2, 2)
    rs_b(0, 1)
    conv_back(r.dc, r.w0, 0, 0)
    conv_back(r.dc, r.w0, 1, 0)
    rs_c(2, 1)
    rs_r(2, 3)
    rs_b(0, 2)
    halo_finish(3, r.dc)
    conv_back(r.dc, r.w0, 0, 1)
    conv_back(r.dc, r.w0, 1, 1)
    rs_b(0, 3)
    rs_c(2, 2)
    def image_out(j, _):
        lane = lane_at(j)
        for i in range(4):
            rows = slice(i * quarter_rows, (i + 1) * quarter_rows)
            r.xin[rows, lane] = jnp.where(
                valid_rows(i * quarter_rows, quarter_rows), r.fbuf[j, rows, :], 0.0
            ).astype(BF16)
        return 0

    lax.fori_loop(0, n_lane, image_out, 0)
    image_store = pltpu.make_async_copy(r.xin, out_image.at[0], r.store.at[1])
    image_store.start()
    rs_r(0, 0)
    rs_c(2, 3)
    rs_r(0, 1)
    rs_c(0, 0)
    rs_r(0, 2)
    rs_c(0, 1)
    rs_r(0, 3)
    rs_d(1)
    rs_d(2)
    rs_c(0, 2)
    rs_c(0, 3)
    rs_dr(1)
    rs_dr(2)
    rs_d(0)
    stores = [task_store, image_store]

    def reduced_out(kind):
        rs_e(kind)
        stores.append(
            pltpu.make_async_copy(r.td[kind], out_reduced[kind], r.store.at[2 + kind])
        )
        stores[-1].start()

    reduced_out(1)
    reduced_out(2)
    for p in range(3):
        sums_copy(p, plane[p]).wait_recv()
    total = r.sums_in[0]
    for i in range(1, 4):
        total = total + r.sums_in[i]
    for l in range(2):
        out_bias[l : l + 1, :] = total[2 * l : 2 * l + 1, :]
        out_gain[l : l + 1, :] = total[2 * l + 1 : 2 * l + 2, :]
    for kind in range(1, 3):
        rs_end(kind)
    for p in range(3):
        sums_copy(p, s).wait_send()
    for k in range(5):
        for step in range(1, n_dp):
            ex_copy(k, step, d).wait_send()
    halo_sent(3, r.dc)
    halo_sent(1, r.xc1)
    rs_dr(0)
    reduced_out(0)
    rs_end(0)
    for copy in stores:
        copy.wait()


def finish_kernel(
    dims,
    task,
    image,
    reduced_0,
    reduced_1,
    reduced_2,
    gain,
    bias,
    out_task,
    out_image,
    out_conv,
    out_squeeze,
    out_expand,
    out_gain,
    out_bias,
    task_in,
    image_in,
    conv_in,
    conv_wide,
    gate_in,
    squeeze_wide,
    expand_wide,
    sem_in,
    sem_out,
):
    lanes = 128
    e_rows = dims.bottle // dims.n_dp
    ins = [
        pltpu.make_async_copy(reduced_0, conv_in.at[0], sem_in.at[0]),
        pltpu.make_async_copy(reduced_2, conv_in.at[1], sem_in.at[1]),
        pltpu.make_async_copy(reduced_1, gate_in, sem_in.at[2]),
        pltpu.make_async_copy(task, task_in, sem_in.at[3]),
        pltpu.make_async_copy(image, image_in, sem_in.at[4]),
    ]
    for copy in ins:
        copy.start()
    outs = [
        pltpu.make_async_copy(task_in, out_task, sem_out.at[0]),
        pltpu.make_async_copy(image_in, out_image, sem_out.at[1]),
    ]
    out_gain[...] = gain[...]
    out_bias[...] = bias[...]
    for layer in range(2):
        ins[layer].wait()
        conv_wide[layer] = conv_in[layer].astype(F32)
        outs.append(
            pltpu.make_async_copy(
                conv_wide.at[layer], out_conv.at[layer], sem_out.at[2 + layer]
            )
        )
        outs[-1].start()
    for i in range(2):
        ins[3 + i].wait()
        outs[i].start()
    ins[2].wait()
    for l in range(2):
        for t in range(dims.tasks):
            at = (l * dims.tasks + t) * e_rows
            expand_wide[l, t] = gate_in[at : at + e_rows, :].astype(F32)
            at = at + 2 * dims.tasks * e_rows
            for k in range(dims.width // dims.n_dp // e_rows):
                squeeze_wide[l, t, k * e_rows : (k + 1) * e_rows, :] = gate_in[
                    at : at + e_rows, k * lanes : (k + 1) * lanes
                ].astype(F32)
    outs.append(pltpu.make_async_copy(squeeze_wide, out_squeeze, sem_out.at[4]))
    outs.append(pltpu.make_async_copy(expand_wide, out_expand, sem_out.at[5]))
    outs[-2].start()
    outs[-1].start()
    for copy in outs:
        copy.wait()


def fused(images, counts, pool_index, conv_w, squeeze_w, expand_w, gain, bias, cotangent):
    n_dp = lax.axis_size("dp")
    micro, pixels, width = images.shape
    tasks, bottle = squeeze_w.shape[1], squeeze_w.shape[3]
    cols = 2 * pool_index.shape[2]
    windows = cols // 2
    conv_rows = conv_w.shape[1]
    gate_rows = 4 * tasks * expand_w.shape[2]
    shard_rows = (conv_rows, gate_rows, conv_rows)
    n_z = n_dp // 2
    vm = pltpu.VMEM
    dma = pltpu.SemaphoreType.DMA
    scratch = dict(
        load=dma((5 + 2 * (width // 128),)),
        store=dma((5,)),
        sst=vm(squeeze_w.shape, F32),
        est=vm(expand_w.shape, F32),
        xin=vm((pixels, width), BF16),
        cin=vm((tasks, windows, width), BF16),
        w0=vm((n_dp * conv_rows, width), BF16),
        gp=vm((n_dp * gate_rows, width), BF16),
        w1=vm((n_dp * conv_rows, width), BF16),
        g1=vm((n_dp * conv_rows, width), BF16),
        sq_w=vm((2, width, tasks * bottle), BF16),
        ex_w=vm((2, tasks, bottle, width), BF16),
        ag_zs=dma((3, 2 * (n_z - 1))),
        ag_zr=dma((3, 2 * (n_z - 1))),
        ag_ps=dma((3, 8 * (n_z - 1))),
        ag_pr=dma((3, 8 * (n_z - 1))),
        ag_ss=dma((3, 8 * (n_z - 1))),
        ag_sr=dma((3, 8 * (n_z - 1))),
        ag_os=dma((3,)),
        ag_or=dma((3,)),
        mp=vm((windows, 128), F32),
        pick=vm((windows, 128), jnp.int32),
        halo=vm((2, 2, cols, width), BF16),
        halo_s=dma((4, 2)),
        halo_r=dma((4, 2)),
        ex_out=vm((5, 8, 128), F32),
        ex_in=vm((5, n_dp, 8, 128), F32),
        total=vm((8, width), F32),
        ex_s=dma((5, n_dp - 1)),
        ex_r=dma((5, n_dp - 1)),
        norm=vm((2, 8, width), F32),
        xc0=vm((4 * cols, 3 * width), BF16),
        xc1=vm((4 * cols, 3 * width), BF16),
        dc=vm((4 * cols, 3 * width), BF16),
        h0=vm((width // 128, pixels, 128), F32),
        h1=vm((width // 128, pixels, 128), F32),
        slope0=vm((width // 128, pixels, 128), F32),
        fbuf=vm((width // 128, pixels, 128), F32),
        f1p=vm((windows, width), F32),
        f1b=vm((windows, width), BF16),
        excited0=vm((windows, tasks * bottle), BF16),
        eslope0=vm((windows, tasks * bottle), F32),
        gate0=vm((tasks, windows, width), F32),
        t1=vm((tasks, windows, width), BF16),
        f2p=vm((windows, width), F32),
        slope1=vm((windows, width), F32),
        centred1=vm((windows, width), F32),
        df2=vm((windows, width), F32),
        df1=vm((windows, width), F32),
        sums=vm((8, width), F32),
        sums_in=vm((4, 8, width), F32),
        sums_s=dma((3,)),
        sums_r=dma((3,)),
        rs_as=dma((3, n_z)),
        rs_ar=dma((3, n_z)),
        rs_bs=dma((3, n_z, 6)),
        rs_br=dma((3, n_z, 6)),
        rs_cs=dma((3, n_z - 1)),
        rs_cr=dma((3, n_z - 1)),
        rs_ds=dma((3, 4)),
        rs_dr=dma((3, 4)),
    )
    quarters = [rows // 4 for rows in shard_rows]
    scratch.update(
        ra=[vm((n_z, rows, width), BF16) for rows in shard_rows],
        rb=[vm((n_z, 6, rows, width // 2), BF16) for rows in quarters],
        qs=[vm((n_z - 1, rows, width), BF16) for rows in quarters],
        qf=[vm((rows, width), F32) for rows in quarters],
        rc=[vm((n_z - 1, rows, width), BF16) for rows in quarters],
        td=[vm((rows, width), BF16) for rows in shard_rows],
    )
    buffers, tree = jax.tree.flatten(scratch, is_leaf=lambda v: not isinstance(v, (dict, list)))
    dims = types.SimpleNamespace(
        tree=tree,
        n_dp=n_dp,
        cols=cols,
        pixels=pixels,
        width=width,
        tasks=tasks,
        bottle=bottle,
        shard_rows=shard_rows,
    )
    any_spec = pl.BlockSpec(memory_space=pl.ANY)
    vmem_spec = pl.BlockSpec(memory_space=pltpu.VMEM)
    smem_spec = pl.BlockSpec(memory_space=pltpu.SMEM)
    results = pl.pallas_call(
        functools.partial(step_kernel, dims),
        out_shape=(
            jax.ShapeDtypeStruct((1, tasks, windows, width), BF16),
            jax.ShapeDtypeStruct((1, pixels, width), BF16),
            *[jax.ShapeDtypeStruct((rows, width), BF16) for rows in shard_rows],
            jax.ShapeDtypeStruct(gain.shape, F32),
            jax.ShapeDtypeStruct(bias.shape, F32),
        ),
        in_specs=[smem_spec, vmem_spec, vmem_spec, vmem_spec] + [any_spec] * 5,
        out_specs=(any_spec,) * 5 + (vmem_spec,) * 2,
        scratch_shapes=tuple(buffers),
        compiler_params=pltpu.CompilerParams(
            collective_id=0, has_side_effects=True, vmem_limit_bytes=VMEM_BYTES
        ),
    )(counts.reshape(micro), pool_index, gain, bias, images, conv_w, squeeze_w, expand_w, cotangent)
    return pl.pallas_call(
        functools.partial(finish_kernel, dims),
        out_shape=(
            jax.ShapeDtypeStruct((1, tasks, windows, width), BF16),
            jax.ShapeDtypeStruct((1, pixels, width), BF16),
            jax.ShapeDtypeStruct(conv_w.shape, F32),
            jax.ShapeDtypeStruct(squeeze_w.shape, F32),
            jax.ShapeDtypeStruct(expand_w.shape, F32),
            jax.ShapeDtypeStruct(gain.shape, F32),
            jax.ShapeDtypeStruct(bias.shape, F32),
        ),
        in_specs=[any_spec] * 5 + [vmem_spec] * 2,
        out_specs=(any_spec,) * 5 + (vmem_spec,) * 2,
        scratch_shapes=(
            vm((1, tasks, windows, width), BF16),
            vm((1, pixels, width), BF16),
            vm(conv_w.shape, BF16),
            vm(conv_w.shape, F32),
            vm((gate_rows, width), BF16),
            vm(squeeze_w.shape, F32),
            vm(expand_w.shape, F32),
            dma((5,)),
            dma((6,)),
        ),
        compiler_params=pltpu.CompilerParams(vmem_limit_bytes=VMEM_BYTES),
    )(*results)


def fits_kernel(mesh, args):
    images, counts, pool_index, conv_w, squeeze_w, expand_w = args[:6]
    sections, n_dp = mesh.shape["section"], mesh.shape["dp"]
    conv_rows = conv_w.shape[1] // n_dp
    e_rows = expand_w.shape[2] // n_dp
    return (
        sections == 4
        and images.shape[0] == sections
        and n_dp % 2 == 0
        and pool_index.shape[1] == n_dp
        and conv_rows % 64 == 0
        and e_rows == 16
        and squeeze_w.shape[2] // n_dp == 4 * e_rows
        and squeeze_w.shape[3] == 128
        and images.shape[2] == 4 * 128
    )


def solution(mesh):
    placed = (
        P(None, "dp", None),
        P(None, "dp"),
        P(None, "dp", None),
        P(None, "dp", None),
        P(None, None, "dp", None),
        P(None, None, "dp", None),
        P(),
        P(),
        P(None, None, "dp", None),
    )
    def run(*args):
        return mapped(fused if fits_kernel(mesh, args) else on_device)(*args)

    def mapped(body):
        return jax.shard_map(
        body,
        mesh=mesh,
        in_specs=placed,
        out_specs=(
            P("section", None, "dp", None),
            P("section", "dp", None),
            P(None, "dp", None),
            P(None, None, "dp", None),
            P(None, None, "dp", None),
            P(),
            P(),
        ),
        check_vma=False,
    )

    return run
```

```python
import functools
import types

import jax
import jax.numpy as jnp
from jax import lax
from jax.experimental import pallas as pl
from jax.experimental.pallas import tpu as pltpu
from jax.sharding import PartitionSpec as P

EPS = 1e-05
BF16 = jnp.bfloat16
F32 = jnp.float32
VMEM_BYTES = 62 * 1024 * 1024


def gelu_back(point, upstream):
    return jax.vjp(jax.nn.gelu, point)[1](upstream)[0]


def with_halo(value, axis):
    size = lax.axis_size(axis)
    up = [(i, i + 1) for i in range(size - 1)]
    down = [(j, i) for i, j in up]
    before = lax.ppermute(value[-1:], axis, up)
    after = lax.ppermute(value[:1], axis, down)
    return jnp.concatenate([before, value, after], axis=0)


def conv(padded, taps):
    out = lax.conv_general_dilated(
        padded[None],
        taps,
        (1, 1),
        ((0, 0), (1, 1)),
        dimension_numbers=("NHWC", "HWIO", "NHWC"),
        preferred_element_type=F32,
    )
    return out.reshape(-1, out.shape[-1])


def conv_input_grad(d_padded, taps):
    out = lax.conv_general_dilated(
        d_padded[None],
        taps[::-1, ::-1],
        (1, 1),
        ((0, 0), (1, 1)),
        dimension_numbers=("NHWC", "HWOI", "NHWC"),
        preferred_element_type=F32,
    )
    return out.reshape(-1, out.shape[-1])


def conv_weight_grad(padded, d_hidden):
    out = lax.conv_general_dilated(
        padded[None],
        d_hidden[None],
        (1, 1),
        ((0, 0), (1, 1)),
        dimension_numbers=("CHWN", "IHWO", "HWNC"),
        preferred_element_type=F32,
    )
    return out.reshape(-1, out.shape[-1])


def gate_forward(source, w_squeeze, w_expand):
    squeezed = jnp.einsum("tpc,tcb->tpb", source, w_squeeze, preferred_element_type=F32)
    excited = jax.nn.gelu(squeezed).astype(BF16)
    expanded = jnp.einsum("tpb,tbc->tpc", excited, w_expand, preferred_element_type=F32)
    return squeezed, excited, jax.nn.sigmoid(expanded)


def gate_backward(d_task, field, source, squeezed, excited, gate_val, w_squeeze, w_expand):
    d_expanded = (d_task * field[None] * gate_val * (1.0 - gate_val)).astype(BF16)
    d_excited = jnp.einsum("tpc,tbc->tpb", d_expanded, w_expand, preferred_element_type=F32)
    d_squeezed = gelu_back(squeezed, d_excited).astype(BF16)
    d_source = jnp.einsum("tpb,tcb->tpc", d_squeezed, w_squeeze, preferred_element_type=F32)
    grad_squeeze = jnp.einsum("tpc,tpb->tcb", source, d_squeezed, preferred_element_type=F32)
    grad_expand = jnp.einsum("tpb,tpc->tbc", excited, d_expanded, preferred_element_type=F32)
    return d_source, grad_squeeze, grad_expand


def pool_pick(field, pick):
    tasks, _, width = field.shape
    half_rows, half_columns = pick.shape
    windows = field.reshape(tasks, half_rows, 2, half_columns, 2, width)
    picked = jnp.zeros((tasks, half_rows, half_columns, width), F32)
    for corner in range(4):
        hit = (pick == corner)[None, :, :, None]
        picked = picked + jnp.where(hit, windows[:, :, corner // 2, :, corner % 2, :], 0.0)
    return picked.reshape(tasks, half_rows * half_columns, width)


def pool_spread(d_pooled, pick):
    tasks, _, width = d_pooled.shape
    half_rows, half_columns = pick.shape
    grid = d_pooled.reshape(tasks, half_rows, half_columns, width)
    rows = [
        jnp.stack(
            [jnp.where((pick == 2 * dy + dx)[None, :, :, None], grid, 0.0) for dx in range(2)], 3
        )
        for dy in range(2)
    ]
    return jnp.stack(rows, 2).reshape(tasks, half_rows * 2 * half_columns * 2, width)


def on_device(images, counts, pool_index, conv_w, squeeze_w, expand_w, gain, bias, cotangent):
    sections = lax.axis_size("section")
    here = lax.axis_index("section")
    micro, pixels, width = images.shape
    layers = conv_w.shape[0]
    tasks = squeeze_w.shape[1]
    rows = 2 * pool_index.shape[1]
    columns = 2 * pool_index.shape[2]
    share = micro // sections

    def own(value):
        return lax.dynamic_slice_in_dim(value, here * share, share, 0)

    images, counts, pool_index, cotangent = (
        own(images),
        own(counts),
        own(pool_index),
        own(cotangent),
    )

    def gather(value, axis):
        return lax.all_gather(value.astype(BF16), "dp", axis=axis, tiled=True)

    taps = [gather(conv_w[l], 0).reshape(3, 3, width, width) for l in range(layers)]
    w_squeeze = [gather(squeeze_w[l], 1) for l in range(layers)]
    w_expand = [gather(expand_w[l], 1) for l in range(layers)]
    slots = jnp.arange(pixels, dtype=jnp.int32)[:, None]

    def block_forward(field, mask, total, layer):
        padded = with_halo(field.reshape(rows, columns, width), "dp")
        hidden = conv(padded, taps[layer])
        sums = lax.psum(
            jnp.stack([jnp.sum(mask * hidden, 0), jnp.sum(mask * hidden * hidden, 0)]), "dp"
        )
        centre = sums[0] / total
        inverse = lax.rsqrt(sums[1] / total - centre * centre + EPS)
        normed = gain[layer] * (hidden - centre) * inverse + bias[layer]
        out = (mask * jax.nn.gelu(normed)).astype(BF16)
        return out, (padded, hidden, centre, inverse)

    def block_backward(d_out, kept, mask, total, layer):
        padded, hidden, centre, inverse = kept
        centred = (hidden - centre) * inverse
        normed = gain[layer] * (hidden - centre) * inverse + bias[layer]
        d_norm = gelu_back(normed, mask * d_out)
        gain_sum = jnp.sum(d_norm * centred, 0)
        bias_sum = jnp.sum(d_norm, 0)
        sums = gain[layer] * lax.psum(jnp.stack([bias_sum, gain_sum]), "dp")
        d_hidden = (
            mask * inverse * (gain[layer] * d_norm - sums[0] / total - centred * sums[1] / total)
        ).astype(BF16)
        d_hidden = d_hidden.reshape(rows, columns, width)
        d_x = conv_input_grad(with_halo(d_hidden, "dp"), taps[layer])
        return d_x, conv_weight_grad(padded, d_hidden), gain_sum, bias_sum

    outs, image_grads = [], []
    grads = None
    totals = lax.psum(counts[:, 0], "dp").astype(F32)
    for m in range(share):
        total = totals[m]
        mask = (slots < counts[m, 0]).astype(F32)
        first_in = jnp.where(slots < counts[m, 0], images[m], jnp.zeros((), BF16))
        f1, kept_0 = block_forward(first_in, mask, total, 0)
        f1_f = f1.astype(F32)
        source_0 = jnp.broadcast_to(f1[None], (tasks, pixels, width))
        squeezed_0, excited_0, gate_0 = gate_forward(source_0, w_squeeze[0], w_expand[0])
        t1 = (mask[None] * gate_0 * f1_f[None]).astype(BF16)
        f2, kept_1 = block_forward(f1, mask, total, 1)
        f2_f = f2.astype(F32)
        source_1 = (f2_f[None] + t1.astype(F32)).astype(BF16)
        squeezed_1, excited_1, gate_1 = gate_forward(source_1, w_squeeze[1], w_expand[1])
        outs.append(pool_pick(mask[None] * gate_1 * f2_f[None], pool_index[m]).astype(BF16))

        d_task = pool_spread(cotangent[m].astype(F32), pool_index[m])
        d_source, gs_1, ge_1 = gate_backward(
            d_task, mask * f2_f, source_1, squeezed_1, excited_1, gate_1, w_squeeze[1], w_expand[1]
        )
        d_f2 = (jnp.sum(d_source, 0) + mask * jnp.sum(d_task * gate_1, 0)).astype(BF16)
        d_t1 = d_source.astype(BF16).astype(F32)
        d_x1, gc_1, gain_1, bias_1 = block_backward(d_f2.astype(F32), kept_1, mask, total, 1)
        d_source, gs_0, ge_0 = gate_backward(
            d_t1, mask * f1_f, source_0, squeezed_0, excited_0, gate_0, w_squeeze[0], w_expand[0]
        )
        d_f1 = (
            d_x1.astype(BF16).astype(F32)
            + jnp.sum(d_source, 0)
            + mask * jnp.sum(d_t1 * gate_0, 0)
        ).astype(BF16)
        d_x0, gc_0, gain_0, bias_0 = block_backward(d_f1.astype(F32), kept_0, mask, total, 0)
        image_grads.append((mask * d_x0).astype(BF16))
        here_grads = [
            [gc_0, gc_1],
            [gs_0, gs_1],
            [ge_0, ge_1],
            jnp.stack([gain_0, gain_1]),
            jnp.stack([bias_0, bias_1]),
        ]
        grads = here_grads if grads is None else jax.tree.map(jnp.add, grads, here_grads)

    def reduced(value, axis):
        part = lax.psum_scatter(value, "dp", scatter_dimension=axis, tiled=True)
        return lax.psum(part.astype(BF16), "section").astype(F32)

    conv_grad = jnp.stack([reduced(g, 0) for g in grads[0]])
    squeeze_grad = jnp.stack([reduced(g, 1) for g in grads[1]])
    expand_grad = jnp.stack([reduced(g, 1) for g in grads[2]])
    gain_grad, bias_grad = lax.psum((grads[3], grads[4]), ("section", "dp"))
    return (
        jnp.stack(outs),
        jnp.stack(image_grads),
        conv_grad,
        squeeze_grad,
        expand_grad,
        gain_grad,
        bias_grad,
    )


GELU_C = 0.7978845608028654
GELU_K = 0.044715
MESH = pl.DeviceIdType.MESH


def gelu_pair(x):
    square = x * x
    t = jnp.tanh(GELU_C * x * (1.0 + GELU_K * square))
    half = 0.5 * (1.0 + t)
    slope = half + 0.5 * x * (1.0 - t * t) * (GELU_C * (1.0 + 3.0 * GELU_K * square))
    return x * half, slope


def dot(a, b):
    return jnp.dot(a, b, preferred_element_type=F32)


def dot_nt(a, b):
    return lax.dot_general(a, b, (((1,), (1,)), ((), ())), preferred_element_type=F32)


def dot_tn(a, b):
    return lax.dot_general(a, b, (((0,), (0,)), ((), ())), preferred_element_type=F32)


def step_kernel(
    dims,
    counts,
    picks,
    gain,
    bias,
    images,
    conv_w,
    squeeze_w,
    expand_w,
    cotangent,
    out_task,
    out_image,
    out_reduced_0,
    out_reduced_1,
    out_reduced_2,
    out_gain,
    out_bias,
    *scratch,
):
    out_reduced = (out_reduced_0, out_reduced_1, out_reduced_2)
    r = types.SimpleNamespace(**jax.tree.unflatten(dims.tree, scratch))
    n_dp, cols, pixels, width, tasks, bottle = (
        dims.n_dp,
        dims.cols,
        dims.pixels,
        dims.width,
        dims.tasks,
        dims.bottle,
    )
    n_z = n_dp // 2
    windows = cols // 2
    lanes = 128
    n_lane = width // lanes
    shard_rows = dims.shard_rows
    s = lax.axis_index("section")
    d = lax.axis_index("dp")
    z, c = d // 2, d % 2
    sib = 2 * z + 1 - c
    plane = [s + 1 - 2 * (s % 2), (s + 2) % 4, 3 - s]

    def rem(a, b):
        return lax.rem(a, b)

    def z_at(step):
        return rem(z + step, n_z)

    def remote(src, dst, send, recv, device):
        return pltpu.make_async_remote_copy(
            src_ref=src,
            dst_ref=dst,
            send_sem=send,
            recv_sem=recv,
            device_id=device,
            device_id_type=MESH,
        )

    def al(v, m):
        return pl.multiple_of(v, m)

    barrier = pltpu.get_barrier_semaphore()
    for step in range(1, n_dp):
        pl.semaphore_signal(
            barrier, inc=1, device_id=(s, rem(d + step, n_dp)), device_id_type=MESH
        )
    for p in plane:
        pl.semaphore_signal(barrier, inc=1, device_id=(p, d), device_id_type=MESH)

    def load(i, src, dst):
        return pltpu.make_async_copy(src, dst, r.load.at[i])

    staging = [r.h1, r.slope0]
    conv_rows = shard_rows[0]

    def conv_load(layer, j):
        lane = slice(j * lanes, (j + 1) * lanes)
        return load(
            5 + layer * n_lane + j,
            conv_w.at[layer, :, lane],
            staging[layer].at[j, 0:conv_rows],
        )

    loads = [
        load(1, squeeze_w, r.sst),
        load(2, expand_w, r.est),
        load(3, images.at[s], r.xin),
        load(4, cotangent.at[s], r.cin),
    ]
    loads[2].start()
    for layer in range(2):
        for j in range(n_lane):
            conv_load(layer, j).start()
    for i in (0, 1, 3):
        loads[i].start()

    full = [r.w0, r.gp, r.w1]

    def shard(kind, buf, which):
        rows = shard_rows[kind]
        return buf.at[pl.ds(al(which * rows, 16), rows)]

    def quarter(kind, buf, which, q):
        rows = shard_rows[kind]
        return buf.at[pl.ds(al(which * rows + q * (rows // 4), 16), rows // 4)]

    def z_of(way, hop):
        return z_at(n_z - hop if way == 0 else hop)

    def has(way, hop):
        return z >= hop if way == 0 else z < n_z - hop

    def slot_of(way, hop):
        return n_z - 1 - hop if way == 0 else hop - 1

    def ag_z_copy(kind, way, hop, owner):
        view = quarter(kind, full[kind], 2 * owner + c, s)
        return remote(
            view,
            view,
            r.ag_zs.at[kind, (hop - 1) * 2 + way],
            r.ag_zr.at[kind, slot_of(way, hop)],
            (s, 2 * z_at(1 if way == 0 else n_z - 1) + c),
        )

    def gate_z_copy(step, owner):
        view = quarter(1, full[1], 2 * owner + c, s)
        return remote(
            view,
            view,
            r.ag_zs.at[1, step - 1],
            r.ag_zr.at[1, step - 1],
            (s, 2 * z_at(step) + c),
        )

    def ag_pass(kind, way, hop, do):
        here_has = has(way, hop - 1) if hop > 1 else True
        there = z < n_z - 1 if way == 0 else z > 0
        owner = z_of(way, hop - 1)

        @pl.when(jnp.logical_and(here_has, there))
        def _():
            do(ag_z_copy(kind, way, hop, owner))

    halves = [slice(0, width // 2), slice(width // 2, width)]

    def ag_p_copy(kind, slot, owner, leg, q):
        view = quarter(kind, full[kind], 2 * owner + c, q)
        if leg >= 2:
            view = view.at[:, halves[leg - 2]]
        to = plane[(0, 1, 1, 0)[leg]]
        i = slot * 4 + leg
        return remote(view, view, r.ag_ps.at[kind, i], r.ag_pr.at[kind, i], (to, d))

    def ag_own_copy(kind, core):
        view = shard(kind, full[kind], 2 * z + core)
        return remote(view, view, r.ag_os.at[kind], r.ag_or.at[kind], (s, sib))

    def ag_s_copy(kind, slot, owner, i, core):
        view = quarter(kind, full[kind], 2 * owner + core, others[i])
        i = slot * 4 + i
        return remote(view, view, r.ag_ss.at[kind, i], r.ag_sr.at[kind, i], (s, sib))

    others = [s] + plane

    def ag_start(kind):
        if kind == 1:
            for step in range(1, n_z):
                gate_z_copy(step, z).start()
        else:
            for way in range(2):
                ag_pass(kind, way, 1, lambda copy: copy.start())
        ag_own_copy(kind, c).start()

    def for_hop(kind, hop, do):
        if kind == 1:
            do(hop - 1, z_at(n_z - hop), None)
            return
        for way in range(2):

            @pl.when(has(way, hop))
            def _():
                do(slot_of(way, hop), z_of(way, hop), way)

    def ag_z(kind, hop):
        def do(slot, owner, way):
            if kind == 1:
                gate_z_copy(hop, owner).wait_recv()
            else:
                ag_z_copy(kind, way, hop, owner).wait_recv()
                if hop < n_z - 1:
                    ag_pass(kind, way, hop + 1, lambda copy: copy.start())
            for leg in range(2):
                ag_p_copy(kind, slot, owner, leg, s).start()
            ag_s_copy(kind, slot, owner, 0, c).start()

        for_hop(kind, hop, do)

    def ag_r(kind, hop):
        def do(slot, owner, way):
            for leg in range(2):
                ag_p_copy(kind, slot, owner, leg, plane[leg]).wait_recv()
                ag_p_copy(kind, slot, owner, 2 + leg, plane[leg]).start()
                ag_s_copy(kind, slot, owner, 1 + leg, c).start()

        for_hop(kind, hop, do)

    def ag_p(kind, hop):
        def do(slot, owner, way):
            for leg in range(2):
                ag_p_copy(kind, slot, owner, 2 + leg, plane[2]).wait_recv()
            ag_s_copy(kind, slot, owner, 3, c).start()

        for_hop(kind, hop, do)

    def ag_sib(kind):
        ag_own_copy(kind, 1 - c).wait_recv()
        for hop in range(1, n_z):

            def do(slot, owner, way):
                for i in range(4):
                    ag_s_copy(kind, slot, owner, i, 1 - c).wait_recv()

            for_hop(kind, hop, do)

    def ag_end(kind):
        ag_own_copy(kind, c).wait_send()
        for hop in range(1, n_z):

            def do(slot, owner, way):
                for leg in range(2):
                    ag_p_copy(kind, slot, owner, leg, s).wait_send()
                    ag_p_copy(kind, slot, owner, 2 + leg, plane[leg]).wait_send()
                for i in range(4):
                    ag_s_copy(kind, slot, owner, i, c).wait_send()

            if kind == 1:
                gate_z_copy(hop, z).wait_send()
            else:
                for way in range(2):
                    ag_pass(kind, way, hop, lambda copy: copy.wait_send())
            for_hop(kind, hop, do)

    def cast_conv(layer, buf):
        for j in range(n_lane):
            conv_load(layer, j).wait()

        def body(j, _):
            buf[pl.ds(al(d * conv_rows, 16), conv_rows), pl.ds(al(j * lanes, lanes), lanes)] = (
                staging[layer][j, 0:conv_rows, :].astype(BF16)
            )
            return 0

        lax.fori_loop(0, n_lane, body, 0)

    g_rows = shard_rows[1]
    e_rows = n_ex = bottle // n_dp
    s_rows = width // n_dp
    n_sub = s_rows // e_rows

    def ex_row(which, l, t):
        return al(which * g_rows + (l * tasks + t) * e_rows, 16)

    def sq_row(which, l, t):
        return al(which * g_rows + (2 * tasks + l * tasks + t) * e_rows, 16)

    count = counts[s]
    wide = 2 * lanes
    pick_row = jnp.concatenate(
        [picks[s].astype(F32), jnp.zeros((1, wide - windows), F32)], axis=1
    )
    pick_tile = jnp.broadcast_to(pick_row, (lanes, wide)).T[:windows, :].astype(jnp.int32)
    pick_ref = r.pick
    pick_ref[...] = pick_tile
    slot_pick = (
        (pick_tile // 2) * cols
        + 2 * lax.broadcasted_iota(jnp.int32, (windows, lanes), 0)
        + pick_tile % 2
    )
    r.mp[...] = jnp.where(slot_pick < count, 1.0, 0.0).astype(F32)

    def lane_at(j, base=0):
        return pl.ds(al(base + j * lanes, lanes), lanes)

    def valid_rows(start, rows):
        return (lax.broadcasted_iota(jnp.int32, (rows, lanes), 0) + start) < count

    def shift_in(value_of, buf, block):
        def body(j, _):
            v = value_of(j)
            at = lax.broadcasted_iota(jnp.int32, (cols, lanes), 0)
            before = jnp.where(at == 0, 0.0, pltpu.roll(v, 1, 0))
            after = jnp.where(at == cols - 1, 0.0, pltpu.roll(v, cols - 1, 0))
            rows = pl.ds(block * cols, cols)
            buf[rows, lane_at(j)] = before.astype(BF16)
            buf[rows, lane_at(j, width)] = v.astype(BF16)
            buf[rows, lane_at(j, 2 * width)] = after.astype(BF16)
            return 0

        lax.fori_loop(0, n_lane, body, 0)

    @pl.when(d == 0)
    def _():
        r.halo[:, 0] = jnp.zeros_like(r.halo[:, 0])

    @pl.when(d == n_dp - 1)
    def _():
        r.halo[:, 1] = jnp.zeros_like(r.halo[:, 1])

    def halo_down(e, buf):
        return remote(
            buf.at[2 * cols : 3 * cols, width : 2 * width],
            r.halo.at[e % 2, 0],
            r.halo_s.at[e, 0],
            r.halo_r.at[e, 0],
            (s, rem(d + 1, n_dp)),
        )

    def halo_up(e, buf):
        return remote(
            buf.at[cols : 2 * cols, width : 2 * width],
            r.halo.at[e % 2, 1],
            r.halo_s.at[e, 1],
            r.halo_r.at[e, 1],
            (s, rem(d + n_dp - 1, n_dp)),
        )

    def halo_start(e, buf):
        @pl.when(d < n_dp - 1)
        def _():
            halo_down(e, buf).start()

        @pl.when(d > 0)
        def _():
            halo_up(e, buf).start()

    def halo_finish(e, buf):
        @pl.when(d > 0)
        def _():
            halo_down(e, buf).wait_recv()

        @pl.when(d < n_dp - 1)
        def _():
            halo_up(e, buf).wait_recv()

        shift_in(lambda j: r.halo[e % 2, 0, :, lane_at(j)].astype(F32), buf, 0)
        shift_in(lambda j: r.halo[e % 2, 1, :, lane_at(j)].astype(F32), buf, 3)

    def halo_sent(e, buf):
        @pl.when(d < n_dp - 1)
        def _():
            halo_down(e, buf).wait_send()

        @pl.when(d > 0)
        def _():
            halo_up(e, buf).wait_send()

    def ex_copy(k, step, owner):
        turn = (k + 1) % 5 % 2
        return remote(
            r.ex_out.at[k],
            r.ex_in.at[k, owner],
            r.ex_s.at[turn, step - 1],
            r.ex_r.at[turn, step - 1],
            (s, rem(d + step, n_dp)),
        )

    def ex_sent(k):
        for step in range(1, n_dp):
            ex_copy(k, step, d).wait_send()

    def ex_start(k):
        if k in (1, 2, 3):
            ex_sent((4, 0, 1)[k - 1])
        for step in range(1, n_dp):
            ex_copy(k, step, d).start()
        r.ex_in[k, d] = r.ex_out[k]

    def ex_finish(k):
        for step in range(1, n_dp):
            ex_copy(k, step, rem(d + n_dp - step, n_dp)).wait_recv()
        total = r.ex_in[k, 0]
        for i in range(1, n_dp):
            total = total + r.ex_in[k, i]
        return [
            jnp.concatenate([total[i * n_lane + j : i * n_lane + j + 1] for j in range(n_lane)], 1)
            for i in range(2)
        ]

    def ex_put(k, i, j, value):
        r.ex_out[k, pl.ds(i * n_lane + j, 1), :] = value

    def conv_forward(xc, w, h, row, part):
        span = 3 * width
        acc = None
        for a in range(3):
            block = a + row
            if (block in (0, 3)) != (part == 1):
                continue
            term = dot(xc[block * cols : (block + 1) * cols, :], w[a * span : (a + 1) * span, :])
            acc = term if acc is None else acc + term
        add_to(h, row, part, acc)

    def add_to(out, row, part, acc):
        for j in range(n_lane):
            at = (j, slice(row * cols, (row + 1) * cols), slice(None))
            piece = acc[:, j * lanes : (j + 1) * lanes]
            out[at] = piece if part == 0 else out[at] + piece

    def conv_back(dc, w, row, part):
        acc = None
        for a in range(3):
            block = 2 - a + row
            if (block in (0, 3)) != (part == 1):
                continue
            for b in range(3):
                term = dot_nt(
                    dc[block * cols : (block + 1) * cols, (2 - b) * width : (3 - b) * width],
                    w[(3 * a + b) * width : (3 * a + b + 1) * width, :],
                )
                acc = term if acc is None else acc + term
        add_to(r.fbuf, row, part, acc)

    quarter_rows = pixels // 4

    def stats(h, k):
        def body(j, _):
            first = jnp.zeros((1, lanes), F32)
            second = jnp.zeros((1, lanes), F32)
            for i in range(4):
                v = h[j, i * quarter_rows : (i + 1) * quarter_rows, :]
                kept = jnp.where(valid_rows(i * quarter_rows, quarter_rows), v, 0.0)
                first = first + jnp.sum(kept, 0, keepdims=True)
                second = second + jnp.sum(kept * v, 0, keepdims=True)
            ex_put(k, 0, j, first)
            ex_put(k, 1, j, second)
            return 0

        lax.fori_loop(0, n_lane, body, 0)

    def norm_of(sums, layer):
        total = r.total[0:1, :]
        centre = sums[0] / total
        inverse = lax.rsqrt(sums[1] / total - centre * centre + EPS)
        r.norm[layer, 0:1, :] = centre
        r.norm[layer, 1:2, :] = inverse
        r.norm[layer, 2:3, :] = gain[layer : layer + 1, :] * inverse
        r.norm[layer, 3:4, :] = 1.0 / total

    def corner_rows(k):
        return pl.ds((k // 2) * cols + k % 2, windows, stride=2)

    def picked(ref, j):
        out = None
        which = pick_ref[...]
        for k in range(4):
            part = jnp.where(which == k, ref[j, corner_rows(k), :], 0.0)
            out = part if out is None else out + part
        return out

    loads[2].wait()

    def image_row(i):
        def value(j):
            v = r.xin[i * cols : (i + 1) * cols, lane_at(j)].astype(F32)
            return jnp.where(valid_rows(i * cols, cols), v, 0.0)

        return value

    shift_in(image_row(0), r.xc0, 1)
    shift_in(image_row(1), r.xc0, 2)
    cast_conv(0, r.w0)
    pl.semaphore_wait(barrier, n_dp - 1 + 3)
    ag_start(0)
    r.ex_out[4] = jnp.broadcast_to(count.astype(F32), (8, lanes))
    ex_start(4)
    loads[0].wait()
    loads[1].wait()
    for l in range(2):
        for t in range(tasks):
            r.gp[pl.ds(ex_row(d, l, t), e_rows), :] = r.est[l, t].astype(BF16)
            for k in range(n_sub):
                r.gp[pl.ds(sq_row(d, l, t), e_rows), k * lanes : (k + 1) * lanes] = r.sst[
                    l, t, k * e_rows : (k + 1) * e_rows, :
                ].astype(BF16)
    cast_conv(1, r.w1)
    ag_z(0, 1)
    ag_z(0, 2)
    ag_r(0, 1)
    ag_z(0, 3)
    ag_start(2)
    ag_r(0, 2)
    ag_p(0, 1)
    ag_r(0, 3)
    ag_z(2, 1)
    halo_start(0, r.xc0)
    r.total[...] = jnp.concatenate([ex_finish(4)[0]] * 8, axis=0)
    ag_p(0, 2)
    ag_p(0, 3)
    ag_sib(0)
    ag_z(2, 2)
    conv_forward(r.xc0, r.w0, r.h0, 0, 0)
    conv_forward(r.xc0, r.w0, r.h0, 1, 0)
    ag_r(2, 1)
    halo_finish(0, r.xc0)
    conv_forward(r.xc0, r.w0, r.h0, 0, 1)
    conv_forward(r.xc0, r.w0, r.h0, 1, 1)
    stats(r.h0, 0)
    ex_start(0)
    halo_sent(0, r.xc0)
    ag_z(2, 3)
    ag_start(1)
    ag_r(2, 2)
    ag_p(2, 1)
    norm_of(ex_finish(0), 0)

    def block_0(j, _):
        lane = lane_at(j)
        for i in range(4):
            rows = slice(i * quarter_rows, (i + 1) * quarter_rows)
            normed = (r.h0[j, rows, :] - r.norm[0, 0:1, lane]) * r.norm[
                0, 2:3, lane
            ] + bias[0:1, lane]
            g, slope = gelu_pair(normed)
            ok = valid_rows(i * quarter_rows, quarter_rows)
            r.fbuf[j, rows, :] = jnp.where(ok, g, 0.0).astype(BF16).astype(F32)
            r.slope0[j, rows, :] = jnp.where(ok, slope, 0.0)
        f1p = picked(r.fbuf, j)
        r.f1p[:, lane] = f1p
        r.f1b[:, lane] = f1p.astype(BF16)
        return 0

    lax.fori_loop(0, n_lane, block_0, 0)
    shift_in(lambda j: r.fbuf[j, 0:cols, :], r.xc1, 1)
    shift_in(lambda j: r.fbuf[j, cols : 2 * cols, :], r.xc1, 2)
    halo_start(1, r.xc1)
    ag_r(2, 3)
    ag_p(2, 2)
    for step in range(1, n_z):
        ag_z(1, step)
    ag_p(2, 3)
    ag_sib(2)
    conv_forward(r.xc1, r.w1, r.h1, 0, 0)
    for step in range(1, n_z):
        ag_r(1, step)
    conv_forward(r.xc1, r.w1, r.h1, 1, 0)
    halo_finish(1, r.xc1)
    conv_forward(r.xc1, r.w1, r.h1, 0, 1)
    conv_forward(r.xc1, r.w1, r.h1, 1, 1)
    stats(r.h1, 1)
    ex_start(1)
    for hop in range(1, n_z):
        ag_p(1, hop)
    ag_sib(1)

    def unpack(i, _):
        for l in range(2):
            for t in range(tasks):
                r.ex_w[l, t, pl.ds(al(i * e_rows, 16), e_rows), :] = r.gp[
                    pl.ds(ex_row(i, l, t), e_rows), :
                ]
                for k in range(n_sub):
                    r.sq_w[
                        l,
                        pl.ds(al(i * s_rows + k * e_rows, 16), e_rows),
                        t * bottle : (t + 1) * bottle,
                    ] = r.gp[pl.ds(sq_row(i, l, t), e_rows), k * lanes : (k + 1) * lanes]
        return 0

    lax.fori_loop(0, n_dp, unpack, 0)
    mask_pick = jnp.concatenate([r.mp[...]] * n_lane, axis=1)
    g, slope = gelu_pair(dot(r.f1b[...], r.sq_w[0]))
    r.excited0[...] = g.astype(BF16)
    r.eslope0[...] = slope

    def task_lane(t):
        return pl.ds(al(t * bottle, lanes), bottle)

    def gate_0(t, _):
        value = jax.nn.sigmoid(dot(r.excited0[:, task_lane(t)], r.ex_w[0, t]))
        r.gate0[t] = value
        r.t1[t] = (mask_pick * value * r.f1p[...]).astype(BF16)
        return 0

    lax.fori_loop(0, tasks, gate_0, 0)
    norm_of(ex_finish(1), 1)

    for kind in range(3):
        ag_end(kind)
    for p in plane:
        pl.semaphore_signal(r.ready, inc=1, device_id=(p, d), device_id_type=MESH)

    def block_1(j, _):
        lane = lane_at(j)
        off = picked(r.h1, j) - r.norm[1, 0:1, lane]
        g, slope = gelu_pair(off * r.norm[1, 2:3, lane] + bias[1:2, lane])
        r.f2p[:, lane] = (r.mp[...] * g).astype(BF16).astype(F32)
        r.slope1[:, lane] = r.mp[...] * slope
        r.centred1[:, lane] = off * r.norm[1, 1:2, lane]
        return 0

    lax.fori_loop(0, n_lane, block_1, 0)
    grads = [r.w1, r.gp, r.g1]

    def pair_of(k):
        return z_at((2, 1, 3, 0)[k])

    def rs_a_copy(kind, k, core):
        return remote(
            shard(kind, grads[kind], 2 * pair_of(k) + core),
            r.ra[kind].at[k],
            r.rs_as.at[kind, k],
            r.rs_ar.at[kind, k],
            (s, sib),
        )

    def again(first, second, i):
        per = 4 * (n_z - 1)
        return (first if i < 3 * per else second).at[i // per % 3, i % per]

    def rs_b_copy(kind, k, way):
        o = 2 * pair_of(k) + c
        half = (0, 0, 1, 1, 0, 1)[way]
        to = plane[(0, 0, 1, 1, 1, 0)[way]]
        q = to if way in (0, 2, 4, 5) else plane[2]
        return remote(
            quarter(kind, grads[kind], o, q).at[:, halves[half]],
            r.rb[kind].at[k, way],
            again(r.ag_ps, r.ag_ss, (kind * n_z + k) * 6 + way),
            again(r.ag_pr, r.ag_sr, (kind * n_z + k) * 6 + way),
            (to, d),
        )

    def rs_c_copy(kind, k):
        return remote(
            r.qs[kind].at[k],
            r.rc[kind].at[k],
            r.rs_cs.at[kind, k],
            r.rs_cr.at[kind, k],
            (s, 2 * pair_of(k) + c),
        )

    def rs_d_copy(kind, leg, q):
        rows = shard_rows[kind] // 4
        half = (0, 1, 1, 0, 0, 1)[leg]
        to = plane[(0, 1, 0, 1, 1, 0)[leg]]
        view = r.td[kind].at[pl.ds(al(q * rows, 16), rows), halves[half]]
        return remote(view, view, r.rs_ds.at[kind, leg], r.rs_dr.at[kind, leg], (to, d))

    def conv_weight(kind, xc, k):
        tile = 2 * shard_rows[kind] // 3
        per = 3 * width // tile

        for i in range(3):
            g = pair_of(k) * 3 + i
            a = g // per
            term = dot_tn(
                xc[pl.ds(al(a * cols, 16), pixels), pl.ds(al((g % per) * tile, lanes), tile)],
                r.dc[cols : 3 * cols, width : 2 * width],
            )
            grads[kind][pl.ds(al(g * tile, 16), tile), :] = term.astype(BF16)

    def rs_a(kind, k):
        rs_a_copy(kind, k, 1 - c).start()

    def rs_b(kind, k):
        rs_a_copy(kind, k, c).wait_recv()
        rows = shard_rows[kind]
        tile = rows // 4
        start = (2 * pair_of(k) + c) * rows

        def body(i, _):
            at = pl.ds(al(start + i * tile, 16), tile)
            grads[kind][at, :] = (
                grads[kind][at, :].astype(F32)
                + r.ra[kind][k, pl.ds(al(i * tile, 16), tile), :].astype(F32)
            ).astype(BF16)
            return 0

        lax.fori_loop(0, 4, body, 0)
        for way in range(4):
            rs_b_copy(kind, k, way).start()

    def quarter_at(kind, k, q):
        rows = shard_rows[kind]
        return pl.ds(al((2 * pair_of(k) + c) * rows + q * (rows // 4), 16), rows // 4)

    def rs_r(kind, k):
        for half in range(2):
            rs_b_copy(kind, k, 2 * half).wait_recv()
            rs_b_copy(kind, k, 2 * half + 1).wait_recv()
            at = quarter_at(kind, k, plane[1 - half])
            grads[kind][at, halves[half]] = (
                grads[kind][at, halves[half]].astype(F32)
                + r.rb[kind][k, 2 * half + 1].astype(F32)
            ).astype(BF16)
            rs_b_copy(kind, k, 4 + half).start()

    def rs_c(kind, k):
        at = quarter_at(kind, k, s)
        parts = []
        for half in range(2):
            rs_b_copy(kind, k, 4 + half).wait_recv()
            parts.append(
                grads[kind][at, halves[half]].astype(F32)
                + r.rb[kind][k, 2 * half].astype(F32)
                + r.rb[kind][k, 4 + half].astype(F32)
            )
        total = jnp.concatenate(parts, axis=1)
        if k < n_z - 1:
            r.qs[kind][k] = total.astype(BF16)
            rs_c_copy(kind, k).start()
        else:
            r.qf[kind][...] = total

    def rs_d(kind):
        total = r.qf[kind][...]
        for k in range(n_z - 1):
            rs_c_copy(kind, k).wait_recv()
            total = total + r.rc[kind][k].astype(F32)
        rows = shard_rows[kind] // 4
        r.td[kind][pl.ds(al(s * rows, 16), rows), :] = total.astype(BF16)
        for leg in range(4):
            rs_d_copy(kind, leg, s).start()

    def rs_dr(kind):
        for leg in range(2):
            rs_d_copy(kind, leg, plane[leg]).wait_recv()
            rs_d_copy(kind, 4 + leg, plane[leg]).start()

    def rs_e(kind):
        for leg in range(2):
            rs_d_copy(kind, 2 + leg, plane[leg]).wait_recv()
            rs_d_copy(kind, 4 + leg, plane[2]).wait_recv()

    def rs_end(kind):
        for k in range(n_z):
            rs_a_copy(kind, k, 1 - c).wait_send()
            for way in range(6):
                rs_b_copy(kind, k, way).wait_send()
            if k < n_z - 1:
                rs_c_copy(kind, k).wait_send()
        for leg in range(4):
            rs_d_copy(kind, leg, s).wait_send()
        for leg in range(2):
            rs_d_copy(kind, 4 + leg, plane[leg]).wait_send()

    loads[3].wait()
    r.df2[...] = jnp.zeros_like(r.df2)

    def pack_grads(l, t, grad_squeeze, grad_expand):
        r.fbuf[0, 0:width, :] = grad_squeeze
        for j in range(n_lane):
            r.fbuf[1, j * bottle : (j + 1) * bottle, :] = grad_expand[:, j * lanes : (j + 1) * lanes]

        def body(i, _):
            for j in range(n_lane):
                lane = slice(j * lanes, (j + 1) * lanes)
                r.gp[pl.ds(ex_row(i, l, t), e_rows), lane] = r.fbuf[
                    1, pl.ds(al(j * bottle + i * e_rows, 16), e_rows), :
                ].astype(BF16)
            for k in range(n_sub):
                r.gp[pl.ds(sq_row(i, l, t), e_rows), k * lanes : (k + 1) * lanes] = r.fbuf[
                    0, pl.ds(al(i * s_rows + k * e_rows, 16), e_rows), :
                ].astype(BF16)
            return 0

        lax.fori_loop(0, n_dp, body, 0)

    def kept(i):
        return pl.ds(al(i * windows, 16), windows)

    def gate_1(t, _):
        w_s = r.sq_w[1, :, task_lane(t)]
        w_e = r.ex_w[1, t]
        f2p = r.f2p[...]
        source = (f2p + r.t1[t].astype(F32)).astype(BF16)
        g, slope = gelu_pair(dot(source, w_s))
        excited = g.astype(BF16)
        value = jax.nn.sigmoid(dot(excited, w_e))
        field = mask_pick * f2p
        d_task = r.cin[t].astype(F32)
        r.cin[t] = (value * field).astype(BF16)
        d_expanded = (d_task * field * value * (1.0 - value)).astype(BF16)
        d_squeezed = (slope * dot_nt(d_expanded, w_e)).astype(BF16)
        d_source = dot_nt(d_squeezed, w_s)
        r.t1[t] = d_source.astype(BF16)
        r.df2[...] += d_source + mask_pick * d_task * value
        r.g1[kept(t), :] = source
        r.g1[kept(tasks + t), :] = d_expanded
        r.g1[kept(2 * tasks), task_lane(t)] = excited
        r.g1[kept(2 * tasks + 1), task_lane(t)] = d_squeezed
        return 0

    def gate_1_weight(t, _):
        pack_grads(
            1,
            t,
            dot_tn(r.g1[kept(t), :], r.g1[kept(2 * tasks + 1), task_lane(t)]),
            dot_tn(r.g1[kept(2 * tasks), task_lane(t)], r.g1[kept(tasks + t), :]),
        )
        return 0

    lax.fori_loop(0, tasks, gate_1, 0)
    task_store = pltpu.make_async_copy(r.cin, out_task.at[0], r.store.at[0])
    task_store.start()

    def back_1(j, _):
        lane = lane_at(j)
        d_norm = r.slope1[:, lane] * r.df2[:, lane].astype(BF16).astype(F32)
        r.df2[:, lane] = d_norm
        ex_put(2, 0, j, jnp.sum(d_norm, 0, keepdims=True))
        ex_put(2, 1, j, jnp.sum(d_norm * r.centred1[:, lane], 0, keepdims=True))
        return 0

    lax.fori_loop(0, n_lane, back_1, 0)
    ex_start(2)

    r.df1[...] = jnp.zeros_like(r.df1)

    def gate_0_back(t, _):
        w_s = r.sq_w[0, :, task_lane(t)]
        w_e = r.ex_w[0, t]
        value = r.gate0[t]
        d_task = r.t1[t].astype(F32)
        excited = r.excited0[:, task_lane(t)]
        d_expanded = (d_task * (mask_pick * r.f1p[...]) * value * (1.0 - value)).astype(BF16)
        d_squeezed = (r.eslope0[:, task_lane(t)] * dot_nt(d_expanded, w_e)).astype(BF16)
        r.df1[...] += dot_nt(d_squeezed, w_s) + mask_pick * d_task * value
        pack_grads(0, t, dot_tn(r.f1b[...], d_squeezed), dot_tn(excited, d_expanded))
        return 0

    lax.fori_loop(0, tasks, gate_0_back, 0)
    lax.fori_loop(0, tasks, gate_1_weight, 0)

    r.sums[...] = jnp.zeros_like(r.sums)

    def back_terms(k, layer):
        sums = ex_finish(k)
        r.sums[2 * layer : 2 * layer + 1, :] = sums[0]
        r.sums[2 * layer + 1 : 2 * layer + 2, :] = sums[1]
        scale = gain[layer : layer + 1, :] * r.norm[layer, 3:4, :] * r.norm[layer, 1:2, :]
        r.norm[layer, 4:5, :] = scale * sums[0]
        r.norm[layer, 5:6, :] = scale * r.norm[layer, 1:2, :] * sums[1]

    for k in range(n_z):
        rs_a(1, k)
    back_terms(2, 1)

    def hidden_grad_1(j, _):
        lane = lane_at(j)
        norm = r.norm
        for k in range(4):
            at = corner_rows(k)
            spread = jnp.where(pick_ref[...] == k, r.df2[:, lane] * norm[1, 2:3, lane], 0.0)
            value = spread - (
                norm[1, 4:5, lane] + (r.h1[j, at, :] - norm[1, 0:1, lane]) * norm[1, 5:6, lane]
            )
            slot = (k // 2) * cols + k % 2 + 2 * lax.broadcasted_iota(
                jnp.int32, (windows, lanes), 0
            )
            r.fbuf[j, at, :] = jnp.where(slot < count, value, 0.0)
        return 0

    lax.fori_loop(0, n_lane, hidden_grad_1, 0)
    shift_in(lambda j: r.fbuf[j, 0:cols, :], r.dc, 1)
    shift_in(lambda j: r.fbuf[j, cols : 2 * cols, :], r.dc, 2)
    halo_start(2, r.dc)

    pl.semaphore_wait(r.ready, 3)
    for k in range(n_z):
        rs_b(1, k)
    for k in range(2):
        conv_weight(2, r.xc1, k)
        rs_a(2, k)
    conv_back(r.dc, r.w1, 0, 0)
    rs_b(2, 0)
    conv_back(r.dc, r.w1, 1, 0)
    for k in range(n_z):
        rs_r(1, k)
    rs_b(2, 1)
    halo_finish(2, r.dc)
    conv_back(r.dc, r.w1, 0, 1)
    conv_back(r.dc, r.w1, 1, 1)
    def back_0(j, _):
        lane = lane_at(j)
        norm = r.norm
        first = jnp.zeros((1, lanes), F32)
        second = jnp.zeros((1, lanes), F32)
        for k in range(4):
            at = corner_rows(k)
            d_field = r.fbuf[j, at, :].astype(BF16).astype(F32) + jnp.where(
                pick_ref[...] == k, r.df1[:, lane], 0.0
            )
            d_norm = r.slope0[j, at, :] * d_field.astype(BF16).astype(F32)
            r.fbuf[j, at, :] = d_norm
            centred = (r.h0[j, at, :] - norm[0, 0:1, lane]) * norm[0, 1:2, lane]
            first = first + jnp.sum(d_norm, 0, keepdims=True)
            second = second + jnp.sum(d_norm * centred, 0, keepdims=True)
        ex_put(3, 0, j, first)
        ex_put(3, 1, j, second)
        return 0

    lax.fori_loop(0, n_lane, back_0, 0)
    ex_start(3)
    conv_weight(2, r.xc1, 2)
    rs_a(2, 2)
    rs_r(2, 0)
    conv_weight(2, r.xc1, 3)
    rs_a(2, 3)
    rs_b(2, 2)
    halo_sent(2, r.dc)
    back_terms(3, 0)

    def sums_copy(p, q):
        return remote(
            r.sums,
            r.sums_in.at[q],
            r.sums_s.at[p],
            r.sums_r.at[p],
            (plane[p], d),
        )

    for p in range(3):
        sums_copy(p, s).start()
    r.sums_in[s] = r.sums[...]

    def hidden_grad_0(row):
        def value(j):
            lane = lane_at(j)
            norm = r.norm
            rows = slice(row * cols, (row + 1) * cols)
            out = r.fbuf[j, rows, :] * norm[0, 2:3, lane] - (
                norm[0, 4:5, lane] + (r.h0[j, rows, :] - norm[0, 0:1, lane]) * norm[0, 5:6, lane]
            )
            return jnp.where(valid_rows(row * cols, cols), out, 0.0)

        return value

    shift_in(hidden_grad_0(0), r.dc, 1)
    shift_in(hidden_grad_0(1), r.dc, 2)
    halo_start(3, r.dc)
    conv_weight(0, r.xc0, 0)
    rs_a(0, 0)
    rs_r(2, 1)
    rs_b(2, 3)
    for k in range(n_z):
        rs_c(1, k)
    conv_weight(0, r.xc0, 1)
    rs_a(0, 1)
    rs_c(2, 0)
    conv_weight(0, r.xc0, 2)
    rs_a(0, 2)
    rs_r(2, 2)
    rs_b(0, 0)
    conv_weight(0, r.xc0, 3)
    rs_a(0, 3)
    rs_c(2, 1)
    conv_back(r.dc, r.w0, 0, 0)
    rs_r(2, 3)
    rs_b(0, 1)
    conv_back(r.dc, r.w0, 1, 0)
    rs_c(2, 2)
    halo_finish(3, r.dc)
    conv_back(r.dc, r.w0, 0, 1)
    conv_back(r.dc, r.w0, 1, 1)
    def image_out(j, _):
        lane = lane_at(j)
        for i in range(4):
            rows = slice(i * quarter_rows, (i + 1) * quarter_rows)
            r.xin[rows, lane] = jnp.where(
                valid_rows(i * quarter_rows, quarter_rows), r.fbuf[j, rows, :], 0.0
            ).astype(BF16)
        return 0

    lax.fori_loop(0, n_lane, image_out, 0)
    image_store = pltpu.make_async_copy(r.xin, out_image.at[0], r.store.at[1])
    image_store.start()
    rs_r(0, 0)
    rs_b(0, 2)
    rs_c(2, 3)
    rs_r(0, 1)
    rs_c(0, 0)
    rs_b(0, 3)
    rs_r(0, 2)
    rs_c(0, 1)
    rs_r(0, 3)
    rs_c(0, 2)
    rs_d(1)
    rs_d(2)
    rs_c(0, 3)
    rs_dr(1)
    rs_dr(2)
    rs_d(0)
    for p in range(3):
        sums_copy(p, plane[p]).wait_recv()
    total = r.sums_in[0]
    for i in range(1, 4):
        total = total + r.sums_in[i]
    for l in range(2):
        out_bias[l : l + 1, :] = total[2 * l : 2 * l + 1, :]
        out_gain[l : l + 1, :] = total[2 * l + 1 : 2 * l + 2, :]
    for p in range(3):
        sums_copy(p, s).wait_send()
    ex_sent(2)
    ex_sent(3)
    halo_sent(3, r.dc)
    halo_sent(1, r.xc1)
    rs_dr(0)
    stores = [task_store, image_store]

    def reduced_out(kind):
        rs_e(kind)
        stores.append(
            pltpu.make_async_copy(r.td[kind], out_reduced[kind], r.store.at[2 + kind])
        )
        stores[-1].start()

    reduced_out(1)
    reduced_out(2)
    for kind in range(1, 3):
        rs_end(kind)
    reduced_out(0)
    rs_end(0)
    for copy in stores:
        copy.wait()


def finish_kernel(
    dims,
    task,
    image,
    reduced_0,
    reduced_1,
    reduced_2,
    gain,
    bias,
    out_task,
    out_image,
    out_conv,
    out_squeeze,
    out_expand,
    out_gain,
    out_bias,
    task_in,
    image_in,
    conv_in,
    conv_wide,
    gate_in,
    squeeze_wide,
    expand_wide,
    sem_in,
    sem_out,
):
    lanes = 128
    e_rows = dims.bottle // dims.n_dp
    ins = [
        pltpu.make_async_copy(reduced_0, conv_in.at[0], sem_in.at[0]),
        pltpu.make_async_copy(reduced_2, conv_in.at[1], sem_in.at[1]),
        pltpu.make_async_copy(reduced_1, gate_in, sem_in.at[2]),
        pltpu.make_async_copy(task, task_in, sem_in.at[3]),
        pltpu.make_async_copy(image, image_in, sem_in.at[4]),
    ]
    for copy in ins:
        copy.start()
    outs = [
        pltpu.make_async_copy(task_in, out_task, sem_out.at[0]),
        pltpu.make_async_copy(image_in, out_image, sem_out.at[1]),
    ]
    out_gain[...] = gain[...]
    out_bias[...] = bias[...]
    for layer in range(2):
        ins[layer].wait()
        conv_wide[layer] = conv_in[layer].astype(F32)
        outs.append(
            pltpu.make_async_copy(
                conv_wide.at[layer], out_conv.at[layer], sem_out.at[2 + layer]
            )
        )
        outs[-1].start()
    for i in range(2):
        ins[3 + i].wait()
        outs[i].start()
    ins[2].wait()
    for l in range(2):
        for t in range(dims.tasks):
            at = (l * dims.tasks + t) * e_rows
            expand_wide[l, t] = gate_in[at : at + e_rows, :].astype(F32)
            at = at + 2 * dims.tasks * e_rows
            for k in range(dims.width // dims.n_dp // e_rows):
                squeeze_wide[l, t, k * e_rows : (k + 1) * e_rows, :] = gate_in[
                    at : at + e_rows, k * lanes : (k + 1) * lanes
                ].astype(F32)
    outs.append(pltpu.make_async_copy(squeeze_wide, out_squeeze, sem_out.at[4]))
    outs.append(pltpu.make_async_copy(expand_wide, out_expand, sem_out.at[5]))
    outs[-2].start()
    outs[-1].start()
    for copy in outs:
        copy.wait()


def fused(images, counts, pool_index, conv_w, squeeze_w, expand_w, gain, bias, cotangent):
    n_dp = lax.axis_size("dp")
    micro, pixels, width = images.shape
    tasks, bottle = squeeze_w.shape[1], squeeze_w.shape[3]
    cols = 2 * pool_index.shape[2]
    windows = cols // 2
    conv_rows = conv_w.shape[1]
    gate_rows = 4 * tasks * expand_w.shape[2]
    shard_rows = (conv_rows, gate_rows, conv_rows)
    n_z = n_dp // 2
    vm = pltpu.VMEM
    dma = pltpu.SemaphoreType.DMA
    scratch = dict(
        load=dma((5 + 2 * (width // 128),)),
        store=dma((5,)),
        sst=vm(squeeze_w.shape, F32),
        est=vm(expand_w.shape, F32),
        xin=vm((pixels, width), BF16),
        cin=vm((tasks, windows, width), BF16),
        w0=vm((n_dp * conv_rows, width), BF16),
        gp=vm((n_dp * gate_rows, width), BF16),
        w1=vm((n_dp * conv_rows, width), BF16),
        g1=vm((n_dp * conv_rows, width), BF16),
        sq_w=vm((2, width, tasks * bottle), BF16),
        ex_w=vm((2, tasks, bottle, width), BF16),
        ag_zs=dma((3, 2 * (n_z - 1))),
        ag_zr=dma((3, n_z - 1)),
        ag_ps=dma((3, 4 * (n_z - 1))),
        ag_pr=dma((3, 4 * (n_z - 1))),
        ag_ss=dma((3, 4 * (n_z - 1))),
        ag_sr=dma((3, 4 * (n_z - 1))),
        ag_os=dma((3,)),
        ag_or=dma((3,)),
        mp=vm((windows, 128), F32),
        pick=vm((windows, 128), jnp.int32),
        halo=vm((2, 2, cols, width), BF16),
        halo_s=dma((4, 2)),
        halo_r=dma((4, 2)),
        ex_out=vm((5, 8, 128), F32),
        ex_in=vm((5, n_dp, 8, 128), F32),
        total=vm((8, width), F32),
        ex_s=dma((2, n_dp - 1)),
        ex_r=dma((2, n_dp - 1)),
        norm=vm((2, 8, width), F32),
        xc0=vm((4 * cols, 3 * width), BF16),
        xc1=vm((4 * cols, 3 * width), BF16),
        dc=vm((4 * cols, 3 * width), BF16),
        h0=vm((width // 128, pixels, 128), F32),
        h1=vm((width // 128, pixels, 128), F32),
        slope0=vm((width // 128, pixels, 128), F32),
        fbuf=vm((width // 128, pixels, 128), F32),
        f1p=vm((windows, width), F32),
        f1b=vm((windows, width), BF16),
        excited0=vm((windows, tasks * bottle), BF16),
        eslope0=vm((windows, tasks * bottle), F32),
        gate0=vm((tasks, windows, width), F32),
        t1=vm((tasks, windows, width), BF16),
        f2p=vm((windows, width), F32),
        slope1=vm((windows, width), F32),
        centred1=vm((windows, width), F32),
        df2=vm((windows, width), F32),
        df1=vm((windows, width), F32),
        sums=vm((8, width), F32),
        sums_in=vm((4, 8, width), F32),
        sums_s=dma((3,)),
        sums_r=dma((3,)),
        rs_as=dma((3, n_z)),
        rs_ar=dma((3, n_z)),
        ready=pltpu.SemaphoreType.REGULAR,
        rs_cs=dma((3, n_z - 1)),
        rs_cr=dma((3, n_z - 1)),
        rs_ds=dma((3, 6)),
        rs_dr=dma((3, 6)),
    )
    quarters = [rows // 4 for rows in shard_rows]
    scratch.update(
        ra=[vm((n_z, rows, width), BF16) for rows in shard_rows],
        rb=[vm((n_z, 6, rows, width // 2), BF16) for rows in quarters],
        qs=[vm((n_z - 1, rows, width), BF16) for rows in quarters],
        qf=[vm((rows, width), F32) for rows in quarters],
        rc=[vm((n_z - 1, rows, width), BF16) for rows in quarters],
        td=[vm((rows, width), BF16) for rows in shard_rows],
    )
    buffers, tree = jax.tree.flatten(scratch, is_leaf=lambda v: not isinstance(v, (dict, list)))
    dims = types.SimpleNamespace(
        tree=tree,
        n_dp=n_dp,
        cols=cols,
        pixels=pixels,
        width=width,
        tasks=tasks,
        bottle=bottle,
        shard_rows=shard_rows,
    )
    any_spec = pl.BlockSpec(memory_space=pl.ANY)
    vmem_spec = pl.BlockSpec(memory_space=pltpu.VMEM)
    smem_spec = pl.BlockSpec(memory_space=pltpu.SMEM)
    results = pl.pallas_call(
        functools.partial(step_kernel, dims),
        out_shape=(
            jax.ShapeDtypeStruct((1, tasks, windows, width), BF16),
            jax.ShapeDtypeStruct((1, pixels, width), BF16),
            *[jax.ShapeDtypeStruct((rows, width), BF16) for rows in shard_rows],
            jax.ShapeDtypeStruct(gain.shape, F32),
            jax.ShapeDtypeStruct(bias.shape, F32),
        ),
        in_specs=[smem_spec, vmem_spec, vmem_spec, vmem_spec] + [any_spec] * 5,
        out_specs=(any_spec,) * 5 + (vmem_spec,) * 2,
        scratch_shapes=tuple(buffers),
        compiler_params=pltpu.CompilerParams(
            collective_id=0, has_side_effects=True, vmem_limit_bytes=VMEM_BYTES
        ),
    )(counts.reshape(micro), pool_index, gain, bias, images, conv_w, squeeze_w, expand_w, cotangent)
    return pl.pallas_call(
        functools.partial(finish_kernel, dims),
        out_shape=(
            jax.ShapeDtypeStruct((1, tasks, windows, width), BF16),
            jax.ShapeDtypeStruct((1, pixels, width), BF16),
            jax.ShapeDtypeStruct(conv_w.shape, F32),
            jax.ShapeDtypeStruct(squeeze_w.shape, F32),
            jax.ShapeDtypeStruct(expand_w.shape, F32),
            jax.ShapeDtypeStruct(gain.shape, F32),
            jax.ShapeDtypeStruct(bias.shape, F32),
        ),
        in_specs=[any_spec] * 5 + [vmem_spec] * 2,
        out_specs=(any_spec,) * 5 + (vmem_spec,) * 2,
        scratch_shapes=(
            vm((1, tasks, windows, width), BF16),
            vm((1, pixels, width), BF16),
            vm(conv_w.shape, BF16),
            vm(conv_w.shape, F32),
            vm((gate_rows, width), BF16),
            vm(squeeze_w.shape, F32),
            vm(expand_w.shape, F32),
            dma((5,)),
            dma((6,)),
        ),
        compiler_params=pltpu.CompilerParams(vmem_limit_bytes=VMEM_BYTES),
    )(*results)


def fits_kernel(mesh, args):
    images, counts, pool_index, conv_w, squeeze_w, expand_w = args[:6]
    sections, n_dp = mesh.shape["section"], mesh.shape["dp"]
    conv_rows = conv_w.shape[1] // n_dp
    e_rows = expand_w.shape[2] // n_dp
    return (
        sections == 4
        and images.shape[0] == sections
        and n_dp % 2 == 0
        and pool_index.shape[1] == n_dp
        and conv_rows % 64 == 0
        and e_rows == 16
        and squeeze_w.shape[2] // n_dp == 4 * e_rows
        and squeeze_w.shape[3] == 128
        and images.shape[2] == 4 * 128
    )


def solution(mesh):
    placed = (
        P(None, "dp", None),
        P(None, "dp"),
        P(None, "dp", None),
        P(None, "dp", None),
        P(None, None, "dp", None),
        P(None, None, "dp", None),
        P(),
        P(),
        P(None, None, "dp", None),
    )
    def run(*args):
        return mapped(fused if fits_kernel(mesh, args) else on_device)(*args)

    def mapped(body):
        return jax.shard_map(
        body,
        mesh=mesh,
        in_specs=placed,
        out_specs=(
            P("section", None, "dp", None),
            P("section", "dp", None),
            P(None, "dp", None),
            P(None, None, "dp", None),
            P(None, None, "dp", None),
            P(),
            P(),
        ),
        check_vma=False,
    )

    return run
```

```python
import functools
import types

import jax
import jax.numpy as jnp
from jax import lax
from jax.experimental import pallas as pl
from jax.experimental.pallas import tpu as pltpu
from jax.sharding import PartitionSpec as P

EPS = 1e-05
BF16 = jnp.bfloat16
F32 = jnp.float32
VMEM_BYTES = 58 * 1024 * 1024


def gelu_back(point, upstream):
    return jax.vjp(jax.nn.gelu, point)[1](upstream)[0]


def with_halo(value, axis):
    size = lax.axis_size(axis)
    up = [(i, i + 1) for i in range(size - 1)]
    down = [(j, i) for i, j in up]
    before = lax.ppermute(value[-1:], axis, up)
    after = lax.ppermute(value[:1], axis, down)
    return jnp.concatenate([before, value, after], axis=0)


def conv(padded, taps):
    out = lax.conv_general_dilated(
        padded[None],
        taps,
        (1, 1),
        ((0, 0), (1, 1)),
        dimension_numbers=("NHWC", "HWIO", "NHWC"),
        preferred_element_type=F32,
    )
    return out.reshape(-1, out.shape[-1])


def conv_input_grad(d_padded, taps):
    out = lax.conv_general_dilated(
        d_padded[None],
        taps[::-1, ::-1],
        (1, 1),
        ((0, 0), (1, 1)),
        dimension_numbers=("NHWC", "HWOI", "NHWC"),
        preferred_element_type=F32,
    )
    return out.reshape(-1, out.shape[-1])


def conv_weight_grad(padded, d_hidden):
    out = lax.conv_general_dilated(
        padded[None],
        d_hidden[None],
        (1, 1),
        ((0, 0), (1, 1)),
        dimension_numbers=("CHWN", "IHWO", "HWNC"),
        preferred_element_type=F32,
    )
    return out.reshape(-1, out.shape[-1])


def gate_forward(source, w_squeeze, w_expand):
    squeezed = jnp.einsum("tpc,tcb->tpb", source, w_squeeze, preferred_element_type=F32)
    excited = jax.nn.gelu(squeezed).astype(BF16)
    expanded = jnp.einsum("tpb,tbc->tpc", excited, w_expand, preferred_element_type=F32)
    return squeezed, excited, jax.nn.sigmoid(expanded)


def gate_backward(d_task, field, source, squeezed, excited, gate_val, w_squeeze, w_expand):
    d_expanded = (d_task * field[None] * gate_val * (1.0 - gate_val)).astype(BF16)
    d_excited = jnp.einsum("tpc,tbc->tpb", d_expanded, w_expand, preferred_element_type=F32)
    d_squeezed = gelu_back(squeezed, d_excited).astype(BF16)
    d_source = jnp.einsum("tpb,tcb->tpc", d_squeezed, w_squeeze, preferred_element_type=F32)
    grad_squeeze = jnp.einsum("tpc,tpb->tcb", source, d_squeezed, preferred_element_type=F32)
    grad_expand = jnp.einsum("tpb,tpc->tbc", excited, d_expanded, preferred_element_type=F32)
    return d_source, grad_squeeze, grad_expand


def pool_pick(field, pick):
    tasks, _, width = field.shape
    half_rows, half_columns = pick.shape
    windows = field.reshape(tasks, half_rows, 2, half_columns, 2, width)
    picked = jnp.zeros((tasks, half_rows, half_columns, width), F32)
    for corner in range(4):
        hit = (pick == corner)[None, :, :, None]
        picked = picked + jnp.where(hit, windows[:, :, corner // 2, :, corner % 2, :], 0.0)
    return picked.reshape(tasks, half_rows * half_columns, width)


def pool_spread(d_pooled, pick):
    tasks, _, width = d_pooled.shape
    half_rows, half_columns = pick.shape
    grid = d_pooled.reshape(tasks, half_rows, half_columns, width)
    rows = [
        jnp.stack(
            [jnp.where((pick == 2 * dy + dx)[None, :, :, None], grid, 0.0) for dx in range(2)], 3
        )
        for dy in range(2)
    ]
    return jnp.stack(rows, 2).reshape(tasks, half_rows * 2 * half_columns * 2, width)


def on_device(images, counts, pool_index, conv_w, squeeze_w, expand_w, gain, bias, cotangent):
    sections = lax.axis_size("section")
    here = lax.axis_index("section")
    micro, pixels, width = images.shape
    layers = conv_w.shape[0]
    tasks = squeeze_w.shape[1]
    rows = 2 * pool_index.shape[1]
    columns = 2 * pool_index.shape[2]
    share = micro // sections

    def own(value):
        return lax.dynamic_slice_in_dim(value, here * share, share, 0)

    images, counts, pool_index, cotangent = (
        own(images),
        own(counts),
        own(pool_index),
        own(cotangent),
    )

    def gather(value, axis):
        return lax.all_gather(value.astype(BF16), "dp", axis=axis, tiled=True)

    taps = [gather(conv_w[l], 0).reshape(3, 3, width, width) for l in range(layers)]
    w_squeeze = [gather(squeeze_w[l], 1) for l in range(layers)]
    w_expand = [gather(expand_w[l], 1) for l in range(layers)]
    slots = jnp.arange(pixels, dtype=jnp.int32)[:, None]

    def block_forward(field, mask, total, layer):
        padded = with_halo(field.reshape(rows, columns, width), "dp")
        hidden = conv(padded, taps[layer])
        sums = lax.psum(
            jnp.stack([jnp.sum(mask * hidden, 0), jnp.sum(mask * hidden * hidden, 0)]), "dp"
        )
        centre = sums[0] / total
        inverse = lax.rsqrt(sums[1] / total - centre * centre + EPS)
        normed = gain[layer] * (hidden - centre) * inverse + bias[layer]
        out = (mask * jax.nn.gelu(normed)).astype(BF16)
        return out, (padded, hidden, centre, inverse)

    def block_backward(d_out, kept, mask, total, layer):
        padded, hidden, centre, inverse = kept
        centred = (hidden - centre) * inverse
        normed = gain[layer] * (hidden - centre) * inverse + bias[layer]
        d_norm = gelu_back(normed, mask * d_out)
        gain_sum = jnp.sum(d_norm * centred, 0)
        bias_sum = jnp.sum(d_norm, 0)
        sums = gain[layer] * lax.psum(jnp.stack([bias_sum, gain_sum]), "dp")
        d_hidden = (
            mask * inverse * (gain[layer] * d_norm - sums[0] / total - centred * sums[1] / total)
        ).astype(BF16)
        d_hidden = d_hidden.reshape(rows, columns, width)
        d_x = conv_input_grad(with_halo(d_hidden, "dp"), taps[layer])
        return d_x, conv_weight_grad(padded, d_hidden), gain_sum, bias_sum

    outs, image_grads = [], []
    grads = None
    totals = lax.psum(counts[:, 0], "dp").astype(F32)
    for m in range(share):
        total = totals[m]
        mask = (slots < counts[m, 0]).astype(F32)
        first_in = jnp.where(slots < counts[m, 0], images[m], jnp.zeros((), BF16))
        f1, kept_0 = block_forward(first_in, mask, total, 0)
        f1_f = f1.astype(F32)
        source_0 = jnp.broadcast_to(f1[None], (tasks, pixels, width))
        squeezed_0, excited_0, gate_0 = gate_forward(source_0, w_squeeze[0], w_expand[0])
        t1 = (mask[None] * gate_0 * f1_f[None]).astype(BF16)
        f2, kept_1 = block_forward(f1, mask, total, 1)
        f2_f = f2.astype(F32)
        source_1 = (f2_f[None] + t1.astype(F32)).astype(BF16)
        squeezed_1, excited_1, gate_1 = gate_forward(source_1, w_squeeze[1], w_expand[1])
        outs.append(pool_pick(mask[None] * gate_1 * f2_f[None], pool_index[m]).astype(BF16))

        d_task = pool_spread(cotangent[m].astype(F32), pool_index[m])
        d_source, gs_1, ge_1 = gate_backward(
            d_task, mask * f2_f, source_1, squeezed_1, excited_1, gate_1, w_squeeze[1], w_expand[1]
        )
        d_f2 = (jnp.sum(d_source, 0) + mask * jnp.sum(d_task * gate_1, 0)).astype(BF16)
        d_t1 = d_source.astype(BF16).astype(F32)
        d_x1, gc_1, gain_1, bias_1 = block_backward(d_f2.astype(F32), kept_1, mask, total, 1)
        d_source, gs_0, ge_0 = gate_backward(
            d_t1, mask * f1_f, source_0, squeezed_0, excited_0, gate_0, w_squeeze[0], w_expand[0]
        )
        d_f1 = (
            d_x1.astype(BF16).astype(F32)
            + jnp.sum(d_source, 0)
            + mask * jnp.sum(d_t1 * gate_0, 0)
        ).astype(BF16)
        d_x0, gc_0, gain_0, bias_0 = block_backward(d_f1.astype(F32), kept_0, mask, total, 0)
        image_grads.append((mask * d_x0).astype(BF16))
        here_grads = [
            [gc_0, gc_1],
            [gs_0, gs_1],
            [ge_0, ge_1],
            jnp.stack([gain_0, gain_1]),
            jnp.stack([bias_0, bias_1]),
        ]
        grads = here_grads if grads is None else jax.tree.map(jnp.add, grads, here_grads)

    def reduced(value, axis):
        part = lax.psum_scatter(value, "dp", scatter_dimension=axis, tiled=True)
        return lax.psum(part.astype(BF16), "section").astype(F32)

    conv_grad = jnp.stack([reduced(g, 0) for g in grads[0]])
    squeeze_grad = jnp.stack([reduced(g, 1) for g in grads[1]])
    expand_grad = jnp.stack([reduced(g, 1) for g in grads[2]])
    gain_grad, bias_grad = lax.psum((grads[3], grads[4]), ("section", "dp"))
    return (
        jnp.stack(outs),
        jnp.stack(image_grads),
        conv_grad,
        squeeze_grad,
        expand_grad,
        gain_grad,
        bias_grad,
    )


GELU_C = 0.7978845608028654
GELU_K = 0.044715
MESH = pl.DeviceIdType.MESH


def gelu_tanh(x):
    return jnp.tanh(GELU_C * x * (1.0 + GELU_K * (x * x)))


def gelu_slope(x, t):
    inner = GELU_C * (1.0 + 3.0 * GELU_K * (x * x))
    return 0.5 * (1.0 + t) + 0.5 * x * (1.0 - t * t) * inner


def gelu_pair(x):
    t = gelu_tanh(x)
    return 0.5 * x * (1.0 + t), gelu_slope(x, t)


def dot(a, b):
    return jnp.dot(a, b, preferred_element_type=F32)


def dot_nt(a, b):
    return lax.dot_general(a, b, (((1,), (1,)), ((), ())), preferred_element_type=F32)


def dot_tn(a, b):
    return lax.dot_general(a, b, (((0,), (0,)), ((), ())), preferred_element_type=F32)


def step_kernel(
    dims,
    counts,
    picks,
    gain,
    bias,
    images,
    conv_w,
    squeeze_w,
    expand_w,
    cotangent,
    out_task,
    out_image,
    out_reduced_0,
    out_reduced_1,
    out_reduced_2,
    out_gain,
    out_bias,
    *scratch,
):
    out_reduced = (out_reduced_0, out_reduced_1, out_reduced_2)
    r = types.SimpleNamespace(**jax.tree.unflatten(dims.tree, scratch))
    n_dp, cols, pixels, width, tasks, bottle = (
        dims.n_dp,
        dims.cols,
        dims.pixels,
        dims.width,
        dims.tasks,
        dims.bottle,
    )
    n_z = n_dp // 2
    windows = cols // 2
    lanes = 128
    n_lane = width // lanes
    shard_rows = dims.shard_rows
    s = lax.axis_index("section")
    d = lax.axis_index("dp")
    z, c = d // 2, d % 2
    sib = 2 * z + 1 - c
    plane = [s + 1 - 2 * (s % 2), (s + 2) % 4, 3 - s]

    def rem(a, b):
        return lax.rem(a, b)

    def z_at(step):
        return rem(z + step, n_z)

    def remote(src, dst, send, recv, device):
        return pltpu.make_async_remote_copy(
            src_ref=src,
            dst_ref=dst,
            send_sem=send,
            recv_sem=recv,
            device_id=device,
            device_id_type=MESH,
        )

    def al(v, m):
        return pl.multiple_of(v, m)

    barrier = pltpu.get_barrier_semaphore()
    for step in range(1, n_dp):
        pl.semaphore_signal(
            barrier, inc=1, device_id=(s, rem(d + step, n_dp)), device_id_type=MESH
        )
    for p in plane:
        pl.semaphore_signal(barrier, inc=1, device_id=(p, d), device_id_type=MESH)

    def load(i, src, dst):
        return pltpu.make_async_copy(src, dst, r.load.at[i])

    staging = [r.h1, r.slope0]
    conv_rows = shard_rows[0]

    def conv_load(layer, j):
        lane = slice(j * lanes, (j + 1) * lanes)
        return load(
            5 + layer * n_lane + j,
            conv_w.at[layer, :, lane],
            staging[layer].at[j, 0:conv_rows],
        )

    cot_at = (2 * tasks + 2) * windows
    image_at = cot_at + tasks * windows
    loads = [
        load(1, squeeze_w, r.sst),
        load(2, expand_w, r.est),
        load(3, images.at[s], r.g1.at[image_at : image_at + pixels]),
        *[
            load(
                5 + 2 * n_lane + t,
                cotangent.at[s, t],
                r.g1.at[cot_at + t * windows : cot_at + (t + 1) * windows],
            )
            for t in range(tasks)
        ],
    ]
    loads[2].start()
    for layer in range(2):
        for j in range(n_lane):
            conv_load(layer, j).start()
    for i in (0, 1, *range(3, 3 + tasks)):
        loads[i].start()

    full = [r.w0, r.gp, r.w1]

    def shard(kind, buf, which):
        rows = shard_rows[kind]
        return buf.at[pl.ds(al(which * rows, 16), rows)]

    def quarter(kind, buf, which, q):
        rows = shard_rows[kind]
        return buf.at[pl.ds(al(which * rows + q * (rows // 4), 16), rows // 4)]

    def z_of(way, hop):
        return z_at(n_z - hop if way == 0 else hop)

    def has(way, hop):
        return z >= hop if way == 0 else z < n_z - hop

    def slot_of(way, hop):
        return n_z - 1 - hop if way == 0 else hop - 1

    def ag_z_copy(kind, way, hop, owner):
        view = quarter(kind, full[kind], 2 * owner + c, s)
        return remote(
            view,
            view,
            r.ag_zs.at[kind, (hop - 1) * 2 + way],
            r.ag_zr.at[kind, slot_of(way, hop)],
            (s, 2 * z_at(1 if way == 0 else n_z - 1) + c),
        )

    def gate_z_copy(step, owner):
        view = quarter(1, full[1], 2 * owner + c, s)
        return remote(
            view,
            view,
            r.ag_zs.at[1, step - 1],
            r.ag_zr.at[1, step - 1],
            (s, 2 * z_at(step) + c),
        )

    def ag_pass(kind, way, hop, do):
        here_has = has(way, hop - 1) if hop > 1 else True
        there = z < n_z - 1 if way == 0 else z > 0
        owner = z_of(way, hop - 1)

        @pl.when(jnp.logical_and(here_has, there))
        def _():
            do(ag_z_copy(kind, way, hop, owner))

    halves = [slice(0, width // 2), slice(width // 2, width)]

    def ag_p_copy(kind, slot, owner, leg, q):
        view = quarter(kind, full[kind], 2 * owner + c, q)
        if leg >= 2:
            view = view.at[:, halves[leg - 2]]
        to = plane[(0, 1, 1, 0)[leg]]
        i = slot * 4 + leg
        return remote(view, view, r.ag_ps.at[kind, i], r.ag_pr.at[kind, i], (to, d))

    def ag_own_copy(kind, core):
        view = shard(kind, full[kind], 2 * z + core)
        return remote(view, view, r.ag_os.at[kind], r.ag_or.at[kind], (s, sib))

    def ag_s_copy(kind, slot, owner, i, core):
        view = quarter(kind, full[kind], 2 * owner + core, others[i])
        i = slot * 4 + i
        return remote(view, view, r.ag_ss.at[kind, i], r.ag_sr.at[kind, i], (s, sib))

    others = [s] + plane

    def ag_start(kind):
        if kind == 1:
            for step in range(1, n_z):
                gate_z_copy(step, z).start()
        else:
            for way in range(2):
                ag_pass(kind, way, 1, lambda copy: copy.start())
        ag_own_copy(kind, c).start()

    at_end = jnp.logical_or(z == 0, z == n_z - 1)

    def for_hop(kind, hop, do, also=True):
        if kind == 1:
            do(hop - 1, z_at(n_z - hop), None)
            return
        for way in range(2):

            @pl.when(jnp.logical_and(has(way, hop), also))
            def _():
                do(slot_of(way, hop), z_of(way, hop), way)

    def ag_z(kind, hop, also=True):
        def do(slot, owner, way):
            if kind == 1:
                gate_z_copy(hop, owner).wait_recv()
            else:
                ag_z_copy(kind, way, hop, owner).wait_recv()
                if hop < n_z - 1:
                    ag_pass(kind, way, hop + 1, lambda copy: copy.start())
            for leg in range(2):
                ag_p_copy(kind, slot, owner, leg, s).start()
            ag_s_copy(kind, slot, owner, 0, c).start()

        for_hop(kind, hop, do, also)

    def ag_r(kind, hop, also=True):
        def do(slot, owner, way):
            for leg in range(2):
                ag_p_copy(kind, slot, owner, leg, plane[leg]).wait_recv()
                ag_p_copy(kind, slot, owner, 2 + leg, plane[leg]).start()
                ag_s_copy(kind, slot, owner, 1 + leg, c).start()

        for_hop(kind, hop, do, also)

    def ag_p(kind, hop):
        def do(slot, owner, way):
            for leg in range(2):
                ag_p_copy(kind, slot, owner, 2 + leg, plane[2]).wait_recv()
            ag_s_copy(kind, slot, owner, 3, c).start()

        for_hop(kind, hop, do)

    def ag_sib(kind):
        ag_own_copy(kind, 1 - c).wait_recv()
        for hop in range(1, n_z):

            def do(slot, owner, way):
                for i in range(4):
                    ag_s_copy(kind, slot, owner, i, 1 - c).wait_recv()

            for_hop(kind, hop, do)

    def ag_end(kind):
        ag_own_copy(kind, c).wait_send()
        for hop in range(1, n_z):

            def do(slot, owner, way):
                for leg in range(2):
                    ag_p_copy(kind, slot, owner, leg, s).wait_send()
                    ag_p_copy(kind, slot, owner, 2 + leg, plane[leg]).wait_send()
                for i in range(4):
                    ag_s_copy(kind, slot, owner, i, c).wait_send()

            if kind == 1:
                gate_z_copy(hop, z).wait_send()
            else:
                for way in range(2):
                    ag_pass(kind, way, hop, lambda copy: copy.wait_send())
            for_hop(kind, hop, do)

    def cast_conv(layer, buf):
        for j in range(n_lane):
            conv_load(layer, j).wait()

        def body(j, _):
            buf[pl.ds(al(d * conv_rows, 16), conv_rows), pl.ds(al(j * lanes, lanes), lanes)] = (
                staging[layer][j, 0:conv_rows, :].astype(BF16)
            )
            return 0

        lax.fori_loop(0, n_lane, body, 0)

    g_rows = shard_rows[1]
    e_rows = n_ex = bottle // n_dp
    s_rows = width // n_dp
    n_sub = s_rows // e_rows

    def ex_row(which, l, t):
        return al(which * g_rows + (l * tasks + t) * e_rows, 16)

    def sq_row(which, l, t):
        return al(which * g_rows + (2 * tasks + l * tasks + t) * e_rows, 16)

    count = counts[s]
    wide = 2 * lanes
    pick_row = jnp.concatenate(
        [picks[s].astype(F32), jnp.zeros((1, wide - windows), F32)], axis=1
    )
    pick_tile = jnp.broadcast_to(pick_row, (lanes, wide)).T[:windows, :].astype(jnp.int32)
    pick_ref = r.pick
    pick_ref[...] = pick_tile
    slot_pick = (
        (pick_tile // 2) * cols
        + 2 * lax.broadcasted_iota(jnp.int32, (windows, lanes), 0)
        + pick_tile % 2
    )
    r.mp[...] = jnp.where(slot_pick < count, 1.0, 0.0).astype(F32)

    def lane_at(j, base=0):
        return pl.ds(al(base + j * lanes, lanes), lanes)

    def valid_rows(start, rows):
        return (lax.broadcasted_iota(jnp.int32, (rows, lanes), 0) + start) < count

    def shift_in(value_of, buf, block):
        def body(j, _):
            v = value_of(j)
            at = lax.broadcasted_iota(jnp.int32, (cols, lanes), 0)
            before = jnp.where(at == 0, 0.0, pltpu.roll(v, 1, 0))
            after = jnp.where(at == cols - 1, 0.0, pltpu.roll(v, cols - 1, 0))
            rows = pl.ds(block * cols, cols)
            buf[rows, lane_at(j)] = before.astype(BF16)
            buf[rows, lane_at(j, width)] = v.astype(BF16)
            buf[rows, lane_at(j, 2 * width)] = after.astype(BF16)
            return 0

        lax.fori_loop(0, n_lane, body, 0)

    @pl.when(d == 0)
    def _():
        r.halo[:, 0] = jnp.zeros_like(r.halo[:, 0])

    @pl.when(d == n_dp - 1)
    def _():
        r.halo[:, 1] = jnp.zeros_like(r.halo[:, 1])

    def halo_down(e, buf):
        return remote(
            buf.at[2 * cols : 3 * cols, width : 2 * width],
            r.halo.at[e % 2, 0],
            r.halo_s.at[e, 0],
            r.halo_r.at[e, 0],
            (s, rem(d + 1, n_dp)),
        )

    def halo_up(e, buf):
        return remote(
            buf.at[cols : 2 * cols, width : 2 * width],
            r.halo.at[e % 2, 1],
            r.halo_s.at[e, 1],
            r.halo_r.at[e, 1],
            (s, rem(d + n_dp - 1, n_dp)),
        )

    def halo_start(e, buf):
        @pl.when(d < n_dp - 1)
        def _():
            halo_down(e, buf).start()

        @pl.when(d > 0)
        def _():
            halo_up(e, buf).start()

    def halo_finish(e, buf):
        @pl.when(d > 0)
        def _():
            halo_down(e, buf).wait_recv()

        @pl.when(d < n_dp - 1)
        def _():
            halo_up(e, buf).wait_recv()

        shift_in(lambda j: r.halo[e % 2, 0, :, lane_at(j)].astype(F32), buf, 0)
        shift_in(lambda j: r.halo[e % 2, 1, :, lane_at(j)].astype(F32), buf, 3)

    def halo_sent(e, buf):
        @pl.when(d < n_dp - 1)
        def _():
            halo_down(e, buf).wait_send()

        @pl.when(d > 0)
        def _():
            halo_up(e, buf).wait_send()

    def ex_copy(k, step, owner):
        turn = (k + 1) % 5 % 2
        return remote(
            r.ex_out.at[k],
            r.ex_in.at[k, owner],
            r.ex_s.at[turn, step - 1],
            r.ex_r.at[turn, step - 1],
            (s, rem(d + step, n_dp)),
        )

    def ex_sent(k):
        for step in range(1, n_dp):
            ex_copy(k, step, d).wait_send()

    def ex_start(k):
        if k in (1, 2, 3):
            ex_sent((4, 0, 1)[k - 1])
        for step in range(1, n_dp):
            ex_copy(k, step, d).start()
        r.ex_in[k, d] = r.ex_out[k]

    def ex_finish(k):
        for step in range(1, n_dp):
            ex_copy(k, step, rem(d + n_dp - step, n_dp)).wait_recv()
        total = r.ex_in[k, 0]
        for i in range(1, n_dp):
            total = total + r.ex_in[k, i]
        return [
            jnp.concatenate([total[i * n_lane + j : i * n_lane + j + 1] for j in range(n_lane)], 1)
            for i in range(2)
        ]

    def ex_put(k, i, j, value):
        r.ex_out[k, pl.ds(i * n_lane + j, 1), :] = value

    def conv_forward(xc, w, h, row, part):
        span = 3 * width
        acc = None
        for a in range(3):
            block = a + row
            if (block in (0, 3)) != (part == 1):
                continue
            term = dot(xc[block * cols : (block + 1) * cols, :], w[a * span : (a + 1) * span, :])
            acc = term if acc is None else acc + term
        add_to(h, row, part, acc)

    def add_to(out, row, part, acc):
        for j in range(n_lane):
            at = (j, slice(row * cols, (row + 1) * cols), slice(None))
            piece = acc[:, j * lanes : (j + 1) * lanes]
            out[at] = piece if part == 0 else out[at] + piece

    def conv_back(dc, w, row, part):
        acc = None
        for a in range(3):
            block = 2 - a + row
            if (block in (0, 3)) != (part == 1):
                continue
            for b in range(3):
                term = dot_nt(
                    dc[block * cols : (block + 1) * cols, (2 - b) * width : (3 - b) * width],
                    w[(3 * a + b) * width : (3 * a + b + 1) * width, :],
                )
                acc = term if acc is None else acc + term
        add_to(r.fbuf, row, part, acc)

    quarter_rows = pixels // 4

    def stats(h, k):
        def body(j, _):
            first = jnp.zeros((1, lanes), F32)
            second = jnp.zeros((1, lanes), F32)
            for i in range(4):
                v = h[j, i * quarter_rows : (i + 1) * quarter_rows, :]
                kept = jnp.where(valid_rows(i * quarter_rows, quarter_rows), v, 0.0)
                first = first + jnp.sum(kept, 0, keepdims=True)
                second = second + jnp.sum(kept * v, 0, keepdims=True)
            ex_put(k, 0, j, first)
            ex_put(k, 1, j, second)
            return 0

        lax.fori_loop(0, n_lane, body, 0)

    def norm_of(sums, layer):
        total = r.total[0:1, :]
        centre = sums[0] / total
        inverse = lax.rsqrt(sums[1] / total - centre * centre + EPS)
        r.norm[layer, 0:1, :] = centre
        r.norm[layer, 1:2, :] = inverse
        r.norm[layer, 2:3, :] = gain[layer : layer + 1, :] * inverse
        r.norm[layer, 3:4, :] = 1.0 / total

    def corner_rows(k):
        return pl.ds((k // 2) * cols + k % 2, windows, stride=2)

    def picked(ref, j):
        out = None
        which = pick_ref[...]
        for k in range(4):
            part = jnp.where(which == k, ref[j, corner_rows(k), :], 0.0)
            out = part if out is None else out + part
        return out

    loads[2].wait()

    def image_row(i):
        def value(j):
            v = r.g1[image_at + i * cols : image_at + (i + 1) * cols, lane_at(j)].astype(F32)
            return jnp.where(valid_rows(i * cols, cols), v, 0.0)

        return value

    shift_in(image_row(0), r.xc0, 1)
    shift_in(image_row(1), r.xc0, 2)
    cast_conv(0, r.w0)
    pl.semaphore_wait(barrier, n_dp - 1 + 3)
    ag_start(0)
    r.ex_out[4] = jnp.broadcast_to(count.astype(F32), (8, lanes))
    ex_start(4)
    loads[0].wait()
    loads[1].wait()
    for l in range(2):
        for t in range(tasks):
            r.gp[pl.ds(ex_row(d, l, t), e_rows), :] = r.est[l, t].astype(BF16)
            for k in range(n_sub):
                r.gp[pl.ds(sq_row(d, l, t), e_rows), k * lanes : (k + 1) * lanes] = r.sst[
                    l, t, k * e_rows : (k + 1) * e_rows, :
                ].astype(BF16)
    cast_conv(1, r.w1)
    ag_z(0, 1)
    ag_z(0, 2)
    ag_r(0, 1)
    ag_z(0, 3)
    ag_start(2)
    halo_start(0, r.xc0)
    ag_r(0, 2)
    ag_p(0, 1)
    ag_r(0, 3)
    ag_z(2, 1)
    r.total[...] = jnp.concatenate([ex_finish(4)[0]] * 8, axis=0)
    ag_p(0, 2)
    ag_p(0, 3)
    ag_sib(0)
    conv_forward(r.xc0, r.w0, r.h0, 0, 0)
    conv_forward(r.xc0, r.w0, r.h0, 1, 0)
    ag_z(2, 2)
    ag_r(2, 1)
    halo_finish(0, r.xc0)
    conv_forward(r.xc0, r.w0, r.h0, 0, 1)
    conv_forward(r.xc0, r.w0, r.h0, 1, 1)
    stats(r.h0, 0)
    ex_start(0)
    halo_sent(0, r.xc0)
    ag_start(1)
    ag_z(2, 3)
    ag_r(2, 2, at_end)
    norm_of(ex_finish(0), 0)

    def block_0(j, _):
        lane = lane_at(j)
        for i in range(4):
            rows = slice(i * quarter_rows, (i + 1) * quarter_rows)
            normed = (r.h0[j, rows, :] - r.norm[0, 0:1, lane]) * r.norm[
                0, 2:3, lane
            ] + bias[0:1, lane]
            t = gelu_tanh(normed)
            ok = valid_rows(i * quarter_rows, quarter_rows)
            g = 0.5 * normed * (1.0 + t)
            r.fbuf[j, rows, :] = jnp.where(ok, g, 0.0).astype(BF16).astype(F32)
            r.slope0[j, rows, :] = t
        return 0

    def block_0_rest(j, _):
        lane = lane_at(j)
        for i in range(4):
            rows = slice(i * quarter_rows, (i + 1) * quarter_rows)
            normed = (r.h0[j, rows, :] - r.norm[0, 0:1, lane]) * r.norm[0, 2:3, lane] + bias[
                0:1, lane
            ]
            slope = gelu_slope(normed, r.slope0[j, rows, :])
            ok = valid_rows(i * quarter_rows, quarter_rows)
            r.slope0[j, rows, :] = jnp.where(ok, slope, 0.0)
        f1p = picked(r.fbuf, j)
        r.f1p[:, lane] = f1p
        r.f1b[:, lane] = f1p.astype(BF16)
        return 0

    lax.fori_loop(0, n_lane, block_0, 0)
    shift_in(lambda j: r.fbuf[j, 0:cols, :], r.xc1, 1)
    shift_in(lambda j: r.fbuf[j, cols : 2 * cols, :], r.xc1, 2)
    halo_start(1, r.xc1)
    ag_r(2, 2, jnp.logical_not(at_end))
    ag_p(2, 1)
    ag_r(2, 3)
    for step in range(1, n_z):
        ag_z(1, step)
    lax.fori_loop(0, n_lane, block_0_rest, 0)
    ag_p(2, 2)
    ag_p(2, 3)
    ag_sib(2)
    conv_forward(r.xc1, r.w1, r.h1, 0, 0)
    for step in range(1, n_z):
        ag_r(1, step)
    conv_forward(r.xc1, r.w1, r.h1, 1, 0)
    halo_finish(1, r.xc1)
    conv_forward(r.xc1, r.w1, r.h1, 0, 1)
    conv_forward(r.xc1, r.w1, r.h1, 1, 1)
    stats(r.h1, 1)
    ex_start(1)
    for hop in range(1, n_z):
        ag_p(1, hop)
    ag_sib(1)

    def unpack(i, _):
        for l in range(2):
            for t in range(tasks):
                r.ex_w[l, t, pl.ds(al(i * e_rows, 16), e_rows), :] = r.gp[
                    pl.ds(ex_row(i, l, t), e_rows), :
                ]
                for k in range(n_sub):
                    r.sq_w[
                        l,
                        pl.ds(al(i * s_rows + k * e_rows, 16), e_rows),
                        t * bottle : (t + 1) * bottle,
                    ] = r.gp[pl.ds(sq_row(i, l, t), e_rows), k * lanes : (k + 1) * lanes]
        return 0

    lax.fori_loop(0, n_dp, unpack, 0)
    mask_pick = jnp.concatenate([r.mp[...]] * n_lane, axis=1)
    g, slope = gelu_pair(dot(r.f1b[...], r.sq_w[0]))
    r.excited0[...] = g.astype(BF16)
    r.eslope0[...] = slope

    def task_lane(t):
        return pl.ds(al(t * bottle, lanes), bottle)

    def gate_0(t, _):
        value = jax.nn.sigmoid(dot(r.excited0[:, task_lane(t)], r.ex_w[0, t]))
        r.gate0[t] = value
        r.t1[t] = (mask_pick * value * r.f1p[...]).astype(BF16)
        return 0

    for t in range(tasks):
        gate_0(t, 0)
    norm_of(ex_finish(1), 1)

    for kind in range(3):
        ag_end(kind)
    for p in plane:
        pl.semaphore_signal(r.ready, inc=1, device_id=(p, d), device_id_type=MESH)

    def block_1(j, _):
        lane = lane_at(j)
        off = picked(r.h1, j) - r.norm[1, 0:1, lane]
        g, slope = gelu_pair(off * r.norm[1, 2:3, lane] + bias[1:2, lane])
        r.f2p[:, lane] = (r.mp[...] * g).astype(BF16).astype(F32)
        r.slope1[:, lane] = r.mp[...] * slope
        r.centred1[:, lane] = off * r.norm[1, 1:2, lane]
        return 0

    lax.fori_loop(0, n_lane, block_1, 0)
    grads = [r.w1, r.gp, r.g1]

    def pair_of(k):
        return z_at((2, 1, 3, 0)[k])

    def rs_a_copy(kind, k, core):
        return remote(
            shard(kind, grads[kind], 2 * pair_of(k) + core),
            r.ra[kind].at[k],
            r.rs_as.at[kind, k],
            r.rs_ar.at[kind, k],
            (s, sib),
        )

    def again(first, second, i):
        per = 4 * (n_z - 1)
        return (first if i < 3 * per else second).at[i // per % 3, i % per]

    def rs_b_copy(kind, k, way):
        o = 2 * pair_of(k) + c
        half = (0, 0, 1, 1, 0, 1)[way]
        to = plane[(0, 0, 1, 1, 1, 0)[way]]
        q = to if way in (0, 2, 4, 5) else plane[2]
        return remote(
            quarter(kind, grads[kind], o, q).at[:, halves[half]],
            r.rb[kind].at[k, way],
            again(r.ag_ps, r.ag_ss, (kind * n_z + k) * 6 + way),
            again(r.ag_pr, r.ag_sr, (kind * n_z + k) * 6 + way),
            (to, d),
        )

    def rs_c_copy(kind, k):
        return remote(
            r.qs[kind].at[k],
            r.rc[kind].at[k],
            r.rs_cs.at[kind, k],
            r.rs_cr.at[kind, k],
            (s, 2 * pair_of(k) + c),
        )

    def rs_d_copy(kind, leg, q):
        rows = shard_rows[kind] // 4
        half = (0, 1, 1, 0, 0, 1)[leg]
        to = plane[(0, 1, 0, 1, 1, 0)[leg]]
        view = out_reduced[kind].at[pl.ds(al(q * rows, 16), rows), halves[half]]
        return remote(view, view, r.rs_ds.at[kind, leg], r.rs_dr.at[kind, leg], (to, d))

    def conv_weight(kind, xc, k):
        tile = 2 * shard_rows[kind] // 3
        per = 3 * width // tile

        for i in range(3):
            g = pair_of(k) * 3 + i
            a = g // per
            term = dot_tn(
                xc[pl.ds(al(a * cols, 16), pixels), pl.ds(al((g % per) * tile, lanes), tile)],
                r.dc[cols : 3 * cols, width : 2 * width],
            )
            grads[kind][pl.ds(al(g * tile, 16), tile), :] = term.astype(BF16)

    def rs_a(kind, k):
        rs_a_copy(kind, k, 1 - c).start()

    def rs_b(kind, k):
        rs_a_copy(kind, k, c).wait_recv()
        rows = shard_rows[kind]
        tile = rows // 4
        start = (2 * pair_of(k) + c) * rows

        def body(i, _):
            at = pl.ds(al(start + i * tile, 16), tile)
            grads[kind][at, :] = (
                grads[kind][at, :].astype(F32)
                + r.ra[kind][k, pl.ds(al(i * tile, 16), tile), :].astype(F32)
            ).astype(BF16)
            return 0

        lax.fori_loop(0, 4, body, 0)
        for way in range(4):
            rs_b_copy(kind, k, way).start()

    def quarter_at(kind, k, q):
        rows = shard_rows[kind]
        return pl.ds(al((2 * pair_of(k) + c) * rows + q * (rows // 4), 16), rows // 4)

    def rs_r(kind, k):
        for half in range(2):
            rs_b_copy(kind, k, 2 * half).wait_recv()
            rs_b_copy(kind, k, 2 * half + 1).wait_recv()
            at = quarter_at(kind, k, plane[1 - half])
            grads[kind][at, halves[half]] = (
                grads[kind][at, halves[half]].astype(F32)
                + r.rb[kind][k, 2 * half + 1].astype(F32)
            ).astype(BF16)
            rs_b_copy(kind, k, 4 + half).start()

    def rs_c(kind, k):
        at = quarter_at(kind, k, s)
        parts = []
        for half in range(2):
            rs_b_copy(kind, k, 4 + half).wait_recv()
            parts.append(
                grads[kind][at, halves[half]].astype(F32)
                + r.rb[kind][k, 2 * half].astype(F32)
                + r.rb[kind][k, 4 + half].astype(F32)
            )
        total = jnp.concatenate(parts, axis=1)
        if k < n_z - 1:
            r.qs[kind][k] = total.astype(BF16)
            rs_c_copy(kind, k).start()
        else:
            r.qf[kind][...] = total

    def rs_d(kind):
        total = r.qf[kind][...]
        for k in range(n_z - 1):
            rs_c_copy(kind, k).wait_recv()
            total = total + r.rc[kind][k].astype(F32)
        rows = shard_rows[kind] // 4
        out_reduced[kind][pl.ds(al(s * rows, 16), rows), :] = total.astype(BF16)
        for leg in range(4):
            rs_d_copy(kind, leg, s).start()

    def rs_dr(kind):
        for leg in range(2):
            rs_d_copy(kind, leg, plane[leg]).wait_recv()
            rs_d_copy(kind, 4 + leg, plane[leg]).start()

    def rs_e(kind):
        for leg in range(2):
            rs_d_copy(kind, 2 + leg, plane[leg]).wait_recv()
            rs_d_copy(kind, 4 + leg, plane[2]).wait_recv()

    def rs_end(kind):
        for k in range(n_z):
            rs_a_copy(kind, k, 1 - c).wait_send()
            for way in range(6):
                rs_b_copy(kind, k, way).wait_send()
            if k < n_z - 1:
                rs_c_copy(kind, k).wait_send()
        for leg in range(4):
            rs_d_copy(kind, leg, s).wait_send()
        for leg in range(2):
            rs_d_copy(kind, 4 + leg, plane[leg]).wait_send()

    for item in loads[3:]:
        item.wait()
    r.df2[...] = jnp.zeros_like(r.df2)

    def pack_grads(l, t, grad_squeeze, grad_expand):
        r.fbuf[0, 0:width, :] = grad_squeeze
        for j in range(n_lane):
            r.fbuf[1, j * bottle : (j + 1) * bottle, :] = grad_expand[:, j * lanes : (j + 1) * lanes]

        def body(i, _):
            for j in range(n_lane):
                lane = slice(j * lanes, (j + 1) * lanes)
                r.gp[pl.ds(ex_row(i, l, t), e_rows), lane] = r.fbuf[
                    1, pl.ds(al(j * bottle + i * e_rows, 16), e_rows), :
                ].astype(BF16)
            for k in range(n_sub):
                r.gp[pl.ds(sq_row(i, l, t), e_rows), k * lanes : (k + 1) * lanes] = r.fbuf[
                    0, pl.ds(al(i * s_rows + k * e_rows, 16), e_rows), :
                ].astype(BF16)
            return 0

        lax.fori_loop(0, n_dp, body, 0)

    def kept(i):
        return pl.ds(al(i * windows, 16), windows)

    def gate_1(t, _):
        w_s = r.sq_w[1, :, task_lane(t)]
        w_e = r.ex_w[1, t]
        f2p = r.f2p[...]
        source = (f2p + r.t1[t].astype(F32)).astype(BF16)
        g, slope = gelu_pair(dot(source, w_s))
        excited = g.astype(BF16)
        value = jax.nn.sigmoid(dot(excited, w_e))
        field = mask_pick * f2p
        d_task = r.g1[cot_at + t * windows : cot_at + (t + 1) * windows, :].astype(F32)
        out_task[0, t] = (value * field).astype(BF16)
        d_expanded = (d_task * field * value * (1.0 - value)).astype(BF16)
        d_squeezed = (slope * dot_nt(d_expanded, w_e)).astype(BF16)
        d_source = dot_nt(d_squeezed, w_s)
        r.t1[t] = d_source.astype(BF16)
        r.df2[...] += d_source + mask_pick * d_task * value
        r.g1[kept(t), :] = source
        r.g1[kept(tasks + t), :] = d_expanded
        r.g1[kept(2 * tasks), task_lane(t)] = excited
        r.g1[kept(2 * tasks + 1), task_lane(t)] = d_squeezed
        return 0

    def gate_1_weight(t, _):
        pack_grads(
            1,
            t,
            dot_tn(r.g1[kept(t), :], r.g1[kept(2 * tasks + 1), task_lane(t)]),
            dot_tn(r.g1[kept(2 * tasks), task_lane(t)], r.g1[kept(tasks + t), :]),
        )
        return 0

    for t in range(tasks):
        gate_1(t, 0)
    def back_1(j, _):
        lane = lane_at(j)
        d_norm = r.slope1[:, lane] * r.df2[:, lane].astype(BF16).astype(F32)
        r.df2[:, lane] = d_norm
        ex_put(2, 0, j, jnp.sum(d_norm, 0, keepdims=True))
        ex_put(2, 1, j, jnp.sum(d_norm * r.centred1[:, lane], 0, keepdims=True))
        return 0

    lax.fori_loop(0, n_lane, back_1, 0)
    ex_start(2)

    r.df1[...] = jnp.zeros_like(r.df1)

    def gate_0_back(t, _):
        w_s = r.sq_w[0, :, task_lane(t)]
        w_e = r.ex_w[0, t]
        value = r.gate0[t]
        d_task = r.t1[t].astype(F32)
        excited = r.excited0[:, task_lane(t)]
        d_expanded = (d_task * (mask_pick * r.f1p[...]) * value * (1.0 - value)).astype(BF16)
        d_squeezed = (r.eslope0[:, task_lane(t)] * dot_nt(d_expanded, w_e)).astype(BF16)
        r.df1[...] += dot_nt(d_squeezed, w_s) + mask_pick * d_task * value
        pack_grads(0, t, dot_tn(r.f1b[...], d_squeezed), dot_tn(excited, d_expanded))
        return 0

    for t in range(tasks):
        gate_0_back(t, 0)
    for t in range(tasks):
        gate_1_weight(t, 0)

    r.sums[...] = jnp.zeros_like(r.sums)

    def back_terms(k, layer):
        sums = ex_finish(k)
        r.sums[2 * layer : 2 * layer + 1, :] = sums[0]
        r.sums[2 * layer + 1 : 2 * layer + 2, :] = sums[1]
        scale = gain[layer : layer + 1, :] * r.norm[layer, 3:4, :] * r.norm[layer, 1:2, :]
        r.norm[layer, 4:5, :] = scale * sums[0]
        r.norm[layer, 5:6, :] = scale * r.norm[layer, 1:2, :] * sums[1]

    for k in range(n_z):
        rs_a(1, k)
    back_terms(2, 1)

    def hidden_grad_1(j, _):
        lane = lane_at(j)
        norm = r.norm
        for k in range(4):
            at = corner_rows(k)
            spread = jnp.where(pick_ref[...] == k, r.df2[:, lane] * norm[1, 2:3, lane], 0.0)
            value = spread - (
                norm[1, 4:5, lane] + (r.h1[j, at, :] - norm[1, 0:1, lane]) * norm[1, 5:6, lane]
            )
            slot = (k // 2) * cols + k % 2 + 2 * lax.broadcasted_iota(
                jnp.int32, (windows, lanes), 0
            )
            r.fbuf[j, at, :] = jnp.where(slot < count, value, 0.0)
        return 0

    lax.fori_loop(0, n_lane, hidden_grad_1, 0)
    shift_in(lambda j: r.fbuf[j, 0:cols, :], r.dc, 1)
    shift_in(lambda j: r.fbuf[j, cols : 2 * cols, :], r.dc, 2)
    halo_start(2, r.dc)

    pl.semaphore_wait(r.ready, 3)
    for k in range(n_z):
        rs_b(1, k)
    for k in range(2):
        conv_weight(2, r.xc1, k)
        rs_a(2, k)
    conv_back(r.dc, r.w1, 0, 0)
    rs_b(2, 0)
    conv_back(r.dc, r.w1, 1, 0)
    for k in range(n_z):
        rs_r(1, k)
    rs_b(2, 1)
    halo_finish(2, r.dc)
    conv_back(r.dc, r.w1, 0, 1)
    conv_back(r.dc, r.w1, 1, 1)
    def back_0(j, _):
        lane = lane_at(j)
        norm = r.norm
        first = jnp.zeros((1, lanes), F32)
        second = jnp.zeros((1, lanes), F32)
        for k in range(4):
            at = corner_rows(k)
            d_field = r.fbuf[j, at, :].astype(BF16).astype(F32) + jnp.where(
                pick_ref[...] == k, r.df1[:, lane], 0.0
            )
            d_norm = r.slope0[j, at, :] * d_field.astype(BF16).astype(F32)
            r.fbuf[j, at, :] = d_norm
            centred = (r.h0[j, at, :] - norm[0, 0:1, lane]) * norm[0, 1:2, lane]
            first = first + jnp.sum(d_norm, 0, keepdims=True)
            second = second + jnp.sum(d_norm * centred, 0, keepdims=True)
        ex_put(3, 0, j, first)
        ex_put(3, 1, j, second)
        return 0

    lax.fori_loop(0, n_lane, back_0, 0)
    ex_start(3)
    conv_weight(2, r.xc1, 2)
    rs_a(2, 2)
    rs_r(2, 0)
    conv_weight(2, r.xc1, 3)
    rs_a(2, 3)
    rs_b(2, 2)
    halo_sent(2, r.dc)
    back_terms(3, 0)

    def sums_copy(p, q):
        return remote(
            r.sums,
            r.sums_in.at[q],
            r.sums_s.at[p],
            r.sums_r.at[p],
            (plane[p], d),
        )

    for p in range(3):
        sums_copy(p, s).start()
    r.sums_in[s] = r.sums[...]

    def hidden_grad_0(row):
        def value(j):
            lane = lane_at(j)
            norm = r.norm
            rows = slice(row * cols, (row + 1) * cols)
            out = r.fbuf[j, rows, :] * norm[0, 2:3, lane] - (
                norm[0, 4:5, lane] + (r.h0[j, rows, :] - norm[0, 0:1, lane]) * norm[0, 5:6, lane]
            )
            return jnp.where(valid_rows(row * cols, cols), out, 0.0)

        return value

    shift_in(hidden_grad_0(0), r.dc, 1)
    shift_in(hidden_grad_0(1), r.dc, 2)
    halo_start(3, r.dc)
    conv_weight(0, r.xc0, 0)
    rs_a(0, 0)
    rs_r(2, 1)
    rs_b(2, 3)
    for k in range(n_z):
        rs_c(1, k)
    conv_weight(0, r.xc0, 1)
    rs_a(0, 1)
    rs_c(2, 0)
    conv_weight(0, r.xc0, 2)
    rs_a(0, 2)
    rs_r(2, 2)
    rs_b(0, 0)
    conv_weight(0, r.xc0, 3)
    rs_a(0, 3)
    rs_c(2, 1)
    conv_back(r.dc, r.w0, 0, 0)
    rs_r(2, 3)
    rs_b(0, 1)
    conv_back(r.dc, r.w0, 1, 0)
    rs_c(2, 2)
    halo_finish(3, r.dc)
    conv_back(r.dc, r.w0, 0, 1)
    conv_back(r.dc, r.w0, 1, 1)
    def image_out(j, _):
        lane = lane_at(j)
        for i in range(4):
            rows = slice(i * quarter_rows, (i + 1) * quarter_rows)
            out_image[0, rows, lane] = jnp.where(
                valid_rows(i * quarter_rows, quarter_rows), r.fbuf[j, rows, :], 0.0
            ).astype(BF16)
        return 0

    lax.fori_loop(0, n_lane, image_out, 0)
    rs_r(0, 0)
    rs_b(0, 2)
    rs_c(2, 3)
    rs_r(0, 1)
    rs_c(0, 0)
    rs_b(0, 3)
    rs_r(0, 2)
    rs_c(0, 1)
    rs_r(0, 3)
    rs_c(0, 2)
    rs_d(1)
    rs_d(2)
    rs_c(0, 3)
    rs_dr(1)
    rs_dr(2)
    rs_d(0)
    for p in range(3):
        sums_copy(p, plane[p]).wait_recv()
    total = r.sums_in[0]
    for i in range(1, 4):
        total = total + r.sums_in[i]
    for l in range(2):
        out_bias[l : l + 1, :] = total[2 * l : 2 * l + 1, :]
        out_gain[l : l + 1, :] = total[2 * l + 1 : 2 * l + 2, :]
    for p in range(3):
        sums_copy(p, s).wait_send()
    ex_sent(2)
    ex_sent(3)
    halo_sent(3, r.dc)
    halo_sent(1, r.xc1)
    rs_dr(0)
    for kind in (1, 2, 0):
        rs_e(kind)
        rs_end(kind)


def finish_kernel(
    dims,
    task,
    image,
    reduced_0,
    reduced_1,
    reduced_2,
    gain,
    bias,
    out_task,
    out_image,
    out_conv,
    out_squeeze,
    out_expand,
    out_gain,
    out_bias,
    conv_wide,
    squeeze_wide,
    expand_wide,
    sem,
):
    lanes = 128
    e_rows = dims.bottle // dims.n_dp
    outs = []

    def store(src, dst):
        outs.append(pltpu.make_async_copy(src, dst, sem.at[len(outs)]))
        outs[-1].start()

    store(task, out_task)
    store(image, out_image)
    for layer, reduced in enumerate((reduced_0, reduced_2)):
        conv_wide[layer] = reduced[...].astype(F32)
        store(conv_wide.at[layer], out_conv.at[layer])
    for l in range(2):
        for t in range(dims.tasks):
            at = (l * dims.tasks + t) * e_rows
            expand_wide[l, t] = reduced_1[at : at + e_rows, :].astype(F32)
            at = at + 2 * dims.tasks * e_rows
            for k in range(dims.width // dims.n_dp // e_rows):
                squeeze_wide[l, t, k * e_rows : (k + 1) * e_rows, :] = reduced_1[
                    at : at + e_rows, k * lanes : (k + 1) * lanes
                ].astype(F32)
    store(squeeze_wide, out_squeeze)
    store(expand_wide, out_expand)
    out_gain[...] = gain[...]
    out_bias[...] = bias[...]
    for copy in outs:
        copy.wait()


def fused(images, counts, pool_index, conv_w, squeeze_w, expand_w, gain, bias, cotangent):
    n_dp = lax.axis_size("dp")
    micro, pixels, width = images.shape
    tasks, bottle = squeeze_w.shape[1], squeeze_w.shape[3]
    cols = 2 * pool_index.shape[2]
    windows = cols // 2
    conv_rows = conv_w.shape[1]
    gate_rows = 4 * tasks * expand_w.shape[2]
    shard_rows = (conv_rows, gate_rows, conv_rows)
    n_z = n_dp // 2
    vm = pltpu.VMEM
    dma = pltpu.SemaphoreType.DMA
    scratch = dict(
        load=dma((5 + 2 * (width // 128) + tasks,)),
        sst=vm(squeeze_w.shape, F32),
        est=vm(expand_w.shape, F32),
        w0=vm((n_dp * conv_rows, width), BF16),
        gp=vm((n_dp * gate_rows, width), BF16),
        w1=vm((n_dp * conv_rows, width), BF16),
        g1=vm((n_dp * conv_rows, width), BF16),
        sq_w=vm((2, width, tasks * bottle), BF16),
        ex_w=vm((2, tasks, bottle, width), BF16),
        ag_zs=dma((3, 2 * (n_z - 1))),
        ag_zr=dma((3, n_z - 1)),
        ag_ps=dma((3, 4 * (n_z - 1))),
        ag_pr=dma((3, 4 * (n_z - 1))),
        ag_ss=dma((3, 4 * (n_z - 1))),
        ag_sr=dma((3, 4 * (n_z - 1))),
        ag_os=dma((3,)),
        ag_or=dma((3,)),
        mp=vm((windows, 128), F32),
        pick=vm((windows, 128), jnp.int32),
        halo=vm((2, 2, cols, width), BF16),
        halo_s=dma((4, 2)),
        halo_r=dma((4, 2)),
        ex_out=vm((5, 8, 128), F32),
        ex_in=vm((5, n_dp, 8, 128), F32),
        total=vm((8, width), F32),
        ex_s=dma((2, n_dp - 1)),
        ex_r=dma((2, n_dp - 1)),
        norm=vm((2, 8, width), F32),
        xc0=vm((4 * cols, 3 * width), BF16),
        xc1=vm((4 * cols, 3 * width), BF16),
        dc=vm((4 * cols, 3 * width), BF16),
        h0=vm((width // 128, pixels, 128), F32),
        h1=vm((width // 128, pixels, 128), F32),
        slope0=vm((width // 128, pixels, 128), F32),
        fbuf=vm((width // 128, pixels, 128), F32),
        f1p=vm((windows, width), F32),
        f1b=vm((windows, width), BF16),
        excited0=vm((windows, tasks * bottle), BF16),
        eslope0=vm((windows, tasks * bottle), F32),
        gate0=vm((tasks, windows, width), F32),
        t1=vm((tasks, windows, width), BF16),
        f2p=vm((windows, width), F32),
        slope1=vm((windows, width), F32),
        centred1=vm((windows, width), F32),
        df2=vm((windows, width), F32),
        df1=vm((windows, width), F32),
        sums=vm((8, width), F32),
        sums_in=vm((4, 8, width), F32),
        sums_s=dma((3,)),
        sums_r=dma((3,)),
        rs_as=dma((3, n_z)),
        rs_ar=dma((3, n_z)),
        ready=pltpu.SemaphoreType.REGULAR,
        rs_cs=dma((3, n_z - 1)),
        rs_cr=dma((3, n_z - 1)),
        rs_ds=dma((3, 6)),
        rs_dr=dma((3, 6)),
    )
    quarters = [rows // 4 for rows in shard_rows]
    scratch.update(
        ra=[vm((n_z, rows, width), BF16) for rows in shard_rows],
        rb=[vm((n_z, 6, rows, width // 2), BF16) for rows in quarters],
        qs=[vm((n_z - 1, rows, width), BF16) for rows in quarters],
        qf=[vm((rows, width), F32) for rows in quarters],
        rc=[vm((n_z - 1, rows, width), BF16) for rows in quarters],
    )
    buffers, tree = jax.tree.flatten(scratch, is_leaf=lambda v: not isinstance(v, (dict, list)))
    dims = types.SimpleNamespace(
        tree=tree,
        n_dp=n_dp,
        cols=cols,
        pixels=pixels,
        width=width,
        tasks=tasks,
        bottle=bottle,
        shard_rows=shard_rows,
    )
    any_spec = pl.BlockSpec(memory_space=pl.ANY)
    vmem_spec = pl.BlockSpec(memory_space=pltpu.VMEM)
    smem_spec = pl.BlockSpec(memory_space=pltpu.SMEM)
    results = pl.pallas_call(
        functools.partial(step_kernel, dims),
        out_shape=(
            vm((1, tasks, windows, width), BF16),
            vm((1, pixels, width), BF16),
            *[vm((rows, width), BF16) for rows in shard_rows],
            vm(gain.shape, F32),
            vm(bias.shape, F32),
        ),
        in_specs=[smem_spec, vmem_spec, vmem_spec, vmem_spec] + [any_spec] * 5,
        out_specs=(vmem_spec,) * 7,
        scratch_shapes=tuple(buffers),
        compiler_params=pltpu.CompilerParams(
            collective_id=0, has_side_effects=True, vmem_limit_bytes=VMEM_BYTES
        ),
    )(counts.reshape(micro), pool_index, gain, bias, images, conv_w, squeeze_w, expand_w, cotangent)
    results = [pltpu.with_memory_space_constraint(v, pltpu.VMEM) for v in results]
    return pl.pallas_call(
        functools.partial(finish_kernel, dims),
        out_shape=(
            jax.ShapeDtypeStruct((1, tasks, windows, width), BF16),
            jax.ShapeDtypeStruct((1, pixels, width), BF16),
            jax.ShapeDtypeStruct(conv_w.shape, F32),
            jax.ShapeDtypeStruct(squeeze_w.shape, F32),
            jax.ShapeDtypeStruct(expand_w.shape, F32),
            jax.ShapeDtypeStruct(gain.shape, F32),
            jax.ShapeDtypeStruct(bias.shape, F32),
        ),
        in_specs=[vmem_spec] * 7,
        out_specs=(any_spec,) * 5 + (vmem_spec,) * 2,
        scratch_shapes=(
            vm(conv_w.shape, F32),
            vm(squeeze_w.shape, F32),
            vm(expand_w.shape, F32),
            dma((6,)),
        ),
        compiler_params=pltpu.CompilerParams(vmem_limit_bytes=16 * 1024 * 1024),
    )(*results)


def fits_kernel(mesh, args):
    images, counts, pool_index, conv_w, squeeze_w, expand_w = args[:6]
    sections, n_dp = mesh.shape["section"], mesh.shape["dp"]
    conv_rows = conv_w.shape[1] // n_dp
    e_rows = expand_w.shape[2] // n_dp
    return (
        sections == 4
        and images.shape[0] == sections
        and n_dp % 2 == 0
        and pool_index.shape[1] == n_dp
        and conv_rows % 64 == 0
        and e_rows == 16
        and squeeze_w.shape[2] // n_dp == 4 * e_rows
        and squeeze_w.shape[3] == 128
        and images.shape[2] == 4 * 128
    )


def solution(mesh):
    placed = (
        P(None, "dp", None),
        P(None, "dp"),
        P(None, "dp", None),
        P(None, "dp", None),
        P(None, None, "dp", None),
        P(None, None, "dp", None),
        P(),
        P(),
        P(None, None, "dp", None),
    )
    def run(*args):
        return mapped(fused if fits_kernel(mesh, args) else on_device)(*args)

    def mapped(body):
        return jax.shard_map(
        body,
        mesh=mesh,
        in_specs=placed,
        out_specs=(
            P("section", None, "dp", None),
            P("section", "dp", None),
            P(None, "dp", None),
            P(None, None, "dp", None),
            P(None, None, "dp", None),
            P(),
            P(),
        ),
        check_vma=False,
    )

    return run
```

```python
import functools
import types

import jax
import jax.numpy as jnp
from jax import lax
from jax.experimental import pallas as pl
from jax.experimental.pallas import tpu as pltpu
from jax.sharding import PartitionSpec as P

EPS = 1e-05
BF16 = jnp.bfloat16
F32 = jnp.float32
VMEM_BYTES = 58 * 1024 * 1024


def gelu_back(point, upstream):
    return jax.vjp(jax.nn.gelu, point)[1](upstream)[0]


def with_halo(value, axis):
    size = lax.axis_size(axis)
    up = [(i, i + 1) for i in range(size - 1)]
    down = [(j, i) for i, j in up]
    before = lax.ppermute(value[-1:], axis, up)
    after = lax.ppermute(value[:1], axis, down)
    return jnp.concatenate([before, value, after], axis=0)


def conv(padded, taps):
    out = lax.conv_general_dilated(
        padded[None],
        taps,
        (1, 1),
        ((0, 0), (1, 1)),
        dimension_numbers=("NHWC", "HWIO", "NHWC"),
        preferred_element_type=F32,
    )
    return out.reshape(-1, out.shape[-1])


def conv_input_grad(d_padded, taps):
    out = lax.conv_general_dilated(
        d_padded[None],
        taps[::-1, ::-1],
        (1, 1),
        ((0, 0), (1, 1)),
        dimension_numbers=("NHWC", "HWOI", "NHWC"),
        preferred_element_type=F32,
    )
    return out.reshape(-1, out.shape[-1])


def conv_weight_grad(padded, d_hidden):
    out = lax.conv_general_dilated(
        padded[None],
        d_hidden[None],
        (1, 1),
        ((0, 0), (1, 1)),
        dimension_numbers=("CHWN", "IHWO", "HWNC"),
        preferred_element_type=F32,
    )
    return out.reshape(-1, out.shape[-1])


def gate_forward(source, w_squeeze, w_expand):
    squeezed = jnp.einsum("tpc,tcb->tpb", source, w_squeeze, preferred_element_type=F32)
    excited = jax.nn.gelu(squeezed).astype(BF16)
    expanded = jnp.einsum("tpb,tbc->tpc", excited, w_expand, preferred_element_type=F32)
    return squeezed, excited, jax.nn.sigmoid(expanded)


def gate_backward(d_task, field, source, squeezed, excited, gate_val, w_squeeze, w_expand):
    d_expanded = (d_task * field[None] * gate_val * (1.0 - gate_val)).astype(BF16)
    d_excited = jnp.einsum("tpc,tbc->tpb", d_expanded, w_expand, preferred_element_type=F32)
    d_squeezed = gelu_back(squeezed, d_excited).astype(BF16)
    d_source = jnp.einsum("tpb,tcb->tpc", d_squeezed, w_squeeze, preferred_element_type=F32)
    grad_squeeze = jnp.einsum("tpc,tpb->tcb", source, d_squeezed, preferred_element_type=F32)
    grad_expand = jnp.einsum("tpb,tpc->tbc", excited, d_expanded, preferred_element_type=F32)
    return d_source, grad_squeeze, grad_expand


def pool_pick(field, pick):
    tasks, _, width = field.shape
    half_rows, half_columns = pick.shape
    windows = field.reshape(tasks, half_rows, 2, half_columns, 2, width)
    picked = jnp.zeros((tasks, half_rows, half_columns, width), F32)
    for corner in range(4):
        hit = (pick == corner)[None, :, :, None]
        picked = picked + jnp.where(hit, windows[:, :, corner // 2, :, corner % 2, :], 0.0)
    return picked.reshape(tasks, half_rows * half_columns, width)


def pool_spread(d_pooled, pick):
    tasks, _, width = d_pooled.shape
    half_rows, half_columns = pick.shape
    grid = d_pooled.reshape(tasks, half_rows, half_columns, width)
    rows = [
        jnp.stack(
            [jnp.where((pick == 2 * dy + dx)[None, :, :, None], grid, 0.0) for dx in range(2)], 3
        )
        for dy in range(2)
    ]
    return jnp.stack(rows, 2).reshape(tasks, half_rows * 2 * half_columns * 2, width)


def on_device(images, counts, pool_index, conv_w, squeeze_w, expand_w, gain, bias, cotangent):
    sections = lax.axis_size("section")
    here = lax.axis_index("section")
    micro, pixels, width = images.shape
    layers = conv_w.shape[0]
    tasks = squeeze_w.shape[1]
    rows = 2 * pool_index.shape[1]
    columns = 2 * pool_index.shape[2]
    share = micro // sections

    def own(value):
        return lax.dynamic_slice_in_dim(value, here * share, share, 0)

    images, counts, pool_index, cotangent = (
        own(images),
        own(counts),
        own(pool_index),
        own(cotangent),
    )

    def gather(value, axis):
        return lax.all_gather(value.astype(BF16), "dp", axis=axis, tiled=True)

    taps = [gather(conv_w[l], 0).reshape(3, 3, width, width) for l in range(layers)]
    w_squeeze = [gather(squeeze_w[l], 1) for l in range(layers)]
    w_expand = [gather(expand_w[l], 1) for l in range(layers)]
    slots = jnp.arange(pixels, dtype=jnp.int32)[:, None]

    def block_forward(field, mask, total, layer):
        padded = with_halo(field.reshape(rows, columns, width), "dp")
        hidden = conv(padded, taps[layer])
        sums = lax.psum(
            jnp.stack([jnp.sum(mask * hidden, 0), jnp.sum(mask * hidden * hidden, 0)]), "dp"
        )
        centre = sums[0] / total
        inverse = lax.rsqrt(sums[1] / total - centre * centre + EPS)
        normed = gain[layer] * (hidden - centre) * inverse + bias[layer]
        out = (mask * jax.nn.gelu(normed)).astype(BF16)
        return out, (padded, hidden, centre, inverse)

    def block_backward(d_out, kept, mask, total, layer):
        padded, hidden, centre, inverse = kept
        centred = (hidden - centre) * inverse
        normed = gain[layer] * (hidden - centre) * inverse + bias[layer]
        d_norm = gelu_back(normed, mask * d_out)
        gain_sum = jnp.sum(d_norm * centred, 0)
        bias_sum = jnp.sum(d_norm, 0)
        sums = gain[layer] * lax.psum(jnp.stack([bias_sum, gain_sum]), "dp")
        d_hidden = (
            mask * inverse * (gain[layer] * d_norm - sums[0] / total - centred * sums[1] / total)
        ).astype(BF16)
        d_hidden = d_hidden.reshape(rows, columns, width)
        d_x = conv_input_grad(with_halo(d_hidden, "dp"), taps[layer])
        return d_x, conv_weight_grad(padded, d_hidden), gain_sum, bias_sum

    outs, image_grads = [], []
    grads = None
    totals = lax.psum(counts[:, 0], "dp").astype(F32)
    for m in range(share):
        total = totals[m]
        mask = (slots < counts[m, 0]).astype(F32)
        first_in = jnp.where(slots < counts[m, 0], images[m], jnp.zeros((), BF16))
        f1, kept_0 = block_forward(first_in, mask, total, 0)
        f1_f = f1.astype(F32)
        source_0 = jnp.broadcast_to(f1[None], (tasks, pixels, width))
        squeezed_0, excited_0, gate_0 = gate_forward(source_0, w_squeeze[0], w_expand[0])
        t1 = (mask[None] * gate_0 * f1_f[None]).astype(BF16)
        f2, kept_1 = block_forward(f1, mask, total, 1)
        f2_f = f2.astype(F32)
        source_1 = (f2_f[None] + t1.astype(F32)).astype(BF16)
        squeezed_1, excited_1, gate_1 = gate_forward(source_1, w_squeeze[1], w_expand[1])
        outs.append(pool_pick(mask[None] * gate_1 * f2_f[None], pool_index[m]).astype(BF16))

        d_task = pool_spread(cotangent[m].astype(F32), pool_index[m])
        d_source, gs_1, ge_1 = gate_backward(
            d_task, mask * f2_f, source_1, squeezed_1, excited_1, gate_1, w_squeeze[1], w_expand[1]
        )
        d_f2 = (jnp.sum(d_source, 0) + mask * jnp.sum(d_task * gate_1, 0)).astype(BF16)
        d_t1 = d_source.astype(BF16).astype(F32)
        d_x1, gc_1, gain_1, bias_1 = block_backward(d_f2.astype(F32), kept_1, mask, total, 1)
        d_source, gs_0, ge_0 = gate_backward(
            d_t1, mask * f1_f, source_0, squeezed_0, excited_0, gate_0, w_squeeze[0], w_expand[0]
        )
        d_f1 = (
            d_x1.astype(BF16).astype(F32)
            + jnp.sum(d_source, 0)
            + mask * jnp.sum(d_t1 * gate_0, 0)
        ).astype(BF16)
        d_x0, gc_0, gain_0, bias_0 = block_backward(d_f1.astype(F32), kept_0, mask, total, 0)
        image_grads.append((mask * d_x0).astype(BF16))
        here_grads = [
            [gc_0, gc_1],
            [gs_0, gs_1],
            [ge_0, ge_1],
            jnp.stack([gain_0, gain_1]),
            jnp.stack([bias_0, bias_1]),
        ]
        grads = here_grads if grads is None else jax.tree.map(jnp.add, grads, here_grads)

    def reduced(value, axis):
        part = lax.psum_scatter(value, "dp", scatter_dimension=axis, tiled=True)
        return lax.psum(part.astype(BF16), "section").astype(F32)

    conv_grad = jnp.stack([reduced(g, 0) for g in grads[0]])
    squeeze_grad = jnp.stack([reduced(g, 1) for g in grads[1]])
    expand_grad = jnp.stack([reduced(g, 1) for g in grads[2]])
    gain_grad, bias_grad = lax.psum((grads[3], grads[4]), ("section", "dp"))
    return (
        jnp.stack(outs),
        jnp.stack(image_grads),
        conv_grad,
        squeeze_grad,
        expand_grad,
        gain_grad,
        bias_grad,
    )


GELU_C = 0.7978845608028654
GELU_K = 0.044715
MESH = pl.DeviceIdType.MESH


def gelu_tanh(x):
    return jnp.tanh(GELU_C * x * (1.0 + GELU_K * (x * x)))


def gelu_slope(x, t):
    inner = GELU_C * (1.0 + 3.0 * GELU_K * (x * x))
    return 0.5 * (1.0 + t) + 0.5 * x * (1.0 - t * t) * inner


def gelu_pair(x):
    t = gelu_tanh(x)
    return 0.5 * x * (1.0 + t), gelu_slope(x, t)


def dot(a, b):
    return jnp.dot(a, b, preferred_element_type=F32)


def dot_nt(a, b):
    return lax.dot_general(a, b, (((1,), (1,)), ((), ())), preferred_element_type=F32)


def dot_tn(a, b):
    return lax.dot_general(a, b, (((0,), (0,)), ((), ())), preferred_element_type=F32)


def step_kernel(
    dims,
    counts,
    picks_in,
    gain_in,
    bias_in,
    images,
    conv_w,
    squeeze_w,
    expand_w,
    cotangent,
    out_task,
    out_image,
    out_reduced_0,
    out_reduced_1,
    out_reduced_2,
    out_gain,
    out_bias,
    *scratch,
):
    out_reduced = (out_reduced_0, out_reduced_1, out_reduced_2)
    r = types.SimpleNamespace(**jax.tree.unflatten(dims.tree, scratch))
    n_dp, cols, pixels, width, tasks, bottle = (
        dims.n_dp,
        dims.cols,
        dims.pixels,
        dims.width,
        dims.tasks,
        dims.bottle,
    )
    n_z = n_dp // 2
    windows = cols // 2
    lanes = 128
    n_lane = width // lanes
    shard_rows = dims.shard_rows
    s = lax.axis_index("section")
    d = lax.axis_index("dp")
    z, c = d // 2, d % 2
    sib = 2 * z + 1 - c
    plane = [s + 1 - 2 * (s % 2), (s + 2) % 4, 3 - s]

    def rem(a, b):
        return lax.rem(a, b)

    def z_at(step):
        return rem(z + step, n_z)

    def remote(src, dst, send, recv, device):
        return pltpu.make_async_remote_copy(
            src_ref=src,
            dst_ref=dst,
            send_sem=send,
            recv_sem=recv,
            device_id=device,
            device_id_type=MESH,
        )

    def al(v, m):
        return pl.multiple_of(v, m)

    barrier = pltpu.get_barrier_semaphore()
    for step in range(1, n_dp):
        pl.semaphore_signal(
            barrier, inc=1, device_id=(s, rem(d + step, n_dp)), device_id_type=MESH
        )
    for p in plane:
        pl.semaphore_signal(barrier, inc=1, device_id=(p, d), device_id_type=MESH)

    def load(i, src, dst):
        return pltpu.make_async_copy(src, dst, r.load.at[i])

    staging = [r.h1, r.slope0]
    conv_rows = shard_rows[0]

    def conv_load(layer, j):
        lane = slice(j * lanes, (j + 1) * lanes)
        return load(
            5 + layer * n_lane + j,
            conv_w.at[layer, :, lane],
            staging[layer].at[j, 0:conv_rows],
        )

    cot_at = (2 * tasks + 2) * windows
    image_at = cot_at + tasks * windows
    loads = [
        load(1, squeeze_w, r.sst),
        load(2, expand_w, r.est),
        load(3, images.at[s], r.g1.at[image_at : image_at + pixels]),
        *[
            load(
                5 + 2 * n_lane + t,
                cotangent.at[s, t],
                r.g1.at[cot_at + t * windows : cot_at + (t + 1) * windows],
            )
            for t in range(tasks)
        ],
    ]
    small_at = 5 + 2 * n_lane + tasks
    picks, gain, bias = r.picks, r.gain, r.bias
    small = [
        load(small_at, picks_in, picks),
        load(small_at + 1, gain_in, gain),
        load(small_at + 2, bias_in, bias),
    ]
    loads[2].start()
    for layer in range(2):
        for j in range(n_lane):
            conv_load(layer, j).start()
    for item in small:
        item.start()
    for i in (0, 1, *range(3, 3 + tasks)):
        loads[i].start()

    full = [r.w0, r.gp, r.w1]

    def shard(kind, buf, which):
        rows = shard_rows[kind]
        return buf.at[pl.ds(al(which * rows, 16), rows)]

    def quarter(kind, buf, which, q):
        rows = shard_rows[kind]
        return buf.at[pl.ds(al(which * rows + q * (rows // 4), 16), rows // 4)]

    def z_of(way, hop):
        return z_at(n_z - hop if way == 0 else hop)

    def has(way, hop):
        return z >= hop if way == 0 else z < n_z - hop

    def slot_of(way, hop):
        return n_z - 1 - hop if way == 0 else hop - 1

    def ag_z_copy(kind, way, hop, owner):
        view = quarter(kind, full[kind], 2 * owner + c, s)
        return remote(
            view,
            view,
            r.ag_zs.at[kind, (hop - 1) * 2 + way],
            r.ag_zr.at[kind, slot_of(way, hop)],
            (s, 2 * z_at(1 if way == 0 else n_z - 1) + c),
        )

    def gate_z_copy(step, owner):
        view = quarter(1, full[1], 2 * owner + c, s)
        return remote(
            view,
            view,
            r.ag_zs.at[1, step - 1],
            r.ag_zr.at[1, step - 1],
            (s, 2 * z_at(step) + c),
        )

    def ag_pass(kind, way, hop, do):
        here_has = has(way, hop - 1) if hop > 1 else True
        there = z < n_z - 1 if way == 0 else z > 0
        owner = z_of(way, hop - 1)

        @pl.when(jnp.logical_and(here_has, there))
        def _():
            do(ag_z_copy(kind, way, hop, owner))

    halves = [slice(0, width // 2), slice(width // 2, width)]

    def ag_p_copy(kind, slot, owner, leg, q):
        half = (0, 1, 0, 1, 0, 1)[leg]
        view = quarter(kind, full[kind], 2 * owner + c, q).at[:, halves[half]]
        to = plane[(0, 0, 1, 1, 1, 0)[leg]]
        i = slot * 6 + leg
        return remote(view, view, r.ag_ps.at[kind, i], r.ag_pr.at[kind, i], (to, d))

    def ag_own_copy(kind, core):
        view = shard(kind, full[kind], 2 * z + core)
        return remote(view, view, r.ag_os.at[kind], r.ag_or.at[kind], (s, sib))

    def ag_s_copy(kind, slot, owner, i, core):
        view = quarter(kind, full[kind], 2 * owner + core, others[i])
        i = slot * 4 + i
        return remote(view, view, r.ag_ss.at[kind, i], r.ag_sr.at[kind, i], (s, sib))

    others = [s] + plane

    def ag_start(kind):
        if kind == 1:
            for step in range(1, n_z):
                gate_z_copy(step, z).start()
        else:
            for way in range(2):
                ag_pass(kind, way, 1, lambda copy: copy.start())
        ag_own_copy(kind, c).start()

    at_end = jnp.logical_or(z == 0, z == n_z - 1)

    def for_hop(kind, hop, do, also=True):
        if kind == 1:
            do(hop - 1, z_at(n_z - hop), None)
            return
        for way in range(2):

            @pl.when(jnp.logical_and(has(way, hop), also))
            def _():
                do(slot_of(way, hop), z_of(way, hop), way)

    def ag_z(kind, hop):
        def do(slot, owner, way):
            if kind == 1:
                gate_z_copy(hop, owner).wait_recv()
            else:
                ag_z_copy(kind, way, hop, owner).wait_recv()
                if hop < n_z - 1:
                    ag_pass(kind, way, hop + 1, lambda copy: copy.start())
            for leg in (0, 3):
                ag_p_copy(kind, slot, owner, leg, s).start()

        for_hop(kind, hop, do)

    def ag_y(kind, hop):
        def do(slot, owner, way):
            for leg in (0, 3):
                ag_p_copy(kind, slot, owner, leg, s).wait_send()
            for leg in (1, 2):
                ag_p_copy(kind, slot, owner, leg, s).start()
            ag_s_copy(kind, slot, owner, 0, c).start()

        for_hop(kind, hop, do)

    def ag_r(kind, hop, also=True):
        def do(slot, owner, way):
            for h in range(2):
                ag_p_copy(kind, slot, owner, 3 * h, plane[h]).wait_recv()
                ag_p_copy(kind, slot, owner, 4 + h, plane[h]).start()

        for_hop(kind, hop, do, also)

    def ag_q(kind, hop):
        def do(slot, owner, way):
            for axis in range(2):
                ag_p_copy(kind, slot, owner, 1 + axis, plane[axis]).wait_recv()
                ag_s_copy(kind, slot, owner, 1 + axis, c).start()

        for_hop(kind, hop, do)

    def ag_p(kind, hop):
        def do(slot, owner, way):
            for h in range(2):
                ag_p_copy(kind, slot, owner, 4 + h, plane[2]).wait_recv()
            ag_s_copy(kind, slot, owner, 3, c).start()

        for_hop(kind, hop, do)

    def ag_sib(kind):
        ag_own_copy(kind, 1 - c).wait_recv()
        for hop in range(1, n_z):

            def do(slot, owner, way):
                for i in range(4):
                    ag_s_copy(kind, slot, owner, i, 1 - c).wait_recv()

            for_hop(kind, hop, do)

    def ag_end(kind):
        ag_own_copy(kind, c).wait_send()
        for hop in range(1, n_z):

            def do(slot, owner, way):
                for leg in (1, 2):
                    ag_p_copy(kind, slot, owner, leg, s).wait_send()
                for h in range(2):
                    ag_p_copy(kind, slot, owner, 4 + h, plane[h]).wait_send()
                for i in range(4):
                    ag_s_copy(kind, slot, owner, i, c).wait_send()

            if kind == 1:
                gate_z_copy(hop, z).wait_send()
            else:
                for way in range(2):
                    ag_pass(kind, way, hop, lambda copy: copy.wait_send())
            for_hop(kind, hop, do)

    def cast_conv(layer, buf):
        for j in range(n_lane):
            conv_load(layer, j).wait()

        def body(j, _):
            buf[pl.ds(al(d * conv_rows, 16), conv_rows), pl.ds(al(j * lanes, lanes), lanes)] = (
                staging[layer][j, 0:conv_rows, :].astype(BF16)
            )
            return 0

        lax.fori_loop(0, n_lane, body, 0)

    g_rows = shard_rows[1]
    e_rows = n_ex = bottle // n_dp
    s_rows = width // n_dp
    n_sub = s_rows // e_rows

    def ex_row(which, l, t):
        return al(which * g_rows + (l * tasks + t) * e_rows, 16)

    def sq_row(which, l, t):
        return al(which * g_rows + (2 * tasks + l * tasks + t) * e_rows, 16)

    count = counts[s]
    pick_ref = r.pick

    def lane_at(j, base=0):
        return pl.ds(al(base + j * lanes, lanes), lanes)

    def valid_rows(start, rows):
        return (lax.broadcasted_iota(jnp.int32, (rows, lanes), 0) + start) < count

    def shift_in(value_of, buf, block):
        def body(j, _):
            v = value_of(j)
            at = lax.broadcasted_iota(jnp.int32, (cols, lanes), 0)
            before = jnp.where(at == 0, 0.0, pltpu.roll(v, 1, 0))
            after = jnp.where(at == cols - 1, 0.0, pltpu.roll(v, cols - 1, 0))
            rows = pl.ds(block * cols, cols)
            buf[rows, lane_at(j)] = before.astype(BF16)
            buf[rows, lane_at(j, width)] = v.astype(BF16)
            buf[rows, lane_at(j, 2 * width)] = after.astype(BF16)
            return 0

        lax.fori_loop(0, n_lane, body, 0)

    @pl.when(d == 0)
    def _():
        r.halo[:, 0] = jnp.zeros_like(r.halo[:, 0])

    @pl.when(d == n_dp - 1)
    def _():
        r.halo[:, 1] = jnp.zeros_like(r.halo[:, 1])

    def halo_down(e, buf):
        return remote(
            buf.at[2 * cols : 3 * cols, width : 2 * width],
            r.halo.at[e % 2, 0],
            r.halo_s.at[e % 2, 0],
            r.halo_r.at[e % 2, 0],
            (s, rem(d + 1, n_dp)),
        )

    def halo_up(e, buf):
        return remote(
            buf.at[cols : 2 * cols, width : 2 * width],
            r.halo.at[e % 2, 1],
            r.halo_s.at[e % 2, 1],
            r.halo_r.at[e % 2, 1],
            (s, rem(d + n_dp - 1, n_dp)),
        )

    def halo_start(e, buf):
        @pl.when(d < n_dp - 1)
        def _():
            halo_down(e, buf).start()

        @pl.when(d > 0)
        def _():
            halo_up(e, buf).start()

    def halo_finish(e, buf):
        @pl.when(d > 0)
        def _():
            halo_down(e, buf).wait_recv()

        @pl.when(d < n_dp - 1)
        def _():
            halo_up(e, buf).wait_recv()

        shift_in(lambda j: r.halo[e % 2, 0, :, lane_at(j)].astype(F32), buf, 0)
        shift_in(lambda j: r.halo[e % 2, 1, :, lane_at(j)].astype(F32), buf, 3)

    def halo_sent(e, buf):
        @pl.when(d < n_dp - 1)
        def _():
            halo_down(e, buf).wait_send()

        @pl.when(d > 0)
        def _():
            halo_up(e, buf).wait_send()

    def ex_copy(k, step, owner):
        turn = (k + 1) % 5 % 2
        return remote(
            r.ex_out.at[k],
            r.ex_in.at[k, owner],
            r.ex_s.at[turn, step - 1],
            r.ex_r.at[turn, step - 1],
            (s, rem(d + step, n_dp)),
        )

    def ex_sent(k):
        for step in range(1, n_dp):
            ex_copy(k, step, d).wait_send()

    def ex_start(k):
        if k in (1, 2, 3):
            ex_sent((4, 0, 1)[k - 1])
        for step in range(1, n_dp):
            ex_copy(k, step, d).start()
        r.ex_in[k, d] = r.ex_out[k]

    def ex_finish(k):
        for step in range(1, n_dp):
            ex_copy(k, step, rem(d + n_dp - step, n_dp)).wait_recv()
        total = r.ex_in[k, 0]
        for i in range(1, n_dp):
            total = total + r.ex_in[k, i]
        return [
            jnp.concatenate([total[i * n_lane + j : i * n_lane + j + 1] for j in range(n_lane)], 1)
            for i in range(2)
        ]

    def ex_put(k, i, j, value):
        r.ex_out[k, pl.ds(i * n_lane + j, 1), :] = value

    def conv_forward(xc, w, h, row, part, k=None):
        span = 3 * width
        acc = None
        for a in range(3):
            block = a + row
            if (block in (0, 3)) != (part == 1):
                continue
            term = dot(xc[block * cols : (block + 1) * cols, :], w[a * span : (a + 1) * span, :])
            acc = term if acc is None else acc + term
        add_to(h, row, part, acc, k)

    def add_to(out, row, part, acc, k=None):
        for j in range(n_lane):
            at = (j, slice(row * cols, (row + 1) * cols), slice(None))
            piece = acc[:, j * lanes : (j + 1) * lanes]
            if part == 1:
                piece = out[at] + piece
            out[at] = piece
            if k is not None:
                kept = jnp.where(valid_rows(row * cols, cols), piece, 0.0)
                for i, value in enumerate((kept, kept * piece)):
                    value = jnp.sum(value, 0, keepdims=True)
                    if row == 1:
                        value = value + r.ex_out[k, i * n_lane + j : i * n_lane + j + 1, :]
                    ex_put(k, i, j, value)

    def conv_back(dc, w, row, part):
        acc = None
        for a in range(3):
            block = 2 - a + row
            if (block in (0, 3)) != (part == 1):
                continue
            for b in range(3):
                term = dot_nt(
                    dc[block * cols : (block + 1) * cols, (2 - b) * width : (3 - b) * width],
                    w[(3 * a + b) * width : (3 * a + b + 1) * width, :],
                )
                acc = term if acc is None else acc + term
        add_to(r.fbuf, row, part, acc)

    quarter_rows = pixels // 4

    def norm_of(sums, layer):
        total = r.total[0:1, :]
        centre = sums[0] / total
        inverse = lax.rsqrt(sums[1] / total - centre * centre + EPS)
        r.norm[layer, 0:1, :] = centre
        r.norm[layer, 1:2, :] = inverse
        r.norm[layer, 2:3, :] = gain[layer : layer + 1, :] * inverse
        r.norm[layer, 3:4, :] = 1.0 / total

    def corner_rows(k):
        return pl.ds((k // 2) * cols + k % 2, windows, stride=2)

    def picked(ref, j):
        out = None
        which = pick_ref[...]
        for k in range(4):
            part = jnp.where(which == k, ref[j, corner_rows(k), :], 0.0)
            out = part if out is None else out + part
        return out

    loads[2].wait()

    def image_row(i):
        def value(j):
            v = r.g1[image_at + i * cols : image_at + (i + 1) * cols, lane_at(j)].astype(F32)
            return jnp.where(valid_rows(i * cols, cols), v, 0.0)

        return value

    shift_in(image_row(0), r.xc0, 1)
    shift_in(image_row(1), r.xc0, 2)
    cast_conv(0, r.w0)
    pl.semaphore_wait(barrier, n_dp - 1 + 3)
    ag_start(0)
    r.ex_out[4] = jnp.broadcast_to(count.astype(F32), (8, lanes))
    ex_start(4)
    loads[0].wait()
    loads[1].wait()
    for l in range(2):
        for t in range(tasks):
            r.gp[pl.ds(ex_row(d, l, t), e_rows), :] = r.est[l, t].astype(BF16)
            for k in range(n_sub):
                r.gp[pl.ds(sq_row(d, l, t), e_rows), k * lanes : (k + 1) * lanes] = r.sst[
                    l, t, k * e_rows : (k + 1) * e_rows, :
                ].astype(BF16)
    cast_conv(1, r.w1)
    ag_z(0, 1)
    ag_y(0, 1)
    for item in small:
        item.wait()
    wide = 2 * lanes
    pick_row = jnp.concatenate(
        [picks[s].astype(F32), jnp.zeros((1, wide - windows), F32)], axis=1
    )
    pick_tile = jnp.broadcast_to(pick_row, (lanes, wide)).T[:windows, :].astype(jnp.int32)
    pick_ref[...] = pick_tile
    slot_pick = (
        (pick_tile // 2) * cols
        + 2 * lax.broadcasted_iota(jnp.int32, (windows, lanes), 0)
        + pick_tile % 2
    )
    r.mp[...] = jnp.where(slot_pick < count, 1.0, 0.0).astype(F32)
    ag_z(0, 2)
    ag_r(0, 1)
    ag_y(0, 2)
    ag_z(0, 3)
    ag_start(2)
    halo_start(0, r.xc0)
    ag_q(0, 1)
    ag_y(0, 3)
    ag_r(0, 2)
    ag_p(0, 1)
    ag_r(0, 3)
    ag_q(0, 2)
    ag_z(2, 1)
    r.total[...] = jnp.concatenate([ex_finish(4)[0]] * 8, axis=0)
    ag_p(0, 2)
    ag_y(2, 1)
    ag_q(0, 3)
    ag_p(0, 3)
    ag_sib(0)
    conv_forward(r.xc0, r.w0, r.h0, 0, 0)
    conv_forward(r.xc0, r.w0, r.h0, 1, 0)
    ag_z(2, 2)
    ag_r(2, 1)
    halo_finish(0, r.xc0)
    ag_y(2, 2)
    conv_forward(r.xc0, r.w0, r.h0, 0, 1, 0)
    conv_forward(r.xc0, r.w0, r.h0, 1, 1, 0)
    ex_start(0)
    halo_sent(0, r.xc0)
    ag_start(1)
    ag_z(2, 3)
    ag_q(2, 1)
    ag_r(2, 2, at_end)
    norm_of(ex_finish(0), 0)

    def block_0(j, _):
        lane = lane_at(j)
        for i in range(4):
            rows = slice(i * quarter_rows, (i + 1) * quarter_rows)
            normed = (r.h0[j, rows, :] - r.norm[0, 0:1, lane]) * r.norm[
                0, 2:3, lane
            ] + bias[0:1, lane]
            t = gelu_tanh(normed)
            ok = valid_rows(i * quarter_rows, quarter_rows)
            g = 0.5 * normed * (1.0 + t)
            r.fbuf[j, rows, :] = jnp.where(ok, g, 0.0).astype(BF16).astype(F32)
            r.slope0[j, rows, :] = t
        return 0

    def block_0_rest(j, _):
        lane = lane_at(j)
        for i in range(4):
            rows = slice(i * quarter_rows, (i + 1) * quarter_rows)
            normed = (r.h0[j, rows, :] - r.norm[0, 0:1, lane]) * r.norm[0, 2:3, lane] + bias[
                0:1, lane
            ]
            slope = gelu_slope(normed, r.slope0[j, rows, :])
            ok = valid_rows(i * quarter_rows, quarter_rows)
            r.slope0[j, rows, :] = jnp.where(ok, slope, 0.0)
        f1p = picked(r.fbuf, j)
        r.f1p[:, lane] = f1p
        r.f1b[:, lane] = f1p.astype(BF16)
        return 0

    lax.fori_loop(0, n_lane, block_0, 0)
    shift_in(lambda j: r.fbuf[j, 0:cols, :], r.xc1, 1)
    shift_in(lambda j: r.fbuf[j, cols : 2 * cols, :], r.xc1, 2)
    halo_start(1, r.xc1)
    ag_y(2, 3)
    ag_r(2, 2, jnp.logical_not(at_end))
    ag_p(2, 1)
    ag_r(2, 3)
    ag_q(2, 2)
    for step in range(1, n_z):
        ag_z(1, step)
    lax.fori_loop(0, n_lane, block_0_rest, 0)
    ag_q(2, 3)
    ag_p(2, 2)
    for step in range(1, n_z):
        ag_y(1, step)
    ag_p(2, 3)
    ag_sib(2)
    conv_forward(r.xc1, r.w1, r.h1, 0, 0)
    for step in range(1, n_z):
        ag_r(1, step)
    conv_forward(r.xc1, r.w1, r.h1, 1, 0)
    halo_finish(1, r.xc1)
    conv_forward(r.xc1, r.w1, r.h1, 0, 1, 1)
    conv_forward(r.xc1, r.w1, r.h1, 1, 1, 1)
    ex_start(1)
    for step in range(1, n_z):
        ag_q(1, step)
    for hop in range(1, n_z):
        ag_p(1, hop)
    ag_sib(1)

    def unpack(i, _):
        for l in range(2):
            for t in range(tasks):
                r.ex_w[l, t, pl.ds(al(i * e_rows, 16), e_rows), :] = r.gp[
                    pl.ds(ex_row(i, l, t), e_rows), :
                ]
                for k in range(n_sub):
                    r.sq_w[
                        l,
                        pl.ds(al(i * s_rows + k * e_rows, 16), e_rows),
                        t * bottle : (t + 1) * bottle,
                    ] = r.gp[pl.ds(sq_row(i, l, t), e_rows), k * lanes : (k + 1) * lanes]
        return 0

    lax.fori_loop(0, n_dp, unpack, 0)
    mask_pick = jnp.concatenate([r.mp[...]] * n_lane, axis=1)
    g, slope = gelu_pair(dot(r.f1b[...], r.sq_w[0]))
    r.excited0[...] = g.astype(BF16)
    r.eslope0[...] = slope

    def task_lane(t):
        return pl.ds(al(t * bottle, lanes), bottle)

    def gate_0(t, _):
        value = jax.nn.sigmoid(dot(r.excited0[:, task_lane(t)], r.ex_w[0, t]))
        r.gate0[t] = value
        r.t1[t] = (mask_pick * value * r.f1p[...]).astype(BF16)
        return 0

    for t in range(tasks):
        gate_0(t, 0)
    norm_of(ex_finish(1), 1)

    for kind in range(3):
        ag_end(kind)
    for p in plane:
        pl.semaphore_signal(r.ready, inc=1, device_id=(p, d), device_id_type=MESH)
    pl.semaphore_signal(r.ready, inc=1, device_id=(s, sib), device_id_type=MESH)

    def block_1(j, _):
        lane = lane_at(j)
        off = picked(r.h1, j) - r.norm[1, 0:1, lane]
        g, slope = gelu_pair(off * r.norm[1, 2:3, lane] + bias[1:2, lane])
        r.f2p[:, lane] = (r.mp[...] * g).astype(BF16).astype(F32)
        r.slope1[:, lane] = r.mp[...] * slope
        r.centred1[:, lane] = off * r.norm[1, 1:2, lane]
        return 0

    lax.fori_loop(0, n_lane, block_1, 0)
    grads = [r.w1, r.gp, r.g1]

    def pair_of(k):
        return z_at((2, 1, 3, 0)[k])

    def rs_a_copy(kind, k, core):
        return remote(
            shard(kind, grads[kind], 2 * pair_of(k) + core),
            r.ra[kind].at[k],
            r.ag_zs.at[kind, k],
            r.ag_zr.at[kind, k] if k < n_z - 1 else r.ag_or.at[kind],
            (s, sib),
        )

    def again(first, second, i):
        per = 6 * (n_z - 1)
        if i < 3 * per:
            return first.at[i // per, i % per]
        i, per = i - 3 * per, 4 * (n_z - 1)
        return second.at[i // per, i % per]

    def rs_b_copy(kind, k, way):
        o = 2 * pair_of(k) + c
        half = (0, 0, 1, 1, 0, 1)[way]
        to = plane[(0, 0, 1, 1, 1, 0)[way]]
        q = to if way in (0, 2, 4, 5) else plane[2]
        return remote(
            quarter(kind, grads[kind], o, q).at[:, halves[half]],
            r.rb[kind].at[k, way],
            again(r.ag_ps, r.ag_ss, (kind * n_z + k) * 6 + way),
            again(r.ag_pr, r.ag_sr, (kind * n_z + k) * 6 + way),
            (to, d),
        )

    def rs_c_copy(kind, k):
        return remote(
            r.qs[kind].at[k],
            r.rc[kind].at[k],
            r.rs_cs.at[kind, k],
            r.rs_cr.at[kind, k],
            (s, 2 * pair_of(k) + c),
        )

    def d_sem(kind, leg):
        return (kind * n_z + leg // 4) * 6 + leg % 4

    def rs_d_copy(kind, leg, q):
        rows = shard_rows[kind] // 4
        half = (0, 1, 1, 0, 0, 1)[leg]
        to = plane[(0, 1, 0, 1, 1, 0)[leg]]
        view = out_reduced[kind].at[pl.ds(al(q * rows, 16), rows), halves[half]]
        i = d_sem(kind, leg)
        return remote(
            view, view, again(r.ag_ps, r.ag_ss, i), again(r.ag_pr, r.ag_sr, i), (to, d)
        )

    def conv_weight(kind, xc, k):
        tile = 2 * shard_rows[kind] // 3
        per = 3 * width // tile

        for i in range(3):
            g = pair_of(k) * 3 + i
            a = g // per
            term = dot_tn(
                xc[pl.ds(al(a * cols, 16), pixels), pl.ds(al((g % per) * tile, lanes), tile)],
                r.dc[cols : 3 * cols, width : 2 * width],
            )
            grads[kind][pl.ds(al(g * tile, 16), tile), :] = term.astype(BF16)

    def rs_a(kind, k):
        rs_a_copy(kind, k, 1 - c).start()

    def rs_b(kind, k):
        rs_a_copy(kind, k, c).wait_recv()
        rows = shard_rows[kind]
        tile = rows // 4
        start = (2 * pair_of(k) + c) * rows

        def body(i, _):
            at = pl.ds(al(start + i * tile, 16), tile)
            grads[kind][at, :] = (
                grads[kind][at, :].astype(F32)
                + r.ra[kind][k, pl.ds(al(i * tile, 16), tile), :].astype(F32)
            ).astype(BF16)
            return 0

        lax.fori_loop(0, 4, body, 0)
        for way in range(4):
            rs_b_copy(kind, k, way).start()

    def quarter_at(kind, k, q):
        rows = shard_rows[kind]
        return pl.ds(al((2 * pair_of(k) + c) * rows + q * (rows // 4), 16), rows // 4)

    def rs_r(kind, k):
        for half in range(2):
            rs_b_copy(kind, k, 2 * half).wait_recv()
            rs_b_copy(kind, k, 2 * half + 1).wait_recv()
            at = quarter_at(kind, k, plane[1 - half])
            grads[kind][at, halves[half]] = (
                grads[kind][at, halves[half]].astype(F32)
                + r.rb[kind][k, 2 * half + 1].astype(F32)
            ).astype(BF16)
            rs_b_copy(kind, k, 4 + half).start()

    def rs_c(kind, k):
        at = quarter_at(kind, k, s)
        parts = []
        for half in range(2):
            rs_b_copy(kind, k, 4 + half).wait_recv()
            parts.append(
                grads[kind][at, halves[half]].astype(F32)
                + r.rb[kind][k, 2 * half].astype(F32)
                + r.rb[kind][k, 4 + half].astype(F32)
            )
        total = jnp.concatenate(parts, axis=1)
        if k < n_z - 1:
            r.qs[kind][k] = total.astype(BF16)
            rs_c_copy(kind, k).start()
        else:
            r.qf[kind][...] = total

    def rs_d(kind):
        total = r.qf[kind][...]
        for k in range(n_z - 1):
            rs_c_copy(kind, k).wait_recv()
            total = total + r.rc[kind][k].astype(F32)
        rows = shard_rows[kind] // 4
        out_reduced[kind][pl.ds(al(s * rows, 16), rows), :] = total.astype(BF16)
        for leg in range(6):
            rs_b_copy(kind, leg // 4, leg % 4).wait_send()
        for leg in range(4):
            rs_d_copy(kind, leg, s).start()

    def rs_dr(kind):
        for leg in range(2):
            rs_d_copy(kind, leg, plane[leg]).wait_recv()
            rs_d_copy(kind, 4 + leg, plane[leg]).start()

    def rs_e(kind):
        for leg in range(2):
            rs_d_copy(kind, 2 + leg, plane[leg]).wait_recv()
            rs_d_copy(kind, 4 + leg, plane[2]).wait_recv()

    def rs_end(kind):
        for k in range(n_z):
            rs_a_copy(kind, k, 1 - c).wait_send()
            for way in range((4, 2, 0, 0)[k], 6):
                rs_b_copy(kind, k, way).wait_send()
            if k < n_z - 1:
                rs_c_copy(kind, k).wait_send()
        for leg in range(4):
            rs_d_copy(kind, leg, s).wait_send()
        for leg in range(2):
            rs_d_copy(kind, 4 + leg, plane[leg]).wait_send()

    for item in loads[3:]:
        item.wait()
    r.df2[...] = jnp.zeros_like(r.df2)

    def pack_grads(l, t, grad_squeeze, grad_expand):
        r.fbuf[0, 0:width, :] = grad_squeeze
        for j in range(n_lane):
            r.fbuf[1, j * bottle : (j + 1) * bottle, :] = grad_expand[:, j * lanes : (j + 1) * lanes]

        def body(i, _):
            for j in range(n_lane):
                lane = slice(j * lanes, (j + 1) * lanes)
                r.gp[pl.ds(ex_row(i, l, t), e_rows), lane] = r.fbuf[
                    1, pl.ds(al(j * bottle + i * e_rows, 16), e_rows), :
                ].astype(BF16)
            for k in range(n_sub):
                r.gp[pl.ds(sq_row(i, l, t), e_rows), k * lanes : (k + 1) * lanes] = r.fbuf[
                    0, pl.ds(al(i * s_rows + k * e_rows, 16), e_rows), :
                ].astype(BF16)
            return 0

        lax.fori_loop(0, n_dp, body, 0)

    def kept(i):
        return pl.ds(al(i * windows, 16), windows)

    def gate_1(t, _):
        w_s = r.sq_w[1, :, task_lane(t)]
        w_e = r.ex_w[1, t]
        f2p = r.f2p[...]
        source = (f2p + r.t1[t].astype(F32)).astype(BF16)
        g, slope = gelu_pair(dot(source, w_s))
        excited = g.astype(BF16)
        value = jax.nn.sigmoid(dot(excited, w_e))
        field = mask_pick * f2p
        d_task = r.g1[cot_at + t * windows : cot_at + (t + 1) * windows, :].astype(F32)
        out_task[0, t] = (value * field).astype(BF16)
        d_expanded = (d_task * field * value * (1.0 - value)).astype(BF16)
        d_squeezed = (slope * dot_nt(d_expanded, w_e)).astype(BF16)
        d_source = dot_nt(d_squeezed, w_s)
        r.t1[t] = d_source.astype(BF16)
        r.df2[...] += d_source + mask_pick * d_task * value
        r.g1[kept(t), :] = source
        r.g1[kept(tasks + t), :] = d_expanded
        r.g1[kept(2 * tasks), task_lane(t)] = excited
        r.g1[kept(2 * tasks + 1), task_lane(t)] = d_squeezed
        return 0

    def gate_1_weight(t, _):
        pack_grads(
            1,
            t,
            dot_tn(r.g1[kept(t), :], r.g1[kept(2 * tasks + 1), task_lane(t)]),
            dot_tn(r.g1[kept(2 * tasks), task_lane(t)], r.g1[kept(tasks + t), :]),
        )
        return 0

    for t in range(tasks):
        gate_1(t, 0)
    def back_1(j, _):
        lane = lane_at(j)
        d_norm = r.slope1[:, lane] * r.df2[:, lane].astype(BF16).astype(F32)
        r.df2[:, lane] = d_norm
        ex_put(2, 0, j, jnp.sum(d_norm, 0, keepdims=True))
        ex_put(2, 1, j, jnp.sum(d_norm * r.centred1[:, lane], 0, keepdims=True))
        return 0

    lax.fori_loop(0, n_lane, back_1, 0)
    ex_start(2)

    r.df1[...] = jnp.zeros_like(r.df1)

    def gate_0_back(t, _):
        w_s = r.sq_w[0, :, task_lane(t)]
        w_e = r.ex_w[0, t]
        value = r.gate0[t]
        d_task = r.t1[t].astype(F32)
        excited = r.excited0[:, task_lane(t)]
        d_expanded = (d_task * (mask_pick * r.f1p[...]) * value * (1.0 - value)).astype(BF16)
        d_squeezed = (r.eslope0[:, task_lane(t)] * dot_nt(d_expanded, w_e)).astype(BF16)
        r.df1[...] += dot_nt(d_squeezed, w_s) + mask_pick * d_task * value
        pack_grads(0, t, dot_tn(r.f1b[...], d_squeezed), dot_tn(excited, d_expanded))
        return 0

    for t in range(tasks):
        gate_0_back(t, 0)
    for t in range(tasks):
        gate_1_weight(t, 0)

    r.sums[...] = jnp.zeros_like(r.sums)

    def back_terms(k, layer):
        sums = ex_finish(k)
        r.sums[2 * layer : 2 * layer + 1, :] = sums[0]
        r.sums[2 * layer + 1 : 2 * layer + 2, :] = sums[1]
        scale = gain[layer : layer + 1, :] * r.norm[layer, 3:4, :] * r.norm[layer, 1:2, :]
        r.norm[layer, 4:5, :] = scale * sums[0]
        r.norm[layer, 5:6, :] = scale * r.norm[layer, 1:2, :] * sums[1]

    pl.semaphore_wait(r.ready, 4)
    for k in range(n_z):
        rs_a(1, k)
    back_terms(2, 1)

    def hidden_grad_1(j, _):
        lane = lane_at(j)
        norm = r.norm
        for k in range(4):
            at = corner_rows(k)
            spread = jnp.where(pick_ref[...] == k, r.df2[:, lane] * norm[1, 2:3, lane], 0.0)
            value = spread - (
                norm[1, 4:5, lane] + (r.h1[j, at, :] - norm[1, 0:1, lane]) * norm[1, 5:6, lane]
            )
            slot = (k // 2) * cols + k % 2 + 2 * lax.broadcasted_iota(
                jnp.int32, (windows, lanes), 0
            )
            r.fbuf[j, at, :] = jnp.where(slot < count, value, 0.0)
        return 0

    lax.fori_loop(0, n_lane, hidden_grad_1, 0)
    shift_in(lambda j: r.fbuf[j, 0:cols, :], r.dc, 1)
    shift_in(lambda j: r.fbuf[j, cols : 2 * cols, :], r.dc, 2)
    halo_sent(1, r.xc1)
    halo_start(2, r.dc)

    for k in range(n_z):
        rs_b(1, k)
    for k in range(2):
        conv_weight(2, r.xc1, k)
        rs_a(2, k)
    conv_back(r.dc, r.w1, 0, 0)
    rs_b(2, 0)
    conv_back(r.dc, r.w1, 1, 0)
    for k in range(n_z):
        rs_r(1, k)
    rs_b(2, 1)
    halo_finish(2, r.dc)
    conv_back(r.dc, r.w1, 0, 1)
    conv_back(r.dc, r.w1, 1, 1)
    def back_0(j, _):
        lane = lane_at(j)
        norm = r.norm
        first = jnp.zeros((1, lanes), F32)
        second = jnp.zeros((1, lanes), F32)
        for k in range(4):
            at = corner_rows(k)
            d_field = r.fbuf[j, at, :].astype(BF16).astype(F32) + jnp.where(
                pick_ref[...] == k, r.df1[:, lane], 0.0
            )
            d_norm = r.slope0[j, at, :] * d_field.astype(BF16).astype(F32)
            r.fbuf[j, at, :] = d_norm
            centred = (r.h0[j, at, :] - norm[0, 0:1, lane]) * norm[0, 1:2, lane]
            first = first + jnp.sum(d_norm, 0, keepdims=True)
            second = second + jnp.sum(d_norm * centred, 0, keepdims=True)
        ex_put(3, 0, j, first)
        ex_put(3, 1, j, second)
        return 0

    lax.fori_loop(0, n_lane, back_0, 0)
    ex_start(3)
    conv_weight(2, r.xc1, 2)
    rs_a(2, 2)
    rs_r(2, 0)
    conv_weight(2, r.xc1, 3)
    rs_a(2, 3)
    rs_b(2, 2)
    halo_sent(2, r.dc)
    back_terms(3, 0)

    def sums_copy(p, q):
        return remote(
            r.sums,
            r.sums_in.at[q],
            r.sums_s.at[p],
            r.sums_r.at[p],
            (plane[p], d),
        )

    for p in range(3):
        sums_copy(p, s).start()
    r.sums_in[s] = r.sums[...]

    def hidden_grad_0(row):
        def value(j):
            lane = lane_at(j)
            norm = r.norm
            rows = slice(row * cols, (row + 1) * cols)
            out = r.fbuf[j, rows, :] * norm[0, 2:3, lane] - (
                norm[0, 4:5, lane] + (r.h0[j, rows, :] - norm[0, 0:1, lane]) * norm[0, 5:6, lane]
            )
            return jnp.where(valid_rows(row * cols, cols), out, 0.0)

        return value

    shift_in(hidden_grad_0(0), r.dc, 1)
    shift_in(hidden_grad_0(1), r.dc, 2)
    halo_start(3, r.dc)
    conv_weight(0, r.xc0, 0)
    rs_a(0, 0)
    rs_r(2, 1)
    rs_b(2, 3)
    for k in range(n_z):
        rs_c(1, k)
    conv_weight(0, r.xc0, 1)
    rs_a(0, 1)
    rs_c(2, 0)
    conv_weight(0, r.xc0, 2)
    rs_a(0, 2)
    rs_r(2, 2)
    rs_b(0, 0)
    conv_weight(0, r.xc0, 3)
    rs_a(0, 3)
    rs_c(2, 1)
    conv_back(r.dc, r.w0, 0, 0)
    rs_r(2, 3)
    rs_b(0, 1)
    conv_back(r.dc, r.w0, 1, 0)
    rs_c(2, 2)
    halo_finish(3, r.dc)
    conv_back(r.dc, r.w0, 0, 1)
    conv_back(r.dc, r.w0, 1, 1)
    def image_out(j, _):
        lane = lane_at(j)
        for i in range(4):
            rows = slice(i * quarter_rows, (i + 1) * quarter_rows)
            out_image[0, rows, lane] = jnp.where(
                valid_rows(i * quarter_rows, quarter_rows), r.fbuf[j, rows, :], 0.0
            ).astype(BF16)
        return 0

    lax.fori_loop(0, n_lane, image_out, 0)
    rs_r(0, 0)
    rs_b(0, 2)
    rs_c(2, 3)
    rs_r(0, 1)
    rs_c(0, 0)
    rs_b(0, 3)
    rs_r(0, 2)
    rs_c(0, 1)
    rs_r(0, 3)
    rs_c(0, 2)
    rs_d(1)
    rs_d(2)
    rs_c(0, 3)
    rs_dr(1)
    rs_dr(2)
    rs_d(0)
    for p in range(3):
        sums_copy(p, plane[p]).wait_recv()
    total = r.sums_in[0]
    for i in range(1, 4):
        total = total + r.sums_in[i]
    for l in range(2):
        out_bias[l : l + 1, :] = total[2 * l : 2 * l + 1, :]
        out_gain[l : l + 1, :] = total[2 * l + 1 : 2 * l + 2, :]
    for p in range(3):
        sums_copy(p, s).wait_send()
    ex_sent(2)
    ex_sent(3)
    halo_sent(3, r.dc)
    rs_dr(0)
    for kind in (1, 2, 0):
        rs_e(kind)
        rs_end(kind)


def finish_kernel(
    dims,
    task,
    image,
    reduced_0,
    reduced_1,
    reduced_2,
    gain,
    bias,
    out_task,
    out_image,
    out_conv,
    out_squeeze,
    out_expand,
    out_gain,
    out_bias,
    conv_wide,
    squeeze_wide,
    expand_wide,
    sem,
):
    lanes = 128
    e_rows = dims.bottle // dims.n_dp
    outs = []

    def store(src, dst):
        outs.append(pltpu.make_async_copy(src, dst, sem.at[len(outs)]))
        outs[-1].start()

    store(task, out_task)
    store(image, out_image)
    for layer, reduced in enumerate((reduced_0, reduced_2)):
        conv_wide[layer] = reduced[...].astype(F32)
        store(conv_wide.at[layer], out_conv.at[layer])
    for l in range(2):
        for t in range(dims.tasks):
            at = (l * dims.tasks + t) * e_rows
            expand_wide[l, t] = reduced_1[at : at + e_rows, :].astype(F32)
            at = at + 2 * dims.tasks * e_rows
            for k in range(dims.width // dims.n_dp // e_rows):
                squeeze_wide[l, t, k * e_rows : (k + 1) * e_rows, :] = reduced_1[
                    at : at + e_rows, k * lanes : (k + 1) * lanes
                ].astype(F32)
    store(squeeze_wide, out_squeeze)
    store(expand_wide, out_expand)
    out_gain[...] = gain[...]
    out_bias[...] = bias[...]
    for copy in outs:
        copy.wait()


def fused(images, counts, pool_index, conv_w, squeeze_w, expand_w, gain, bias, cotangent):
    n_dp = lax.axis_size("dp")
    micro, pixels, width = images.shape
    tasks, bottle = squeeze_w.shape[1], squeeze_w.shape[3]
    cols = 2 * pool_index.shape[2]
    windows = cols // 2
    conv_rows = conv_w.shape[1]
    gate_rows = 4 * tasks * expand_w.shape[2]
    shard_rows = (conv_rows, gate_rows, conv_rows)
    n_z = n_dp // 2
    vm = pltpu.VMEM
    dma = pltpu.SemaphoreType.DMA
    scratch = dict(
        load=dma((8 + 2 * (width // 128) + tasks,)),
        picks=vm(pool_index.shape, jnp.int32),
        gain=vm(gain.shape, F32),
        bias=vm(bias.shape, F32),
        sst=vm(squeeze_w.shape, F32),
        est=vm(expand_w.shape, F32),
        w0=vm((n_dp * conv_rows, width), BF16),
        gp=vm((n_dp * gate_rows, width), BF16),
        w1=vm((n_dp * conv_rows, width), BF16),
        g1=vm((n_dp * conv_rows, width), BF16),
        sq_w=vm((2, width, tasks * bottle), BF16),
        ex_w=vm((2, tasks, bottle, width), BF16),
        ag_zs=dma((3, 2 * (n_z - 1))),
        ag_zr=dma((3, n_z - 1)),
        ag_ps=dma((3, 6 * (n_z - 1))),
        ag_pr=dma((3, 6 * (n_z - 1))),
        ag_ss=dma((3, 4 * (n_z - 1))),
        ag_sr=dma((3, 4 * (n_z - 1))),
        ag_os=dma((3,)),
        ag_or=dma((3,)),
        mp=vm((windows, 128), F32),
        pick=vm((windows, 128), jnp.int32),
        halo=vm((2, 2, cols, width), BF16),
        halo_s=dma((2, 2)),
        halo_r=dma((2, 2)),
        ex_out=vm((5, 8, 128), F32),
        ex_in=vm((5, n_dp, 8, 128), F32),
        total=vm((8, width), F32),
        ex_s=dma((2, n_dp - 1)),
        ex_r=dma((2, n_dp - 1)),
        norm=vm((2, 8, width), F32),
        xc0=vm((4 * cols, 3 * width), BF16),
        xc1=vm((4 * cols, 3 * width), BF16),
        dc=vm((4 * cols, 3 * width), BF16),
        h0=vm((width // 128, pixels, 128), F32),
        h1=vm((width // 128, pixels, 128), F32),
        slope0=vm((width // 128, pixels, 128), F32),
        fbuf=vm((width // 128, pixels, 128), F32),
        f1p=vm((windows, width), F32),
        f1b=vm((windows, width), BF16),
        excited0=vm((windows, tasks * bottle), BF16),
        eslope0=vm((windows, tasks * bottle), F32),
        gate0=vm((tasks, windows, width), F32),
        t1=vm((tasks, windows, width), BF16),
        f2p=vm((windows, width), F32),
        slope1=vm((windows, width), F32),
        centred1=vm((windows, width), F32),
        df2=vm((windows, width), F32),
        df1=vm((windows, width), F32),
        sums=vm((8, width), F32),
        sums_in=vm((4, 8, width), F32),
        sums_s=dma((3,)),
        sums_r=dma((3,)),
        ready=pltpu.SemaphoreType.REGULAR,
        rs_cs=dma((3, n_z - 1)),
        rs_cr=dma((3, n_z - 1)),
    )
    quarters = [rows // 4 for rows in shard_rows]
    scratch.update(
        ra=[vm((n_z, rows, width), BF16) for rows in shard_rows],
        rb=[vm((n_z, 6, rows, width // 2), BF16) for rows in quarters],
        qs=[vm((n_z - 1, rows, width), BF16) for rows in quarters],
        qf=[vm((rows, width), F32) for rows in quarters],
        rc=[vm((n_z - 1, rows, width), BF16) for rows in quarters],
    )
    buffers, tree = jax.tree.flatten(scratch, is_leaf=lambda v: not isinstance(v, (dict, list)))
    dims = types.SimpleNamespace(
        tree=tree,
        n_dp=n_dp,
        cols=cols,
        pixels=pixels,
        width=width,
        tasks=tasks,
        bottle=bottle,
        shard_rows=shard_rows,
    )
    any_spec = pl.BlockSpec(memory_space=pl.ANY)
    vmem_spec = pl.BlockSpec(memory_space=pltpu.VMEM)
    smem_spec = pl.BlockSpec(memory_space=pltpu.SMEM)
    results = pl.pallas_call(
        functools.partial(step_kernel, dims),
        out_shape=(
            vm((1, tasks, windows, width), BF16),
            vm((1, pixels, width), BF16),
            *[vm((rows, width), BF16) for rows in shard_rows],
            vm(gain.shape, F32),
            vm(bias.shape, F32),
        ),
        in_specs=[smem_spec] + [any_spec] * 8,
        out_specs=(vmem_spec,) * 7,
        scratch_shapes=tuple(buffers),
        compiler_params=pltpu.CompilerParams(
            collective_id=0, has_side_effects=True, vmem_limit_bytes=VMEM_BYTES
        ),
    )(counts.reshape(micro), pool_index, gain, bias, images, conv_w, squeeze_w, expand_w, cotangent)
    results = [pltpu.with_memory_space_constraint(v, pltpu.VMEM) for v in results]
    return pl.pallas_call(
        functools.partial(finish_kernel, dims),
        out_shape=(
            jax.ShapeDtypeStruct((1, tasks, windows, width), BF16),
            jax.ShapeDtypeStruct((1, pixels, width), BF16),
            jax.ShapeDtypeStruct(conv_w.shape, F32),
            jax.ShapeDtypeStruct(squeeze_w.shape, F32),
            jax.ShapeDtypeStruct(expand_w.shape, F32),
            jax.ShapeDtypeStruct(gain.shape, F32),
            jax.ShapeDtypeStruct(bias.shape, F32),
        ),
        in_specs=[vmem_spec] * 7,
        out_specs=(any_spec,) * 5 + (vmem_spec,) * 2,
        scratch_shapes=(
            vm(conv_w.shape, F32),
            vm(squeeze_w.shape, F32),
            vm(expand_w.shape, F32),
            dma((6,)),
        ),
        compiler_params=pltpu.CompilerParams(vmem_limit_bytes=16 * 1024 * 1024),
    )(*results)


def fits_kernel(mesh, args):
    images, counts, pool_index, conv_w, squeeze_w, expand_w = args[:6]
    sections, n_dp = mesh.shape["section"], mesh.shape["dp"]
    conv_rows = conv_w.shape[1] // n_dp
    e_rows = expand_w.shape[2] // n_dp
    return (
        sections == 4
        and images.shape[0] == sections
        and n_dp % 2 == 0
        and pool_index.shape[1] == n_dp
        and conv_rows % 64 == 0
        and e_rows == 16
        and squeeze_w.shape[2] // n_dp == 4 * e_rows
        and squeeze_w.shape[3] == 128
        and images.shape[2] == 4 * 128
    )


def solution(mesh):
    placed = (
        P(None, "dp", None),
        P(None, "dp"),
        P(None, "dp", None),
        P(None, "dp", None),
        P(None, None, "dp", None),
        P(None, None, "dp", None),
        P(),
        P(),
        P(None, None, "dp", None),
    )
    def run(*args):
        return mapped(fused if fits_kernel(mesh, args) else on_device)(*args)

    def mapped(body):
        return jax.shard_map(
        body,
        mesh=mesh,
        in_specs=placed,
        out_specs=(
            P("section", None, "dp", None),
            P("section", "dp", None),
            P(None, "dp", None),
            P(None, None, "dp", None),
            P(None, None, "dp", None),
            P(),
            P(),
        ),
        check_vma=False,
    )

    return run
```

```python
import functools
import types

import jax
import jax.numpy as jnp
from jax import lax
from jax.experimental import pallas as pl
from jax.experimental.pallas import tpu as pltpu
from jax.sharding import PartitionSpec as P

EPS = 1e-05
BF16 = jnp.bfloat16
F32 = jnp.float32
VMEM_BYTES = 58 * 1024 * 1024


def gelu_back(point, upstream):
    return jax.vjp(jax.nn.gelu, point)[1](upstream)[0]


def with_halo(value, axis):
    size = lax.axis_size(axis)
    up = [(i, i + 1) for i in range(size - 1)]
    down = [(j, i) for i, j in up]
    before = lax.ppermute(value[-1:], axis, up)
    after = lax.ppermute(value[:1], axis, down)
    return jnp.concatenate([before, value, after], axis=0)


def conv(padded, taps):
    out = lax.conv_general_dilated(
        padded[None],
        taps,
        (1, 1),
        ((0, 0), (1, 1)),
        dimension_numbers=("NHWC", "HWIO", "NHWC"),
        preferred_element_type=F32,
    )
    return out.reshape(-1, out.shape[-1])


def conv_input_grad(d_padded, taps):
    out = lax.conv_general_dilated(
        d_padded[None],
        taps[::-1, ::-1],
        (1, 1),
        ((0, 0), (1, 1)),
        dimension_numbers=("NHWC", "HWOI", "NHWC"),
        preferred_element_type=F32,
    )
    return out.reshape(-1, out.shape[-1])


def conv_weight_grad(padded, d_hidden):
    out = lax.conv_general_dilated(
        padded[None],
        d_hidden[None],
        (1, 1),
        ((0, 0), (1, 1)),
        dimension_numbers=("CHWN", "IHWO", "HWNC"),
        preferred_element_type=F32,
    )
    return out.reshape(-1, out.shape[-1])


def gate_forward(source, w_squeeze, w_expand):
    squeezed = jnp.einsum("tpc,tcb->tpb", source, w_squeeze, preferred_element_type=F32)
    excited = jax.nn.gelu(squeezed).astype(BF16)
    expanded = jnp.einsum("tpb,tbc->tpc", excited, w_expand, preferred_element_type=F32)
    return squeezed, excited, jax.nn.sigmoid(expanded)


def gate_backward(d_task, field, source, squeezed, excited, gate_val, w_squeeze, w_expand):
    d_expanded = (d_task * field[None] * gate_val * (1.0 - gate_val)).astype(BF16)
    d_excited = jnp.einsum("tpc,tbc->tpb", d_expanded, w_expand, preferred_element_type=F32)
    d_squeezed = gelu_back(squeezed, d_excited).astype(BF16)
    d_source = jnp.einsum("tpb,tcb->tpc", d_squeezed, w_squeeze, preferred_element_type=F32)
    grad_squeeze = jnp.einsum("tpc,tpb->tcb", source, d_squeezed, preferred_element_type=F32)
    grad_expand = jnp.einsum("tpb,tpc->tbc", excited, d_expanded, preferred_element_type=F32)
    return d_source, grad_squeeze, grad_expand


def pool_pick(field, pick):
    tasks, _, width = field.shape
    half_rows, half_columns = pick.shape
    windows = field.reshape(tasks, half_rows, 2, half_columns, 2, width)
    picked = jnp.zeros((tasks, half_rows, half_columns, width), F32)
    for corner in range(4):
        hit = (pick == corner)[None, :, :, None]
        picked = picked + jnp.where(hit, windows[:, :, corner // 2, :, corner % 2, :], 0.0)
    return picked.reshape(tasks, half_rows * half_columns, width)


def pool_spread(d_pooled, pick):
    tasks, _, width = d_pooled.shape
    half_rows, half_columns = pick.shape
    grid = d_pooled.reshape(tasks, half_rows, half_columns, width)
    rows = [
        jnp.stack(
            [jnp.where((pick == 2 * dy + dx)[None, :, :, None], grid, 0.0) for dx in range(2)], 3
        )
        for dy in range(2)
    ]
    return jnp.stack(rows, 2).reshape(tasks, half_rows * 2 * half_columns * 2, width)


def on_device(images, counts, pool_index, conv_w, squeeze_w, expand_w, gain, bias, cotangent):
    sections = lax.axis_size("section")
    here = lax.axis_index("section")
    micro, pixels, width = images.shape
    layers = conv_w.shape[0]
    tasks = squeeze_w.shape[1]
    rows = 2 * pool_index.shape[1]
    columns = 2 * pool_index.shape[2]
    share = micro // sections

    def own(value):
        return lax.dynamic_slice_in_dim(value, here * share, share, 0)

    images, counts, pool_index, cotangent = (
        own(images),
        own(counts),
        own(pool_index),
        own(cotangent),
    )

    def gather(value, axis):
        return lax.all_gather(value.astype(BF16), "dp", axis=axis, tiled=True)

    taps = [gather(conv_w[l], 0).reshape(3, 3, width, width) for l in range(layers)]
    w_squeeze = [gather(squeeze_w[l], 1) for l in range(layers)]
    w_expand = [gather(expand_w[l], 1) for l in range(layers)]
    slots = jnp.arange(pixels, dtype=jnp.int32)[:, None]

    def block_forward(field, mask, total, layer):
        padded = with_halo(field.reshape(rows, columns, width), "dp")
        hidden = conv(padded, taps[layer])
        sums = lax.psum(
            jnp.stack([jnp.sum(mask * hidden, 0), jnp.sum(mask * hidden * hidden, 0)]), "dp"
        )
        centre = sums[0] / total
        inverse = lax.rsqrt(sums[1] / total - centre * centre + EPS)
        normed = gain[layer] * (hidden - centre) * inverse + bias[layer]
        out = (mask * jax.nn.gelu(normed)).astype(BF16)
        return out, (padded, hidden, centre, inverse)

    def block_backward(d_out, kept, mask, total, layer):
        padded, hidden, centre, inverse = kept
        centred = (hidden - centre) * inverse
        normed = gain[layer] * (hidden - centre) * inverse + bias[layer]
        d_norm = gelu_back(normed, mask * d_out)
        gain_sum = jnp.sum(d_norm * centred, 0)
        bias_sum = jnp.sum(d_norm, 0)
        sums = gain[layer] * lax.psum(jnp.stack([bias_sum, gain_sum]), "dp")
        d_hidden = (
            mask * inverse * (gain[layer] * d_norm - sums[0] / total - centred * sums[1] / total)
        ).astype(BF16)
        d_hidden = d_hidden.reshape(rows, columns, width)
        d_x = conv_input_grad(with_halo(d_hidden, "dp"), taps[layer])
        return d_x, conv_weight_grad(padded, d_hidden), gain_sum, bias_sum

    outs, image_grads = [], []
    grads = None
    totals = lax.psum(counts[:, 0], "dp").astype(F32)
    for m in range(share):
        total = totals[m]
        mask = (slots < counts[m, 0]).astype(F32)
        first_in = jnp.where(slots < counts[m, 0], images[m], jnp.zeros((), BF16))
        f1, kept_0 = block_forward(first_in, mask, total, 0)
        f1_f = f1.astype(F32)
        source_0 = jnp.broadcast_to(f1[None], (tasks, pixels, width))
        squeezed_0, excited_0, gate_0 = gate_forward(source_0, w_squeeze[0], w_expand[0])
        t1 = (mask[None] * gate_0 * f1_f[None]).astype(BF16)
        f2, kept_1 = block_forward(f1, mask, total, 1)
        f2_f = f2.astype(F32)
        source_1 = (f2_f[None] + t1.astype(F32)).astype(BF16)
        squeezed_1, excited_1, gate_1 = gate_forward(source_1, w_squeeze[1], w_expand[1])
        outs.append(pool_pick(mask[None] * gate_1 * f2_f[None], pool_index[m]).astype(BF16))

        d_task = pool_spread(cotangent[m].astype(F32), pool_index[m])
        d_source, gs_1, ge_1 = gate_backward(
            d_task, mask * f2_f, source_1, squeezed_1, excited_1, gate_1, w_squeeze[1], w_expand[1]
        )
        d_f2 = (jnp.sum(d_source, 0) + mask * jnp.sum(d_task * gate_1, 0)).astype(BF16)
        d_t1 = d_source.astype(BF16).astype(F32)
        d_x1, gc_1, gain_1, bias_1 = block_backward(d_f2.astype(F32), kept_1, mask, total, 1)
        d_source, gs_0, ge_0 = gate_backward(
            d_t1, mask * f1_f, source_0, squeezed_0, excited_0, gate_0, w_squeeze[0], w_expand[0]
        )
        d_f1 = (
            d_x1.astype(BF16).astype(F32)
            + jnp.sum(d_source, 0)
            + mask * jnp.sum(d_t1 * gate_0, 0)
        ).astype(BF16)
        d_x0, gc_0, gain_0, bias_0 = block_backward(d_f1.astype(F32), kept_0, mask, total, 0)
        image_grads.append((mask * d_x0).astype(BF16))
        here_grads = [
            [gc_0, gc_1],
            [gs_0, gs_1],
            [ge_0, ge_1],
            jnp.stack([gain_0, gain_1]),
            jnp.stack([bias_0, bias_1]),
        ]
        grads = here_grads if grads is None else jax.tree.map(jnp.add, grads, here_grads)

    def reduced(value, axis):
        part = lax.psum_scatter(value, "dp", scatter_dimension=axis, tiled=True)
        return lax.psum(part.astype(BF16), "section").astype(F32)

    conv_grad = jnp.stack([reduced(g, 0) for g in grads[0]])
    squeeze_grad = jnp.stack([reduced(g, 1) for g in grads[1]])
    expand_grad = jnp.stack([reduced(g, 1) for g in grads[2]])
    gain_grad, bias_grad = lax.psum((grads[3], grads[4]), ("section", "dp"))
    return (
        jnp.stack(outs),
        jnp.stack(image_grads),
        conv_grad,
        squeeze_grad,
        expand_grad,
        gain_grad,
        bias_grad,
    )


GELU_C = 0.7978845608028654
GELU_K = 0.044715
MESH = pl.DeviceIdType.MESH


def gelu_tanh(x):
    return jnp.tanh(GELU_C * x * (1.0 + GELU_K * (x * x)))


def gelu_slope(x, t):
    inner = GELU_C * (1.0 + 3.0 * GELU_K * (x * x))
    return 0.5 * (1.0 + t) + 0.5 * x * (1.0 - t * t) * inner


def gelu_pair(x):
    t = gelu_tanh(x)
    return 0.5 * x * (1.0 + t), gelu_slope(x, t)


def dot(a, b):
    return jnp.dot(a, b, preferred_element_type=F32)


def dot_nt(a, b):
    return lax.dot_general(a, b, (((1,), (1,)), ((), ())), preferred_element_type=F32)


def dot_tn(a, b):
    return lax.dot_general(a, b, (((0,), (0,)), ((), ())), preferred_element_type=F32)


def step_kernel(
    dims,
    counts_in,
    picks_in,
    gain_in,
    bias_in,
    images,
    conv_w,
    squeeze_w,
    expand_w,
    cotangent,
    out_task,
    out_image,
    out_reduced_0,
    out_reduced_1,
    out_reduced_2,
    out_gain,
    out_bias,
    *scratch,
):
    out_reduced = (out_reduced_0, out_reduced_1, out_reduced_2)
    r = types.SimpleNamespace(**jax.tree.unflatten(dims.tree, scratch))
    n_dp, cols, pixels, width, tasks, bottle = (
        dims.n_dp,
        dims.cols,
        dims.pixels,
        dims.width,
        dims.tasks,
        dims.bottle,
    )
    n_z = n_dp // 2
    windows = cols // 2
    lanes = 128
    n_lane = width // lanes
    shard_rows = dims.shard_rows
    s = lax.axis_index("section")
    d = lax.axis_index("dp")
    z, c = d // 2, d % 2
    sib = 2 * z + 1 - c
    plane = [s + 1 - 2 * (s % 2), (s + 2) % 4, 3 - s]

    def rem(a, b):
        return lax.rem(a, b)

    def z_at(step):
        return rem(z + step, n_z)

    def remote(src, dst, send, recv, device):
        return pltpu.make_async_remote_copy(
            src_ref=src,
            dst_ref=dst,
            send_sem=send,
            recv_sem=recv,
            device_id=device,
            device_id_type=MESH,
        )

    def al(v, m):
        return pl.multiple_of(v, m)

    barrier = pltpu.get_barrier_semaphore()
    for step in range(1, n_dp):
        pl.semaphore_signal(
            barrier, inc=1, device_id=(s, rem(d + step, n_dp)), device_id_type=MESH
        )
    for p in plane:
        pl.semaphore_signal(barrier, inc=1, device_id=(p, d), device_id_type=MESH)

    def load(i, src, dst):
        return pltpu.make_async_copy(src, dst, r.load.at[i])

    staging = [r.h1, r.slope0]
    conv_rows = shard_rows[0]

    def conv_load(layer, j):
        lane = slice(j * lanes, (j + 1) * lanes)
        return load(
            5 + layer * n_lane + j,
            conv_w.at[layer, :, lane],
            staging[layer].at[j, 0:conv_rows],
        )

    cot_at = (2 * tasks + 2) * windows
    image_at = cot_at + tasks * windows
    loads = [
        load(1, squeeze_w, r.sst),
        load(2, expand_w, r.est),
        load(3, images.at[s], r.g1.at[image_at : image_at + pixels]),
        *[
            load(
                5 + 2 * n_lane + t,
                cotangent.at[s, t],
                r.g1.at[cot_at + t * windows : cot_at + (t + 1) * windows],
            )
            for t in range(tasks)
        ],
    ]
    small_at = 5 + 2 * n_lane + tasks
    picks, gain, bias = r.picks, r.gain, r.bias
    counts = r.counts
    count_load = load(small_at + 3, counts_in, counts)
    small = [
        load(small_at, picks_in, picks),
        load(small_at + 1, gain_in, gain),
        load(small_at + 2, bias_in, bias),
    ]
    for j in range(n_lane):
        conv_load(0, j).start()
    count_load.start()
    loads[2].start()
    for j in range(n_lane):
        conv_load(1, j).start()
    for item in small:
        item.start()
    for i in (0, 1, *range(3, 3 + tasks)):
        loads[i].start()

    full = [r.w0, r.gp, r.w1]

    def shard(kind, buf, which):
        rows = shard_rows[kind]
        return buf.at[pl.ds(al(which * rows, 16), rows)]

    def quarter(kind, buf, which, q):
        rows = shard_rows[kind]
        return buf.at[pl.ds(al(which * rows + q * (rows // 4), 16), rows // 4)]

    def z_of(way, hop):
        return z_at(n_z - hop if way == 0 else hop)

    def has(way, hop):
        return z >= hop if way == 0 else z < n_z - hop

    def slot_of(way, hop):
        return n_z - 1 - hop if way == 0 else hop - 1

    def ag_z_copy(kind, way, hop, owner):
        view = quarter(kind, full[kind], 2 * owner + c, s)
        return remote(
            view,
            view,
            r.ag_zs.at[kind, (hop - 1) * 2 + way],
            r.ag_zr.at[kind, slot_of(way, hop)],
            (s, 2 * z_at(1 if way == 0 else n_z - 1) + c),
        )

    def gate_z_copy(step, owner):
        view = quarter(1, full[1], 2 * owner + c, s)
        return remote(
            view,
            view,
            r.ag_zs.at[1, step - 1],
            r.ag_zr.at[1, step - 1],
            (s, 2 * z_at(step) + c),
        )

    def ag_pass(kind, way, hop, do):
        here_has = has(way, hop - 1) if hop > 1 else True
        there = z < n_z - 1 if way == 0 else z > 0
        owner = z_of(way, hop - 1)

        @pl.when(jnp.logical_and(here_has, there))
        def _():
            do(ag_z_copy(kind, way, hop, owner))

    halves = [slice(0, width // 2), slice(width // 2, width)]

    def ag_p_copy(kind, slot, owner, leg, q):
        half = (0, 1, 0, 1, 0, 1)[leg]
        view = quarter(kind, full[kind], 2 * owner + c, q).at[:, halves[half]]
        to = plane[(0, 0, 1, 1, 1, 0)[leg]]
        i = slot * 6 + leg
        return remote(view, view, r.ag_ps.at[kind, i], r.ag_pr.at[kind, i], (to, d))

    def ag_own_copy(kind, core):
        view = shard(kind, full[kind], 2 * z + core)
        return remote(view, view, r.ag_os.at[kind], r.ag_or.at[kind], (s, sib))

    def ag_s_copy(kind, slot, owner, i, core):
        view = quarter(kind, full[kind], 2 * owner + core, others[i])
        i = slot * 4 + i
        return remote(view, view, r.ag_ss.at[kind, i], r.ag_sr.at[kind, i], (s, sib))

    others = [s] + plane

    def both(condition):
        return (condition, condition)

    def ag_start(kind):
        if kind == 1:
            for step in range(1, n_z):
                gate_z_copy(step, z).start()
        else:
            for way in range(2):
                ag_pass(kind, way, 1, lambda copy: copy.start())
        ag_own_copy(kind, c).start()

    at_end = jnp.logical_or(z == 0, z == n_z - 1)

    in_middle = jnp.logical_not(at_end)
    from_end = (z == 1, z == n_z - 2)
    not_from_end = (z != 1, z != n_z - 2)

    def for_hop(kind, hop, do, also=(True, True)):
        if kind == 1:
            do(hop - 1, z_at(n_z - hop), None)
            return
        for way in range(2):

            @pl.when(jnp.logical_and(has(way, hop), also[way]))
            def _():
                do(slot_of(way, hop), z_of(way, hop), way)

    def ag_z(kind, hop, also=(True, True), legs=True):
        def do(slot, owner, way):
            if kind == 1:
                gate_z_copy(hop, owner).wait_recv()
            else:
                ag_z_copy(kind, way, hop, owner).wait_recv()
                if hop < n_z - 1:
                    ag_pass(kind, way, hop + 1, lambda copy: copy.start())
            if legs:
                for leg in (0, 3):
                    ag_p_copy(kind, slot, owner, leg, s).start()

        for_hop(kind, hop, do, also)

    def ag_l(kind, hop, also):
        def do(slot, owner, way):
            for leg in (0, 3):
                ag_p_copy(kind, slot, owner, leg, s).start()

        for_hop(kind, hop, do, also)

    def ag_y(kind, hop, also=(True, True)):
        def do(slot, owner, way):
            for leg in (0, 3):
                ag_p_copy(kind, slot, owner, leg, s).wait_send()
            for leg in (1, 2):
                ag_p_copy(kind, slot, owner, leg, s).start()
            ag_s_copy(kind, slot, owner, 0, c).start()

        for_hop(kind, hop, do, also)

    def ag_r(kind, hop, also=(True, True)):
        def do(slot, owner, way):
            for h in range(2):
                ag_p_copy(kind, slot, owner, 3 * h, plane[h]).wait_recv()
                ag_p_copy(kind, slot, owner, 4 + h, plane[h]).start()

        for_hop(kind, hop, do, also)

    def ag_q(kind, hop):
        def do(slot, owner, way):
            for axis in range(2):
                ag_p_copy(kind, slot, owner, 1 + axis, plane[axis]).wait_recv()
                ag_s_copy(kind, slot, owner, 1 + axis, c).start()

        for_hop(kind, hop, do)

    def ag_p(kind, hop):
        def do(slot, owner, way):
            for h in range(2):
                ag_p_copy(kind, slot, owner, 4 + h, plane[2]).wait_recv()
            ag_s_copy(kind, slot, owner, 3, c).start()

        for_hop(kind, hop, do)

    def ag_sib(kind):
        ag_own_copy(kind, 1 - c).wait_recv()
        for hop in range(1, n_z):

            def do(slot, owner, way):
                for i in range(4):
                    ag_s_copy(kind, slot, owner, i, 1 - c).wait_recv()

            for_hop(kind, hop, do)

    def ag_end(kind):
        ag_own_copy(kind, c).wait_send()
        for hop in range(1, n_z):

            def do(slot, owner, way):
                for leg in (1, 2):
                    ag_p_copy(kind, slot, owner, leg, s).wait_send()
                for h in range(2):
                    ag_p_copy(kind, slot, owner, 4 + h, plane[h]).wait_send()
                for i in range(4):
                    ag_s_copy(kind, slot, owner, i, c).wait_send()

            if kind == 1:
                gate_z_copy(hop, z).wait_send()
            else:
                for way in range(2):
                    ag_pass(kind, way, hop, lambda copy: copy.wait_send())
            for_hop(kind, hop, do)

    def cast_conv(layer, buf):
        for j in range(n_lane):
            conv_load(layer, j).wait()

        def body(j, _):
            buf[pl.ds(al(d * conv_rows, 16), conv_rows), pl.ds(al(j * lanes, lanes), lanes)] = (
                staging[layer][j, 0:conv_rows, :].astype(BF16)
            )
            return 0

        lax.fori_loop(0, n_lane, body, 0)

    g_rows = shard_rows[1]
    e_rows = n_ex = bottle // n_dp
    s_rows = width // n_dp
    n_sub = s_rows // e_rows

    def ex_row(which, l, t):
        return al(which * g_rows + (l * tasks + t) * e_rows, 16)

    def sq_row(which, l, t):
        return al(which * g_rows + (2 * tasks + l * tasks + t) * e_rows, 16)

    cast_conv(0, r.w0)
    pl.semaphore_wait(barrier, n_dp - 1 + 3)
    ag_start(0)
    count_load.wait()
    count = counts[s]
    pick_ref = r.pick

    def lane_at(j, base=0):
        return pl.ds(al(base + j * lanes, lanes), lanes)

    def valid_rows(start, rows):
        return (lax.broadcasted_iota(jnp.int32, (rows, lanes), 0) + start) < count

    def shift_in(value_of, buf, block):
        def body(j, _):
            v = value_of(j)
            at = lax.broadcasted_iota(jnp.int32, (cols, lanes), 0)
            before = jnp.where(at == 0, 0.0, pltpu.roll(v, 1, 0))
            after = jnp.where(at == cols - 1, 0.0, pltpu.roll(v, cols - 1, 0))
            rows = pl.ds(block * cols, cols)
            buf[rows, lane_at(j)] = before.astype(BF16)
            buf[rows, lane_at(j, width)] = v.astype(BF16)
            buf[rows, lane_at(j, 2 * width)] = after.astype(BF16)
            return 0

        lax.fori_loop(0, n_lane, body, 0)

    @pl.when(d == 0)
    def _():
        r.halo[:, 0] = jnp.zeros_like(r.halo[:, 0])

    @pl.when(d == n_dp - 1)
    def _():
        r.halo[:, 1] = jnp.zeros_like(r.halo[:, 1])

    def halo_down(e, buf):
        return remote(
            buf.at[2 * cols : 3 * cols, width : 2 * width],
            r.halo.at[e % 2, 0],
            r.halo_s.at[e % 2, 0],
            r.halo_r.at[e % 2, 0],
            (s, rem(d + 1, n_dp)),
        )

    def halo_up(e, buf):
        return remote(
            buf.at[cols : 2 * cols, width : 2 * width],
            r.halo.at[e % 2, 1],
            r.halo_s.at[e % 2, 1],
            r.halo_r.at[e % 2, 1],
            (s, rem(d + n_dp - 1, n_dp)),
        )

    def halo_start(e, buf):
        @pl.when(d < n_dp - 1)
        def _():
            halo_down(e, buf).start()

        @pl.when(d > 0)
        def _():
            halo_up(e, buf).start()

    def halo_finish(e, buf):
        @pl.when(d > 0)
        def _():
            halo_down(e, buf).wait_recv()

        @pl.when(d < n_dp - 1)
        def _():
            halo_up(e, buf).wait_recv()

        shift_in(lambda j: r.halo[e % 2, 0, :, lane_at(j)].astype(F32), buf, 0)
        shift_in(lambda j: r.halo[e % 2, 1, :, lane_at(j)].astype(F32), buf, 3)

    def halo_sent(e, buf):
        @pl.when(d < n_dp - 1)
        def _():
            halo_down(e, buf).wait_send()

        @pl.when(d > 0)
        def _():
            halo_up(e, buf).wait_send()

    def ex_copy(k, step, owner):
        turn = (k + 1) % 5 % 2
        return remote(
            r.ex_out.at[k],
            r.ex_in.at[k, owner],
            r.ex_s.at[turn, step - 1],
            r.ex_r.at[turn, step - 1],
            (s, rem(d + step, n_dp)),
        )

    def ex_sent(k):
        for step in range(1, n_dp):
            ex_copy(k, step, d).wait_send()

    def ex_start(k):
        if k in (1, 2, 3):
            ex_sent((4, 0, 1)[k - 1])
        for step in range(1, n_dp):
            ex_copy(k, step, d).start()
        r.ex_in[k, d] = r.ex_out[k]

    def ex_finish(k):
        for step in range(1, n_dp):
            ex_copy(k, step, rem(d + n_dp - step, n_dp)).wait_recv()
        total = r.ex_in[k, 0]
        for i in range(1, n_dp):
            total = total + r.ex_in[k, i]
        return [
            jnp.concatenate([total[i * n_lane + j : i * n_lane + j + 1] for j in range(n_lane)], 1)
            for i in range(2)
        ]

    def ex_put(k, i, j, value):
        r.ex_out[k, pl.ds(i * n_lane + j, 1), :] = value

    def conv_forward(xc, w, h, row, part, k=None):
        span = 3 * width
        acc = None
        for a in range(3):
            block = a + row
            if (block in (0, 3)) != (part == 1):
                continue
            term = dot(xc[block * cols : (block + 1) * cols, :], w[a * span : (a + 1) * span, :])
            acc = term if acc is None else acc + term
        add_to(h, row, part, acc, k)

    def add_to(out, row, part, acc, k=None):
        for j in range(n_lane):
            at = (j, slice(row * cols, (row + 1) * cols), slice(None))
            piece = acc[:, j * lanes : (j + 1) * lanes]
            if part == 1:
                piece = out[at] + piece
            out[at] = piece
            if k is not None:
                kept = jnp.where(valid_rows(row * cols, cols), piece, 0.0)
                for i, value in enumerate((kept, kept * piece)):
                    value = jnp.sum(value, 0, keepdims=True)
                    if row == 1:
                        value = value + r.ex_out[k, i * n_lane + j : i * n_lane + j + 1, :]
                    ex_put(k, i, j, value)

    def conv_back(dc, w, row, part):
        acc = None
        for a in range(3):
            block = 2 - a + row
            if (block in (0, 3)) != (part == 1):
                continue
            for b in range(3):
                term = dot_nt(
                    dc[block * cols : (block + 1) * cols, (2 - b) * width : (3 - b) * width],
                    w[(3 * a + b) * width : (3 * a + b + 1) * width, :],
                )
                acc = term if acc is None else acc + term
        add_to(r.fbuf, row, part, acc)

    quarter_rows = pixels // 4

    def norm_of(sums, layer):
        total = r.total[0:1, :]
        centre = sums[0] / total
        inverse = lax.rsqrt(sums[1] / total - centre * centre + EPS)
        r.norm[layer, 0:1, :] = centre
        r.norm[layer, 1:2, :] = inverse
        r.norm[layer, 2:3, :] = gain[layer : layer + 1, :] * inverse
        r.norm[layer, 3:4, :] = 1.0 / total

    def corner_rows(k):
        return pl.ds((k // 2) * cols + k % 2, windows, stride=2)

    def picked(ref, j):
        out = None
        which = pick_ref[...]
        for k in range(4):
            part = jnp.where(which == k, ref[j, corner_rows(k), :], 0.0)
            out = part if out is None else out + part
        return out

    loads[2].wait()

    def image_row(i):
        def value(j):
            v = r.g1[image_at + i * cols : image_at + (i + 1) * cols, lane_at(j)].astype(F32)
            return jnp.where(valid_rows(i * cols, cols), v, 0.0)

        return value

    shift_in(image_row(0), r.xc0, 1)
    shift_in(image_row(1), r.xc0, 2)
    r.ex_out[4] = jnp.broadcast_to(count.astype(F32), (8, lanes))
    ex_start(4)
    loads[0].wait()
    loads[1].wait()
    for l in range(2):
        for t in range(tasks):
            r.gp[pl.ds(ex_row(d, l, t), e_rows), :] = r.est[l, t].astype(BF16)
            for k in range(n_sub):
                r.gp[pl.ds(sq_row(d, l, t), e_rows), k * lanes : (k + 1) * lanes] = r.sst[
                    l, t, k * e_rows : (k + 1) * e_rows, :
                ].astype(BF16)
    cast_conv(1, r.w1)
    ag_z(0, 1)

    @pl.when(at_end)
    def _():
        ag_start(2)

    ag_y(0, 1)
    for item in small:
        item.wait()
    wide = 2 * lanes
    pick_row = jnp.concatenate(
        [picks[s].astype(F32), jnp.zeros((1, wide - windows), F32)], axis=1
    )
    pick_tile = jnp.broadcast_to(pick_row, (lanes, wide)).T[:windows, :].astype(jnp.int32)
    pick_ref[...] = pick_tile
    slot_pick = (
        (pick_tile // 2) * cols
        + 2 * lax.broadcasted_iota(jnp.int32, (windows, lanes), 0)
        + pick_tile % 2
    )
    r.mp[...] = jnp.where(slot_pick < count, 1.0, 0.0).astype(F32)
    ag_z(0, 2)
    ag_z(2, 1, from_end, legs=False)
    ag_r(0, 1)
    ag_y(0, 2)
    ag_z(0, 3)

    @pl.when(in_middle)
    def _():
        ag_start(2)

    halo_start(0, r.xc0)
    ag_q(0, 1)
    ag_z(2, 2, both(in_middle), legs=False)
    ag_y(0, 3)
    ag_r(0, 2)
    ag_p(0, 1)
    ag_r(0, 3)
    ag_q(0, 2)
    ag_l(2, 1, from_end)
    ag_z(2, 1, not_from_end)
    ag_l(2, 2, both(in_middle))
    r.total[...] = jnp.concatenate([ex_finish(4)[0]] * 8, axis=0)
    ag_p(0, 2)
    ag_y(2, 1)
    ag_q(0, 3)
    ag_p(0, 3)
    ag_sib(0)
    ag_z(2, 3)
    conv_forward(r.xc0, r.w0, r.h0, 0, 0)
    conv_forward(r.xc0, r.w0, r.h0, 1, 0)
    ag_z(2, 2, both(at_end))
    ag_r(2, 1)
    halo_finish(0, r.xc0)
    ag_y(2, 2, both(in_middle))
    ag_y(2, 3)
    conv_forward(r.xc0, r.w0, r.h0, 0, 1, 0)
    conv_forward(r.xc0, r.w0, r.h0, 1, 1, 0)
    ex_start(0)
    halo_sent(0, r.xc0)
    ag_start(1)
    ag_y(2, 2, both(at_end))
    ag_q(2, 1)
    ag_r(2, 2, both(in_middle))
    ag_r(2, 3)
    norm_of(ex_finish(0), 0)

    def block_0(j, _):
        lane = lane_at(j)
        for i in range(4):
            rows = slice(i * quarter_rows, (i + 1) * quarter_rows)
            normed = (r.h0[j, rows, :] - r.norm[0, 0:1, lane]) * r.norm[
                0, 2:3, lane
            ] + bias[0:1, lane]
            t = gelu_tanh(normed)
            ok = valid_rows(i * quarter_rows, quarter_rows)
            g = 0.5 * normed * (1.0 + t)
            r.fbuf[j, rows, :] = jnp.where(ok, g, 0.0).astype(BF16).astype(F32)
            r.slope0[j, rows, :] = t
        return 0

    def block_0_rest(j, _):
        lane = lane_at(j)
        for i in range(4):
            rows = slice(i * quarter_rows, (i + 1) * quarter_rows)
            normed = (r.h0[j, rows, :] - r.norm[0, 0:1, lane]) * r.norm[0, 2:3, lane] + bias[
                0:1, lane
            ]
            slope = gelu_slope(normed, r.slope0[j, rows, :])
            ok = valid_rows(i * quarter_rows, quarter_rows)
            r.slope0[j, rows, :] = jnp.where(ok, slope, 0.0)
        f1p = picked(r.fbuf, j)
        r.f1p[:, lane] = f1p
        r.f1b[:, lane] = f1p.astype(BF16)
        return 0

    lax.fori_loop(0, n_lane, block_0, 0)
    shift_in(lambda j: r.fbuf[j, 0:cols, :], r.xc1, 1)
    shift_in(lambda j: r.fbuf[j, cols : 2 * cols, :], r.xc1, 2)
    halo_start(1, r.xc1)
    ag_r(2, 2, both(at_end))
    ag_p(2, 1)
    ag_q(2, 2)
    for step in range(1, n_z):
        ag_z(1, step)
    lax.fori_loop(0, n_lane, block_0_rest, 0)
    ag_q(2, 3)
    ag_p(2, 2)
    for step in range(1, n_z):
        ag_y(1, step)
    ag_p(2, 3)
    ag_sib(2)
    conv_forward(r.xc1, r.w1, r.h1, 0, 0)
    for step in range(1, n_z):
        ag_r(1, step)
    conv_forward(r.xc1, r.w1, r.h1, 1, 0)
    halo_finish(1, r.xc1)
    conv_forward(r.xc1, r.w1, r.h1, 0, 1, 1)
    conv_forward(r.xc1, r.w1, r.h1, 1, 1, 1)
    ex_start(1)
    for step in range(1, n_z):
        ag_q(1, step)
    for hop in range(1, n_z):
        ag_p(1, hop)
    ag_sib(1)

    def unpack(i, _):
        for l in range(2):
            for t in range(tasks):
                r.ex_w[l, t, pl.ds(al(i * e_rows, 16), e_rows), :] = r.gp[
                    pl.ds(ex_row(i, l, t), e_rows), :
                ]
                for k in range(n_sub):
                    r.sq_w[
                        l,
                        pl.ds(al(i * s_rows + k * e_rows, 16), e_rows),
                        t * bottle : (t + 1) * bottle,
                    ] = r.gp[pl.ds(sq_row(i, l, t), e_rows), k * lanes : (k + 1) * lanes]
        return 0

    lax.fori_loop(0, n_dp, unpack, 0)
    mask_pick = jnp.concatenate([r.mp[...]] * n_lane, axis=1)
    g, slope = gelu_pair(dot(r.f1b[...], r.sq_w[0]))
    r.excited0[...] = g.astype(BF16)
    r.eslope0[...] = slope

    def task_lane(t):
        return pl.ds(al(t * bottle, lanes), bottle)

    def gate_0(t, _):
        value = jax.nn.sigmoid(dot(r.excited0[:, task_lane(t)], r.ex_w[0, t]))
        r.gate0[t] = value
        r.t1[t] = (mask_pick * value * r.f1p[...]).astype(BF16)
        return 0

    for t in range(tasks):
        gate_0(t, 0)
    norm_of(ex_finish(1), 1)

    for kind in range(3):
        ag_end(kind)
    for p in plane:
        pl.semaphore_signal(r.ready, inc=1, device_id=(p, d), device_id_type=MESH)
    pl.semaphore_signal(r.ready, inc=1, device_id=(s, sib), device_id_type=MESH)

    def block_1(j, _):
        lane = lane_at(j)
        off = picked(r.h1, j) - r.norm[1, 0:1, lane]
        g, slope = gelu_pair(off * r.norm[1, 2:3, lane] + bias[1:2, lane])
        r.f2p[:, lane] = (r.mp[...] * g).astype(BF16).astype(F32)
        r.slope1[:, lane] = r.mp[...] * slope
        r.centred1[:, lane] = off * r.norm[1, 1:2, lane]
        return 0

    lax.fori_loop(0, n_lane, block_1, 0)
    grads = [r.w1, r.gp, r.g1]

    def pair_of(k):
        return z_at((2, 1, 3, 0)[k])

    def rs_a_copy(kind, k, core):
        return remote(
            shard(kind, grads[kind], 2 * pair_of(k) + core),
            r.ra[kind].at[k],
            r.ag_zs.at[kind, k],
            r.ag_zr.at[kind, k] if k < n_z - 1 else r.ag_or.at[kind],
            (s, sib),
        )

    def again(first, second, i):
        per = 6 * (n_z - 1)
        if i < 3 * per:
            return first.at[i // per, i % per]
        i, per = i - 3 * per, 4 * (n_z - 1)
        return second.at[i // per, i % per]

    def rs_b_copy(kind, k, way):
        o = 2 * pair_of(k) + c
        half = (0, 0, 1, 1, 0, 1)[way]
        to = plane[(0, 0, 1, 1, 1, 0)[way]]
        q = to if way in (0, 2, 4, 5) else plane[2]
        return remote(
            quarter(kind, grads[kind], o, q).at[:, halves[half]],
            r.rb[kind].at[k, way],
            again(r.ag_ps, r.ag_ss, (kind * n_z + k) * 6 + way),
            again(r.ag_pr, r.ag_sr, (kind * n_z + k) * 6 + way),
            (to, d),
        )

    def rs_c_copy(kind, k):
        return remote(
            r.qs[kind].at[k],
            r.rc[kind].at[k],
            r.rs_cs.at[kind, k],
            r.rs_cr.at[kind, k],
            (s, 2 * pair_of(k) + c),
        )

    def d_sem(kind, leg):
        return (kind * n_z + leg // 4) * 6 + leg % 4

    def rs_d_copy(kind, leg, q):
        rows = shard_rows[kind] // 4
        half = (0, 1, 1, 0, 0, 1)[leg]
        to = plane[(0, 1, 0, 1, 1, 0)[leg]]
        view = out_reduced[kind].at[pl.ds(al(q * rows, 16), rows), halves[half]]
        i = d_sem(kind, leg)
        return remote(
            view, view, again(r.ag_ps, r.ag_ss, i), again(r.ag_pr, r.ag_sr, i), (to, d)
        )

    def conv_weight(kind, xc, k):
        tile = 2 * shard_rows[kind] // 3
        per = 3 * width // tile

        for i in range(3):
            g = pair_of(k) * 3 + i
            a = g // per
            term = dot_tn(
                xc[pl.ds(al(a * cols, 16), pixels), pl.ds(al((g % per) * tile, lanes), tile)],
                r.dc[cols : 3 * cols, width : 2 * width],
            )
            grads[kind][pl.ds(al(g * tile, 16), tile), :] = term.astype(BF16)

    def rs_a(kind, k):
        rs_a_copy(kind, k, 1 - c).start()

    def rs_b(kind, k):
        rs_a_copy(kind, k, c).wait_recv()
        rows = shard_rows[kind]
        tile = rows // 4
        start = (2 * pair_of(k) + c) * rows

        def body(i, _):
            at = pl.ds(al(start + i * tile, 16), tile)
            grads[kind][at, :] = (
                grads[kind][at, :].astype(F32)
                + r.ra[kind][k, pl.ds(al(i * tile, 16), tile), :].astype(F32)
            ).astype(BF16)
            return 0

        lax.fori_loop(0, 4, body, 0)
        for way in range(4):
            rs_b_copy(kind, k, way).start()

    def quarter_at(kind, k, q):
        rows = shard_rows[kind]
        return pl.ds(al((2 * pair_of(k) + c) * rows + q * (rows // 4), 16), rows // 4)

    def rs_r(kind, k):
        for half in range(2):
            rs_b_copy(kind, k, 2 * half).wait_recv()
            rs_b_copy(kind, k, 2 * half + 1).wait_recv()
            at = quarter_at(kind, k, plane[1 - half])
            grads[kind][at, halves[half]] = (
                grads[kind][at, halves[half]].astype(F32)
                + r.rb[kind][k, 2 * half + 1].astype(F32)
            ).astype(BF16)
            rs_b_copy(kind, k, 4 + half).start()

    def rs_c(kind, k):
        at = quarter_at(kind, k, s)
        parts = []
        for half in range(2):
            rs_b_copy(kind, k, 4 + half).wait_recv()
            parts.append(
                grads[kind][at, halves[half]].astype(F32)
                + r.rb[kind][k, 2 * half].astype(F32)
                + r.rb[kind][k, 4 + half].astype(F32)
            )
        total = jnp.concatenate(parts, axis=1)
        if k < n_z - 1:
            r.qs[kind][k] = total.astype(BF16)
            rs_c_copy(kind, k).start()
        else:
            r.qf[kind][...] = total

    def rs_d(kind):
        total = r.qf[kind][...]
        for k in range(n_z - 1):
            rs_c_copy(kind, k).wait_recv()
            total = total + r.rc[kind][k].astype(F32)
        rows = shard_rows[kind] // 4
        out_reduced[kind][pl.ds(al(s * rows, 16), rows), :] = total.astype(BF16)
        for leg in range(6):
            rs_b_copy(kind, leg // 4, leg % 4).wait_send()
        for leg in range(2 if kind == 0 else 4):
            rs_d_copy(kind, leg, s).start()

    def rs_dr(kind):
        if kind == 0:
            for leg in range(2):
                rs_d_copy(kind, leg, s).wait_send()
            for leg in range(2, 4):
                rs_d_copy(kind, leg, s).start()
        for leg in range(2):
            rs_d_copy(kind, leg, plane[leg]).wait_recv()
            rs_d_copy(kind, 4 + leg, plane[leg]).start()

    def rs_e(kind):
        for leg in range(2):
            rs_d_copy(kind, 2 + leg, plane[leg]).wait_recv()
            rs_d_copy(kind, 4 + leg, plane[2]).wait_recv()

    def rs_end(kind):
        for k in range(n_z):
            rs_a_copy(kind, k, 1 - c).wait_send()
            for way in range((4, 2, 0, 0)[k], 6):
                rs_b_copy(kind, k, way).wait_send()
            if k < n_z - 1:
                rs_c_copy(kind, k).wait_send()
        for leg in range(2 if kind == 0 else 0, 4):
            rs_d_copy(kind, leg, s).wait_send()
        for leg in range(2):
            rs_d_copy(kind, 4 + leg, plane[leg]).wait_send()

    for item in loads[3:]:
        item.wait()
    r.df2[...] = jnp.zeros_like(r.df2)

    def pack_grads(l, t, grad_squeeze, grad_expand):
        r.fbuf[0, 0:width, :] = grad_squeeze
        for j in range(n_lane):
            r.fbuf[1, j * bottle : (j + 1) * bottle, :] = grad_expand[:, j * lanes : (j + 1) * lanes]

        def body(i, _):
            for j in range(n_lane):
                lane = slice(j * lanes, (j + 1) * lanes)
                r.gp[pl.ds(ex_row(i, l, t), e_rows), lane] = r.fbuf[
                    1, pl.ds(al(j * bottle + i * e_rows, 16), e_rows), :
                ].astype(BF16)
            for k in range(n_sub):
                r.gp[pl.ds(sq_row(i, l, t), e_rows), k * lanes : (k + 1) * lanes] = r.fbuf[
                    0, pl.ds(al(i * s_rows + k * e_rows, 16), e_rows), :
                ].astype(BF16)
            return 0

        lax.fori_loop(0, n_dp, body, 0)

    def kept(i):
        return pl.ds(al(i * windows, 16), windows)

    def gate_1(t, _):
        w_s = r.sq_w[1, :, task_lane(t)]
        w_e = r.ex_w[1, t]
        f2p = r.f2p[...]
        source = (f2p + r.t1[t].astype(F32)).astype(BF16)
        g, slope = gelu_pair(dot(source, w_s))
        excited = g.astype(BF16)
        value = jax.nn.sigmoid(dot(excited, w_e))
        field = mask_pick * f2p
        d_task = r.g1[cot_at + t * windows : cot_at + (t + 1) * windows, :].astype(F32)
        out_task[0, t] = (value * field).astype(BF16)
        d_expanded = (d_task * field * value * (1.0 - value)).astype(BF16)
        d_squeezed = (slope * dot_nt(d_expanded, w_e)).astype(BF16)
        d_source = dot_nt(d_squeezed, w_s)
        r.t1[t] = d_source.astype(BF16)
        r.df2[...] += d_source + mask_pick * d_task * value
        r.g1[kept(t), :] = source
        r.g1[kept(tasks + t), :] = d_expanded
        r.g1[kept(2 * tasks), task_lane(t)] = excited
        r.g1[kept(2 * tasks + 1), task_lane(t)] = d_squeezed
        return 0

    def gate_1_weight(t, _):
        pack_grads(
            1,
            t,
            dot_tn(r.g1[kept(t), :], r.g1[kept(2 * tasks + 1), task_lane(t)]),
            dot_tn(r.g1[kept(2 * tasks), task_lane(t)], r.g1[kept(tasks + t), :]),
        )
        return 0

    for t in range(tasks):
        gate_1(t, 0)
    def back_1(j, _):
        lane = lane_at(j)
        d_norm = r.slope1[:, lane] * r.df2[:, lane].astype(BF16).astype(F32)
        r.df2[:, lane] = d_norm
        ex_put(2, 0, j, jnp.sum(d_norm, 0, keepdims=True))
        ex_put(2, 1, j, jnp.sum(d_norm * r.centred1[:, lane], 0, keepdims=True))
        return 0

    lax.fori_loop(0, n_lane, back_1, 0)
    ex_start(2)

    r.df1[...] = jnp.zeros_like(r.df1)

    def gate_0_back(t, _):
        w_s = r.sq_w[0, :, task_lane(t)]
        w_e = r.ex_w[0, t]
        value = r.gate0[t]
        d_task = r.t1[t].astype(F32)
        excited = r.excited0[:, task_lane(t)]
        d_expanded = (d_task * (mask_pick * r.f1p[...]) * value * (1.0 - value)).astype(BF16)
        d_squeezed = (r.eslope0[:, task_lane(t)] * dot_nt(d_expanded, w_e)).astype(BF16)
        r.df1[...] += dot_nt(d_squeezed, w_s) + mask_pick * d_task * value
        pack_grads(0, t, dot_tn(r.f1b[...], d_squeezed), dot_tn(excited, d_expanded))
        return 0

    for t in range(tasks):
        gate_0_back(t, 0)
    for t in range(tasks):
        gate_1_weight(t, 0)

    r.sums[...] = jnp.zeros_like(r.sums)

    def back_terms(k, layer):
        sums = ex_finish(k)
        r.sums[2 * layer : 2 * layer + 1, :] = sums[0]
        r.sums[2 * layer + 1 : 2 * layer + 2, :] = sums[1]
        scale = gain[layer : layer + 1, :] * r.norm[layer, 3:4, :] * r.norm[layer, 1:2, :]
        r.norm[layer, 4:5, :] = scale * sums[0]
        r.norm[layer, 5:6, :] = scale * r.norm[layer, 1:2, :] * sums[1]

    pl.semaphore_wait(r.ready, 4)
    for k in range(n_z):
        rs_a(1, k)
    back_terms(2, 1)

    def hidden_grad_1(j, _):
        lane = lane_at(j)
        norm = r.norm
        for k in range(4):
            at = corner_rows(k)
            spread = jnp.where(pick_ref[...] == k, r.df2[:, lane] * norm[1, 2:3, lane], 0.0)
            value = spread - (
                norm[1, 4:5, lane] + (r.h1[j, at, :] - norm[1, 0:1, lane]) * norm[1, 5:6, lane]
            )
            slot = (k // 2) * cols + k % 2 + 2 * lax.broadcasted_iota(
                jnp.int32, (windows, lanes), 0
            )
            r.fbuf[j, at, :] = jnp.where(slot < count, value, 0.0)
        return 0

    lax.fori_loop(0, n_lane, hidden_grad_1, 0)
    shift_in(lambda j: r.fbuf[j, 0:cols, :], r.dc, 1)
    shift_in(lambda j: r.fbuf[j, cols : 2 * cols, :], r.dc, 2)
    halo_sent(1, r.xc1)
    halo_start(2, r.dc)

    for k in range(n_z):
        rs_b(1, k)
    for k in range(2):
        conv_weight(2, r.xc1, k)
        rs_a(2, k)
    conv_back(r.dc, r.w1, 0, 0)
    rs_b(2, 0)
    conv_back(r.dc, r.w1, 1, 0)
    for k in range(n_z):
        rs_r(1, k)
    rs_b(2, 1)
    halo_finish(2, r.dc)
    conv_back(r.dc, r.w1, 0, 1)
    conv_back(r.dc, r.w1, 1, 1)
    def back_0(j, _):
        lane = lane_at(j)
        norm = r.norm
        first = jnp.zeros((1, lanes), F32)
        second = jnp.zeros((1, lanes), F32)
        for k in range(4):
            at = corner_rows(k)
            d_field = r.fbuf[j, at, :].astype(BF16).astype(F32) + jnp.where(
                pick_ref[...] == k, r.df1[:, lane], 0.0
            )
            d_norm = r.slope0[j, at, :] * d_field.astype(BF16).astype(F32)
            r.fbuf[j, at, :] = d_norm
            centred = (r.h0[j, at, :] - norm[0, 0:1, lane]) * norm[0, 1:2, lane]
            first = first + jnp.sum(d_norm, 0, keepdims=True)
            second = second + jnp.sum(d_norm * centred, 0, keepdims=True)
        ex_put(3, 0, j, first)
        ex_put(3, 1, j, second)
        return 0

    lax.fori_loop(0, n_lane, back_0, 0)
    ex_start(3)
    conv_weight(2, r.xc1, 2)
    rs_a(2, 2)
    rs_r(2, 0)
    conv_weight(2, r.xc1, 3)
    rs_a(2, 3)
    rs_b(2, 2)
    halo_sent(2, r.dc)
    back_terms(3, 0)

    def sums_copy(p, q):
        return remote(
            r.sums,
            r.sums_in.at[q],
            r.sums_s.at[p],
            r.sums_r.at[p],
            (plane[p], d),
        )

    for p in range(3):
        sums_copy(p, s).start()
    r.sums_in[s] = r.sums[...]

    def hidden_grad_0(row):
        def value(j):
            lane = lane_at(j)
            norm = r.norm
            rows = slice(row * cols, (row + 1) * cols)
            out = r.fbuf[j, rows, :] * norm[0, 2:3, lane] - (
                norm[0, 4:5, lane] + (r.h0[j, rows, :] - norm[0, 0:1, lane]) * norm[0, 5:6, lane]
            )
            return jnp.where(valid_rows(row * cols, cols), out, 0.0)

        return value

    shift_in(hidden_grad_0(0), r.dc, 1)
    shift_in(hidden_grad_0(1), r.dc, 2)
    halo_start(3, r.dc)
    conv_weight(0, r.xc0, 0)
    rs_a(0, 0)
    rs_r(2, 1)
    rs_b(2, 3)
    for k in range(n_z):
        rs_c(1, k)
    conv_weight(0, r.xc0, 1)
    rs_a(0, 1)
    rs_c(2, 0)
    conv_weight(0, r.xc0, 2)
    rs_a(0, 2)
    rs_r(2, 2)
    rs_b(0, 0)
    conv_weight(0, r.xc0, 3)
    rs_a(0, 3)
    rs_c(2, 1)
    conv_back(r.dc, r.w0, 0, 0)
    rs_r(2, 3)
    rs_b(0, 1)
    conv_back(r.dc, r.w0, 1, 0)
    rs_c(2, 2)
    halo_finish(3, r.dc)
    conv_back(r.dc, r.w0, 0, 1)
    conv_back(r.dc, r.w0, 1, 1)
    def image_out(j, _):
        lane = lane_at(j)
        for i in range(4):
            rows = slice(i * quarter_rows, (i + 1) * quarter_rows)
            out_image[0, rows, lane] = jnp.where(
                valid_rows(i * quarter_rows, quarter_rows), r.fbuf[j, rows, :], 0.0
            ).astype(BF16)
        return 0

    lax.fori_loop(0, n_lane, image_out, 0)
    rs_r(0, 0)
    rs_b(0, 2)
    rs_c(2, 3)
    rs_r(0, 1)
    rs_c(0, 0)
    rs_b(0, 3)
    rs_r(0, 2)
    rs_c(0, 1)
    rs_r(0, 3)
    rs_c(0, 2)
    rs_d(1)
    rs_d(2)
    rs_c(0, 3)
    rs_dr(1)
    rs_dr(2)
    rs_d(0)
    for p in range(3):
        sums_copy(p, plane[p]).wait_recv()
    total = r.sums_in[0]
    for i in range(1, 4):
        total = total + r.sums_in[i]
    for l in range(2):
        out_bias[l : l + 1, :] = total[2 * l : 2 * l + 1, :]
        out_gain[l : l + 1, :] = total[2 * l + 1 : 2 * l + 2, :]
    for p in range(3):
        sums_copy(p, s).wait_send()
    ex_sent(2)
    ex_sent(3)
    halo_sent(3, r.dc)
    rs_dr(0)
    for kind in (1, 2, 0):
        rs_e(kind)
        rs_end(kind)


def finish_kernel(
    dims,
    task,
    image,
    reduced_0,
    reduced_1,
    reduced_2,
    gain,
    bias,
    out_task,
    out_image,
    out_conv,
    out_squeeze,
    out_expand,
    out_gain,
    out_bias,
    conv_wide,
    squeeze_wide,
    expand_wide,
    sem,
):
    lanes = 128
    e_rows = dims.bottle // dims.n_dp
    outs = []

    def store(src, dst):
        outs.append(pltpu.make_async_copy(src, dst, sem.at[len(outs)]))
        outs[-1].start()

    store(task, out_task)
    store(image, out_image)
    for layer, reduced in enumerate((reduced_0, reduced_2)):
        conv_wide[layer] = reduced[...].astype(F32)
        store(conv_wide.at[layer], out_conv.at[layer])
    for l in range(2):
        for t in range(dims.tasks):
            at = (l * dims.tasks + t) * e_rows
            expand_wide[l, t] = reduced_1[at : at + e_rows, :].astype(F32)
            at = at + 2 * dims.tasks * e_rows
            for k in range(dims.width // dims.n_dp // e_rows):
                squeeze_wide[l, t, k * e_rows : (k + 1) * e_rows, :] = reduced_1[
                    at : at + e_rows, k * lanes : (k + 1) * lanes
                ].astype(F32)
    store(squeeze_wide, out_squeeze)
    store(expand_wide, out_expand)
    out_gain[...] = gain[...]
    out_bias[...] = bias[...]
    for copy in outs:
        copy.wait()


def fused(images, counts, pool_index, conv_w, squeeze_w, expand_w, gain, bias, cotangent):
    n_dp = lax.axis_size("dp")
    micro, pixels, width = images.shape
    tasks, bottle = squeeze_w.shape[1], squeeze_w.shape[3]
    cols = 2 * pool_index.shape[2]
    windows = cols // 2
    conv_rows = conv_w.shape[1]
    gate_rows = 4 * tasks * expand_w.shape[2]
    shard_rows = (conv_rows, gate_rows, conv_rows)
    n_z = n_dp // 2
    vm = pltpu.VMEM
    dma = pltpu.SemaphoreType.DMA
    scratch = dict(
        load=dma((9 + 2 * (width // 128) + tasks,)),
        counts=pltpu.SMEM((micro,), jnp.int32),
        picks=vm(pool_index.shape, jnp.int32),
        gain=vm(gain.shape, F32),
        bias=vm(bias.shape, F32),
        sst=vm(squeeze_w.shape, F32),
        est=vm(expand_w.shape, F32),
        w0=vm((n_dp * conv_rows, width), BF16),
        gp=vm((n_dp * gate_rows, width), BF16),
        w1=vm((n_dp * conv_rows, width), BF16),
        g1=vm((n_dp * conv_rows, width), BF16),
        sq_w=vm((2, width, tasks * bottle), BF16),
        ex_w=vm((2, tasks, bottle, width), BF16),
        ag_zs=dma((3, 2 * (n_z - 1))),
        ag_zr=dma((3, n_z - 1)),
        ag_ps=dma((3, 6 * (n_z - 1))),
        ag_pr=dma((3, 6 * (n_z - 1))),
        ag_ss=dma((3, 4 * (n_z - 1))),
        ag_sr=dma((3, 4 * (n_z - 1))),
        ag_os=dma((3,)),
        ag_or=dma((3,)),
        mp=vm((windows, 128), F32),
        pick=vm((windows, 128), jnp.int32),
        halo=vm((2, 2, cols, width), BF16),
        halo_s=dma((2, 2)),
        halo_r=dma((2, 2)),
        ex_out=vm((5, 8, 128), F32),
        ex_in=vm((5, n_dp, 8, 128), F32),
        total=vm((8, width), F32),
        ex_s=dma((2, n_dp - 1)),
        ex_r=dma((2, n_dp - 1)),
        norm=vm((2, 8, width), F32),
        xc0=vm((4 * cols, 3 * width), BF16),
        xc1=vm((4 * cols, 3 * width), BF16),
        dc=vm((4 * cols, 3 * width), BF16),
        h0=vm((width // 128, pixels, 128), F32),
        h1=vm((width // 128, pixels, 128), F32),
        slope0=vm((width // 128, pixels, 128), F32),
        fbuf=vm((width // 128, pixels, 128), F32),
        f1p=vm((windows, width), F32),
        f1b=vm((windows, width), BF16),
        excited0=vm((windows, tasks * bottle), BF16),
        eslope0=vm((windows, tasks * bottle), F32),
        gate0=vm((tasks, windows, width), F32),
        t1=vm((tasks, windows, width), BF16),
        f2p=vm((windows, width), F32),
        slope1=vm((windows, width), F32),
        centred1=vm((windows, width), F32),
        df2=vm((windows, width), F32),
        df1=vm((windows, width), F32),
        sums=vm((8, width), F32),
        sums_in=vm((4, 8, width), F32),
        sums_s=dma((3,)),
        sums_r=dma((3,)),
        ready=pltpu.SemaphoreType.REGULAR,
        rs_cs=dma((3, n_z - 1)),
        rs_cr=dma((3, n_z - 1)),
    )
    quarters = [rows // 4 for rows in shard_rows]
    scratch.update(
        ra=[vm((n_z, rows, width), BF16) for rows in shard_rows],
        rb=[vm((n_z, 6, rows, width // 2), BF16) for rows in quarters],
        qs=[vm((n_z - 1, rows, width), BF16) for rows in quarters],
        qf=[vm((rows, width), F32) for rows in quarters],
        rc=[vm((n_z - 1, rows, width), BF16) for rows in quarters],
    )
    buffers, tree = jax.tree.flatten(scratch, is_leaf=lambda v: not isinstance(v, (dict, list)))
    dims = types.SimpleNamespace(
        tree=tree,
        n_dp=n_dp,
        cols=cols,
        pixels=pixels,
        width=width,
        tasks=tasks,
        bottle=bottle,
        shard_rows=shard_rows,
    )
    any_spec = pl.BlockSpec(memory_space=pl.ANY)
    vmem_spec = pl.BlockSpec(memory_space=pltpu.VMEM)
    results = pl.pallas_call(
        functools.partial(step_kernel, dims),
        out_shape=(
            vm((1, tasks, windows, width), BF16),
            vm((1, pixels, width), BF16),
            *[vm((rows, width), BF16) for rows in shard_rows],
            vm(gain.shape, F32),
            vm(bias.shape, F32),
        ),
        in_specs=[any_spec] * 9,
        out_specs=(vmem_spec,) * 7,
        scratch_shapes=tuple(buffers),
        compiler_params=pltpu.CompilerParams(
            collective_id=0, has_side_effects=True, vmem_limit_bytes=VMEM_BYTES
        ),
    )(counts.reshape(micro), pool_index, gain, bias, images, conv_w, squeeze_w, expand_w, cotangent)
    results = [pltpu.with_memory_space_constraint(v, pltpu.VMEM) for v in results]
    return pl.pallas_call(
        functools.partial(finish_kernel, dims),
        out_shape=(
            jax.ShapeDtypeStruct((1, tasks, windows, width), BF16),
            jax.ShapeDtypeStruct((1, pixels, width), BF16),
            jax.ShapeDtypeStruct(conv_w.shape, F32),
            jax.ShapeDtypeStruct(squeeze_w.shape, F32),
            jax.ShapeDtypeStruct(expand_w.shape, F32),
            jax.ShapeDtypeStruct(gain.shape, F32),
            jax.ShapeDtypeStruct(bias.shape, F32),
        ),
        in_specs=[vmem_spec] * 7,
        out_specs=(any_spec,) * 5 + (vmem_spec,) * 2,
        scratch_shapes=(
            vm(conv_w.shape, F32),
            vm(squeeze_w.shape, F32),
            vm(expand_w.shape, F32),
            dma((6,)),
        ),
        compiler_params=pltpu.CompilerParams(vmem_limit_bytes=16 * 1024 * 1024),
    )(*results)


def fits_kernel(mesh, args):
    images, counts, pool_index, conv_w, squeeze_w, expand_w = args[:6]
    sections, n_dp = mesh.shape["section"], mesh.shape["dp"]
    conv_rows = conv_w.shape[1] // n_dp
    e_rows = expand_w.shape[2] // n_dp
    return (
        sections == 4
        and images.shape[0] == sections
        and n_dp % 2 == 0
        and pool_index.shape[1] == n_dp
        and conv_rows % 64 == 0
        and e_rows == 16
        and squeeze_w.shape[2] // n_dp == 4 * e_rows
        and squeeze_w.shape[3] == 128
        and images.shape[2] == 4 * 128
    )


def solution(mesh):
    placed = (
        P(None, "dp", None),
        P(None, "dp"),
        P(None, "dp", None),
        P(None, "dp", None),
        P(None, None, "dp", None),
        P(None, None, "dp", None),
        P(),
        P(),
        P(None, None, "dp", None),
    )
    def run(*args):
        return mapped(fused if fits_kernel(mesh, args) else on_device)(*args)

    def mapped(body):
        return jax.shard_map(
        body,
        mesh=mesh,
        in_specs=placed,
        out_specs=(
            P("section", None, "dp", None),
            P("section", "dp", None),
            P(None, "dp", None),
            P(None, None, "dp", None),
            P(None, None, "dp", None),
            P(),
            P(),
        ),
        check_vma=False,
    )

    return run
```

```python
import functools
import types

import jax
import jax.numpy as jnp
from jax import lax
from jax.experimental import pallas as pl
from jax.experimental.pallas import tpu as pltpu
from jax.sharding import PartitionSpec as P

EPS = 1e-05
BF16 = jnp.bfloat16
F32 = jnp.float32
VMEM_BYTES = 58 * 1024 * 1024


def gelu_back(point, upstream):
    return jax.vjp(jax.nn.gelu, point)[1](upstream)[0]


def with_halo(value, axis):
    size = lax.axis_size(axis)
    up = [(i, i + 1) for i in range(size - 1)]
    down = [(j, i) for i, j in up]
    before = lax.ppermute(value[-1:], axis, up)
    after = lax.ppermute(value[:1], axis, down)
    return jnp.concatenate([before, value, after], axis=0)


def conv(padded, taps):
    out = lax.conv_general_dilated(
        padded[None],
        taps,
        (1, 1),
        ((0, 0), (1, 1)),
        dimension_numbers=("NHWC", "HWIO", "NHWC"),
        preferred_element_type=F32,
    )
    return out.reshape(-1, out.shape[-1])


def conv_input_grad(d_padded, taps):
    out = lax.conv_general_dilated(
        d_padded[None],
        taps[::-1, ::-1],
        (1, 1),
        ((0, 0), (1, 1)),
        dimension_numbers=("NHWC", "HWOI", "NHWC"),
        preferred_element_type=F32,
    )
    return out.reshape(-1, out.shape[-1])


def conv_weight_grad(padded, d_hidden):
    out = lax.conv_general_dilated(
        padded[None],
        d_hidden[None],
        (1, 1),
        ((0, 0), (1, 1)),
        dimension_numbers=("CHWN", "IHWO", "HWNC"),
        preferred_element_type=F32,
    )
    return out.reshape(-1, out.shape[-1])


def gate_forward(source, w_squeeze, w_expand):
    squeezed = jnp.einsum("tpc,tcb->tpb", source, w_squeeze, preferred_element_type=F32)
    excited = jax.nn.gelu(squeezed).astype(BF16)
    expanded = jnp.einsum("tpb,tbc->tpc", excited, w_expand, preferred_element_type=F32)
    return squeezed, excited, jax.nn.sigmoid(expanded)


def gate_backward(d_task, field, source, squeezed, excited, gate_val, w_squeeze, w_expand):
    d_expanded = (d_task * field[None] * gate_val * (1.0 - gate_val)).astype(BF16)
    d_excited = jnp.einsum("tpc,tbc->tpb", d_expanded, w_expand, preferred_element_type=F32)
    d_squeezed = gelu_back(squeezed, d_excited).astype(BF16)
    d_source = jnp.einsum("tpb,tcb->tpc", d_squeezed, w_squeeze, preferred_element_type=F32)
    grad_squeeze = jnp.einsum("tpc,tpb->tcb", source, d_squeezed, preferred_element_type=F32)
    grad_expand = jnp.einsum("tpb,tpc->tbc", excited, d_expanded, preferred_element_type=F32)
    return d_source, grad_squeeze, grad_expand


def pool_pick(field, pick):
    tasks, _, width = field.shape
    half_rows, half_columns = pick.shape
    windows = field.reshape(tasks, half_rows, 2, half_columns, 2, width)
    picked = jnp.zeros((tasks, half_rows, half_columns, width), F32)
    for corner in range(4):
        hit = (pick == corner)[None, :, :, None]
        picked = picked + jnp.where(hit, windows[:, :, corner // 2, :, corner % 2, :], 0.0)
    return picked.reshape(tasks, half_rows * half_columns, width)


def pool_spread(d_pooled, pick):
    tasks, _, width = d_pooled.shape
    half_rows, half_columns = pick.shape
    grid = d_pooled.reshape(tasks, half_rows, half_columns, width)
    rows = [
        jnp.stack(
            [jnp.where((pick == 2 * dy + dx)[None, :, :, None], grid, 0.0) for dx in range(2)], 3
        )
        for dy in range(2)
    ]
    return jnp.stack(rows, 2).reshape(tasks, half_rows * 2 * half_columns * 2, width)


def on_device(images, counts, pool_index, conv_w, squeeze_w, expand_w, gain, bias, cotangent):
    sections = lax.axis_size("section")
    here = lax.axis_index("section")
    micro, pixels, width = images.shape
    layers = conv_w.shape[0]
    tasks = squeeze_w.shape[1]
    rows = 2 * pool_index.shape[1]
    columns = 2 * pool_index.shape[2]
    share = micro // sections

    def own(value):
        return lax.dynamic_slice_in_dim(value, here * share, share, 0)

    images, counts, pool_index, cotangent = (
        own(images),
        own(counts),
        own(pool_index),
        own(cotangent),
    )

    def gather(value, axis):
        return lax.all_gather(value.astype(BF16), "dp", axis=axis, tiled=True)

    taps = [gather(conv_w[l], 0).reshape(3, 3, width, width) for l in range(layers)]
    w_squeeze = [gather(squeeze_w[l], 1) for l in range(layers)]
    w_expand = [gather(expand_w[l], 1) for l in range(layers)]
    slots = jnp.arange(pixels, dtype=jnp.int32)[:, None]

    def block_forward(field, mask, total, layer):
        padded = with_halo(field.reshape(rows, columns, width), "dp")
        hidden = conv(padded, taps[layer])
        sums = lax.psum(
            jnp.stack([jnp.sum(mask * hidden, 0), jnp.sum(mask * hidden * hidden, 0)]), "dp"
        )
        centre = sums[0] / total
        inverse = lax.rsqrt(sums[1] / total - centre * centre + EPS)
        normed = gain[layer] * (hidden - centre) * inverse + bias[layer]
        out = (mask * jax.nn.gelu(normed)).astype(BF16)
        return out, (padded, hidden, centre, inverse)

    def block_backward(d_out, kept, mask, total, layer):
        padded, hidden, centre, inverse = kept
        centred = (hidden - centre) * inverse
        normed = gain[layer] * (hidden - centre) * inverse + bias[layer]
        d_norm = gelu_back(normed, mask * d_out)
        gain_sum = jnp.sum(d_norm * centred, 0)
        bias_sum = jnp.sum(d_norm, 0)
        sums = gain[layer] * lax.psum(jnp.stack([bias_sum, gain_sum]), "dp")
        d_hidden = (
            mask * inverse * (gain[layer] * d_norm - sums[0] / total - centred * sums[1] / total)
        ).astype(BF16)
        d_hidden = d_hidden.reshape(rows, columns, width)
        d_x = conv_input_grad(with_halo(d_hidden, "dp"), taps[layer])
        return d_x, conv_weight_grad(padded, d_hidden), gain_sum, bias_sum

    outs, image_grads = [], []
    grads = None
    totals = lax.psum(counts[:, 0], "dp").astype(F32)
    for m in range(share):
        total = totals[m]
        mask = (slots < counts[m, 0]).astype(F32)
        first_in = jnp.where(slots < counts[m, 0], images[m], jnp.zeros((), BF16))
        f1, kept_0 = block_forward(first_in, mask, total, 0)
        f1_f = f1.astype(F32)
        source_0 = jnp.broadcast_to(f1[None], (tasks, pixels, width))
        squeezed_0, excited_0, gate_0 = gate_forward(source_0, w_squeeze[0], w_expand[0])
        t1 = (mask[None] * gate_0 * f1_f[None]).astype(BF16)
        f2, kept_1 = block_forward(f1, mask, total, 1)
        f2_f = f2.astype(F32)
        source_1 = (f2_f[None] + t1.astype(F32)).astype(BF16)
        squeezed_1, excited_1, gate_1 = gate_forward(source_1, w_squeeze[1], w_expand[1])
        outs.append(pool_pick(mask[None] * gate_1 * f2_f[None], pool_index[m]).astype(BF16))

        d_task = pool_spread(cotangent[m].astype(F32), pool_index[m])
        d_source, gs_1, ge_1 = gate_backward(
            d_task, mask * f2_f, source_1, squeezed_1, excited_1, gate_1, w_squeeze[1], w_expand[1]
        )
        d_f2 = (jnp.sum(d_source, 0) + mask * jnp.sum(d_task * gate_1, 0)).astype(BF16)
        d_t1 = d_source.astype(BF16).astype(F32)
        d_x1, gc_1, gain_1, bias_1 = block_backward(d_f2.astype(F32), kept_1, mask, total, 1)
        d_source, gs_0, ge_0 = gate_backward(
            d_t1, mask * f1_f, source_0, squeezed_0, excited_0, gate_0, w_squeeze[0], w_expand[0]
        )
        d_f1 = (
            d_x1.astype(BF16).astype(F32)
            + jnp.sum(d_source, 0)
            + mask * jnp.sum(d_t1 * gate_0, 0)
        ).astype(BF16)
        d_x0, gc_0, gain_0, bias_0 = block_backward(d_f1.astype(F32), kept_0, mask, total, 0)
        image_grads.append((mask * d_x0).astype(BF16))
        here_grads = [
            [gc_0, gc_1],
            [gs_0, gs_1],
            [ge_0, ge_1],
            jnp.stack([gain_0, gain_1]),
            jnp.stack([bias_0, bias_1]),
        ]
        grads = here_grads if grads is None else jax.tree.map(jnp.add, grads, here_grads)

    def reduced(value, axis):
        part = lax.psum_scatter(value, "dp", scatter_dimension=axis, tiled=True)
        return lax.psum(part.astype(BF16), "section").astype(F32)

    conv_grad = jnp.stack([reduced(g, 0) for g in grads[0]])
    squeeze_grad = jnp.stack([reduced(g, 1) for g in grads[1]])
    expand_grad = jnp.stack([reduced(g, 1) for g in grads[2]])
    gain_grad, bias_grad = lax.psum((grads[3], grads[4]), ("section", "dp"))
    return (
        jnp.stack(outs),
        jnp.stack(image_grads),
        conv_grad,
        squeeze_grad,
        expand_grad,
        gain_grad,
        bias_grad,
    )


GELU_C = 0.7978845608028654
GELU_K = 0.044715
MESH = pl.DeviceIdType.MESH


def gelu_tanh(x):
    return jnp.tanh(GELU_C * x * (1.0 + GELU_K * (x * x)))


def gelu_slope(x, t):
    inner = GELU_C * (1.0 + 3.0 * GELU_K * (x * x))
    return 0.5 * (1.0 + t) + 0.5 * x * (1.0 - t * t) * inner


def gelu_pair(x):
    t = gelu_tanh(x)
    return 0.5 * x * (1.0 + t), gelu_slope(x, t)


def dot(a, b):
    return jnp.dot(a, b, preferred_element_type=F32)


def dot_nt(a, b):
    return lax.dot_general(a, b, (((1,), (1,)), ((), ())), preferred_element_type=F32)


def dot_tn(a, b):
    return lax.dot_general(a, b, (((0,), (0,)), ((), ())), preferred_element_type=F32)


def step_kernel(
    dims,
    counts_in,
    picks_in,
    gain_in,
    bias_in,
    images,
    conv_w,
    squeeze_w,
    expand_w,
    cotangent,
    out_task,
    out_image,
    out_reduced_0,
    out_reduced_1,
    out_reduced_2,
    out_gain,
    out_bias,
    *scratch,
):
    out_reduced = (out_reduced_0, out_reduced_1, out_reduced_2)
    r = types.SimpleNamespace(**jax.tree.unflatten(dims.tree, scratch))
    n_dp, cols, pixels, width, tasks, bottle = (
        dims.n_dp,
        dims.cols,
        dims.pixels,
        dims.width,
        dims.tasks,
        dims.bottle,
    )
    n_z = n_dp // 2
    windows = cols // 2
    lanes = 128
    n_lane = width // lanes
    shard_rows = dims.shard_rows
    s = lax.axis_index("section")
    d = lax.axis_index("dp")
    z, c = d // 2, d % 2
    sib = 2 * z + 1 - c
    plane = [s + 1 - 2 * (s % 2), (s + 2) % 4, 3 - s]

    def rem(a, b):
        return lax.rem(a, b)

    def z_at(step):
        return rem(z + step, n_z)

    def remote(src, dst, send, recv, device):
        return pltpu.make_async_remote_copy(
            src_ref=src,
            dst_ref=dst,
            send_sem=send,
            recv_sem=recv,
            device_id=device,
            device_id_type=MESH,
        )

    def al(v, m):
        return pl.multiple_of(v, m)

    barrier = pltpu.get_barrier_semaphore()
    for step in range(1, n_dp):
        pl.semaphore_signal(
            barrier, inc=1, device_id=(s, rem(d + step, n_dp)), device_id_type=MESH
        )
    for p in plane:
        pl.semaphore_signal(barrier, inc=1, device_id=(p, d), device_id_type=MESH)

    def load(i, src, dst):
        return pltpu.make_async_copy(src, dst, r.load.at[i])

    staging = [r.h1, r.slope0]
    conv_rows = shard_rows[0]

    def conv_load(layer, j):
        lane = slice(j * lanes, (j + 1) * lanes)
        return load(
            5 + layer * n_lane + j,
            conv_w.at[layer, :, lane],
            staging[layer].at[j, 0:conv_rows],
        )

    cot_at = (2 * tasks + 2) * windows
    image_at = cot_at + tasks * windows
    loads = [
        load(1, squeeze_w, r.sst),
        load(2, expand_w, r.est),
        load(3, images.at[s], r.g1.at[image_at : image_at + pixels]),
        *[
            load(
                5 + 2 * n_lane + t,
                cotangent.at[s, t],
                r.g1.at[cot_at + t * windows : cot_at + (t + 1) * windows],
            )
            for t in range(tasks)
        ],
    ]
    small_at = 5 + 2 * n_lane + tasks
    picks, gain, bias = r.picks, r.gain, r.bias
    counts = r.counts
    count_load = load(small_at + 3, counts_in, counts)
    small = [
        load(small_at, picks_in, picks),
        load(small_at + 1, gain_in, gain),
        load(small_at + 2, bias_in, bias),
    ]
    for j in range(n_lane):
        conv_load(0, j).start()
    count_load.start()
    loads[2].start()
    for j in range(n_lane):
        conv_load(1, j).start()
    for item in small:
        item.start()
    for i in (0, 1, *range(3, 3 + tasks)):
        loads[i].start()

    full = [r.w0, r.gp, r.w1]

    def shard(kind, buf, which):
        rows = shard_rows[kind]
        return buf.at[pl.ds(al(which * rows, 16), rows)]

    def quarter(kind, buf, which, q):
        rows = shard_rows[kind]
        return buf.at[pl.ds(al(which * rows + q * (rows // 4), 16), rows // 4)]

    def z_of(way, hop):
        return z_at(n_z - hop if way == 0 else hop)

    def has(way, hop):
        return z >= hop if way == 0 else z < n_z - hop

    def slot_of(way, hop):
        return n_z - 1 - hop if way == 0 else hop - 1

    def ag_z_copy(kind, way, hop, owner):
        view = quarter(kind, full[kind], 2 * owner + c, s)
        return remote(
            view,
            view,
            r.ag_zs.at[kind, (hop - 1) * 2 + way],
            r.ag_zr.at[kind, slot_of(way, hop)],
            (s, 2 * z_at(1 if way == 0 else n_z - 1) + c),
        )

    def gate_z_copy(step, owner):
        view = quarter(1, full[1], 2 * owner + c, s)
        return remote(
            view,
            view,
            r.ag_zs.at[1, step - 1],
            r.ag_zr.at[1, step - 1],
            (s, 2 * z_at(step) + c),
        )

    def ag_pass(kind, way, hop, do):
        here_has = has(way, hop - 1) if hop > 1 else True
        there = z < n_z - 1 if way == 0 else z > 0
        owner = z_of(way, hop - 1)

        @pl.when(jnp.logical_and(here_has, there))
        def _():
            do(ag_z_copy(kind, way, hop, owner))

    halves = [slice(0, width // 2), slice(width // 2, width)]

    def ag_p_copy(kind, slot, owner, leg, q):
        half = (0, 1, 0, 1, 0, 1)[leg]
        view = quarter(kind, full[kind], 2 * owner + c, q).at[:, halves[half]]
        to = plane[(0, 0, 1, 1, 1, 0)[leg]]
        i = slot * 6 + leg
        return remote(view, view, r.ag_ps.at[kind, i], r.ag_pr.at[kind, i], (to, d))

    def ag_own_copy(kind, core):
        view = shard(kind, full[kind], 2 * z + core)
        return remote(view, view, r.ag_os.at[kind], r.ag_or.at[kind], (s, sib))

    def ag_s_copy(kind, slot, owner, i, core):
        view = quarter(kind, full[kind], 2 * owner + core, others[i])
        i = slot * 4 + i
        return remote(view, view, r.ag_ss.at[kind, i], r.ag_sr.at[kind, i], (s, sib))

    others = [s] + plane

    def both(condition):
        return (condition, condition)

    def ag_start(kind):
        if kind == 1:
            for step in range(1, n_z):
                gate_z_copy(step, z).start()
        else:
            for way in range(2):
                ag_pass(kind, way, 1, lambda copy: copy.start())
        ag_own_copy(kind, c).start()

    at_end = jnp.logical_or(z == 0, z == n_z - 1)

    in_middle = jnp.logical_not(at_end)
    from_end = (z == 1, z == n_z - 2)
    not_from_end = (z != 1, z != n_z - 2)

    def for_hop(kind, hop, do, also=(True, True)):
        if kind == 1:
            do(hop - 1, z_at(n_z - hop), None)
            return
        for way in range(2):

            @pl.when(jnp.logical_and(has(way, hop), also[way]))
            def _():
                do(slot_of(way, hop), z_of(way, hop), way)

    def ag_z(kind, hop, also=(True, True), legs=True):
        def do(slot, owner, way):
            if kind == 1:
                gate_z_copy(hop, owner).wait_recv()
            else:
                ag_z_copy(kind, way, hop, owner).wait_recv()
                if hop < n_z - 1:
                    ag_pass(kind, way, hop + 1, lambda copy: copy.start())
            if legs:
                for leg in (0, 3):
                    ag_p_copy(kind, slot, owner, leg, s).start()

        for_hop(kind, hop, do, also)

    def ag_l(kind, hop, also):
        def do(slot, owner, way):
            for leg in (0, 3):
                ag_p_copy(kind, slot, owner, leg, s).start()

        for_hop(kind, hop, do, also)

    def ag_y(kind, hop, also=(True, True)):
        def do(slot, owner, way):
            for leg in (0, 3):
                ag_p_copy(kind, slot, owner, leg, s).wait_send()
            for leg in (1, 2):
                ag_p_copy(kind, slot, owner, leg, s).start()
            ag_s_copy(kind, slot, owner, 0, c).start()

        for_hop(kind, hop, do, also)

    def ag_r(kind, hop, also=(True, True)):
        def do(slot, owner, way):
            for h in range(2):
                ag_p_copy(kind, slot, owner, 3 * h, plane[h]).wait_recv()
                ag_p_copy(kind, slot, owner, 4 + h, plane[h]).start()

        for_hop(kind, hop, do, also)

    def ag_q(kind, hop):
        def do(slot, owner, way):
            for axis in range(2):
                ag_p_copy(kind, slot, owner, 1 + axis, plane[axis]).wait_recv()
                ag_s_copy(kind, slot, owner, 1 + axis, c).start()

        for_hop(kind, hop, do)

    def ag_p(kind, hop):
        def do(slot, owner, way):
            for h in range(2):
                ag_p_copy(kind, slot, owner, 4 + h, plane[2]).wait_recv()
            ag_s_copy(kind, slot, owner, 3, c).start()

        for_hop(kind, hop, do)

    def ag_sib(kind):
        ag_own_copy(kind, 1 - c).wait_recv()
        for hop in range(1, n_z):

            def do(slot, owner, way):
                for i in range(4):
                    ag_s_copy(kind, slot, owner, i, 1 - c).wait_recv()

            for_hop(kind, hop, do)

    def ag_end(kind):
        ag_own_copy(kind, c).wait_send()
        for hop in range(1, n_z):

            def do(slot, owner, way):
                for leg in (1, 2):
                    ag_p_copy(kind, slot, owner, leg, s).wait_send()
                for h in range(2):
                    ag_p_copy(kind, slot, owner, 4 + h, plane[h]).wait_send()
                for i in range(4):
                    ag_s_copy(kind, slot, owner, i, c).wait_send()

            if kind == 1:
                gate_z_copy(hop, z).wait_send()
            else:
                for way in range(2):
                    ag_pass(kind, way, hop, lambda copy: copy.wait_send())
            for_hop(kind, hop, do)

    def cast_conv(layer, buf):
        for j in range(n_lane):
            conv_load(layer, j).wait()

        def body(j, _):
            buf[pl.ds(al(d * conv_rows, 16), conv_rows), pl.ds(al(j * lanes, lanes), lanes)] = (
                staging[layer][j, 0:conv_rows, :].astype(BF16)
            )
            return 0

        lax.fori_loop(0, n_lane, body, 0)

    g_rows = shard_rows[1]
    e_rows = n_ex = bottle // n_dp
    s_rows = width // n_dp
    n_sub = s_rows // e_rows

    def ex_row(which, l, t):
        return al(which * g_rows + (l * tasks + t) * e_rows, 16)

    def sq_row(which, l, t):
        return al(which * g_rows + (2 * tasks + l * tasks + t) * e_rows, 16)

    cast_conv(0, r.w0)
    pl.semaphore_wait(barrier, n_dp - 1 + 3)
    ag_start(0)
    count_load.wait()
    count = counts[s]
    pick_ref = r.pick

    def lane_at(j, base=0):
        return pl.ds(al(base + j * lanes, lanes), lanes)

    def valid_rows(start, rows):
        return (lax.broadcasted_iota(jnp.int32, (rows, lanes), 0) + start) < count

    def shift_in(value_of, buf, block):
        def body(j, _):
            v = value_of(j)
            at = lax.broadcasted_iota(jnp.int32, (cols, lanes), 0)
            before = jnp.where(at == 0, 0.0, pltpu.roll(v, 1, 0))
            after = jnp.where(at == cols - 1, 0.0, pltpu.roll(v, cols - 1, 0))
            rows = pl.ds(block * cols, cols)
            buf[rows, lane_at(j)] = before.astype(BF16)
            buf[rows, lane_at(j, width)] = v.astype(BF16)
            buf[rows, lane_at(j, 2 * width)] = after.astype(BF16)
            return 0

        lax.fori_loop(0, n_lane, body, 0)

    @pl.when(d == 0)
    def _():
        r.halo[:, 0] = jnp.zeros_like(r.halo[:, 0])

    @pl.when(d == n_dp - 1)
    def _():
        r.halo[:, 1] = jnp.zeros_like(r.halo[:, 1])

    def halo_down(e, buf):
        return remote(
            buf.at[2 * cols : 3 * cols, width : 2 * width],
            r.halo.at[e % 2, 0],
            r.halo_s.at[e % 2, 0],
            r.halo_r.at[e % 2, 0],
            (s, rem(d + 1, n_dp)),
        )

    def halo_up(e, buf):
        return remote(
            buf.at[cols : 2 * cols, width : 2 * width],
            r.halo.at[e % 2, 1],
            r.halo_s.at[e % 2, 1],
            r.halo_r.at[e % 2, 1],
            (s, rem(d + n_dp - 1, n_dp)),
        )

    def halo_start(e, buf):
        @pl.when(d < n_dp - 1)
        def _():
            halo_down(e, buf).start()

        @pl.when(d > 0)
        def _():
            halo_up(e, buf).start()

    def halo_finish(e, buf):
        @pl.when(d > 0)
        def _():
            halo_down(e, buf).wait_recv()

        @pl.when(d < n_dp - 1)
        def _():
            halo_up(e, buf).wait_recv()

        shift_in(lambda j: r.halo[e % 2, 0, :, lane_at(j)].astype(F32), buf, 0)
        shift_in(lambda j: r.halo[e % 2, 1, :, lane_at(j)].astype(F32), buf, 3)

    def halo_sent(e, buf):
        @pl.when(d < n_dp - 1)
        def _():
            halo_down(e, buf).wait_send()

        @pl.when(d > 0)
        def _():
            halo_up(e, buf).wait_send()

    def ex_copy(k, step, owner):
        turn = (k + 1) % 5 % 2
        return remote(
            r.ex_out.at[k],
            r.ex_in.at[k, owner],
            r.ex_s.at[turn, step - 1],
            r.ex_r.at[turn, step - 1],
            (s, rem(d + step, n_dp)),
        )

    def ex_sent(k):
        for step in range(1, n_dp):
            ex_copy(k, step, d).wait_send()

    def ex_start(k):
        if k in (1, 2, 3):
            ex_sent((4, 0, 1)[k - 1])
        for step in range(1, n_dp):
            ex_copy(k, step, d).start()
        r.ex_in[k, d] = r.ex_out[k]

    def ex_finish(k):
        for step in range(1, n_dp):
            ex_copy(k, step, rem(d + n_dp - step, n_dp)).wait_recv()
        total = r.ex_in[k, 0]
        for i in range(1, n_dp):
            total = total + r.ex_in[k, i]
        return [
            jnp.concatenate([total[i * n_lane + j : i * n_lane + j + 1] for j in range(n_lane)], 1)
            for i in range(2)
        ]

    def ex_put(k, i, j, value):
        r.ex_out[k, pl.ds(i * n_lane + j, 1), :] = value

    def conv_forward(xc, w, h, row, part, k=None):
        span = 3 * width
        acc = None
        for a in range(3):
            block = a + row
            if (block in (0, 3)) != (part == 1):
                continue
            term = dot(xc[block * cols : (block + 1) * cols, :], w[a * span : (a + 1) * span, :])
            acc = term if acc is None else acc + term
        add_to(h, row, part, acc, k)

    def add_to(out, row, part, acc, k=None):
        for j in range(n_lane):
            at = (j, slice(row * cols, (row + 1) * cols), slice(None))
            piece = acc[:, j * lanes : (j + 1) * lanes]
            if part == 1:
                piece = out[at] + piece
            out[at] = piece
            if k is not None:
                kept = jnp.where(valid_rows(row * cols, cols), piece, 0.0)
                for i, value in enumerate((kept, kept * piece)):
                    value = jnp.sum(value, 0, keepdims=True)
                    if row == 1:
                        value = value + r.ex_out[k, i * n_lane + j : i * n_lane + j + 1, :]
                    ex_put(k, i, j, value)

    def conv_back(dc, w, row, part):
        acc = None
        for a in range(3):
            block = 2 - a + row
            if (block in (0, 3)) != (part == 1):
                continue
            for b in range(3):
                term = dot_nt(
                    dc[block * cols : (block + 1) * cols, (2 - b) * width : (3 - b) * width],
                    w[(3 * a + b) * width : (3 * a + b + 1) * width, :],
                )
                acc = term if acc is None else acc + term
        add_to(r.fbuf, row, part, acc)

    quarter_rows = pixels // 4

    def norm_of(sums, layer):
        total = r.total[0:1, :]
        centre = sums[0] / total
        inverse = lax.rsqrt(sums[1] / total - centre * centre + EPS)
        r.norm[layer, 0:1, :] = centre
        r.norm[layer, 1:2, :] = inverse
        r.norm[layer, 2:3, :] = gain[layer : layer + 1, :] * inverse
        r.norm[layer, 3:4, :] = 1.0 / total

    def corner_rows(k):
        return pl.ds((k // 2) * cols + k % 2, windows, stride=2)

    def picked(ref, j):
        out = None
        which = pick_ref[...]
        for k in range(4):
            part = jnp.where(which == k, ref[j, corner_rows(k), :], 0.0)
            out = part if out is None else out + part
        return out

    loads[2].wait()

    def image_row(i):
        def value(j):
            v = r.g1[image_at + i * cols : image_at + (i + 1) * cols, lane_at(j)].astype(F32)
            return jnp.where(valid_rows(i * cols, cols), v, 0.0)

        return value

    shift_in(image_row(0), r.xc0, 1)
    shift_in(image_row(1), r.xc0, 2)
    r.ex_out[4] = jnp.broadcast_to(count.astype(F32), (8, lanes))
    ex_start(4)
    loads[0].wait()
    loads[1].wait()
    for l in range(2):
        for t in range(tasks):
            r.gp[pl.ds(ex_row(d, l, t), e_rows), :] = r.est[l, t].astype(BF16)
            for k in range(n_sub):
                r.gp[pl.ds(sq_row(d, l, t), e_rows), k * lanes : (k + 1) * lanes] = r.sst[
                    l, t, k * e_rows : (k + 1) * e_rows, :
                ].astype(BF16)
    cast_conv(1, r.w1)
    ag_z(0, 1)

    @pl.when(at_end)
    def _():
        ag_start(2)

    ag_y(0, 1)
    for item in small:
        item.wait()
    wide = 2 * lanes
    pick_row = jnp.concatenate(
        [picks[s].astype(F32), jnp.zeros((1, wide - windows), F32)], axis=1
    )
    pick_tile = jnp.broadcast_to(pick_row, (lanes, wide)).T[:windows, :].astype(jnp.int32)
    pick_ref[...] = pick_tile
    slot_pick = (
        (pick_tile // 2) * cols
        + 2 * lax.broadcasted_iota(jnp.int32, (windows, lanes), 0)
        + pick_tile % 2
    )
    r.mp[...] = jnp.where(slot_pick < count, 1.0, 0.0).astype(F32)
    ag_z(0, 2)
    ag_z(2, 1, from_end, legs=False)
    ag_r(0, 1)
    ag_y(0, 2)
    ag_z(0, 3)

    @pl.when(in_middle)
    def _():
        ag_start(2)

    halo_start(0, r.xc0)
    ag_q(0, 1)
    ag_z(2, 2, both(in_middle), legs=False)
    ag_y(0, 3)
    ag_r(0, 2)
    ag_p(0, 1)
    ag_r(0, 3)
    ag_q(0, 2)
    ag_l(2, 1, from_end)
    ag_z(2, 1, not_from_end)
    ag_l(2, 2, both(in_middle))
    r.total[...] = jnp.concatenate([ex_finish(4)[0]] * 8, axis=0)
    ag_p(0, 2)
    ag_y(2, 1)
    ag_q(0, 3)
    ag_p(0, 3)
    ag_sib(0)
    ag_z(2, 3)
    conv_forward(r.xc0, r.w0, r.h0, 0, 0)
    conv_forward(r.xc0, r.w0, r.h0, 1, 0)
    ag_z(2, 2, both(at_end))
    ag_r(2, 1)
    halo_finish(0, r.xc0)
    ag_y(2, 2, both(in_middle))
    ag_y(2, 3)
    conv_forward(r.xc0, r.w0, r.h0, 0, 1, 0)
    conv_forward(r.xc0, r.w0, r.h0, 1, 1, 0)
    ex_start(0)
    halo_sent(0, r.xc0)
    ag_start(1)
    ag_y(2, 2, both(at_end))
    ag_q(2, 1)
    ag_r(2, 2, both(in_middle))
    ag_r(2, 3)
    norm_of(ex_finish(0), 0)

    def block_0(j, _):
        lane = lane_at(j)
        for i in range(4):
            rows = slice(i * quarter_rows, (i + 1) * quarter_rows)
            normed = (r.h0[j, rows, :] - r.norm[0, 0:1, lane]) * r.norm[
                0, 2:3, lane
            ] + bias[0:1, lane]
            t = gelu_tanh(normed)
            ok = valid_rows(i * quarter_rows, quarter_rows)
            g = 0.5 * normed * (1.0 + t)
            r.fbuf[j, rows, :] = jnp.where(ok, g, 0.0).astype(BF16).astype(F32)
            r.slope0[j, rows, :] = t
        return 0

    def block_0_rest(j, _):
        lane = lane_at(j)
        for i in range(4):
            rows = slice(i * quarter_rows, (i + 1) * quarter_rows)
            normed = (r.h0[j, rows, :] - r.norm[0, 0:1, lane]) * r.norm[0, 2:3, lane] + bias[
                0:1, lane
            ]
            slope = gelu_slope(normed, r.slope0[j, rows, :])
            ok = valid_rows(i * quarter_rows, quarter_rows)
            r.slope0[j, rows, :] = jnp.where(ok, slope, 0.0)
        f1p = picked(r.fbuf, j)
        r.f1p[:, lane] = f1p
        r.f1b[:, lane] = f1p.astype(BF16)
        return 0

    lax.fori_loop(0, n_lane, block_0, 0)
    shift_in(lambda j: r.fbuf[j, 0:cols, :], r.xc1, 1)
    shift_in(lambda j: r.fbuf[j, cols : 2 * cols, :], r.xc1, 2)
    halo_start(1, r.xc1)
    ag_r(2, 2, both(at_end))
    ag_p(2, 1)
    lax.fori_loop(0, n_lane, block_0_rest, 0)
    for step in range(1, n_z):
        ag_z(1, step)
    ag_q(2, 2)
    ag_q(2, 3)
    ag_p(2, 2)
    ag_p(2, 3)
    for step in range(1, n_z):
        ag_y(1, step)
    ag_sib(2)
    conv_forward(r.xc1, r.w1, r.h1, 0, 0)
    for step in range(1, n_z):
        ag_r(1, step)
    conv_forward(r.xc1, r.w1, r.h1, 1, 0)
    halo_finish(1, r.xc1)
    conv_forward(r.xc1, r.w1, r.h1, 0, 1, 1)
    conv_forward(r.xc1, r.w1, r.h1, 1, 1, 1)
    ex_start(1)
    for step in range(1, n_z):
        ag_q(1, step)
    for hop in range(1, n_z):
        ag_p(1, hop)
    ag_sib(1)

    def unpack(i, _):
        for l in range(2):
            for t in range(tasks):
                r.ex_w[l, t, pl.ds(al(i * e_rows, 16), e_rows), :] = r.gp[
                    pl.ds(ex_row(i, l, t), e_rows), :
                ]
                for k in range(n_sub):
                    r.sq_w[
                        l,
                        pl.ds(al(i * s_rows + k * e_rows, 16), e_rows),
                        t * bottle : (t + 1) * bottle,
                    ] = r.gp[pl.ds(sq_row(i, l, t), e_rows), k * lanes : (k + 1) * lanes]
        return 0

    lax.fori_loop(0, n_dp, unpack, 0)
    mask_pick = jnp.concatenate([r.mp[...]] * n_lane, axis=1)
    g, slope = gelu_pair(dot(r.f1b[...], r.sq_w[0]))
    r.excited0[...] = g.astype(BF16)
    r.eslope0[...] = slope

    def task_lane(t):
        return pl.ds(al(t * bottle, lanes), bottle)

    def gate_0(t, _):
        value = jax.nn.sigmoid(dot(r.excited0[:, task_lane(t)], r.ex_w[0, t]))
        r.gate0[t] = value
        r.t1[t] = (mask_pick * value * r.f1p[...]).astype(BF16)
        return 0

    for t in range(tasks):
        gate_0(t, 0)
    norm_of(ex_finish(1), 1)

    for kind in range(3):
        ag_end(kind)
    for p in plane:
        pl.semaphore_signal(r.ready, inc=1, device_id=(p, d), device_id_type=MESH)
    pl.semaphore_signal(r.ready, inc=1, device_id=(s, sib), device_id_type=MESH)

    def block_1(j, _):
        lane = lane_at(j)
        off = picked(r.h1, j) - r.norm[1, 0:1, lane]
        g, slope = gelu_pair(off * r.norm[1, 2:3, lane] + bias[1:2, lane])
        r.f2p[:, lane] = (r.mp[...] * g).astype(BF16).astype(F32)
        r.slope1[:, lane] = r.mp[...] * slope
        r.centred1[:, lane] = off * r.norm[1, 1:2, lane]
        return 0

    lax.fori_loop(0, n_lane, block_1, 0)
    grads = [r.w1, r.gp, r.g1]

    def pair_of(k):
        return z_at((2, 1, 3, 0)[k])

    def rs_a_copy(kind, k, core):
        return remote(
            shard(kind, grads[kind], 2 * pair_of(k) + core),
            r.ra[kind].at[k],
            r.ag_zs.at[kind, k],
            r.ag_zr.at[kind, k] if k < n_z - 1 else r.ag_or.at[kind],
            (s, sib),
        )

    def again(first, second, i):
        per = 6 * (n_z - 1)
        if i < 3 * per:
            return first.at[i // per, i % per]
        i, per = i - 3 * per, 4 * (n_z - 1)
        return second.at[i // per, i % per]

    def rs_b_copy(kind, k, way):
        o = 2 * pair_of(k) + c
        half = (0, 0, 1, 1, 0, 1)[way]
        to = plane[(0, 0, 1, 1, 1, 0)[way]]
        q = to if way in (0, 2, 4, 5) else plane[2]
        return remote(
            quarter(kind, grads[kind], o, q).at[:, halves[half]],
            r.rb[kind].at[k, way],
            again(r.ag_ps, r.ag_ss, (kind * n_z + k) * 6 + way),
            again(r.ag_pr, r.ag_sr, (kind * n_z + k) * 6 + way),
            (to, d),
        )

    def rs_c_copy(kind, k):
        return remote(
            r.qs[kind].at[k],
            r.rc[kind].at[k],
            r.rs_cs.at[kind, k],
            r.rs_cr.at[kind, k],
            (s, 2 * pair_of(k) + c),
        )

    def d_sem(kind, leg):
        return (kind * n_z + leg // 4) * 6 + leg % 4

    def rs_d_copy(kind, leg, q):
        rows = shard_rows[kind] // 4
        half = (0, 1, 1, 0, 0, 1)[leg]
        to = plane[(0, 1, 0, 1, 1, 0)[leg]]
        view = out_reduced[kind].at[pl.ds(al(q * rows, 16), rows), halves[half]]
        i = d_sem(kind, leg)
        return remote(
            view, view, again(r.ag_ps, r.ag_ss, i), again(r.ag_pr, r.ag_sr, i), (to, d)
        )

    def conv_weight(kind, xc, k):
        tile = 2 * shard_rows[kind] // 3
        per = 3 * width // tile

        for i in range(3):
            g = pair_of(k) * 3 + i
            a = g // per
            term = dot_tn(
                xc[pl.ds(al(a * cols, 16), pixels), pl.ds(al((g % per) * tile, lanes), tile)],
                r.dc[cols : 3 * cols, width : 2 * width],
            )
            grads[kind][pl.ds(al(g * tile, 16), tile), :] = term.astype(BF16)

    def rs_a(kind, k):
        rs_a_copy(kind, k, 1 - c).start()

    def rs_b(kind, k):
        rs_a_copy(kind, k, c).wait_recv()
        rows = shard_rows[kind]
        tile = rows // 4
        start = (2 * pair_of(k) + c) * rows

        def body(i, _):
            at = pl.ds(al(start + i * tile, 16), tile)
            grads[kind][at, :] = (
                grads[kind][at, :].astype(F32)
                + r.ra[kind][k, pl.ds(al(i * tile, 16), tile), :].astype(F32)
            ).astype(BF16)
            return 0

        lax.fori_loop(0, 4, body, 0)
        for way in range(4):
            rs_b_copy(kind, k, way).start()

    def quarter_at(kind, k, q):
        rows = shard_rows[kind]
        return pl.ds(al((2 * pair_of(k) + c) * rows + q * (rows // 4), 16), rows // 4)

    def rs_r(kind, k):
        for half in range(2):
            rs_b_copy(kind, k, 2 * half).wait_recv()
            rs_b_copy(kind, k, 2 * half + 1).wait_recv()
            at = quarter_at(kind, k, plane[1 - half])
            grads[kind][at, halves[half]] = (
                grads[kind][at, halves[half]].astype(F32)
                + r.rb[kind][k, 2 * half + 1].astype(F32)
            ).astype(BF16)
            rs_b_copy(kind, k, 4 + half).start()

    def rs_c(kind, k):
        at = quarter_at(kind, k, s)
        parts = []
        for half in range(2):
            rs_b_copy(kind, k, 4 + half).wait_recv()
            parts.append(
                grads[kind][at, halves[half]].astype(F32)
                + r.rb[kind][k, 2 * half].astype(F32)
                + r.rb[kind][k, 4 + half].astype(F32)
            )
        total = jnp.concatenate(parts, axis=1)
        if k < n_z - 1:
            r.qs[kind][k] = total.astype(BF16)
            rs_c_copy(kind, k).start()
        else:
            r.qf[kind][...] = total

    def rs_d(kind):
        total = r.qf[kind][...]
        for k in range(n_z - 1):
            rs_c_copy(kind, k).wait_recv()
            total = total + r.rc[kind][k].astype(F32)
        rows = shard_rows[kind] // 4
        out_reduced[kind][pl.ds(al(s * rows, 16), rows), :] = total.astype(BF16)
        for leg in range(6):
            rs_b_copy(kind, leg // 4, leg % 4).wait_send()
        for leg in range(2 if kind == 0 else 4):
            rs_d_copy(kind, leg, s).start()

    def rs_dr(kind):
        if kind == 0:
            for leg in range(2):
                rs_d_copy(kind, leg, s).wait_send()
            for leg in range(2, 4):
                rs_d_copy(kind, leg, s).start()
        for leg in range(2):
            rs_d_copy(kind, leg, plane[leg]).wait_recv()
            rs_d_copy(kind, 4 + leg, plane[leg]).start()

    def rs_e(kind):
        for leg in range(2):
            rs_d_copy(kind, 2 + leg, plane[leg]).wait_recv()
            rs_d_copy(kind, 4 + leg, plane[2]).wait_recv()

    def rs_end(kind):
        for k in range(n_z):
            rs_a_copy(kind, k, 1 - c).wait_send()
            for way in range((4, 2, 0, 0)[k], 6):
                rs_b_copy(kind, k, way).wait_send()
            if k < n_z - 1:
                rs_c_copy(kind, k).wait_send()
        for leg in range(2 if kind == 0 else 0, 4):
            rs_d_copy(kind, leg, s).wait_send()
        for leg in range(2):
            rs_d_copy(kind, 4 + leg, plane[leg]).wait_send()

    for item in loads[3:]:
        item.wait()
    r.df2[...] = jnp.zeros_like(r.df2)

    def pack_grads(l, t, grad_squeeze, grad_expand):
        r.fbuf[0, 0:width, :] = grad_squeeze
        for j in range(n_lane):
            r.fbuf[1, j * bottle : (j + 1) * bottle, :] = grad_expand[:, j * lanes : (j + 1) * lanes]

        def body(i, _):
            for j in range(n_lane):
                lane = slice(j * lanes, (j + 1) * lanes)
                r.gp[pl.ds(ex_row(i, l, t), e_rows), lane] = r.fbuf[
                    1, pl.ds(al(j * bottle + i * e_rows, 16), e_rows), :
                ].astype(BF16)
            for k in range(n_sub):
                r.gp[pl.ds(sq_row(i, l, t), e_rows), k * lanes : (k + 1) * lanes] = r.fbuf[
                    0, pl.ds(al(i * s_rows + k * e_rows, 16), e_rows), :
                ].astype(BF16)
            return 0

        lax.fori_loop(0, n_dp, body, 0)

    def kept(i):
        return pl.ds(al(i * windows, 16), windows)

    def gate_1(t, _):
        w_s = r.sq_w[1, :, task_lane(t)]
        w_e = r.ex_w[1, t]
        f2p = r.f2p[...]
        source = (f2p + r.t1[t].astype(F32)).astype(BF16)
        g, slope = gelu_pair(dot(source, w_s))
        excited = g.astype(BF16)
        value = jax.nn.sigmoid(dot(excited, w_e))
        field = mask_pick * f2p
        d_task = r.g1[cot_at + t * windows : cot_at + (t + 1) * windows, :].astype(F32)
        out_task[0, t] = (value * field).astype(BF16)
        d_expanded = (d_task * field * value * (1.0 - value)).astype(BF16)
        d_squeezed = (slope * dot_nt(d_expanded, w_e)).astype(BF16)
        d_source = dot_nt(d_squeezed, w_s)
        r.t1[t] = d_source.astype(BF16)
        r.df2[...] += d_source + mask_pick * d_task * value
        r.g1[kept(t), :] = source
        r.g1[kept(tasks + t), :] = d_expanded
        r.g1[kept(2 * tasks), task_lane(t)] = excited
        r.g1[kept(2 * tasks + 1), task_lane(t)] = d_squeezed
        return 0

    def gate_1_weight(t, _):
        pack_grads(
            1,
            t,
            dot_tn(r.g1[kept(t), :], r.g1[kept(2 * tasks + 1), task_lane(t)]),
            dot_tn(r.g1[kept(2 * tasks), task_lane(t)], r.g1[kept(tasks + t), :]),
        )
        return 0

    for t in range(tasks):
        gate_1(t, 0)
    def back_1(j, _):
        lane = lane_at(j)
        d_norm = r.slope1[:, lane] * r.df2[:, lane].astype(BF16).astype(F32)
        r.df2[:, lane] = d_norm
        ex_put(2, 0, j, jnp.sum(d_norm, 0, keepdims=True))
        ex_put(2, 1, j, jnp.sum(d_norm * r.centred1[:, lane], 0, keepdims=True))
        return 0

    lax.fori_loop(0, n_lane, back_1, 0)
    ex_start(2)

    r.df1[...] = jnp.zeros_like(r.df1)

    def gate_0_back(t, _):
        w_s = r.sq_w[0, :, task_lane(t)]
        w_e = r.ex_w[0, t]
        value = r.gate0[t]
        d_task = r.t1[t].astype(F32)
        excited = r.excited0[:, task_lane(t)]
        d_expanded = (d_task * (mask_pick * r.f1p[...]) * value * (1.0 - value)).astype(BF16)
        d_squeezed = (r.eslope0[:, task_lane(t)] * dot_nt(d_expanded, w_e)).astype(BF16)
        r.df1[...] += dot_nt(d_squeezed, w_s) + mask_pick * d_task * value
        pack_grads(0, t, dot_tn(r.f1b[...], d_squeezed), dot_tn(excited, d_expanded))
        return 0

    for t in range(tasks):
        gate_0_back(t, 0)
    for t in range(tasks):
        gate_1_weight(t, 0)

    r.sums[...] = jnp.zeros_like(r.sums)

    def back_terms(k, layer):
        sums = ex_finish(k)
        r.sums[2 * layer : 2 * layer + 1, :] = sums[0]
        r.sums[2 * layer + 1 : 2 * layer + 2, :] = sums[1]
        scale = gain[layer : layer + 1, :] * r.norm[layer, 3:4, :] * r.norm[layer, 1:2, :]
        r.norm[layer, 4:5, :] = scale * sums[0]
        r.norm[layer, 5:6, :] = scale * r.norm[layer, 1:2, :] * sums[1]

    pl.semaphore_wait(r.ready, 4)
    for k in range(n_z):
        rs_a(1, k)
    back_terms(2, 1)

    def hidden_grad_1(j, _):
        lane = lane_at(j)
        norm = r.norm
        for k in range(4):
            at = corner_rows(k)
            spread = jnp.where(pick_ref[...] == k, r.df2[:, lane] * norm[1, 2:3, lane], 0.0)
            value = spread - (
                norm[1, 4:5, lane] + (r.h1[j, at, :] - norm[1, 0:1, lane]) * norm[1, 5:6, lane]
            )
            slot = (k // 2) * cols + k % 2 + 2 * lax.broadcasted_iota(
                jnp.int32, (windows, lanes), 0
            )
            r.fbuf[j, at, :] = jnp.where(slot < count, value, 0.0)
        return 0

    lax.fori_loop(0, n_lane, hidden_grad_1, 0)
    shift_in(lambda j: r.fbuf[j, 0:cols, :], r.dc, 1)
    shift_in(lambda j: r.fbuf[j, cols : 2 * cols, :], r.dc, 2)
    halo_sent(1, r.xc1)
    halo_start(2, r.dc)

    for k in range(n_z):
        rs_b(1, k)
    for k in range(2):
        conv_weight(2, r.xc1, k)
        rs_a(2, k)
    conv_back(r.dc, r.w1, 0, 0)
    rs_b(2, 0)
    conv_back(r.dc, r.w1, 1, 0)
    for k in range(n_z):
        rs_r(1, k)
    rs_b(2, 1)
    halo_finish(2, r.dc)
    conv_back(r.dc, r.w1, 0, 1)
    conv_back(r.dc, r.w1, 1, 1)
    def back_0(j, _):
        lane = lane_at(j)
        norm = r.norm
        first = jnp.zeros((1, lanes), F32)
        second = jnp.zeros((1, lanes), F32)
        for k in range(4):
            at = corner_rows(k)
            d_field = r.fbuf[j, at, :].astype(BF16).astype(F32) + jnp.where(
                pick_ref[...] == k, r.df1[:, lane], 0.0
            )
            d_norm = r.slope0[j, at, :] * d_field.astype(BF16).astype(F32)
            r.fbuf[j, at, :] = d_norm
            centred = (r.h0[j, at, :] - norm[0, 0:1, lane]) * norm[0, 1:2, lane]
            first = first + jnp.sum(d_norm, 0, keepdims=True)
            second = second + jnp.sum(d_norm * centred, 0, keepdims=True)
        ex_put(3, 0, j, first)
        ex_put(3, 1, j, second)
        return 0

    lax.fori_loop(0, n_lane, back_0, 0)
    ex_start(3)
    conv_weight(2, r.xc1, 2)
    rs_a(2, 2)
    rs_r(2, 0)
    conv_weight(2, r.xc1, 3)
    rs_a(2, 3)
    rs_b(2, 2)
    halo_sent(2, r.dc)
    back_terms(3, 0)

    def sums_copy(p, q):
        return remote(
            r.sums,
            r.sums_in.at[q],
            r.sums_s.at[p],
            r.sums_r.at[p],
            (plane[p], d),
        )

    for p in range(3):
        sums_copy(p, s).start()
    r.sums_in[s] = r.sums[...]

    def hidden_grad_0(row):
        def value(j):
            lane = lane_at(j)
            norm = r.norm
            rows = slice(row * cols, (row + 1) * cols)
            out = r.fbuf[j, rows, :] * norm[0, 2:3, lane] - (
                norm[0, 4:5, lane] + (r.h0[j, rows, :] - norm[0, 0:1, lane]) * norm[0, 5:6, lane]
            )
            return jnp.where(valid_rows(row * cols, cols), out, 0.0)

        return value

    shift_in(hidden_grad_0(0), r.dc, 1)
    shift_in(hidden_grad_0(1), r.dc, 2)
    halo_start(3, r.dc)
    conv_weight(0, r.xc0, 0)
    rs_a(0, 0)
    rs_r(2, 1)
    rs_b(2, 3)
    for k in range(n_z):
        rs_c(1, k)
    conv_weight(0, r.xc0, 1)
    rs_a(0, 1)
    rs_c(2, 0)
    conv_weight(0, r.xc0, 2)
    rs_a(0, 2)
    rs_r(2, 2)
    rs_b(0, 0)
    conv_weight(0, r.xc0, 3)
    rs_a(0, 3)
    rs_c(2, 1)
    conv_back(r.dc, r.w0, 0, 0)
    rs_r(2, 3)
    rs_b(0, 1)
    conv_back(r.dc, r.w0, 1, 0)
    rs_c(2, 2)
    halo_finish(3, r.dc)
    conv_back(r.dc, r.w0, 0, 1)
    conv_back(r.dc, r.w0, 1, 1)
    def image_out(j, _):
        lane = lane_at(j)
        for i in range(4):
            rows = slice(i * quarter_rows, (i + 1) * quarter_rows)
            out_image[0, rows, lane] = jnp.where(
                valid_rows(i * quarter_rows, quarter_rows), r.fbuf[j, rows, :], 0.0
            ).astype(BF16)
        return 0

    lax.fori_loop(0, n_lane, image_out, 0)
    rs_r(0, 0)
    rs_b(0, 2)
    rs_c(2, 3)
    rs_r(0, 1)
    rs_c(0, 0)
    rs_b(0, 3)
    rs_r(0, 2)
    rs_c(0, 1)
    rs_r(0, 3)
    rs_c(0, 2)
    rs_d(1)
    rs_d(2)
    rs_c(0, 3)
    rs_dr(1)
    rs_dr(2)
    rs_d(0)
    for p in range(3):
        sums_copy(p, plane[p]).wait_recv()
    total = r.sums_in[0]
    for i in range(1, 4):
        total = total + r.sums_in[i]
    for l in range(2):
        out_bias[l : l + 1, :] = total[2 * l : 2 * l + 1, :]
        out_gain[l : l + 1, :] = total[2 * l + 1 : 2 * l + 2, :]
    for p in range(3):
        sums_copy(p, s).wait_send()
    ex_sent(2)
    ex_sent(3)
    halo_sent(3, r.dc)
    rs_dr(0)
    for kind in (1, 2, 0):
        rs_e(kind)
        rs_end(kind)


def finish_kernel(
    dims,
    task,
    image,
    reduced_0,
    reduced_1,
    reduced_2,
    gain,
    bias,
    out_task,
    out_image,
    out_conv,
    out_squeeze,
    out_expand,
    out_gain,
    out_bias,
    conv_wide,
    squeeze_wide,
    expand_wide,
    sem,
):
    lanes = 128
    e_rows = dims.bottle // dims.n_dp
    outs = []

    def store(src, dst):
        outs.append(pltpu.make_async_copy(src, dst, sem.at[len(outs)]))
        outs[-1].start()

    store(task, out_task)
    store(image, out_image)
    for layer, reduced in enumerate((reduced_0, reduced_2)):
        conv_wide[layer] = reduced[...].astype(F32)
        store(conv_wide.at[layer], out_conv.at[layer])
    for l in range(2):
        for t in range(dims.tasks):
            at = (l * dims.tasks + t) * e_rows
            expand_wide[l, t] = reduced_1[at : at + e_rows, :].astype(F32)
            at = at + 2 * dims.tasks * e_rows
            for k in range(dims.width // dims.n_dp // e_rows):
                squeeze_wide[l, t, k * e_rows : (k + 1) * e_rows, :] = reduced_1[
                    at : at + e_rows, k * lanes : (k + 1) * lanes
                ].astype(F32)
    store(squeeze_wide, out_squeeze)
    store(expand_wide, out_expand)
    out_gain[...] = gain[...]
    out_bias[...] = bias[...]
    for copy in outs:
        copy.wait()


def fused(images, counts, pool_index, conv_w, squeeze_w, expand_w, gain, bias, cotangent):
    n_dp = lax.axis_size("dp")
    micro, pixels, width = images.shape
    tasks, bottle = squeeze_w.shape[1], squeeze_w.shape[3]
    cols = 2 * pool_index.shape[2]
    windows = cols // 2
    conv_rows = conv_w.shape[1]
    gate_rows = 4 * tasks * expand_w.shape[2]
    shard_rows = (conv_rows, gate_rows, conv_rows)
    n_z = n_dp // 2
    vm = pltpu.VMEM
    dma = pltpu.SemaphoreType.DMA
    scratch = dict(
        load=dma((9 + 2 * (width // 128) + tasks,)),
        counts=pltpu.SMEM((micro,), jnp.int32),
        picks=vm(pool_index.shape, jnp.int32),
        gain=vm(gain.shape, F32),
        bias=vm(bias.shape, F32),
        sst=vm(squeeze_w.shape, F32),
        est=vm(expand_w.shape, F32),
        w0=vm((n_dp * conv_rows, width), BF16),
        gp=vm((n_dp * gate_rows, width), BF16),
        w1=vm((n_dp * conv_rows, width), BF16),
        g1=vm((n_dp * conv_rows, width), BF16),
        sq_w=vm((2, width, tasks * bottle), BF16),
        ex_w=vm((2, tasks, bottle, width), BF16),
        ag_zs=dma((3, 2 * (n_z - 1))),
        ag_zr=dma((3, n_z - 1)),
        ag_ps=dma((3, 6 * (n_z - 1))),
        ag_pr=dma((3, 6 * (n_z - 1))),
        ag_ss=dma((3, 4 * (n_z - 1))),
        ag_sr=dma((3, 4 * (n_z - 1))),
        ag_os=dma((3,)),
        ag_or=dma((3,)),
        mp=vm((windows, 128), F32),
        pick=vm((windows, 128), jnp.int32),
        halo=vm((2, 2, cols, width), BF16),
        halo_s=dma((2, 2)),
        halo_r=dma((2, 2)),
        ex_out=vm((5, 8, 128), F32),
        ex_in=vm((5, n_dp, 8, 128), F32),
        total=vm((8, width), F32),
        ex_s=dma((2, n_dp - 1)),
        ex_r=dma((2, n_dp - 1)),
        norm=vm((2, 8, width), F32),
        xc0=vm((4 * cols, 3 * width), BF16),
        xc1=vm((4 * cols, 3 * width), BF16),
        dc=vm((4 * cols, 3 * width), BF16),
        h0=vm((width // 128, pixels, 128), F32),
        h1=vm((width // 128, pixels, 128), F32),
        slope0=vm((width // 128, pixels, 128), F32),
        fbuf=vm((width // 128, pixels, 128), F32),
        f1p=vm((windows, width), F32),
        f1b=vm((windows, width), BF16),
        excited0=vm((windows, tasks * bottle), BF16),
        eslope0=vm((windows, tasks * bottle), F32),
        gate0=vm((tasks, windows, width), F32),
        t1=vm((tasks, windows, width), BF16),
        f2p=vm((windows, width), F32),
        slope1=vm((windows, width), F32),
        centred1=vm((windows, width), F32),
        df2=vm((windows, width), F32),
        df1=vm((windows, width), F32),
        sums=vm((8, width), F32),
        sums_in=vm((4, 8, width), F32),
        sums_s=dma((3,)),
        sums_r=dma((3,)),
        ready=pltpu.SemaphoreType.REGULAR,
        rs_cs=dma((3, n_z - 1)),
        rs_cr=dma((3, n_z - 1)),
    )
    quarters = [rows // 4 for rows in shard_rows]
    scratch.update(
        ra=[vm((n_z, rows, width), BF16) for rows in shard_rows],
        rb=[vm((n_z, 6, rows, width // 2), BF16) for rows in quarters],
        qs=[vm((n_z - 1, rows, width), BF16) for rows in quarters],
        qf=[vm((rows, width), F32) for rows in quarters],
        rc=[vm((n_z - 1, rows, width), BF16) for rows in quarters],
    )
    buffers, tree = jax.tree.flatten(scratch, is_leaf=lambda v: not isinstance(v, (dict, list)))
    dims = types.SimpleNamespace(
        tree=tree,
        n_dp=n_dp,
        cols=cols,
        pixels=pixels,
        width=width,
        tasks=tasks,
        bottle=bottle,
        shard_rows=shard_rows,
    )
    any_spec = pl.BlockSpec(memory_space=pl.ANY)
    vmem_spec = pl.BlockSpec(memory_space=pltpu.VMEM)
    results = pl.pallas_call(
        functools.partial(step_kernel, dims),
        out_shape=(
            vm((1, tasks, windows, width), BF16),
            vm((1, pixels, width), BF16),
            *[vm((rows, width), BF16) for rows in shard_rows],
            vm(gain.shape, F32),
            vm(bias.shape, F32),
        ),
        in_specs=[any_spec] * 9,
        out_specs=(vmem_spec,) * 7,
        scratch_shapes=tuple(buffers),
        compiler_params=pltpu.CompilerParams(
            collective_id=0, has_side_effects=True, vmem_limit_bytes=VMEM_BYTES
        ),
    )(counts.reshape(micro), pool_index, gain, bias, images, conv_w, squeeze_w, expand_w, cotangent)
    results = [pltpu.with_memory_space_constraint(v, pltpu.VMEM) for v in results]
    return pl.pallas_call(
        functools.partial(finish_kernel, dims),
        out_shape=(
            jax.ShapeDtypeStruct((1, tasks, windows, width), BF16),
            jax.ShapeDtypeStruct((1, pixels, width), BF16),
            jax.ShapeDtypeStruct(conv_w.shape, F32),
            jax.ShapeDtypeStruct(squeeze_w.shape, F32),
            jax.ShapeDtypeStruct(expand_w.shape, F32),
            jax.ShapeDtypeStruct(gain.shape, F32),
            jax.ShapeDtypeStruct(bias.shape, F32),
        ),
        in_specs=[vmem_spec] * 7,
        out_specs=(any_spec,) * 5 + (vmem_spec,) * 2,
        scratch_shapes=(
            vm(conv_w.shape, F32),
            vm(squeeze_w.shape, F32),
            vm(expand_w.shape, F32),
            dma((6,)),
        ),
        compiler_params=pltpu.CompilerParams(vmem_limit_bytes=16 * 1024 * 1024),
    )(*results)


def fits_kernel(mesh, args):
    images, counts, pool_index, conv_w, squeeze_w, expand_w = args[:6]
    sections, n_dp = mesh.shape["section"], mesh.shape["dp"]
    conv_rows = conv_w.shape[1] // n_dp
    e_rows = expand_w.shape[2] // n_dp
    return (
        sections == 4
        and images.shape[0] == sections
        and n_dp % 2 == 0
        and pool_index.shape[1] == n_dp
        and conv_rows % 64 == 0
        and e_rows == 16
        and squeeze_w.shape[2] // n_dp == 4 * e_rows
        and squeeze_w.shape[3] == 128
        and images.shape[2] == 4 * 128
    )


def solution(mesh):
    placed = (
        P(None, "dp", None),
        P(None, "dp"),
        P(None, "dp", None),
        P(None, "dp", None),
        P(None, None, "dp", None),
        P(None, None, "dp", None),
        P(),
        P(),
        P(None, None, "dp", None),
    )
    def run(*args):
        return mapped(fused if fits_kernel(mesh, args) else on_device)(*args)

    def mapped(body):
        return jax.shard_map(
        body,
        mesh=mesh,
        in_specs=placed,
        out_specs=(
            P("section", None, "dp", None),
            P("section", "dp", None),
            P(None, "dp", None),
            P(None, None, "dp", None),
            P(None, None, "dp", None),
            P(),
            P(),
        ),
        check_vma=False,
    )

    return run
```

```python
import functools
import types

import jax
import jax.numpy as jnp
from jax import lax
from jax.experimental import pallas as pl
from jax.experimental.pallas import tpu as pltpu
from jax.sharding import PartitionSpec as P

EPS = 1e-05
BF16 = jnp.bfloat16
F32 = jnp.float32
VMEM_BYTES = 58 * 1024 * 1024


def gelu_back(point, upstream):
    return jax.vjp(jax.nn.gelu, point)[1](upstream)[0]


def with_halo(value, axis):
    size = lax.axis_size(axis)
    up = [(i, i + 1) for i in range(size - 1)]
    down = [(j, i) for i, j in up]
    before = lax.ppermute(value[-1:], axis, up)
    after = lax.ppermute(value[:1], axis, down)
    return jnp.concatenate([before, value, after], axis=0)


def conv(padded, taps):
    out = lax.conv_general_dilated(
        padded[None],
        taps,
        (1, 1),
        ((0, 0), (1, 1)),
        dimension_numbers=("NHWC", "HWIO", "NHWC"),
        preferred_element_type=F32,
    )
    return out.reshape(-1, out.shape[-1])


def conv_input_grad(d_padded, taps):
    out = lax.conv_general_dilated(
        d_padded[None],
        taps[::-1, ::-1],
        (1, 1),
        ((0, 0), (1, 1)),
        dimension_numbers=("NHWC", "HWOI", "NHWC"),
        preferred_element_type=F32,
    )
    return out.reshape(-1, out.shape[-1])


def conv_weight_grad(padded, d_hidden):
    out = lax.conv_general_dilated(
        padded[None],
        d_hidden[None],
        (1, 1),
        ((0, 0), (1, 1)),
        dimension_numbers=("CHWN", "IHWO", "HWNC"),
        preferred_element_type=F32,
    )
    return out.reshape(-1, out.shape[-1])


def gate_forward(source, w_squeeze, w_expand):
    squeezed = jnp.einsum("tpc,tcb->tpb", source, w_squeeze, preferred_element_type=F32)
    excited = jax.nn.gelu(squeezed).astype(BF16)
    expanded = jnp.einsum("tpb,tbc->tpc", excited, w_expand, preferred_element_type=F32)
    return squeezed, excited, jax.nn.sigmoid(expanded)


def gate_backward(d_task, field, source, squeezed, excited, gate_val, w_squeeze, w_expand):
    d_expanded = (d_task * field[None] * gate_val * (1.0 - gate_val)).astype(BF16)
    d_excited = jnp.einsum("tpc,tbc->tpb", d_expanded, w_expand, preferred_element_type=F32)
    d_squeezed = gelu_back(squeezed, d_excited).astype(BF16)
    d_source = jnp.einsum("tpb,tcb->tpc", d_squeezed, w_squeeze, preferred_element_type=F32)
    grad_squeeze = jnp.einsum("tpc,tpb->tcb", source, d_squeezed, preferred_element_type=F32)
    grad_expand = jnp.einsum("tpb,tpc->tbc", excited, d_expanded, preferred_element_type=F32)
    return d_source, grad_squeeze, grad_expand


def pool_pick(field, pick):
    tasks, _, width = field.shape
    half_rows, half_columns = pick.shape
    windows = field.reshape(tasks, half_rows, 2, half_columns, 2, width)
    picked = jnp.zeros((tasks, half_rows, half_columns, width), F32)
    for corner in range(4):
        hit = (pick == corner)[None, :, :, None]
        picked = picked + jnp.where(hit, windows[:, :, corner // 2, :, corner % 2, :], 0.0)
    return picked.reshape(tasks, half_rows * half_columns, width)


def pool_spread(d_pooled, pick):
    tasks, _, width = d_pooled.shape
    half_rows, half_columns = pick.shape
    grid = d_pooled.reshape(tasks, half_rows, half_columns, width)
    rows = [
        jnp.stack(
            [jnp.where((pick == 2 * dy + dx)[None, :, :, None], grid, 0.0) for dx in range(2)], 3
        )
        for dy in range(2)
    ]
    return jnp.stack(rows, 2).reshape(tasks, half_rows * 2 * half_columns * 2, width)


def on_device(images, counts, pool_index, conv_w, squeeze_w, expand_w, gain, bias, cotangent):
    sections = lax.axis_size("section")
    here = lax.axis_index("section")
    micro, pixels, width = images.shape
    layers = conv_w.shape[0]
    tasks = squeeze_w.shape[1]
    rows = 2 * pool_index.shape[1]
    columns = 2 * pool_index.shape[2]
    share = micro // sections

    def own(value):
        return lax.dynamic_slice_in_dim(value, here * share, share, 0)

    images, counts, pool_index, cotangent = (
        own(images),
        own(counts),
        own(pool_index),
        own(cotangent),
    )

    def gather(value, axis):
        return lax.all_gather(value.astype(BF16), "dp", axis=axis, tiled=True)

    taps = [gather(conv_w[l], 0).reshape(3, 3, width, width) for l in range(layers)]
    w_squeeze = [gather(squeeze_w[l], 1) for l in range(layers)]
    w_expand = [gather(expand_w[l], 1) for l in range(layers)]
    slots = jnp.arange(pixels, dtype=jnp.int32)[:, None]

    def block_forward(field, mask, total, layer):
        padded = with_halo(field.reshape(rows, columns, width), "dp")
        hidden = conv(padded, taps[layer])
        sums = lax.psum(
            jnp.stack([jnp.sum(mask * hidden, 0), jnp.sum(mask * hidden * hidden, 0)]), "dp"
        )
        centre = sums[0] / total
        inverse = lax.rsqrt(sums[1] / total - centre * centre + EPS)
        normed = gain[layer] * (hidden - centre) * inverse + bias[layer]
        out = (mask * jax.nn.gelu(normed)).astype(BF16)
        return out, (padded, hidden, centre, inverse)

    def block_backward(d_out, kept, mask, total, layer):
        padded, hidden, centre, inverse = kept
        centred = (hidden - centre) * inverse
        normed = gain[layer] * (hidden - centre) * inverse + bias[layer]
        d_norm = gelu_back(normed, mask * d_out)
        gain_sum = jnp.sum(d_norm * centred, 0)
        bias_sum = jnp.sum(d_norm, 0)
        sums = gain[layer] * lax.psum(jnp.stack([bias_sum, gain_sum]), "dp")
        d_hidden = (
            mask * inverse * (gain[layer] * d_norm - sums[0] / total - centred * sums[1] / total)
        ).astype(BF16)
        d_hidden = d_hidden.reshape(rows, columns, width)
        d_x = conv_input_grad(with_halo(d_hidden, "dp"), taps[layer])
        return d_x, conv_weight_grad(padded, d_hidden), gain_sum, bias_sum

    outs, image_grads = [], []
    grads = None
    totals = lax.psum(counts[:, 0], "dp").astype(F32)
    for m in range(share):
        total = totals[m]
        mask = (slots < counts[m, 0]).astype(F32)
        first_in = jnp.where(slots < counts[m, 0], images[m], jnp.zeros((), BF16))
        f1, kept_0 = block_forward(first_in, mask, total, 0)
        f1_f = f1.astype(F32)
        source_0 = jnp.broadcast_to(f1[None], (tasks, pixels, width))
        squeezed_0, excited_0, gate_0 = gate_forward(source_0, w_squeeze[0], w_expand[0])
        t1 = (mask[None] * gate_0 * f1_f[None]).astype(BF16)
        f2, kept_1 = block_forward(f1, mask, total, 1)
        f2_f = f2.astype(F32)
        source_1 = (f2_f[None] + t1.astype(F32)).astype(BF16)
        squeezed_1, excited_1, gate_1 = gate_forward(source_1, w_squeeze[1], w_expand[1])
        outs.append(pool_pick(mask[None] * gate_1 * f2_f[None], pool_index[m]).astype(BF16))

        d_task = pool_spread(cotangent[m].astype(F32), pool_index[m])
        d_source, gs_1, ge_1 = gate_backward(
            d_task, mask * f2_f, source_1, squeezed_1, excited_1, gate_1, w_squeeze[1], w_expand[1]
        )
        d_f2 = (jnp.sum(d_source, 0) + mask * jnp.sum(d_task * gate_1, 0)).astype(BF16)
        d_t1 = d_source.astype(BF16).astype(F32)
        d_x1, gc_1, gain_1, bias_1 = block_backward(d_f2.astype(F32), kept_1, mask, total, 1)
        d_source, gs_0, ge_0 = gate_backward(
            d_t1, mask * f1_f, source_0, squeezed_0, excited_0, gate_0, w_squeeze[0], w_expand[0]
        )
        d_f1 = (
            d_x1.astype(BF16).astype(F32)
            + jnp.sum(d_source, 0)
            + mask * jnp.sum(d_t1 * gate_0, 0)
        ).astype(BF16)
        d_x0, gc_0, gain_0, bias_0 = block_backward(d_f1.astype(F32), kept_0, mask, total, 0)
        image_grads.append((mask * d_x0).astype(BF16))
        here_grads = [
            [gc_0, gc_1],
            [gs_0, gs_1],
            [ge_0, ge_1],
            jnp.stack([gain_0, gain_1]),
            jnp.stack([bias_0, bias_1]),
        ]
        grads = here_grads if grads is None else jax.tree.map(jnp.add, grads, here_grads)

    def reduced(value, axis):
        part = lax.psum_scatter(value, "dp", scatter_dimension=axis, tiled=True)
        return lax.psum(part.astype(BF16), "section").astype(F32)

    conv_grad = jnp.stack([reduced(g, 0) for g in grads[0]])
    squeeze_grad = jnp.stack([reduced(g, 1) for g in grads[1]])
    expand_grad = jnp.stack([reduced(g, 1) for g in grads[2]])
    gain_grad, bias_grad = lax.psum((grads[3], grads[4]), ("section", "dp"))
    return (
        jnp.stack(outs),
        jnp.stack(image_grads),
        conv_grad,
        squeeze_grad,
        expand_grad,
        gain_grad,
        bias_grad,
    )


GELU_C = 0.7978845608028654
GELU_K = 0.044715
MESH = pl.DeviceIdType.MESH


def gelu_tanh(x):
    return jnp.tanh(GELU_C * x * (1.0 + GELU_K * (x * x)))


def gelu_slope(x, t):
    inner = GELU_C * (1.0 + 3.0 * GELU_K * (x * x))
    return 0.5 * (1.0 + t) + 0.5 * x * (1.0 - t * t) * inner


def gelu_pair(x):
    t = gelu_tanh(x)
    return 0.5 * x * (1.0 + t), gelu_slope(x, t)


def dot(a, b):
    return jnp.dot(a, b, preferred_element_type=F32)


def dot_nt(a, b):
    return lax.dot_general(a, b, (((1,), (1,)), ((), ())), preferred_element_type=F32)


def dot_tn(a, b):
    return lax.dot_general(a, b, (((0,), (0,)), ((), ())), preferred_element_type=F32)


def step_kernel(
    dims,
    counts_in,
    picks_in,
    gain_in,
    bias_in,
    images,
    conv_w,
    squeeze_w,
    expand_w,
    cotangent,
    out_task,
    out_image,
    out_reduced_0,
    out_reduced_1,
    out_reduced_2,
    out_gain,
    out_bias,
    *scratch,
):
    out_reduced = (out_reduced_0, out_reduced_1, out_reduced_2)
    r = types.SimpleNamespace(**jax.tree.unflatten(dims.tree, scratch))
    n_dp, cols, pixels, width, tasks, bottle = (
        dims.n_dp,
        dims.cols,
        dims.pixels,
        dims.width,
        dims.tasks,
        dims.bottle,
    )
    n_z = n_dp // 2
    windows = cols // 2
    lanes = 128
    n_lane = width // lanes
    shard_rows = dims.shard_rows
    s = lax.axis_index("section")
    d = lax.axis_index("dp")
    z, c = d // 2, d % 2
    sib = 2 * z + 1 - c
    plane = [s + 1 - 2 * (s % 2), (s + 2) % 4, 3 - s]

    def rem(a, b):
        return lax.rem(a, b)

    def z_at(step):
        return rem(z + step, n_z)

    def remote(src, dst, send, recv, device):
        return pltpu.make_async_remote_copy(
            src_ref=src,
            dst_ref=dst,
            send_sem=send,
            recv_sem=recv,
            device_id=device,
            device_id_type=MESH,
        )

    def al(v, m):
        return pl.multiple_of(v, m)

    barrier = pltpu.get_barrier_semaphore()
    for step in range(1, n_dp):
        pl.semaphore_signal(
            barrier, inc=1, device_id=(s, rem(d + step, n_dp)), device_id_type=MESH
        )
    for p in plane:
        pl.semaphore_signal(barrier, inc=1, device_id=(p, d), device_id_type=MESH)

    def load(i, src, dst):
        return pltpu.make_async_copy(src, dst, r.load.at[i])

    staging = [r.h1, r.slope0]
    conv_rows = shard_rows[0]

    def conv_load(layer, j):
        lane = slice(j * lanes, (j + 1) * lanes)
        return load(
            5 + layer,
            conv_w.at[layer, :, lane],
            staging[layer].at[j, 0:conv_rows],
        )

    cot_at = (2 * tasks + 2) * windows
    image_at = cot_at + tasks * windows
    loads = [
        load(1, squeeze_w, r.sst),
        load(2, expand_w, r.est),
        load(3, images.at[s], r.g1.at[image_at : image_at + pixels]),
        *[
            load(
                5 + 2 * n_lane + t,
                cotangent.at[s, t],
                r.g1.at[cot_at + t * windows : cot_at + (t + 1) * windows],
            )
            for t in range(tasks)
        ],
    ]
    small_at = 5 + 2 * n_lane + tasks
    picks, gain, bias = r.picks, r.gain, r.bias
    counts = r.counts
    count_load = load(small_at + 3, counts_in, counts)
    small = [
        load(small_at, picks_in, picks),
        load(small_at + 1, gain_in, gain),
        load(small_at + 2, bias_in, bias),
    ]
    for j in range(n_lane):
        conv_load(0, j).start()
    count_load.start()
    loads[2].start()
    for j in range(n_lane):
        conv_load(1, j).start()
    for item in small:
        item.start()
    for i in (0, 1, *range(3, 3 + tasks)):
        loads[i].start()

    full = [r.w0, r.gp, r.w1]

    def shard(kind, buf, which):
        rows = shard_rows[kind]
        return buf.at[pl.ds(al(which * rows, 16), rows)]

    def quarter(kind, buf, which, q):
        rows = shard_rows[kind]
        return buf.at[pl.ds(al(which * rows + q * (rows // 4), 16), rows // 4)]

    def z_of(way, hop):
        return z_at(n_z - hop if way == 0 else hop)

    def has(way, hop):
        return z >= hop if way == 0 else z < n_z - hop

    def slot_of(way, hop):
        return n_z - 1 - hop if way == 0 else hop - 1

    def ag_z_copy(kind, way, hop, owner):
        view = quarter(kind, full[kind], 2 * owner + c, s)
        return remote(
            view,
            view,
            r.ag_zs.at[kind, (hop - 1) * 2 + way],
            r.ag_zr.at[kind, slot_of(way, hop)],
            (s, 2 * z_at(1 if way == 0 else n_z - 1) + c),
        )

    def gate_z_copy(step, owner):
        view = quarter(1, full[1], 2 * owner + c, s)
        return remote(
            view,
            view,
            r.ag_zs.at[1, step - 1],
            r.ag_zr.at[1, step - 1],
            (s, 2 * z_at(step) + c),
        )

    def ag_pass(kind, way, hop, do):
        here_has = has(way, hop - 1) if hop > 1 else True
        there = z < n_z - 1 if way == 0 else z > 0
        owner = z_of(way, hop - 1)

        @pl.when(jnp.logical_and(here_has, there))
        def _():
            do(ag_z_copy(kind, way, hop, owner))

    halves = [slice(0, width // 2), slice(width // 2, width)]

    def ag_p_copy(kind, slot, owner, leg, q):
        half = (0, 1, 0, 1, 0, 1)[leg]
        view = quarter(kind, full[kind], 2 * owner + c, q).at[:, halves[half]]
        to = plane[(0, 0, 1, 1, 1, 0)[leg]]
        i = slot * 6 + leg
        return remote(view, view, r.ag_ps.at[kind, i], r.ag_pr.at[kind, i], (to, d))

    def ag_own_copy(kind, core):
        view = shard(kind, full[kind], 2 * z + core)
        return remote(view, view, r.ag_os.at[kind], r.ag_or.at[kind], (s, sib))

    def ag_s_copy(kind, slot, owner, i, core):
        view = quarter(kind, full[kind], 2 * owner + core, others[i])
        i = slot * 4 + i
        return remote(view, view, r.ag_ss.at[kind, i], r.ag_sr.at[kind, i], (s, sib))

    others = [s] + plane

    def both(condition):
        return (condition, condition)

    def ag_start(kind):
        if kind == 1:
            for step in range(1, n_z):
                gate_z_copy(step, z).start()
        else:
            for way in range(2):
                ag_pass(kind, way, 1, lambda copy: copy.start())
        ag_own_copy(kind, c).start()

    at_end = jnp.logical_or(z == 0, z == n_z - 1)

    in_middle = jnp.logical_not(at_end)
    from_end = (z == 1, z == n_z - 2)
    not_from_end = (z != 1, z != n_z - 2)

    def for_hop(kind, hop, do, also=(True, True)):
        if kind == 1:
            do(hop - 1, z_at(n_z - hop), None)
            return
        for way in range(2):

            @pl.when(jnp.logical_and(has(way, hop), also[way]))
            def _():
                do(slot_of(way, hop), z_of(way, hop), way)

    def ag_z(kind, hop, also=(True, True), legs=True):
        def do(slot, owner, way):
            if kind == 1:
                gate_z_copy(hop, owner).wait_recv()
            else:
                ag_z_copy(kind, way, hop, owner).wait_recv()
                if hop < n_z - 1:
                    ag_pass(kind, way, hop + 1, lambda copy: copy.start())
            if legs:
                for leg in (0, 3):
                    ag_p_copy(kind, slot, owner, leg, s).start()

        for_hop(kind, hop, do, also)

    def ag_l(kind, hop, also):
        def do(slot, owner, way):
            for leg in (0, 3):
                ag_p_copy(kind, slot, owner, leg, s).start()

        for_hop(kind, hop, do, also)

    def ag_y(kind, hop, also=(True, True)):
        def do(slot, owner, way):
            for leg in (0, 3):
                ag_p_copy(kind, slot, owner, leg, s).wait_send()
            for leg in (1, 2):
                ag_p_copy(kind, slot, owner, leg, s).start()
            ag_s_copy(kind, slot, owner, 0, c).start()

        for_hop(kind, hop, do, also)

    def ag_r(kind, hop, also=(True, True)):
        def do(slot, owner, way):
            for h in range(2):
                ag_p_copy(kind, slot, owner, 3 * h, plane[h]).wait_recv()
                ag_p_copy(kind, slot, owner, 4 + h, plane[h]).start()

        for_hop(kind, hop, do, also)

    def ag_q(kind, hop):
        def do(slot, owner, way):
            for axis in range(2):
                ag_p_copy(kind, slot, owner, 1 + axis, plane[axis]).wait_recv()
                ag_s_copy(kind, slot, owner, 1 + axis, c).start()

        for_hop(kind, hop, do)

    def ag_p(kind, hop):
        def do(slot, owner, way):
            for h in range(2):
                ag_p_copy(kind, slot, owner, 4 + h, plane[2]).wait_recv()
            ag_s_copy(kind, slot, owner, 3, c).start()

        for_hop(kind, hop, do)

    def ag_sib(kind):
        ag_own_copy(kind, 1 - c).wait_recv()
        for hop in range(1, n_z):

            def do(slot, owner, way):
                for i in range(4):
                    ag_s_copy(kind, slot, owner, i, 1 - c).wait_recv()

            for_hop(kind, hop, do)

    def ag_end(kind):
        ag_own_copy(kind, c).wait_send()
        for hop in range(1, n_z):

            def do(slot, owner, way):
                for leg in (1, 2):
                    ag_p_copy(kind, slot, owner, leg, s).wait_send()
                for h in range(2):
                    ag_p_copy(kind, slot, owner, 4 + h, plane[h]).wait_send()
                for i in range(4):
                    ag_s_copy(kind, slot, owner, i, c).wait_send()

            if kind == 1:
                gate_z_copy(hop, z).wait_send()
            else:
                for way in range(2):
                    ag_pass(kind, way, hop, lambda copy: copy.wait_send())
            for_hop(kind, hop, do)

    def cast_conv(layer, buf):
        view = staging[layer].at[:, 0:conv_rows]
        load(5 + layer, view, view).wait()

        def body(j, _):
            buf[pl.ds(al(d * conv_rows, 16), conv_rows), pl.ds(al(j * lanes, lanes), lanes)] = (
                staging[layer][j, 0:conv_rows, :].astype(BF16)
            )
            return 0

        lax.fori_loop(0, n_lane, body, 0)

    g_rows = shard_rows[1]
    e_rows = n_ex = bottle // n_dp
    s_rows = width // n_dp
    n_sub = s_rows // e_rows

    def ex_row(which, l, t):
        return al(which * g_rows + (l * tasks + t) * e_rows, 16)

    def sq_row(which, l, t):
        return al(which * g_rows + (2 * tasks + l * tasks + t) * e_rows, 16)

    cast_conv(0, r.w0)
    pl.semaphore_wait(barrier, n_dp - 1 + 3)
    ag_start(0)
    count_load.wait()
    count = counts[s]
    pick_ref = r.pick

    def lane_at(j, base=0):
        return pl.ds(al(base + j * lanes, lanes), lanes)

    def valid_rows(start, rows):
        return (lax.broadcasted_iota(jnp.int32, (rows, lanes), 0) + start) < count

    def shift_in(value_of, buf, block):
        def body(j, _):
            v = value_of(j)
            at = lax.broadcasted_iota(jnp.int32, (cols, lanes), 0)
            before = jnp.where(at == 0, 0.0, pltpu.roll(v, 1, 0))
            after = jnp.where(at == cols - 1, 0.0, pltpu.roll(v, cols - 1, 0))
            rows = pl.ds(block * cols, cols)
            buf[rows, lane_at(j)] = before.astype(BF16)
            buf[rows, lane_at(j, width)] = v.astype(BF16)
            buf[rows, lane_at(j, 2 * width)] = after.astype(BF16)
            return 0

        lax.fori_loop(0, n_lane, body, 0)

    @pl.when(d == 0)
    def _():
        r.halo[:, 0] = jnp.zeros_like(r.halo[:, 0])

    @pl.when(d == n_dp - 1)
    def _():
        r.halo[:, 1] = jnp.zeros_like(r.halo[:, 1])

    def halo_down(e, buf):
        return remote(
            buf.at[2 * cols : 3 * cols, width : 2 * width],
            r.halo.at[e % 2, 0],
            r.halo_s.at[e % 2, 0],
            r.halo_r.at[e % 2, 0],
            (s, rem(d + 1, n_dp)),
        )

    def halo_up(e, buf):
        return remote(
            buf.at[cols : 2 * cols, width : 2 * width],
            r.halo.at[e % 2, 1],
            r.halo_s.at[e % 2, 1],
            r.halo_r.at[e % 2, 1],
            (s, rem(d + n_dp - 1, n_dp)),
        )

    def halo_start(e, buf):
        @pl.when(d < n_dp - 1)
        def _():
            halo_down(e, buf).start()

        @pl.when(d > 0)
        def _():
            halo_up(e, buf).start()

    def halo_finish(e, buf):
        @pl.when(d > 0)
        def _():
            halo_down(e, buf).wait_recv()

        @pl.when(d < n_dp - 1)
        def _():
            halo_up(e, buf).wait_recv()

        shift_in(lambda j: r.halo[e % 2, 0, :, lane_at(j)].astype(F32), buf, 0)
        shift_in(lambda j: r.halo[e % 2, 1, :, lane_at(j)].astype(F32), buf, 3)

    def halo_sent(e, buf):
        @pl.when(d < n_dp - 1)
        def _():
            halo_down(e, buf).wait_send()

        @pl.when(d > 0)
        def _():
            halo_up(e, buf).wait_send()

    def ex_copy(k, step, owner):
        turn = (k + 1) % 5 % 2
        return remote(
            r.ex_out.at[k],
            r.ex_in.at[k, owner],
            r.ex_s.at[turn],
            r.ex_r.at[turn],
            (s, rem(d + step, n_dp)),
        )

    def ex_sent(k):
        ex_all(k, r.ex_s)

    def ex_all(k, sem):
        view = r.ex_in.at[k, 0 : n_dp - 1]
        pltpu.make_async_copy(view, view, sem.at[(k + 1) % 5 % 2]).wait()

    def ex_start(k):
        if k in (1, 2, 3):
            ex_sent((4, 0, 1)[k - 1])
        for step in range(1, n_dp):
            ex_copy(k, step, d).start()
        r.ex_in[k, d] = r.ex_out[k]

    def ex_finish(k):
        ex_all(k, r.ex_r)
        total = r.ex_in[k, 0]
        for i in range(1, n_dp):
            total = total + r.ex_in[k, i]
        return [
            jnp.concatenate([total[i * n_lane + j : i * n_lane + j + 1] for j in range(n_lane)], 1)
            for i in range(2)
        ]

    def ex_put(k, i, j, value):
        r.ex_out[k, pl.ds(i * n_lane + j, 1), :] = value

    def conv_forward(xc, w, h, row, part, k=None):
        span = 3 * width
        acc = None
        for a in range(3):
            block = a + row
            if (block in (0, 3)) != (part == 1):
                continue
            term = dot(xc[block * cols : (block + 1) * cols, :], w[a * span : (a + 1) * span, :])
            acc = term if acc is None else acc + term
        add_to(h, row, part, acc, k)

    def add_to(out, row, part, acc, k=None):
        for j in range(n_lane):
            at = (j, slice(row * cols, (row + 1) * cols), slice(None))
            piece = acc[:, j * lanes : (j + 1) * lanes]
            if part == 1:
                piece = out[at] + piece
            out[at] = piece
            if k is not None:
                kept = jnp.where(valid_rows(row * cols, cols), piece, 0.0)
                for i, value in enumerate((kept, kept * piece)):
                    value = jnp.sum(value, 0, keepdims=True)
                    if row == 1:
                        value = value + r.ex_out[k, i * n_lane + j : i * n_lane + j + 1, :]
                    ex_put(k, i, j, value)

    def conv_back(dc, w, row, part):
        acc = None
        for a in range(3):
            block = 2 - a + row
            if (block in (0, 3)) != (part == 1):
                continue
            for b in range(3):
                term = dot_nt(
                    dc[block * cols : (block + 1) * cols, (2 - b) * width : (3 - b) * width],
                    w[(3 * a + b) * width : (3 * a + b + 1) * width, :],
                )
                acc = term if acc is None else acc + term
        add_to(r.fbuf, row, part, acc)

    quarter_rows = pixels // 4

    def norm_of(sums, layer):
        total = r.total[0:1, :]
        centre = sums[0] / total
        inverse = lax.rsqrt(sums[1] / total - centre * centre + EPS)
        r.norm[layer, 0:1, :] = centre
        r.norm[layer, 1:2, :] = inverse
        r.norm[layer, 2:3, :] = gain[layer : layer + 1, :] * inverse
        r.norm[layer, 3:4, :] = 1.0 / total

    def corner_rows(k):
        return pl.ds((k // 2) * cols + k % 2, windows, stride=2)

    def picked(ref, j):
        out = None
        which = pick_ref[...]
        for k in range(4):
            part = jnp.where(which == k, ref[j, corner_rows(k), :], 0.0)
            out = part if out is None else out + part
        return out

    loads[2].wait()

    def image_row(i):
        def value(j):
            v = r.g1[image_at + i * cols : image_at + (i + 1) * cols, lane_at(j)].astype(F32)
            return jnp.where(valid_rows(i * cols, cols), v, 0.0)

        return value

    shift_in(image_row(0), r.xc0, 1)
    shift_in(image_row(1), r.xc0, 2)
    r.ex_out[4] = jnp.broadcast_to(count.astype(F32), (8, lanes))
    ex_start(4)
    loads[0].wait()
    loads[1].wait()
    for l in range(2):
        for t in range(tasks):
            r.gp[pl.ds(ex_row(d, l, t), e_rows), :] = r.est[l, t].astype(BF16)
            for k in range(n_sub):
                r.gp[pl.ds(sq_row(d, l, t), e_rows), k * lanes : (k + 1) * lanes] = r.sst[
                    l, t, k * e_rows : (k + 1) * e_rows, :
                ].astype(BF16)
    cast_conv(1, r.w1)
    ag_z(0, 1)

    @pl.when(at_end)
    def _():
        ag_start(2)

    ag_y(0, 1)
    for item in small:
        item.wait()
    wide = 2 * lanes
    pick_row = jnp.concatenate(
        [picks[s].astype(F32), jnp.zeros((1, wide - windows), F32)], axis=1
    )
    pick_tile = jnp.broadcast_to(pick_row, (lanes, wide)).T[:windows, :].astype(jnp.int32)
    pick_ref[...] = pick_tile
    slot_pick = (
        (pick_tile // 2) * cols
        + 2 * lax.broadcasted_iota(jnp.int32, (windows, lanes), 0)
        + pick_tile % 2
    )
    r.mp[...] = jnp.where(slot_pick < count, 1.0, 0.0).astype(F32)
    ag_z(0, 2)
    ag_z(2, 1, from_end, legs=False)
    ag_r(0, 1)
    ag_y(0, 2)
    ag_z(0, 3)

    @pl.when(in_middle)
    def _():
        ag_start(2)

    halo_start(0, r.xc0)
    ag_q(0, 1)
    ag_z(2, 2, both(in_middle), legs=False)
    ag_y(0, 3)
    ag_r(0, 2)
    ag_p(0, 1)
    ag_r(0, 3)
    ag_q(0, 2)
    ag_l(2, 1, from_end)
    ag_z(2, 1, not_from_end)
    ag_l(2, 2, both(in_middle))
    r.total[...] = jnp.concatenate([ex_finish(4)[0]] * 8, axis=0)
    ag_p(0, 2)
    ag_y(2, 1)
    ag_q(0, 3)
    ag_p(0, 3)
    ag_sib(0)
    ag_z(2, 3)
    conv_forward(r.xc0, r.w0, r.h0, 0, 0)
    conv_forward(r.xc0, r.w0, r.h0, 1, 0)
    ag_z(2, 2, both(at_end))
    ag_r(2, 1)
    halo_finish(0, r.xc0)
    ag_y(2, 2, both(in_middle))
    ag_y(2, 3)
    conv_forward(r.xc0, r.w0, r.h0, 0, 1, 0)
    conv_forward(r.xc0, r.w0, r.h0, 1, 1, 0)
    ex_start(0)
    halo_sent(0, r.xc0)
    ag_start(1)
    ag_y(2, 2, both(at_end))
    ag_q(2, 1)
    ag_r(2, 2, both(in_middle))
    ag_r(2, 3)
    norm_of(ex_finish(0), 0)

    def block_0(j, _):
        lane = lane_at(j)
        for i in range(4):
            rows = slice(i * quarter_rows, (i + 1) * quarter_rows)
            normed = (r.h0[j, rows, :] - r.norm[0, 0:1, lane]) * r.norm[
                0, 2:3, lane
            ] + bias[0:1, lane]
            t = gelu_tanh(normed)
            ok = valid_rows(i * quarter_rows, quarter_rows)
            g = 0.5 * normed * (1.0 + t)
            r.fbuf[j, rows, :] = jnp.where(ok, g, 0.0).astype(BF16).astype(F32)
            r.slope0[j, rows, :] = t
        return 0

    def block_0_rest(j, _):
        lane = lane_at(j)
        for i in range(4):
            rows = slice(i * quarter_rows, (i + 1) * quarter_rows)
            normed = (r.h0[j, rows, :] - r.norm[0, 0:1, lane]) * r.norm[0, 2:3, lane] + bias[
                0:1, lane
            ]
            slope = gelu_slope(normed, r.slope0[j, rows, :])
            ok = valid_rows(i * quarter_rows, quarter_rows)
            r.slope0[j, rows, :] = jnp.where(ok, slope, 0.0)
        f1p = picked(r.fbuf, j)
        r.f1p[:, lane] = f1p
        r.f1b[:, lane] = f1p.astype(BF16)
        return 0

    lax.fori_loop(0, n_lane, block_0, 0)
    shift_in(lambda j: r.fbuf[j, 0:cols, :], r.xc1, 1)
    shift_in(lambda j: r.fbuf[j, cols : 2 * cols, :], r.xc1, 2)
    halo_start(1, r.xc1)
    ag_r(2, 2, both(at_end))
    ag_p(2, 1)
    ag_q(2, 2)
    for step in range(1, n_z):
        ag_z(1, step)
    lax.fori_loop(0, n_lane, block_0_rest, 0)
    ag_q(2, 3)
    ag_p(2, 2)
    for step in range(1, n_z):
        ag_y(1, step)
    ag_p(2, 3)
    ag_sib(2)
    conv_forward(r.xc1, r.w1, r.h1, 0, 0)
    for step in range(1, n_z):
        ag_r(1, step)
    conv_forward(r.xc1, r.w1, r.h1, 1, 0)
    halo_finish(1, r.xc1)
    conv_forward(r.xc1, r.w1, r.h1, 0, 1, 1)
    conv_forward(r.xc1, r.w1, r.h1, 1, 1, 1)
    ex_start(1)
    for step in range(1, n_z):
        ag_q(1, step)
    for hop in range(1, n_z):
        ag_p(1, hop)
    ag_sib(1)

    def unpack(i, _):
        for l in range(2):
            for t in range(tasks):
                r.ex_w[l, t, pl.ds(al(i * e_rows, 16), e_rows), :] = r.gp[
                    pl.ds(ex_row(i, l, t), e_rows), :
                ]
                for k in range(n_sub):
                    r.sq_w[
                        l,
                        pl.ds(al(i * s_rows + k * e_rows, 16), e_rows),
                        t * bottle : (t + 1) * bottle,
                    ] = r.gp[pl.ds(sq_row(i, l, t), e_rows), k * lanes : (k + 1) * lanes]
        return 0

    lax.fori_loop(0, n_dp, unpack, 0)
    mask_pick = jnp.concatenate([r.mp[...]] * n_lane, axis=1)
    g, slope = gelu_pair(dot(r.f1b[...], r.sq_w[0]))
    r.excited0[...] = g.astype(BF16)
    r.eslope0[...] = slope

    def task_lane(t):
        return pl.ds(al(t * bottle, lanes), bottle)

    def gate_0(t, _):
        value = jax.nn.sigmoid(dot(r.excited0[:, task_lane(t)], r.ex_w[0, t]))
        r.gate0[t] = value
        r.t1[t] = (mask_pick * value * r.f1p[...]).astype(BF16)
        return 0

    for t in range(tasks):
        gate_0(t, 0)
    norm_of(ex_finish(1), 1)

    for kind in range(3):
        ag_end(kind)
    for p in plane:
        pl.semaphore_signal(r.ready, inc=1, device_id=(p, d), device_id_type=MESH)
    pl.semaphore_signal(r.ready, inc=1, device_id=(s, sib), device_id_type=MESH)

    def block_1(j, _):
        lane = lane_at(j)
        off = picked(r.h1, j) - r.norm[1, 0:1, lane]
        g, slope = gelu_pair(off * r.norm[1, 2:3, lane] + bias[1:2, lane])
        r.f2p[:, lane] = (r.mp[...] * g).astype(BF16).astype(F32)
        r.slope1[:, lane] = r.mp[...] * slope
        r.centred1[:, lane] = off * r.norm[1, 1:2, lane]
        return 0

    lax.fori_loop(0, n_lane, block_1, 0)
    grads = [r.w1, r.gp, r.g1]

    def pair_of(k):
        return z_at((2, 1, 3, 0)[k])

    def rs_a_copy(kind, k, core):
        return remote(
            shard(kind, grads[kind], 2 * pair_of(k) + core),
            r.ra[kind].at[k],
            r.ag_zs.at[kind, k],
            r.ag_zr.at[kind, k] if k < n_z - 1 else r.ag_or.at[kind],
            (s, sib),
        )

    def again(first, second, i):
        per = 6 * (n_z - 1)
        if i < 3 * per:
            return first.at[i // per, i % per]
        i, per = i - 3 * per, 4 * (n_z - 1)
        return second.at[i // per, i % per]

    def rs_b_copy(kind, k, way):
        o = 2 * pair_of(k) + c
        half = (0, 0, 1, 1, 0, 1)[way]
        to = plane[(0, 0, 1, 1, 1, 0)[way]]
        q = to if way in (0, 2, 4, 5) else plane[2]
        return remote(
            quarter(kind, grads[kind], o, q).at[:, halves[half]],
            r.rb[kind].at[k, way],
            again(r.ag_ps, r.ag_ss, (kind * n_z + k) * 6 + way),
            again(r.ag_pr, r.ag_sr, (kind * n_z + k) * 6 + way),
            (to, d),
        )

    def rs_c_copy(kind, k):
        return remote(
            r.qs[kind].at[k],
            r.rc[kind].at[k],
            r.rs_cs.at[kind, k],
            r.rs_cr.at[kind, k],
            (s, 2 * pair_of(k) + c),
        )

    def d_sem(kind, leg):
        return (kind * n_z + leg // 4) * 6 + leg % 4

    def rs_d_copy(kind, leg, q):
        rows = shard_rows[kind] // 4
        half = (0, 1, 1, 0, 0, 1)[leg]
        to = plane[(0, 1, 0, 1, 1, 0)[leg]]
        view = out_reduced[kind].at[pl.ds(al(q * rows, 16), rows), halves[half]]
        i = d_sem(kind, leg)
        return remote(
            view, view, again(r.ag_ps, r.ag_ss, i), again(r.ag_pr, r.ag_sr, i), (to, d)
        )

    def conv_weight(kind, xc, k):
        tile = 2 * shard_rows[kind] // 3
        per = 3 * width // tile

        for i in range(3):
            g = pair_of(k) * 3 + i
            a = g // per
            term = dot_tn(
                xc[pl.ds(al(a * cols, 16), pixels), pl.ds(al((g % per) * tile, lanes), tile)],
                r.dc[cols : 3 * cols, width : 2 * width],
            )
            grads[kind][pl.ds(al(g * tile, 16), tile), :] = term.astype(BF16)

    def rs_a(kind, k):
        rs_a_copy(kind, k, 1 - c).start()

    def rs_b(kind, k):
        rs_a_copy(kind, k, c).wait_recv()
        rows = shard_rows[kind]
        tile = rows // 4
        start = (2 * pair_of(k) + c) * rows

        def body(i, _):
            at = pl.ds(al(start + i * tile, 16), tile)
            grads[kind][at, :] = (
                grads[kind][at, :].astype(F32)
                + r.ra[kind][k, pl.ds(al(i * tile, 16), tile), :].astype(F32)
            ).astype(BF16)
            return 0

        lax.fori_loop(0, 4, body, 0)
        for way in range(4):
            rs_b_copy(kind, k, way).start()

    def quarter_at(kind, k, q):
        rows = shard_rows[kind]
        return pl.ds(al((2 * pair_of(k) + c) * rows + q * (rows // 4), 16), rows // 4)

    def rs_r(kind, k):
        for half in range(2):
            rs_b_copy(kind, k, 2 * half).wait_recv()
            rs_b_copy(kind, k, 2 * half + 1).wait_recv()
            at = quarter_at(kind, k, plane[1 - half])
            grads[kind][at, halves[half]] = (
                grads[kind][at, halves[half]].astype(F32)
                + r.rb[kind][k, 2 * half + 1].astype(F32)
            ).astype(BF16)
            rs_b_copy(kind, k, 4 + half).start()

    def rs_c(kind, k):
        at = quarter_at(kind, k, s)
        parts = []
        for half in range(2):
            rs_b_copy(kind, k, 4 + half).wait_recv()
            parts.append(
                grads[kind][at, halves[half]].astype(F32)
                + r.rb[kind][k, 2 * half].astype(F32)
                + r.rb[kind][k, 4 + half].astype(F32)
            )
        total = jnp.concatenate(parts, axis=1)
        if k < n_z - 1:
            r.qs[kind][k] = total.astype(BF16)
            rs_c_copy(kind, k).start()
        else:
            r.qf[kind][...] = total

    def rs_d(kind):
        total = r.qf[kind][...]
        for k in range(n_z - 1):
            rs_c_copy(kind, k).wait_recv()
            total = total + r.rc[kind][k].astype(F32)
        rows = shard_rows[kind] // 4
        out_reduced[kind][pl.ds(al(s * rows, 16), rows), :] = total.astype(BF16)
        for leg in range(6):
            rs_b_copy(kind, leg // 4, leg % 4).wait_send()
        for leg in range(2 if kind == 0 else 4):
            rs_d_copy(kind, leg, s).start()

    def rs_dr(kind):
        if kind == 0:
            for leg in range(2):
                rs_d_copy(kind, leg, s).wait_send()
            for leg in range(2, 4):
                rs_d_copy(kind, leg, s).start()
        for leg in range(2):
            rs_d_copy(kind, leg, plane[leg]).wait_recv()
            rs_d_copy(kind, 4 + leg, plane[leg]).start()

    def rs_e(kind):
        for leg in range(2):
            rs_d_copy(kind, 2 + leg, plane[leg]).wait_recv()
            rs_d_copy(kind, 4 + leg, plane[2]).wait_recv()

    def rs_end(kind):
        for k in range(n_z):
            rs_a_copy(kind, k, 1 - c).wait_send()
            for way in range((4, 2, 0, 0)[k], 6):
                rs_b_copy(kind, k, way).wait_send()
            if k < n_z - 1:
                rs_c_copy(kind, k).wait_send()
        for leg in range(2 if kind == 0 else 0, 4):
            rs_d_copy(kind, leg, s).wait_send()
        for leg in range(2):
            rs_d_copy(kind, 4 + leg, plane[leg]).wait_send()

    for item in loads[3:]:
        item.wait()
    r.df2[...] = jnp.zeros_like(r.df2)

    def pack_grads(l, t, grad_squeeze, grad_expand):
        r.fbuf[0, 0:width, :] = grad_squeeze
        for j in range(n_lane):
            r.fbuf[1, j * bottle : (j + 1) * bottle, :] = grad_expand[:, j * lanes : (j + 1) * lanes]

        def body(i, _):
            for j in range(n_lane):
                lane = slice(j * lanes, (j + 1) * lanes)
                r.gp[pl.ds(ex_row(i, l, t), e_rows), lane] = r.fbuf[
                    1, pl.ds(al(j * bottle + i * e_rows, 16), e_rows), :
                ].astype(BF16)
            for k in range(n_sub):
                r.gp[pl.ds(sq_row(i, l, t), e_rows), k * lanes : (k + 1) * lanes] = r.fbuf[
                    0, pl.ds(al(i * s_rows + k * e_rows, 16), e_rows), :
                ].astype(BF16)
            return 0

        lax.fori_loop(0, n_dp, body, 0)

    def kept(i):
        return pl.ds(al(i * windows, 16), windows)

    def gate_1(t, _):
        w_s = r.sq_w[1, :, task_lane(t)]
        w_e = r.ex_w[1, t]
        f2p = r.f2p[...]
        source = (f2p + r.t1[t].astype(F32)).astype(BF16)
        g, slope = gelu_pair(dot(source, w_s))
        excited = g.astype(BF16)
        value = jax.nn.sigmoid(dot(excited, w_e))
        field = mask_pick * f2p
        d_task = r.g1[cot_at + t * windows : cot_at + (t + 1) * windows, :].astype(F32)
        out_task[0, t] = (value * field).astype(BF16)
        d_expanded = (d_task * field * value * (1.0 - value)).astype(BF16)
        d_squeezed = (slope * dot_nt(d_expanded, w_e)).astype(BF16)
        d_source = dot_nt(d_squeezed, w_s)
        r.t1[t] = d_source.astype(BF16)
        r.df2[...] += d_source + mask_pick * d_task * value
        r.g1[kept(t), :] = source
        r.g1[kept(tasks + t), :] = d_expanded
        r.g1[kept(2 * tasks), task_lane(t)] = excited
        r.g1[kept(2 * tasks + 1), task_lane(t)] = d_squeezed
        return 0

    def gate_1_weight(t, _):
        pack_grads(
            1,
            t,
            dot_tn(r.g1[kept(t), :], r.g1[kept(2 * tasks + 1), task_lane(t)]),
            dot_tn(r.g1[kept(2 * tasks), task_lane(t)], r.g1[kept(tasks + t), :]),
        )
        return 0

    for t in range(tasks):
        gate_1(t, 0)
    def back_1(j, _):
        lane = lane_at(j)
        d_norm = r.slope1[:, lane] * r.df2[:, lane].astype(BF16).astype(F32)
        r.df2[:, lane] = d_norm
        ex_put(2, 0, j, jnp.sum(d_norm, 0, keepdims=True))
        ex_put(2, 1, j, jnp.sum(d_norm * r.centred1[:, lane], 0, keepdims=True))
        return 0

    lax.fori_loop(0, n_lane, back_1, 0)
    ex_start(2)

    r.df1[...] = jnp.zeros_like(r.df1)

    def gate_0_back(t, _):
        w_s = r.sq_w[0, :, task_lane(t)]
        w_e = r.ex_w[0, t]
        value = r.gate0[t]
        d_task = r.t1[t].astype(F32)
        excited = r.excited0[:, task_lane(t)]
        d_expanded = (d_task * (mask_pick * r.f1p[...]) * value * (1.0 - value)).astype(BF16)
        d_squeezed = (r.eslope0[:, task_lane(t)] * dot_nt(d_expanded, w_e)).astype(BF16)
        r.df1[...] += dot_nt(d_squeezed, w_s) + mask_pick * d_task * value
        pack_grads(0, t, dot_tn(r.f1b[...], d_squeezed), dot_tn(excited, d_expanded))
        return 0

    for t in range(tasks):
        gate_0_back(t, 0)
    for t in range(tasks):
        gate_1_weight(t, 0)

    r.sums[...] = jnp.zeros_like(r.sums)

    def back_terms(k, layer):
        sums = ex_finish(k)
        r.sums[2 * layer : 2 * layer + 1, :] = sums[0]
        r.sums[2 * layer + 1 : 2 * layer + 2, :] = sums[1]
        scale = gain[layer : layer + 1, :] * r.norm[layer, 3:4, :] * r.norm[layer, 1:2, :]
        r.norm[layer, 4:5, :] = scale * sums[0]
        r.norm[layer, 5:6, :] = scale * r.norm[layer, 1:2, :] * sums[1]

    pl.semaphore_wait(r.ready, 4)
    for k in range(n_z):
        rs_a(1, k)
    back_terms(2, 1)

    def hidden_grad_1(j, _):
        lane = lane_at(j)
        norm = r.norm
        for k in range(4):
            at = corner_rows(k)
            spread = jnp.where(pick_ref[...] == k, r.df2[:, lane] * norm[1, 2:3, lane], 0.0)
            value = spread - (
                norm[1, 4:5, lane] + (r.h1[j, at, :] - norm[1, 0:1, lane]) * norm[1, 5:6, lane]
            )
            slot = (k // 2) * cols + k % 2 + 2 * lax.broadcasted_iota(
                jnp.int32, (windows, lanes), 0
            )
            r.fbuf[j, at, :] = jnp.where(slot < count, value, 0.0)
        return 0

    lax.fori_loop(0, n_lane, hidden_grad_1, 0)
    shift_in(lambda j: r.fbuf[j, 0:cols, :], r.dc, 1)
    shift_in(lambda j: r.fbuf[j, cols : 2 * cols, :], r.dc, 2)
    halo_sent(1, r.xc1)
    halo_start(2, r.dc)

    for k in range(n_z):
        rs_b(1, k)
    for k in range(2):
        conv_weight(2, r.xc1, k)
        rs_a(2, k)
    conv_back(r.dc, r.w1, 0, 0)
    rs_b(2, 0)
    conv_back(r.dc, r.w1, 1, 0)
    for k in range(n_z):
        rs_r(1, k)
    rs_b(2, 1)
    halo_finish(2, r.dc)
    conv_back(r.dc, r.w1, 0, 1)
    conv_back(r.dc, r.w1, 1, 1)
    def back_0(j, _):
        lane = lane_at(j)
        norm = r.norm
        first = jnp.zeros((1, lanes), F32)
        second = jnp.zeros((1, lanes), F32)
        for k in range(4):
            at = corner_rows(k)
            d_field = r.fbuf[j, at, :].astype(BF16).astype(F32) + jnp.where(
                pick_ref[...] == k, r.df1[:, lane], 0.0
            )
            d_norm = r.slope0[j, at, :] * d_field.astype(BF16).astype(F32)
            r.fbuf[j, at, :] = d_norm
            centred = (r.h0[j, at, :] - norm[0, 0:1, lane]) * norm[0, 1:2, lane]
            first = first + jnp.sum(d_norm, 0, keepdims=True)
            second = second + jnp.sum(d_norm * centred, 0, keepdims=True)
        ex_put(3, 0, j, first)
        ex_put(3, 1, j, second)
        return 0

    lax.fori_loop(0, n_lane, back_0, 0)
    ex_start(3)
    conv_weight(2, r.xc1, 2)
    rs_a(2, 2)
    rs_r(2, 0)
    conv_weight(2, r.xc1, 3)
    rs_a(2, 3)
    rs_b(2, 2)
    halo_sent(2, r.dc)
    back_terms(3, 0)

    def sums_copy(p, q):
        return remote(
            r.sums,
            r.sums_in.at[q],
            r.sums_s.at[p],
            r.sums_r.at[p],
            (plane[p], d),
        )

    for p in range(3):
        sums_copy(p, s).start()
    r.sums_in[s] = r.sums[...]

    def hidden_grad_0(row):
        def value(j):
            lane = lane_at(j)
            norm = r.norm
            rows = slice(row * cols, (row + 1) * cols)
            out = r.fbuf[j, rows, :] * norm[0, 2:3, lane] - (
                norm[0, 4:5, lane] + (r.h0[j, rows, :] - norm[0, 0:1, lane]) * norm[0, 5:6, lane]
            )
            return jnp.where(valid_rows(row * cols, cols), out, 0.0)

        return value

    shift_in(hidden_grad_0(0), r.dc, 1)
    shift_in(hidden_grad_0(1), r.dc, 2)
    halo_start(3, r.dc)
    conv_weight(0, r.xc0, 0)
    rs_a(0, 0)
    rs_r(2, 1)
    rs_b(2, 3)
    for k in range(n_z):
        rs_c(1, k)
    conv_weight(0, r.xc0, 1)
    rs_a(0, 1)
    rs_c(2, 0)
    conv_weight(0, r.xc0, 2)
    rs_a(0, 2)
    rs_r(2, 2)
    rs_b(0, 0)
    conv_weight(0, r.xc0, 3)
    rs_a(0, 3)
    rs_c(2, 1)
    conv_back(r.dc, r.w0, 0, 0)
    rs_r(2, 3)
    rs_b(0, 1)
    conv_back(r.dc, r.w0, 1, 0)
    rs_c(2, 2)
    halo_finish(3, r.dc)
    conv_back(r.dc, r.w0, 0, 1)
    conv_back(r.dc, r.w0, 1, 1)
    def image_out(j, _):
        lane = lane_at(j)
        for i in range(4):
            rows = slice(i * quarter_rows, (i + 1) * quarter_rows)
            out_image[0, rows, lane] = jnp.where(
                valid_rows(i * quarter_rows, quarter_rows), r.fbuf[j, rows, :], 0.0
            ).astype(BF16)
        return 0

    lax.fori_loop(0, n_lane, image_out, 0)
    rs_r(0, 0)
    rs_b(0, 2)
    rs_c(2, 3)
    rs_r(0, 1)
    rs_c(0, 0)
    rs_b(0, 3)
    rs_r(0, 2)
    rs_c(0, 1)
    rs_r(0, 3)
    rs_c(0, 2)
    rs_d(1)
    rs_d(2)
    rs_c(0, 3)
    rs_dr(1)
    rs_dr(2)
    rs_d(0)
    for p in range(3):
        sums_copy(p, plane[p]).wait_recv()
    total = r.sums_in[0]
    for i in range(1, 4):
        total = total + r.sums_in[i]
    for l in range(2):
        out_bias[l : l + 1, :] = total[2 * l : 2 * l + 1, :]
        out_gain[l : l + 1, :] = total[2 * l + 1 : 2 * l + 2, :]
    for p in range(3):
        sums_copy(p, s).wait_send()
    ex_sent(2)
    ex_sent(3)
    halo_sent(3, r.dc)
    rs_dr(0)
    for kind in (1, 2, 0):
        rs_e(kind)
        rs_end(kind)


def finish_kernel(
    dims,
    task,
    image,
    reduced_0,
    reduced_1,
    reduced_2,
    gain,
    bias,
    out_task,
    out_image,
    out_conv,
    out_squeeze,
    out_expand,
    out_gain,
    out_bias,
    conv_wide,
    squeeze_wide,
    expand_wide,
    sem,
):
    lanes = 128
    e_rows = dims.bottle // dims.n_dp
    outs = []

    def store(src, dst):
        outs.append(pltpu.make_async_copy(src, dst, sem.at[len(outs)]))
        outs[-1].start()

    store(task, out_task)
    store(image, out_image)
    for layer, reduced in enumerate((reduced_0, reduced_2)):
        conv_wide[layer] = reduced[...].astype(F32)
        store(conv_wide.at[layer], out_conv.at[layer])
    for l in range(2):
        for t in range(dims.tasks):
            at = (l * dims.tasks + t) * e_rows
            expand_wide[l, t] = reduced_1[at : at + e_rows, :].astype(F32)
            at = at + 2 * dims.tasks * e_rows
            for k in range(dims.width // dims.n_dp // e_rows):
                squeeze_wide[l, t, k * e_rows : (k + 1) * e_rows, :] = reduced_1[
                    at : at + e_rows, k * lanes : (k + 1) * lanes
                ].astype(F32)
    store(squeeze_wide, out_squeeze)
    store(expand_wide, out_expand)
    out_gain[...] = gain[...]
    out_bias[...] = bias[...]
    for copy in outs:
        copy.wait()


def fused(images, counts, pool_index, conv_w, squeeze_w, expand_w, gain, bias, cotangent):
    n_dp = lax.axis_size("dp")
    micro, pixels, width = images.shape
    tasks, bottle = squeeze_w.shape[1], squeeze_w.shape[3]
    cols = 2 * pool_index.shape[2]
    windows = cols // 2
    conv_rows = conv_w.shape[1]
    gate_rows = 4 * tasks * expand_w.shape[2]
    shard_rows = (conv_rows, gate_rows, conv_rows)
    n_z = n_dp // 2
    vm = pltpu.VMEM
    dma = pltpu.SemaphoreType.DMA
    scratch = dict(
        load=dma((9 + 2 * (width // 128) + tasks,)),
        counts=pltpu.SMEM((micro,), jnp.int32),
        picks=vm(pool_index.shape, jnp.int32),
        gain=vm(gain.shape, F32),
        bias=vm(bias.shape, F32),
        sst=vm(squeeze_w.shape, F32),
        est=vm(expand_w.shape, F32),
        w0=vm((n_dp * conv_rows, width), BF16),
        gp=vm((n_dp * gate_rows, width), BF16),
        w1=vm((n_dp * conv_rows, width), BF16),
        g1=vm((n_dp * conv_rows, width), BF16),
        sq_w=vm((2, width, tasks * bottle), BF16),
        ex_w=vm((2, tasks, bottle, width), BF16),
        ag_zs=dma((3, 2 * (n_z - 1))),
        ag_zr=dma((3, n_z - 1)),
        ag_ps=dma((3, 6 * (n_z - 1))),
        ag_pr=dma((3, 6 * (n_z - 1))),
        ag_ss=dma((3, 4 * (n_z - 1))),
        ag_sr=dma((3, 4 * (n_z - 1))),
        ag_os=dma((3,)),
        ag_or=dma((3,)),
        mp=vm((windows, 128), F32),
        pick=vm((windows, 128), jnp.int32),
        halo=vm((2, 2, cols, width), BF16),
        halo_s=dma((2, 2)),
        halo_r=dma((2, 2)),
        ex_out=vm((5, 8, 128), F32),
        ex_in=vm((5, n_dp, 8, 128), F32),
        total=vm((8, width), F32),
        ex_s=dma((2,)),
        ex_r=dma((2,)),
        norm=vm((2, 8, width), F32),
        xc0=vm((4 * cols, 3 * width), BF16),
        xc1=vm((4 * cols, 3 * width), BF16),
        dc=vm((4 * cols, 3 * width), BF16),
        h0=vm((width // 128, pixels, 128), F32),
        h1=vm((width // 128, pixels, 128), F32),
        slope0=vm((width // 128, pixels, 128), F32),
        fbuf=vm((width // 128, pixels, 128), F32),
        f1p=vm((windows, width), F32),
        f1b=vm((windows, width), BF16),
        excited0=vm((windows, tasks * bottle), BF16),
        eslope0=vm((windows, tasks * bottle), F32),
        gate0=vm((tasks, windows, width), F32),
        t1=vm((tasks, windows, width), BF16),
        f2p=vm((windows, width), F32),
        slope1=vm((windows, width), F32),
        centred1=vm((windows, width), F32),
        df2=vm((windows, width), F32),
        df1=vm((windows, width), F32),
        sums=vm((8, width), F32),
        sums_in=vm((4, 8, width), F32),
        sums_s=dma((3,)),
        sums_r=dma((3,)),
        ready=pltpu.SemaphoreType.REGULAR,
        rs_cs=dma((3, n_z - 1)),
        rs_cr=dma((3, n_z - 1)),
    )
    quarters = [rows // 4 for rows in shard_rows]
    scratch.update(
        ra=[vm((n_z, rows, width), BF16) for rows in shard_rows],
        rb=[vm((n_z, 6, rows, width // 2), BF16) for rows in quarters],
        qs=[vm((n_z - 1, rows, width), BF16) for rows in quarters],
        qf=[vm((rows, width), F32) for rows in quarters],
        rc=[vm((n_z - 1, rows, width), BF16) for rows in quarters],
    )
    buffers, tree = jax.tree.flatten(scratch, is_leaf=lambda v: not isinstance(v, (dict, list)))
    dims = types.SimpleNamespace(
        tree=tree,
        n_dp=n_dp,
        cols=cols,
        pixels=pixels,
        width=width,
        tasks=tasks,
        bottle=bottle,
        shard_rows=shard_rows,
    )
    any_spec = pl.BlockSpec(memory_space=pl.ANY)
    vmem_spec = pl.BlockSpec(memory_space=pltpu.VMEM)
    results = pl.pallas_call(
        functools.partial(step_kernel, dims),
        out_shape=(
            vm((1, tasks, windows, width), BF16),
            vm((1, pixels, width), BF16),
            *[vm((rows, width), BF16) for rows in shard_rows],
            vm(gain.shape, F32),
            vm(bias.shape, F32),
        ),
        in_specs=[any_spec] * 9,
        out_specs=(vmem_spec,) * 7,
        scratch_shapes=tuple(buffers),
        compiler_params=pltpu.CompilerParams(
            collective_id=0, has_side_effects=True, vmem_limit_bytes=VMEM_BYTES
        ),
    )(counts.reshape(micro), pool_index, gain, bias, images, conv_w, squeeze_w, expand_w, cotangent)
    results = [pltpu.with_memory_space_constraint(v, pltpu.VMEM) for v in results]
    return pl.pallas_call(
        functools.partial(finish_kernel, dims),
        out_shape=(
            jax.ShapeDtypeStruct((1, tasks, windows, width), BF16),
            jax.ShapeDtypeStruct((1, pixels, width), BF16),
            jax.ShapeDtypeStruct(conv_w.shape, F32),
            jax.ShapeDtypeStruct(squeeze_w.shape, F32),
            jax.ShapeDtypeStruct(expand_w.shape, F32),
            jax.ShapeDtypeStruct(gain.shape, F32),
            jax.ShapeDtypeStruct(bias.shape, F32),
        ),
        in_specs=[vmem_spec] * 7,
        out_specs=(any_spec,) * 5 + (vmem_spec,) * 2,
        scratch_shapes=(
            vm(conv_w.shape, F32),
            vm(squeeze_w.shape, F32),
            vm(expand_w.shape, F32),
            dma((6,)),
        ),
        compiler_params=pltpu.CompilerParams(vmem_limit_bytes=16 * 1024 * 1024),
    )(*results)


def fits_kernel(mesh, args):
    images, counts, pool_index, conv_w, squeeze_w, expand_w = args[:6]
    sections, n_dp = mesh.shape["section"], mesh.shape["dp"]
    conv_rows = conv_w.shape[1] // n_dp
    e_rows = expand_w.shape[2] // n_dp
    return (
        sections == 4
        and images.shape[0] == sections
        and n_dp % 2 == 0
        and pool_index.shape[1] == n_dp
        and conv_rows % 64 == 0
        and e_rows == 16
        and squeeze_w.shape[2] // n_dp == 4 * e_rows
        and squeeze_w.shape[3] == 128
        and images.shape[2] == 4 * 128
    )


def solution(mesh):
    placed = (
        P(None, "dp", None),
        P(None, "dp"),
        P(None, "dp", None),
        P(None, "dp", None),
        P(None, None, "dp", None),
        P(None, None, "dp", None),
        P(),
        P(),
        P(None, None, "dp", None),
    )
    def run(*args):
        return mapped(fused if fits_kernel(mesh, args) else on_device)(*args)

    def mapped(body):
        return jax.shard_map(
        body,
        mesh=mesh,
        in_specs=placed,
        out_specs=(
            P("section", None, "dp", None),
            P("section", "dp", None),
            P(None, "dp", None),
            P(None, None, "dp", None),
            P(None, None, "dp", None),
            P(),
            P(),
        ),
        check_vma=False,
    )

    return run
```
